32 devices in a mesh: dp: 8 (over z, y), chan: 4 (over x, core).
Axes of the slice: x: 2, y: 2, z: 4, core: 2. Of those that a mesh axis runs over, the one named last changes fastest.
Arguments:
- feat_fine: bfloat16 [8, 128, 1600], P('dp', 'chan'), may hold values from -6 to 6
- feat_mid: bfloat16 [8, 256, 400], P('dp', 'chan'), may hold values from -6 to 6
- feat_coarse: bfloat16 [8, 512, 100], P('dp', 'chan'), may hold values from -6 to 6
- image_units: int32 [8], P('dp'), may hold values from 6 to 10, as said below
- stem_fine: bfloat16 [128, 128], P('chan'), may hold values from -0.5 to 0.5
- stem_mid: bfloat16 [128, 256], P('chan'), may hold values from -0.375 to 0.375
- stem_coarse: bfloat16 [128, 512], P('chan'), may hold values from -0.25 to 0.25
- conv_weights: bfloat16 [3, 4, 9, 128, 128], P(None, None, None, 'chan'), may hold values from -0.1875 to 0.1875
- norm_gains: float32 [3, 5, 128], P(None, None, 'chan'), may hold values from 0.1 to 1.9
- norm_shifts: float32 [3, 5, 128], P(None, None, 'chan'), may hold values from -3 to 3
- class_weights: bfloat16 [3, 80, 128], P(None, 'chan'), may hold values from -0.5 to 0.5
- class_bias: float32 [3, 80], P(None, 'chan'), may hold values from -3 to 3
- box_weights: bfloat16 [3, 5, 128], P(None, None, 'chan'), may hold values from -0.5 to 0.5
- box_bias: float32 [3, 5], replicated, may hold values from -3 to 3
- class_cot: bfloat16 [8, 80, 2100], P('dp', 'chan'), may hold values from -6 to 6
- box_cot: bfloat16 [8, 5, 2100], P('dp'), may hold values from -6 to 6
Outputs:
- class_out: bfloat16 [8, 80, 2100], P('dp', 'chan')
- box_out: bfloat16 [8, 5, 2100], P('dp')
- grad_fine: bfloat16 [8, 128, 1600], P('dp', 'chan')
- grad_mid: bfloat16 [8, 256, 400], P('dp', 'chan')
- grad_coarse: bfloat16 [8, 512, 100], P('dp', 'chan')
- grad_stem_fine: float32 [128, 128], P('chan')
- grad_stem_mid: float32 [128, 256], P('chan')
- grad_stem_coarse: float32 [128, 512], P('chan')
- grad_conv: float32 [3, 4, 9, 128, 128], P(None, None, None, 'chan')
- grad_gains: float32 [3, 5, 128], P(None, None, 'chan')
- grad_shifts: float32 [3, 5, 128], P(None, None, 'chan')
- grad_class_weights: float32 [3, 80, 128], P(None, 'chan')
- grad_class_bias: float32 [3, 80], P(None, 'chan')
- grad_box_weights: float32 [3, 5, 128], P(None, None, 'chan')
- grad_box_bias: float32 [3, 5], replicated
The draws below stay inside these ranges and needn't reach their ends.
Inputs may be any that keep to these rules, and one draw needn't show every extreme that they name: `image_units`: each entry is 6, 8 or 10; both 6 and 10 occur in every draw.
All inputs are finite; a program needn't handle non-finite values.
Results may differ from the reference program's by a relative error of at most 0.024.
Values may be sent and summed in bfloat16 or wider, within the bound.
No kernel may reach another device: no remote copies, remote signals or barrier semaphores. Data moves between devices by JAX's collectives and lax.ppermute only.
A program may use at most 576 MiB of HBM per device.

```python
import math
from functools import partial
import jax
import jax.numpy as jnp
from jax import lax

CIN0 = 128
CIN1 = 256
CIN2 = 512
HID = 128
CLASSES = 80
BOXES = 5
S_SMALL = 6
S_MID = 8
S_LARGE = 10
IMAGES = 8
P0 = 1600
P1 = 400
P2 = 100
PIX = 2100


def draw_image_units(key, part):
    key = jax.random.fold_in(key, 7)
    first_key, second_key = jax.random.split(key)
    picks = jax.random.randint(first_key, (IMAGES,), 0, 3)
    side_table = jnp.array([S_SMALL, S_MID, S_LARGE], dtype=jnp.int32)
    drawn = side_table[picks]
    spot_index = jax.random.randint(second_key, (), 0, IMAGES)
    drawn = drawn.at[spot_index].set(S_LARGE)
    drawn = drawn.at[(spot_index + 1) % IMAGES].set(S_SMALL)
    return drawn.astype(jnp.int32)


def block_scale(stream_key, extent, cuts, smallest, high):
    factor_of = 1.0
    for position, parts in cuts:
        draws = jax.random.uniform(jax.random.fold_in(jax.random.fold_in(stream_key, 6), position), (parts,), jnp.float32, smallest / len(cuts), high / len(cuts))
        factor_of = factor_of * jnp.repeat(jnp.exp(draws), extent[position] // parts).reshape((-1,) + (1,) * (len(extent) - 1 - position))
    return factor_of


def normal_values(own_key, shape, width, reach, cuts=(), kind=jnp.bfloat16):
    values = jax.random.normal(own_key, shape, jnp.float32) * width
    if len(cuts) > 0:
        values = block_scale(own_key, shape, cuts, -0.22, 0.18) * values
    return jnp.clip(values, min=-reach, max=reach).astype(kind)


def setup_inputs(seed: int = 0) -> dict:
    keys = jax.random.split(jax.random.key(seed), 17)
    feat_fine = normal_values(keys[0], (IMAGES, CIN0, P0), 1.0, 6.0, ((0, 8), (1, 4)))
    feat_mid = normal_values(keys[1], (IMAGES, CIN1, P1), 1.0, 6.0, ((0, 8), (1, 4)))
    feat_coarse = normal_values(keys[2], (IMAGES, CIN2, P2), 1.0, 6.0, ((0, 8), (1, 4)))
    image_units = draw_image_units(jax.random.fold_in(keys[16], 71), 0)
    stem_fine = normal_values(keys[4], (HID, CIN0), CIN0 ** -0.5, 0.5, ((0, 4),))
    stem_mid = normal_values(keys[5], (HID, CIN1), CIN1 ** -0.5, 0.375, ((0, 4),))
    stem_coarse = normal_values(keys[6], (HID, CIN2), CIN2 ** -0.5, 0.25, ((0, 4),))
    conv_weights = normal_values(keys[7], (3, 4, 9, HID, HID), (9 * HID) ** -0.5, 0.1875, ((3, 4),))
    norm_gains = jnp.clip(1.0 + 0.18 * jax.random.normal(keys[8], (3, 5, HID), jnp.float32), 0.1, 1.9)
    norm_shifts = normal_values(keys[9], (3, 5, HID), 0.5, 3.0, ((2, 4),), jnp.float32)
    class_weights = normal_values(keys[10], (3, CLASSES, HID), HID ** -0.5, 0.5, ((1, 4),))
    class_bias = normal_values(keys[11], (3, CLASSES), 0.5, 3.0, ((1, 4),), jnp.float32)
    box_weights = normal_values(keys[12], (3, BOXES, HID), HID ** -0.5, 0.5, ((2, 4),))
    box_bias = normal_values(keys[13], (3, BOXES), 0.5, 3.0, (), jnp.float32)
    class_cot = normal_values(keys[14], (IMAGES, CLASSES, PIX), 1.0, 6.0, ((0, 8), (1, 4)))
    box_cot = normal_values(keys[15], (IMAGES, BOXES, PIX), 1.0, 6.0, ((0, 8),))
    return {"feat_fine": feat_fine, "feat_mid": feat_mid, "feat_coarse": feat_coarse, "image_units": image_units, "stem_fine": stem_fine, "stem_mid": stem_mid, "stem_coarse": stem_coarse, "conv_weights": conv_weights, "norm_gains": norm_gains, "norm_shifts": norm_shifts, "class_weights": class_weights, "class_bias": class_bias, "box_weights": box_weights, "box_bias": box_bias, "class_cot": class_cot, "box_cot": box_cot}


epsilon = 0.001
layout = ('NCHW', 'OIHW', 'NCHW')
highest = lax.Precision.HIGHEST

@jax.custom_vjp
def low(v):
    return lax.optimization_barrier(v.astype(jnp.bfloat16)).astype(jnp.float32)

@jax.custom_vjp
def low_back(v):
    return v

def low_keep(v):
    return (low(v), None)

def low_pass(kept, grad):
    return (grad,)

def back_keep(v):
    return (v, None)

def back_low(kept, grad):
    return (low(grad),)
low.defvjp(low_keep, low_pass)
low_back.defvjp(back_keep, back_low)

def level_mask(image_units, level_id):
    edge_len = S_LARGE * 2 ** (2 - level_id)
    pixels = jnp.arange(edge_len * edge_len, dtype=jnp.int32)
    row_at = pixels // edge_len
    col_at = pixels % edge_len
    bounds = image_units * 2 ** (2 - level_id)
    inside = (row_at[None, :] < bounds[:, None]) & (col_at[None, :] < bounds[:, None])
    return inside.astype(jnp.float32)[:, None, :]

def conv_apply(values, weights):
    images, channels, pixels = values.shape
    edge_len = math.isqrt(pixels)
    planes = values.reshape(images, channels, edge_len, edge_len)
    kernel = weights.reshape(3, 3, weights.shape[1], weights.shape[2]).transpose(2, 3, 0, 1)
    output = lax.conv_general_dilated(planes, kernel, (1, 1), ((1, 1), (1, 1)), dimension_numbers=layout, precision=highest)
    return output.reshape(images, weights.shape[1], pixels)

def norm_act(values, valid_mask, total_count, gain_row, bias_term):
    first_sum = lax.optimization_barrier(jnp.sum(values * valid_mask, axis=(0, 2)))
    second = lax.optimization_barrier(jnp.sum(values * values * valid_mask, axis=(0, 2)))
    center = first_sum / total_count
    inv_std = lax.rsqrt(second / total_count - center * center + epsilon)
    normed = (values - center[None, :, None]) * inv_std[None, :, None]
    shifted = normed * gain_row[None, :, None] + bias_term[None, :, None]
    return low(jax.nn.silu(shifted) * valid_mask)

@jax.checkpoint
def stem_layer(features, weights, valid_mask, total_count, gain_row, bias_term):
    values = low_back(jnp.einsum('oc,ncp->nop', weights, features, precision=highest))
    return norm_act(values, valid_mask, total_count, gain_row, bias_term)

@jax.checkpoint
def conv_layer(features, weights, valid_mask, total_count, gain_row, bias_term):
    values = low_back(conv_apply(features, weights))
    return norm_act(values, valid_mask, total_count, gain_row, bias_term)

def head_forward(feature_set, stem_set, conv_weights, norm_gains, norm_shifts, class_weights, class_bias, box_weights, box_bias, masks=None, counts=None):
    class_parts = []
    box_parts = []
    for level_id in range(3):
        valid_mask = masks[level_id]
        total_count = counts[level_id]
        stem_act = stem_layer(feature_set[level_id], stem_set[level_id], valid_mask, total_count, norm_gains[level_id, 0], norm_shifts[level_id, 0])
        class_one = conv_layer(stem_act, conv_weights[level_id, 0], valid_mask, total_count, norm_gains[level_id, 1], norm_shifts[level_id, 1])
        box_one = conv_layer(stem_act, conv_weights[level_id, 2], valid_mask, total_count, norm_gains[level_id, 3], norm_shifts[level_id, 3])
        class_two = conv_layer(class_one, conv_weights[level_id, 1], valid_mask, total_count, norm_gains[level_id, 2], norm_shifts[level_id, 2])
        box_two = conv_layer(box_one, conv_weights[level_id, 3], valid_mask, total_count, norm_gains[level_id, 4], norm_shifts[level_id, 4])
        class_logits = jnp.einsum('kc,ncp->nkp', class_weights[level_id], class_two, precision=highest)
        class_parts.append((class_logits + class_bias[level_id][None, :, None]) * valid_mask)
        box_logits = jnp.einsum('kc,ncp->nkp', box_weights[level_id], box_two, precision=highest)
        box_parts.append((box_logits + box_bias[level_id][None, :, None]) * valid_mask)
    return (jnp.concatenate(class_parts, axis=2), jnp.concatenate(box_parts, axis=2))

def reference(feat_fine, feat_mid, feat_coarse, image_units, stem_fine, stem_mid, stem_coarse, conv_weights, norm_gains, norm_shifts, class_weights, class_bias, box_weights, box_bias, class_cot, box_cot):
    masks = [level_mask(image_units, level_id) for level_id in range(3)]
    counts = [jnp.sum(valid_mask) for valid_mask in masks]
    forward = partial(head_forward, masks=masks, counts=counts)
    feature_set = (feat_fine.astype(jnp.float32), feat_mid.astype(jnp.float32), feat_coarse.astype(jnp.float32))
    stem_set = (stem_fine.astype(jnp.float32), stem_mid.astype(jnp.float32), stem_coarse.astype(jnp.float32))
    outputs, pullback = jax.vjp(forward, feature_set, stem_set, conv_weights.astype(jnp.float32), norm_gains.astype(jnp.float32), norm_shifts.astype(jnp.float32), class_weights.astype(jnp.float32), class_bias.astype(jnp.float32), box_weights.astype(jnp.float32), box_bias.astype(jnp.float32))
    grads = pullback((class_cot.astype(jnp.float32), box_cot.astype(jnp.float32)))
    grad_feats, grad_stems, grad_conv, grad_gains, grad_shifts, grad_cw, grad_cb, grad_bw, grad_bb = grads
    return (outputs[0].astype(jnp.bfloat16), outputs[1].astype(jnp.bfloat16), grad_feats[0].astype(jnp.bfloat16), grad_feats[1].astype(jnp.bfloat16), grad_feats[2].astype(jnp.bfloat16), grad_stems[0], grad_stems[1], grad_stems[2], grad_conv, grad_gains, grad_shifts, grad_cw, grad_cb, grad_bw, grad_bb)
```

```python
import functools

import jax
import jax.numpy as jnp
from jax import lax
from jax.experimental import pallas as pl
from jax.experimental.pallas import tpu as pltpu
from jax.sharding import PartitionSpec as P

BF = jnp.bfloat16
F32 = jnp.float32
EPS = 0.001
ST = 48
ROWS = 40
PX = ST * ROWS
CR = 8
CH = CR * ST
NCH = ROWS // CR
SLOT = (0, 0, 0, 1, 1)
CUT = 24 * ST
CP = 1664
MID = 512
E0, E1, E2 = 40, 20, 10
WIDE = CP + 768
CLS = CP + 512
NT = (((1,), (1,)), ((), ()))
TN = (((0,), (0,)), ((), ()))


def dot(a, b, dims=(((1,), (0,)), ((), ()))):
    return lax.dot_general(a, b, dims, preferred_element_type=F32)


def limits(meta, slot):
    group, units = meta[0], meta[3]
    if slot == 0:
        edge = jnp.where(group == 0, 4 * units, 2 * units)
        return edge, edge
    return (
        jnp.where(group == 0, 4 * units, 24 + units),
        jnp.where(group == 0, 4 * units, units),
    )


def mask_of(meta, j):
    row_end, col_end = limits(meta, SLOT[j])
    row = lax.broadcasted_iota(jnp.int32, (CR, ST, 128), 0) + CR * j
    col = lax.broadcasted_iota(jnp.int32, (CR, ST, 128), 1)
    inside = (row < row_end) & (col < col_end)
    return jnp.where(inside, 1.0, 0.0).reshape(CH, 128)


def pick(meta, first, second):
    total = first + second
    return jnp.where(meta[0] == 0, total, first), jnp.where(meta[0] == 0, total, second)


def level_rows(meta, base, layer):
    fine = meta[0] == 0
    return base + layer + jnp.where(fine, 0, 5), base + layer + jnp.where(fine, 0, 10)


def norm_constants(meta, st, par, layer, cst):
    total = jnp.sum(st[...], axis=0)
    row = [total[i : i + 1] for i in range(6)]
    first = pick(meta, row[0], row[1])
    second = pick(meta, row[2], row[3])
    count = pick(meta, row[4], row[5])
    gain_at = level_rows(meta, 0, layer)
    shift_at = level_rows(meta, 16, layer)
    for s in range(2):
        rn = 1.0 / count[s]
        mean = first[s] * rn
        inv = lax.rsqrt(second[s] * rn - mean * mean + EPS)
        cst[s : s + 1] = mean
        cst[2 + s : 3 + s] = inv
        cst[4 + s : 5 + s] = par[pl.ds(gain_at[s], 1), :]
        cst[6 + s : 7 + s] = par[pl.ds(shift_at[s], 1), :]
        cst[8 + s : 9 + s] = rn
        cst[10 + s : 11 + s] = count[s]
    cst[12:16] = jnp.zeros((4, 128), F32)


def normed(cst, y, s):
    xhat = (y - cst[s : s + 1]) * cst[2 + s : 3 + s]
    return xhat, xhat * cst[4 + s : 5 + s] + cst[6 + s : 7 + s]


def sigmoid(z):
    return 0.5 * jnp.tanh(0.5 * z) + 0.5


def slope(z):
    s = sigmoid(z)
    return s * (1.0 + z * (1.0 - s))


def spread_out(st, rows):
    block = jnp.concatenate(rows + [jnp.zeros((8 - len(rows), 128), F32)], axis=0)
    st[...] = jnp.broadcast_to(block[None], st.shape)


def colsum(v):
    return jnp.sum(v, axis=0, keepdims=True)


def guard(field, shifts):
    field[0:8] = jnp.zeros((8, 128), F32)
    field[8 + PX : 16 + PX] = jnp.zeros((8, 128), F32)
    for k in range(3):
        shifts[k, 0:ST] = jnp.zeros((ST, 128), BF)
        shifts[k, ST + PX :] = jnp.zeros((ST, 128), BF)


def fill_shifts(field, shifts):
    for k in range(3):
        for j in range(NCH):
            at = 8 + CH * j + k - 1
            shifts[k, ST + CH * j : ST + CH * (j + 1)] = field[at : at + CH].astype(BF)


def taps(shifts, begin, size, back=False):
    parts = []
    for kr in range(3):
        for kc in range(3):
            k, r = (2 - kc, 1 - kr) if back else (kc, kr - 1)
            at = ST + begin + ST * r
            parts.append(shifts[k, at : at + size])
    return jnp.concatenate(parts, axis=1)


def slices_of(meta):
    c = meta[2]
    return (c, c ^ 2, c ^ 1, c ^ 3)


def at32(s, extra=0):
    return pl.ds(pl.multiple_of(32 * s + extra, 32), 32)


def weight_slot(meta, j):
    return jnp.where(meta[0] == 0, 0, SLOT[j])


def to_compact(meta, canvas, out):
    @pl.when(meta[0] == 0)
    def _():
        for r in range(E0):
            out[E0 * r : E0 * (r + 1)] = canvas[ST * r : ST * r + E0]

    @pl.when(meta[0] == 1)
    def _():
        for r in range(E1):
            out[E1 * r : E1 * (r + 1)] = canvas[ST * r : ST * r + E1]
        for r in range(E2):
            at = CUT + ST * r
            out[MID + E2 * r : MID + E2 * (r + 1)] = canvas[at : at + E2]


def to_canvas(meta, compact, out):
    @pl.when(meta[0] == 0)
    def _():
        for r in range(E0):
            out[ST * r : ST * r + E0] = compact[E0 * r : E0 * (r + 1)]

    @pl.when(meta[0] == 1)
    def _():
        for r in range(E1):
            out[ST * r : ST * r + E1] = compact[E1 * r : E1 * (r + 1)]
        for r in range(E2):
            at = CUT + ST * r
            out[at : at + E2] = compact[MID + E2 * r : MID + E2 * (r + 1)]


def load_inputs(meta, pieces, feat, stem):
    for s, u in zip(slices_of(meta), pieces):

        @pl.when(meta[0] == 0)
        def _():
            feat[at32(s), :] = u[:, 0:CP]
            stem[at32(s), 0:128] = u[:, CP : CP + 128]

        @pl.when(meta[0] == 1)
        def _():
            for i in range(2):
                at = pl.ds(pl.multiple_of(64 * s + 32 * i, 32), 32)
                feat[at, 0:MID] = u[:, MID * i : MID * (i + 1)]
            for i in range(4):
                at = pl.ds(pl.multiple_of(128 * s + 32 * i, 32), 32)
                feat[at, MID : MID + 128] = u[:, 1024 + 128 * i : 1152 + 128 * i]
            stem[at32(s), :] = u[:, CP : CP + 768]


def stem_kernel(meta, u0, u1, u2, u3, y, st, feat, stem, flat):
    load_inputs(meta, (u0, u1, u2, u3), feat, stem)
    y[...] = jnp.zeros((PX, 128), F32)

    @pl.when(meta[0] == 0)
    def _():
        flat[...] = dot(stem[:, 0:128], feat[0:128, :]).T

    @pl.when(meta[0] == 1)
    def _():
        flat[0:MID] = dot(stem[:, 0:256], feat[0:256, 0:MID]).T
        flat[MID : MID + 128] = dot(stem[:, 256:768], feat[0:512, MID : MID + 128]).T

    to_canvas(meta, flat, y)
    sums = [jnp.zeros((1, 128), F32) for _ in range(6)]
    for j in range(NCH):
        m = mask_of(meta, j)
        v = y[CH * j : CH * (j + 1)] * m
        s = SLOT[j]
        sums[s] += colsum(v)
        sums[2 + s] += colsum(v * v)
        sums[4 + s] += colsum(m)
    spread_out(st, sums)


def forward_kernel(first, meta, y, st, *refs):
    if first:
        p0, p1, p2, p3, cnt = refs[:5]
        refs = refs[5:]
    else:
        par, cnt = refs[:2]
        refs = refs[2:]
    w = refs[:4]
    act, out, st_out, cst = refs[4:8]
    refs = refs[8:]
    if first:
        par = refs[0]
        refs = refs[1:]
        par[...] = p0[...] + p1[...] + p2[...] + p3[...]
    field, shifts, weights = refs
    layer = 0 if first else 1 + 2 * meta[1]
    norm_constants(meta, st, par, layer, cst)
    guard(field, shifts)
    for j in range(NCH):
        rows = slice(CH * j, CH * (j + 1))
        _, z = normed(cst, y[rows], SLOT[j])
        v = z * sigmoid(z) * mask_of(meta, j)
        act[rows] = v.astype(BF)
        field[8 + CH * j : 8 + CH * (j + 1)] = v
    fill_shifts(field, shifts)
    for s, piece in zip(slices_of(meta), w):
        for slot in range(2):
            for t in range(9):
                weights[slot, at32(s), 128 * t : 128 * (t + 1)] = piece[slot, t]
    sums = [jnp.zeros((1, 128), F32) for _ in range(4)]
    for j in range(NCH):
        v = dot(taps(shifts, CH * j, CH), weights[weight_slot(meta, j)], NT)
        out[CH * j : CH * (j + 1)] = v
        v = v * mask_of(meta, j)
        s = SLOT[j]
        sums[s] += colsum(v)
        sums[2 + s] += colsum(v * v)
    spread_out(st_out, sums + [cnt[0:1], cnt[1:2]])


def heads_kernel(meta, y, st, par, k0, k1, k2, k3, logits, dz, st_out, cst, gw, cot, wp, x2, field, flat):
    norm_constants(meta, st, par, 2 + 2 * meta[1], cst)
    cot[...] = jnp.zeros((128, CP), BF)
    wp[...] = jnp.zeros((2, 128, 256), BF)

    @pl.when(meta[1] == 0)
    def _():
        for s, k in zip(slices_of(meta), (k0, k1, k2, k3)):
            cot[at32(s), :] = k[:, 0:CP]
            for slot in range(2):
                wp[slot, at32(s), :] = k[:, CP + 256 * slot : CP + 256 * (slot + 1)]

    @pl.when(meta[1] == 1)
    def _():
        cot[0:32, :] = k0[:, 0:CP]
        fine = meta[0] == 0
        for slot in range(2):
            rows = jnp.where(fine, par[32:37], par[37 + 5 * slot : 42 + 5 * slot])
            rows = jnp.concatenate([rows, jnp.zeros((27, 128), F32)], axis=0).astype(BF)
            wp[slot, 0:32, 0:128] = rows
            wp[slot, 0:32, 128:256] = k0[:, CP + 256 * slot + 128 : CP + 256 * (slot + 1)]

    for part in range(2):
        for j in range(NCH):
            m = mask_of(meta, j)
            if part == 0:
                _, z = normed(cst, y[CH * j : CH * (j + 1)], SLOT[j])
                m = z * sigmoid(z) * m
            field[CH * j : CH * (j + 1)] = m
        flat[...] = jnp.zeros((CP, 128), F32)
        to_compact(meta, field, flat)
        x2[:, 128 * part : 128 * (part + 1)] = flat[...].astype(BF)

    @pl.when(meta[0] == 0)
    def _():
        logits[...] = dot(wp[0], x2[...], NT).astype(BF)
        gw[0] = dot(cot[...], x2[...])
        gw[1] = jnp.zeros((128, 256), F32)
        flat[...] = dot(cot[...], wp[0, :, 0:128], TN)

    @pl.when(meta[0] == 1)
    def _():
        logits[...] = jnp.zeros((128, CP), BF)
        for slot, a, b in ((0, 0, MID), (1, MID, MID + 128)):
            logits[:, a:b] = dot(wp[slot], x2[a:b], NT).astype(BF)
            gw[slot] = dot(cot[:, a:b], x2[a:b])
            flat[a:b] = dot(cot[:, a:b], wp[slot, :, 0:128], TN)

    field[...] = jnp.zeros((PX, 128), F32)
    to_canvas(meta, flat, field)
    sums = [jnp.zeros((1, 128), F32) for _ in range(4)]
    for j in range(NCH):
        rows = slice(CH * j, CH * (j + 1))
        s = SLOT[j]
        xhat, z = normed(cst, y[rows], s)
        v = field[rows] * slope(z) * mask_of(meta, j)
        dz[rows] = v
        sums[s] += colsum(v)
        sums[2 + s] += colsum(v * xhat)
    spread_out(st_out, sums)


def grad_sums(meta, total, sums):
    shift = pick(meta, total[0:1], total[1:2])
    gain = pick(meta, total[2:3], total[3:4])
    sums[...] = jnp.concatenate(list(shift) + list(gain) + [jnp.zeros((4, 128), F32)], axis=0)


def input_grad(meta, dz, y, cst, sums, j):
    s = SLOT[j]
    xhat, _ = normed(cst, y[CH * j : CH * (j + 1)], s)
    factor = cst[4 + s : 5 + s] * cst[2 + s : 3 + s]
    mean = (sums[s : s + 1] + xhat * sums[2 + s : 3 + s]) * cst[8 + s : 9 + s]
    return mask_of(meta, j) * factor * (dz - mean)


def backward_kernel(last, meta, dz, y, cst, st, w0, w1, w2, w3, act, y_in, cst_in, *refs):
    grad, st_out, sums, wg, field, shifts, weights, dyt = refs
    grad_sums(meta, jnp.sum(st[...], axis=0), sums)
    guard(field, shifts)
    for j in range(NCH):
        rows = slice(CH * j, CH * (j + 1))
        v = input_grad(meta, dz[rows], y, cst, sums, j)
        field[8 + CH * j : 8 + CH * (j + 1)] = v
        dyt[:, rows] = v.T.astype(BF)
    fill_shifts(field, shifts)
    for s, piece in zip(slices_of(meta), (w0, w1, w2, w3)):
        for slot in range(2):
            for t in range(9):
                weights[slot, at32(s, 128 * t), :] = piece[slot, t]
    total = [jnp.zeros((1, 128), F32) for _ in range(4)]
    for j in range(NCH):
        rows = slice(CH * j, CH * (j + 1))
        s = SLOT[j]
        v = dot(taps(shifts, CH * j, CH, True), weights[weight_slot(meta, j)])
        xhat, z = normed(cst_in, y_in[rows], s)
        d = v * slope(z) * mask_of(meta, j)
        grad[rows] = v.astype(BF) if last else d
        total[s] += colsum(d)
        total[2 + s] += colsum(d * xhat)
    spread_out(st_out, total)
    for j in range(NCH):
        field[8 + CH * j : 8 + CH * (j + 1)] = act[CH * j : CH * (j + 1)].astype(F32)
    fill_shifts(field, shifts)
    for slot, a, b in ((0, 0, CUT), (1, CUT, PX)):
        v = dot(dyt[:, a:b], taps(shifts, a, b - a))
        for t in range(9):
            wg[slot, t] = v[:, 128 * t : 128 * (t + 1)]

    @pl.when(meta[0] == 0)
    def _():
        wg[0] = wg[0] + wg[1]


def final_kernel(meta, d0, d1, y, cst, st0, st1, u0, u1, u2, u3, own, other, gs, sums, feat, stem, field, flat, dyt, gf):
    load_inputs(meta, (u0, u1, u2, u3), feat, stem)
    grad_sums(meta, jnp.sum(st0[...] + st1[...], axis=0), sums)
    for j in range(NCH):
        rows = slice(CH * j, CH * (j + 1))
        _, z = normed(cst, y[rows], SLOT[j])
        v = (d0[rows].astype(F32) + d1[rows].astype(F32)) * slope(z) * mask_of(meta, j)
        field[rows] = input_grad(meta, v, y, cst, sums, j)
    flat[...] = jnp.zeros((CP, 128), F32)
    to_compact(meta, field, flat)
    dyt[...] = flat[...].T.astype(BF)
    c = meta[2]
    outs = ((own, c), (other, c ^ 2))

    @pl.when(meta[0] == 0)
    def _():
        gf[0:128, :] = dot(stem[:, 0:128], dyt[...], TN).astype(BF)
        gs[:, 0:128] = dot(dyt[...], feat[0:128, :], NT)
        gs[:, 128:768] = jnp.zeros((128, 640), F32)
        for out, s in outs:
            out[...] = gf[at32(s), :]

    @pl.when(meta[0] == 1)
    def _():
        gf[0:256, 0:MID] = dot(stem[:, 0:256], dyt[:, 0:MID], TN).astype(BF)
        gf[:, MID : MID + 128] = dot(stem[:, 256:768], dyt[:, MID : MID + 128], TN).astype(BF)
        gs[:, 0:256] = dot(dyt[:, 0:MID], feat[0:256, 0:MID], NT)
        gs[:, 256:768] = dot(dyt[:, MID : MID + 128], feat[:, MID : MID + 128], NT)
        for out, s in outs:
            out[...] = jnp.zeros((32, CP), BF)
            for i in range(2):
                at = pl.ds(pl.multiple_of(64 * s + 32 * i, 32), 32)
                out[:, MID * i : MID * (i + 1)] = gf[at, 0:MID]
            for i in range(4):
                at = pl.ds(pl.multiple_of(128 * s + 32 * i, 32), 32)
                out[:, 1024 + 128 * i : 1152 + 128 * i] = gf[at, MID : MID + 128]


def call(body, outs, scratch, args):
    specs = [pl.BlockSpec(memory_space=pltpu.SMEM)]
    specs += [pl.BlockSpec(memory_space=pltpu.VMEM)] * (len(args) - 1)
    return pl.pallas_call(
        body,
        out_shape=[jax.ShapeDtypeStruct(s, d) for s, d in outs],
        in_specs=specs,
        out_specs=[pl.BlockSpec(memory_space=pltpu.VMEM)] * len(outs),
        scratch_shapes=[pltpu.VMEM(s, d) for s, d in scratch],
        compiler_params=pltpu.CompilerParams(vmem_limit_bytes=56 * 2**20),
    )(*args)


def lanes(v, size):
    return jnp.pad(v, ((0, 0), (0, size - v.shape[1])))


def rows(v, size):
    return jnp.pad(v, ((0, size - v.shape[0]), (0, 0)))


def triple(v):
    high = lax.reduce_precision(v, 8, 7)
    mid = lax.reduce_precision(v - high, 8, 7)
    return jnp.stack([high, mid, v - high - mid], axis=1).astype(BF)


def shards(f0, f1, f2, units, s0, s1, s2, conv, gains, shifts, cw, cb, bw, bb, ccot, bcot):
    dp = lax.axis_size("dp")
    c = lax.axis_index("chan")
    group, branch = c // 2, c % 2
    fine = group == 0
    meta = jnp.stack([group, branch, c, units[0]]).astype(jnp.int32)

    def across(v):
        return lax.ppermute(v, "chan", [(i, i ^ 2) for i in range(4)])

    def beside(v, pairs=((0, 1), (1, 0), (2, 3), (3, 2))):
        return lax.ppermute(v, "chan", list(pairs))

    def exchange(st):
        return lax.all_to_all(st, "dp", 0, 0, tiled=True)

    def bring(keep, send):
        r = across(send)
        return keep, r, beside(keep), beside(r)

    f0, f1, f2 = f0[0], f1[0], f2[0]
    fine_pack = jnp.concatenate([lanes(f0, CP), lanes(s0, 768)], axis=1)
    f1p = lanes(f1, MID)
    f2p = lanes(f2, 128)
    rest_pack = jnp.concatenate(
        [f1p[:32], f1p[32:]] + [f2p[32 * i : 32 * (i + 1)] for i in range(4)] + [jnp.zeros((32, 128), BF), s1, s2], axis=1
    )
    u = bring(jnp.where(fine, fine_pack, rest_pack), jnp.where(fine, rest_pack, fine_pack))

    lane = lax.broadcasted_iota(jnp.int32, (48, 128), 1)
    small = jnp.concatenate(
        [rows(gains.reshape(15, 32), 16), rows(shifts.reshape(15, 32), 16), rows(bw.reshape(15, 32).astype(F32), 16)]
    )
    small = jnp.where(lane // 32 == c, jnp.tile(small, (1, 4)), 0.0)
    par = bring(small, small)

    def pred_pack(cot, first, w_first, b_first, second, w_second, b_second):
        if second is None:
            body = lanes(cot[:, :first], CP)
            w_second, b_second = w_first, b_first
        else:
            body = lanes(jnp.concatenate([lanes(cot[:, first : first + second], MID), cot[:, first + second :]], axis=1), CP)
        return rows(jnp.concatenate([body, w_first, lanes(triple(b_first), 128), w_second, lanes(triple(b_second), 128)], axis=1), 32)

    n0, n1 = f0.shape[1], f1.shape[1]
    fine_cls = pred_pack(ccot[0], n0, cw[0], cb[0], None, None, None)
    rest_cls = pred_pack(ccot[0], n0, cw[1], cb[1], n1, cw[2], cb[2])
    zero = jnp.zeros((5, 128), BF)
    fine_box = pred_pack(bcot[0], n0, zero, bb[0], None, None, None)
    rest_box = pred_pack(bcot[0], n0, zero, bb[1], n1, zero, bb[2])
    own_cls = jnp.where(fine, fine_cls, rest_cls)
    own_box = jnp.where(fine, fine_box, rest_box)
    r = across(jnp.where(fine, rest_cls, fine_cls))
    to_class = ((1, 0), (3, 2))
    pred = (jnp.where(branch == 0, own_cls, own_box), r, beside(own_cls, to_class), beside(r, to_class))

    def conv_pieces(layer):
        mine = lax.dynamic_slice_in_dim(conv[:, layer::2], group, 2, 0)
        theirs = lax.dynamic_slice_in_dim(conv[:, layer::2], 1 - group, 2, 0)
        r = across(theirs)

        def of(v, b):
            return lax.dynamic_index_in_dim(v, b, 1, keepdims=False)

        return of(mine, branch), of(r, branch), beside(of(mine, 1 - branch)), beside(of(r, 1 - branch))

    w1 = conv_pieces(0)
    w2 = conv_pieces(1)

    canvas = (PX, 128)
    stat = (dp, 8, 128)
    half = ((PX + 2 * ST), 128)
    padded = (PX + 16, 128)
    y0, st = call(
        stem_kernel,
        [(canvas, F32), (stat, F32)],
        [((512, CP), BF), ((128, 768), BF), ((CP, 128), F32)],
        (meta, *u),
    )
    cnt = st[0, 4:6]
    st = exchange(st)
    forward_outs = [(canvas, BF), (canvas, F32), (stat, F32), ((16, 128), F32)]
    forward_scratch = [(padded, F32), ((3, *half), BF), ((2, 128, 1152), BF)]
    act0, y1, st, cst0, par = call(
        functools.partial(forward_kernel, True),
        forward_outs + [((48, 128), F32)],
        forward_scratch,
        (meta, y0, st, *par, cnt, *w1),
    )
    st = exchange(st)
    act1, y2, st, cst1 = call(
        functools.partial(forward_kernel, False), forward_outs, forward_scratch, (meta, y1, st, par, cnt, *w2)
    )
    st = exchange(st)
    logits, dz2, st, cst2, gw = call(
        heads_kernel,
        [((128, CP), BF), (canvas, F32), (stat, F32), ((16, 128), F32), ((2, 128, 256), F32)],
        [((128, CP), BF), ((2, 128, 256), BF), ((CP, 256), BF), (canvas, F32), ((CP, 128), F32)],
        (meta, y2, st, par, *pred),
    )
    st = exchange(st)
    backward_scratch = [(padded, F32), ((3, *half), BF), ((2, 1152, 128), BF), ((128, PX), BF)]
    wg_shape = (2, 9, 128, 128)
    dz1, st, sums2, wg2 = call(
        functools.partial(backward_kernel, False),
        [(canvas, F32), (stat, F32), ((8, 128), F32), (wg_shape, F32)],
        backward_scratch,
        (meta, dz2, y2, cst2, st, *w2, act1, y1, cst1),
    )
    st = exchange(st)
    d0, st, sums1, wg1 = call(
        functools.partial(backward_kernel, True),
        [(canvas, BF), (stat, F32), ((8, 128), F32), (wg_shape, F32)],
        backward_scratch,
        (meta, dz1, y1, cst1, st, *w1, act0, y0, cst0),
    )
    d0_other = beside(d0)
    st = exchange(st)
    st_other = beside(st)
    own, other, gs, sums0 = call(
        final_kernel,
        [((32, CP), BF), ((32, CP), BF), ((128, 768), F32), ((8, 128), F32)],
        [((512, CP), BF), ((128, 768), BF), (canvas, F32), ((CP, 128), F32), ((128, CP), BF), ((512, CP), BF)],
        (meta, d0, d0_other, y0, cst0, st, st_other, *u),
    )

    received = across(other)
    g_fine = jnp.where(fine, own, received)
    g_rest = jnp.where(fine, received, own)
    grad_fine = g_fine[:, :n0]
    grad_mid = jnp.concatenate([g_rest[:, 0:n1], g_rest[:, MID : MID + n1]], axis=0)
    grad_coarse = jnp.concatenate([g_rest[:, 1024 + 128 * i : 1024 + 128 * i + f2.shape[1]] for i in range(4)], axis=0)

    blocks = logits.reshape(4, 32, CP)
    far = across(blocks)
    near = beside(blocks)
    far_near = beside(far)
    mine_cls = jnp.where(branch == 0, blocks, near)
    far_cls = jnp.where(branch == 0, far, far_near)
    mine_box = jnp.where(branch == 0, near, blocks)
    far_box = jnp.where(branch == 0, far_near, far)

    def assemble(mine, theirs):
        a = jnp.where(fine, mine, theirs)
        b = jnp.where(fine, theirs, mine)
        return jnp.concatenate([a[:, :n0], b[:, :n1], b[:, MID : MID + f2.shape[1]]], axis=1)

    def take(v, i):
        return lax.dynamic_index_in_dim(v, i, 0, keepdims=False)

    class_out = assemble(take(mine_cls, c)[: ccot.shape[1]], take(far_cls, c)[: ccot.shape[1]])
    box_out = assemble(mine_box[0, :5], far_box[0, :5])

    wg1, wg2, gw, gs = lax.psum((wg1, wg2, gw, gs), "dp")
    wg = jnp.stack([wg1, wg2]).reshape(2, 2, 9, 4, 32, 128).transpose(3, 0, 1, 2, 4, 5)
    wg = lax.all_to_all(wg, "chan", 0, 0, tiled=True)
    grad_conv = jnp.stack(
        [
            jnp.stack([wg[2 * g + b, k, slot] for b in range(2) for k in range(2)])
            for g, slot in ((0, 0), (1, 0), (1, 1))
        ]
    )
    gs = lax.all_to_all(gs.reshape(4, 32, 768), "chan", 0, 0, tiled=True)
    grad_s0 = gs[0, :, 0:128]
    grad_s1 = gs[2, :, 0:256]
    grad_s2 = gs[2, :, 256:768]
    gw = lax.all_gather(gw, "chan")
    gc = jnp.stack([gw[0, 0], gw[2, 0], gw[2, 1]])
    gb = jnp.stack([gw[1, 0], gw[3, 0], gw[3, 1]])
    gc = lax.dynamic_slice_in_dim(gc, 32 * c, 32, 1)[:, : cw.shape[1]]
    grad_cw, grad_cb = gc[:, :, :128], gc[:, :, 128]
    grad_bw = lax.dynamic_slice_in_dim(gb[:, :5], 32 * c, 32, 2)
    grad_bb = gb[:, :5, 128]
    norm = lax.all_gather(jnp.stack([sums0, sums1, sums2]), "chan")
    norm = lax.dynamic_slice_in_dim(norm, 32 * c, 32, 3)

    def norm_out(base):
        return jnp.stack(
            [
                jnp.stack([norm[2 * g, 0, base + s]] + [norm[2 * g + b, k, base + s] for b in range(2) for k in (1, 2)])
                for g, s in ((0, 0), (1, 0), (1, 1))
            ]
        )

    return (
        class_out[None],
        box_out[None],
        grad_fine[None],
        grad_mid[None],
        grad_coarse[None],
        grad_s0,
        grad_s1,
        grad_s2,
        grad_conv,
        norm_out(2),
        norm_out(0),
        grad_cw,
        grad_cb,
        grad_bw,
        grad_bb,
    )


def solution(mesh):
    placed = (
        P("dp", "chan", None),
        P("dp", "chan", None),
        P("dp", "chan", None),
        P("dp"),
        P("chan", None),
        P("chan", None),
        P("chan", None),
        P(None, None, None, "chan", None),
        P(None, None, "chan"),
        P(None, None, "chan"),
        P(None, "chan", None),
        P(None, "chan"),
        P(None, None, "chan"),
        P(),
        P("dp", "chan", None),
        P("dp", None, None),
    )
    return jax.shard_map(
        shards,
        mesh=mesh,
        in_specs=placed,
        out_specs=(
            P("dp", "chan", None),
            P("dp", None, None),
            P("dp", "chan", None),
            P("dp", "chan", None),
            P("dp", "chan", None),
            P("chan", None),
            P("chan", None),
            P("chan", None),
            P(None, None, None, "chan", None),
            P(None, None, "chan"),
            P(None, None, "chan"),
            P(None, "chan", None),
            P(None, "chan"),
            P(None, None, "chan"),
            P(),
        ),
        check_vma=False,
    )
```

```python
import functools

import jax
import jax.numpy as jnp
from jax import lax
from jax.experimental import pallas as pl
from jax.experimental.pallas import tpu as pltpu
from jax.sharding import PartitionSpec as P

BF = jnp.bfloat16
F32 = jnp.float32
EPS = 0.001
ST = 48
ROWS = 40
PX = ST * ROWS
CR = 8
CH = CR * ST
NCH = ROWS // CR
SLOT = (0, 0, 0, 1, 1)
CUT = 24 * ST
CP = 1664
MID = 512
E0, E1, E2 = 40, 20, 10
STEM = 1536
PAR = STEM + 768
WIDE = PAR + 256
CLS = CP + 512
VMEM = 12 * 2**20
WHOLE = 56 * 2**20
OWNER = (0, 2, 1, 3)
NT = (((1,), (1,)), ((), ()))
TN = (((0,), (0,)), ((), ()))


def dot(a, b, dims=(((1,), (0,)), ((), ()))):
    return lax.dot_general(a, b, dims, preferred_element_type=F32)


def limits(meta, slot):
    group, units = meta[0], meta[3]
    if slot == 0:
        edge = jnp.where(group == 0, 4 * units, 2 * units)
        return edge, edge
    return (
        jnp.where(group == 0, 4 * units, 24 + units),
        jnp.where(group == 0, 4 * units, units),
    )


def mask_of(meta, j):
    row_end, col_end = limits(meta, SLOT[j])
    row = lax.broadcasted_iota(jnp.int32, (CR, ST, 128), 0) + CR * j
    col = lax.broadcasted_iota(jnp.int32, (CR, ST, 128), 1)
    inside = (row < row_end) & (col < col_end)
    return jnp.where(inside, 1.0, 0.0).reshape(CH, 128)


def pick(meta, first, second):
    total = first + second
    return jnp.where(meta[0] == 0, total, first), jnp.where(meta[0] == 0, total, second)


def level_rows(meta, base, layer):
    fine = meta[0] == 0
    at = base + 3 * layer
    return at + jnp.where(fine, 0, 1), at + jnp.where(fine, 0, 2)


def norm_constants(meta, st, par, layer, cst):
    total = jnp.sum(st[...], axis=0)
    row = [total[i : i + 1] for i in range(6)]
    first = pick(meta, row[0], row[1])
    second = pick(meta, row[2], row[3])
    count = pick(meta, row[4], row[5])
    gain_at = level_rows(meta, 0, layer)
    shift_at = level_rows(meta, 16, layer)
    for s in range(2):
        rn = 1.0 / count[s]
        mean = first[s] * rn
        inv = lax.rsqrt(second[s] * rn - mean * mean + EPS)
        cst[s : s + 1] = mean
        cst[2 + s : 3 + s] = inv
        cst[4 + s : 5 + s] = par[pl.ds(gain_at[s], 1), :]
        cst[6 + s : 7 + s] = par[pl.ds(shift_at[s], 1), :]
        cst[8 + s : 9 + s] = rn
        cst[10 + s : 11 + s] = count[s]
    cst[12:16] = jnp.zeros((4, 128), F32)


def normed(cst, y, s):
    xhat = (y - cst[s : s + 1]) * cst[2 + s : 3 + s]
    return xhat, xhat * cst[4 + s : 5 + s] + cst[6 + s : 7 + s]


def sigmoid(z):
    return 0.5 * jnp.tanh(0.5 * z) + 0.5


def slope(z):
    s = sigmoid(z)
    return s * (1.0 + z * (1.0 - s))


def spread_out(st, rows):
    block = jnp.concatenate(rows + [jnp.zeros((8 - len(rows), 128), F32)], axis=0)
    st[...] = jnp.broadcast_to(block[None], st.shape)


def colsum(v):
    return jnp.sum(v, axis=0, keepdims=True)


def guard(field, shifts):
    field[0:8] = jnp.zeros((8, 128), F32)
    field[8 + PX : 16 + PX] = jnp.zeros((8, 128), F32)
    for k in range(3):
        shifts[k, 0:ST] = jnp.zeros((ST, 128), BF)
        shifts[k, ST + PX :] = jnp.zeros((ST, 128), BF)


def fill_shifts(field, shifts):
    for k in range(3):
        for j in range(NCH):
            at = 8 + CH * j + k - 1
            shifts[k, ST + CH * j : ST + CH * (j + 1)] = field[at : at + CH].astype(BF)


def taps(shifts, begin, size, back=False):
    parts = []
    for kr in range(3):
        for kc in range(3):
            k, r = (2 - kc, 1 - kr) if back else (kc, kr - 1)
            at = ST + begin + ST * r
            parts.append(shifts[k, at : at + size])
    return jnp.concatenate(parts, axis=1)


def slices_of(meta):
    c = meta[2]
    return (c, c ^ 2, c ^ 1, c ^ 3)


def at32(s, extra=0):
    return pl.ds(pl.multiple_of(32 * s + extra, 32), 32)


def weight_slot(meta, j):
    return jnp.where(meta[0] == 0, 0, SLOT[j])


def to_compact(meta, canvas, out):
    @pl.when(meta[0] == 0)
    def _():
        for r in range(E0):
            out[E0 * r : E0 * (r + 1)] = canvas[ST * r : ST * r + E0]

    @pl.when(meta[0] == 1)
    def _():
        for r in range(E1):
            out[E1 * r : E1 * (r + 1)] = canvas[ST * r : ST * r + E1]
        for r in range(E2):
            at = CUT + ST * r
            out[MID + E2 * r : MID + E2 * (r + 1)] = canvas[at : at + E2]


def to_canvas(meta, compact, out):
    @pl.when(meta[0] == 0)
    def _():
        for r in range(E0):
            out[ST * r : ST * r + E0] = compact[E0 * r : E0 * (r + 1)]

    @pl.when(meta[0] == 1)
    def _():
        for r in range(E1):
            out[ST * r : ST * r + E1] = compact[E1 * r : E1 * (r + 1)]
        for r in range(E2):
            at = CUT + ST * r
            out[at : at + E2] = compact[MID + E2 * r : MID + E2 * (r + 1)]


def load_inputs(meta, pieces, feat, stem):
    for s, u in zip(slices_of(meta), pieces):

        @pl.when(meta[0] == 0)
        def _():
            feat[at32(s), :] = u[:, 0:CP]
            stem[at32(s), 0:128] = u[:, CP : CP + 128]

        @pl.when(meta[0] == 1)
        def _():
            for i in range(2):
                at = pl.ds(pl.multiple_of(64 * s + 32 * i, 32), 32)
                feat[at, 0:MID] = u[:, MID * i : MID * (i + 1)]
            for i in range(4):
                at = pl.ds(pl.multiple_of(128 * s + 32 * i, 32), 32)
                feat[at, MID : MID + 128] = u[:, 1024 + 128 * i : 1152 + 128 * i]
            stem[at32(s), :] = u[:, STEM:PAR]


def stem_kernel(meta, u0, u1, u2, u3, y, st, cnt, par, feat, stem, flat):
    load_inputs(meta, (u0, u1, u2, u3), feat, stem)
    lane = lax.broadcasted_iota(jnp.int32, (32, 128), 1) // 32
    for i in range(2):
        total = jnp.zeros((32, 128), F32)
        for s, u in zip(slices_of(meta), (u0, u1, u2, u3)):
            v = u[:, PAR + 128 * i : PAR + 128 * (i + 1)].astype(F32)
            v = v[:, 0:32] + v[:, 32:64] + v[:, 64:96]
            total = jnp.where(lane == s, jnp.concatenate([v] * 4, axis=1), total)
        par[32 * i : 32 * (i + 1)] = total
    y[...] = jnp.zeros((PX, 128), F32)

    @pl.when(meta[0] == 0)
    def _():
        flat[...] = dot(stem[:, 0:128], feat[0:128, :]).T

    @pl.when(meta[0] == 1)
    def _():
        flat[0:MID] = dot(stem[:, 0:256], feat[0:256, 0:MID]).T
        flat[MID : MID + 128] = dot(stem[:, 256:768], feat[0:512, MID : MID + 128]).T

    to_canvas(meta, flat, y)
    sums = [jnp.zeros((1, 128), F32) for _ in range(6)]
    for j in range(NCH):
        m = mask_of(meta, j)
        v = y[CH * j : CH * (j + 1)] * m
        s = SLOT[j]
        sums[s] += colsum(v)
        sums[2 + s] += colsum(v * v)
        sums[4 + s] += colsum(m)
    spread_out(st, sums)
    cnt[...] = jnp.concatenate(sums[4:6] + [jnp.zeros((6, 128), F32)], axis=0)


def forward_kernel(first, meta, y, st, cnt, w, *refs):
    par, act, out, st_out, cst, field, shifts = refs
    layer = 0 if first else 1 + 2 * meta[1]
    norm_constants(meta, st, par, layer, cst)
    guard(field, shifts)
    for j in range(NCH):
        rows = slice(CH * j, CH * (j + 1))
        _, z = normed(cst, y[rows], SLOT[j])
        v = z * sigmoid(z) * mask_of(meta, j)
        act[rows] = v.astype(BF)
        field[8 + CH * j : 8 + CH * (j + 1)] = v
    fill_shifts(field, shifts)
    sums = [jnp.zeros((1, 128), F32) for _ in range(4)]
    for j in range(NCH):
        v = dot(taps(shifts, CH * j, CH), w[weight_slot(meta, j)], NT)
        out[CH * j : CH * (j + 1)] = v
        v = v * mask_of(meta, j)
        s = SLOT[j]
        sums[s] += colsum(v)
        sums[2 + s] += colsum(v * v)
    spread_out(st_out, sums + [cnt[0:1], cnt[1:2]])


def weight_kernel(layer, meta, mine, near, far, cross, flat, tall):
    group, branch, c = meta[0], meta[1], meta[2]
    conv = 2 * branch + layer
    for slot in range(2):
        level = group + slot
        for t in range(9):
            for s, piece in (
                (c, mine[level, conv, t]),
                (c ^ 1, near[level, conv, t]),
                (c ^ 2, far[slot, branch, t]),
                (c ^ 3, cross[slot, branch, t]),
            ):
                flat[slot, at32(s), 128 * t : 128 * (t + 1)] = piece
                tall[slot, at32(s, 128 * t), :] = piece


def heads_kernel(meta, y, st, par, k0, k1, k2, k3, box_pack, dz, st_out, cst, x2, cot, wp, field, flat):
    norm_constants(meta, st, par, 2 + 2 * meta[1], cst)
    cot[...] = jnp.zeros((128, CP), BF)
    wp[...] = jnp.zeros((2, 128, 256), BF)

    @pl.when(meta[1] == 0)
    def _():
        for s, k in zip(slices_of(meta), (k0, k1, k2, k3)):
            cot[at32(s), :] = k[:, 0:CP]
            for slot in range(2):
                wp[slot, at32(s), :] = k[:, CP + 256 * slot : CP + 256 * (slot + 1)]

    @pl.when(meta[1] == 1)
    def _():
        cot[0:32, :] = box_pack[:, 0:CP]
        fine = meta[0] == 0
        for slot in range(2):
            row = lax.broadcasted_iota(jnp.int32, (32, 128), 0)
            box = jnp.zeros((32, 128), F32)
            for i in range(5):
                at = 32 + 3 * i
                line = jnp.where(fine, par[at : at + 1], par[at + 1 + slot : at + 2 + slot])
                box = jnp.where(row == i, line, box)
            wp[slot, 0:32, 0:128] = box.astype(BF)
            wp[slot, 0:32, 128:256] = box_pack[:, CP + 256 * slot + 128 : CP + 256 * (slot + 1)]

    for part in range(2):
        for j in range(NCH):
            m = mask_of(meta, j)
            if part == 0:
                _, z = normed(cst, y[CH * j : CH * (j + 1)], SLOT[j])
                m = z * sigmoid(z) * m
            field[CH * j : CH * (j + 1)] = m
        flat[...] = jnp.zeros((CP, 128), F32)
        to_compact(meta, field, flat)
        x2[:, 128 * part : 128 * (part + 1)] = flat[...].astype(BF)

    @pl.when(meta[0] == 0)
    def _():
        flat[...] = dot(cot[...], wp[0, :, 0:128], TN)

    @pl.when(meta[0] == 1)
    def _():
        for slot, a, b in ((0, 0, MID), (1, MID, MID + 128)):
            flat[a:b] = dot(cot[:, a:b], wp[slot, :, 0:128], TN)

    field[...] = jnp.zeros((PX, 128), F32)
    to_canvas(meta, flat, field)
    sums = [jnp.zeros((1, 128), F32) for _ in range(4)]
    for j in range(NCH):
        rows = slice(CH * j, CH * (j + 1))
        s = SLOT[j]
        xhat, z = normed(cst, y[rows], s)
        v = field[rows] * slope(z) * mask_of(meta, j)
        dz[rows] = v
        sums[s] += colsum(v)
        sums[2 + s] += colsum(v * xhat)
    spread_out(st_out, sums)


def logits_kernel(meta, x2, cot, wp, gw, mine, far, logits):
    def store(slot, v):
        bias = v[:, 128:256]

        @pl.when(meta[1] == 0)
        def _():
            gw_block(gw, slot, v[:, 0:128])

        @pl.when(meta[1] == 1)
        def _():
            gw_block(gw, slot, v[:, 0:128].T)

        return bias

    def finish(first, second):
        lane = lax.broadcasted_iota(jnp.int32, (128, 128), 1)
        cls = jnp.where(lane == 0, first, jnp.where(lane == 1, second, 0.0))
        a, b = first.T, second.T
        box = jnp.where((lane >= 7) & (lane < 12), pltpu.roll(b, 7, 1), 0.0)
        box = jnp.where((lane >= 2) & (lane < 7), pltpu.roll(a, 2, 1), box)
        gw_block(gw, 2, jnp.where(meta[1] == 0, cls, box))

    @pl.when(meta[0] == 0)
    def _():
        logits[...] = dot(wp[0], x2[...], NT).astype(BF)
        first = store(0, dot(cot[...], x2[...]))
        gw_block(gw, 1, jnp.zeros((128, 128), F32))
        finish(first, jnp.zeros((128, 128), F32))

    @pl.when(meta[0] == 1)
    def _():
        logits[...] = jnp.zeros((128, CP), BF)
        bias = []
        for slot, a, b in ((0, 0, MID), (1, MID, MID + 128)):
            logits[:, a:b] = dot(wp[slot], x2[a:b], NT).astype(BF)
            bias.append(store(slot, dot(cot[:, a:b], x2[a:b])))
        finish(*bias)

    for out, group in ((mine, meta[0]), (far, 1 - meta[0])):
        for i in range(2):
            out[i] = logits[at32(jnp.where(meta[1] == 0, 2 * group + i, 0)), :]


def gw_block(gw, i, v):
    for j in range(8):
        gw[j, i] = v[16 * j : 16 * (j + 1)].astype(BF)


def grad_sums(meta, total, sums):
    shift = pick(meta, total[0:1], total[1:2])
    gain = pick(meta, total[2:3], total[3:4])
    sums[...] = jnp.concatenate(list(shift) + list(gain) + [jnp.zeros((4, 128), F32)], axis=0)


def input_grad(meta, dz, y, cst, sums, j):
    s = SLOT[j]
    xhat, _ = normed(cst, y[CH * j : CH * (j + 1)], s)
    factor = cst[4 + s : 5 + s] * cst[2 + s : 3 + s]
    mean = (sums[s : s + 1] + xhat * sums[2 + s : 3 + s]) * cst[8 + s : 9 + s]
    return mask_of(meta, j) * factor * (dz - mean)


def out_grad(meta, dz, y, cst, st, sums, field, dyt):
    grad_sums(meta, jnp.sum(st[...], axis=0), sums)
    for j in range(NCH):
        rows = slice(CH * j, CH * (j + 1))
        v = input_grad(meta, dz[rows], y, cst, sums, j)
        field[8 + CH * j : 8 + CH * (j + 1)] = v
        dyt[:, rows] = v.T.astype(BF)


def conv_back(meta, last, w, y_in, cst_in, shifts, grad, st_out):
    total = [jnp.zeros((1, 128), F32) for _ in range(4)]
    for j in range(NCH):
        rows = slice(CH * j, CH * (j + 1))
        s = SLOT[j]
        v = dot(taps(shifts, CH * j, CH, True), w[weight_slot(meta, j)])
        xhat, z = normed(cst_in, y_in[rows], s)
        d = v * slope(z) * mask_of(meta, j)
        grad[rows] = v.astype(BF) if last else d
        total[s] += colsum(d)
        total[2 + s] += colsum(d * xhat)
    spread_out(st_out, total)
    return total


def as_parts(rows):
    v = jnp.concatenate(rows, axis=0)
    high = v.astype(BF).astype(F32)
    mid = (v - high).astype(BF).astype(F32)
    return jnp.concatenate([high, mid, v - high - mid, jnp.zeros((4, 128), F32)], axis=0).astype(BF)


def from_parts(block):
    v = block.astype(F32)
    return v[0:4] + v[4:8] + v[8:12]


def place_of(direct, j):
    return 2 * OWNER[j // 2] + j % 2 if direct else j


def weight_grad(direct, meta, dyt, act, field, shifts, wg):
    for j in range(NCH):
        field[8 + CH * j : 8 + CH * (j + 1)] = act[CH * j : CH * (j + 1)].astype(F32)
    fill_shifts(field, shifts)

    def store(slot, v):
        for t in range(9):
            for j in range(8):
                block = v[16 * j : 16 * (j + 1), 128 * t : 128 * (t + 1)].astype(BF)
                wg[place_of(direct, j), 9 * slot + t] = block

    @pl.when(meta[0] == 0)
    def _():
        store(0, dot(dyt[...], taps(shifts, 0, PX)))
        store(1, jnp.zeros((128, 1152), F32))

    @pl.when(meta[0] == 1)
    def _():
        store(0, dot(dyt[:, 0:CUT], taps(shifts, 0, CUT)))
        store(1, dot(dyt[:, CUT:PX], taps(shifts, CUT, PX - CUT)))


def second_back_kernel(direct, meta, dz, y, cst, st, w, act, y_in, cst_in, gw, grad, st_out, sums, wg, field, shifts, dyt):
    guard(field, shifts)
    out_grad(meta, dz, y, cst, st, sums, field, dyt)
    fill_shifts(field, shifts)
    block = as_parts(conv_back(meta, False, w, y_in, cst_in, shifts, grad, st_out))
    weight_grad(direct, meta, dyt, act, field, shifts, wg)
    for j in range(8):
        for i in range(3):
            wg[place_of(direct, j), 18 + i] = gw[j, i]
        wg[j, 21] = block


def first_back_kernel(direct, meta, dz, y, cst, st, w, act, y_in, cst_in, grad, st_out, sums, wg, field, shifts, dyt):
    guard(field, shifts)
    out_grad(meta, dz, y, cst, st, sums, field, dyt)
    fill_shifts(field, shifts)
    block = as_parts(conv_back(meta, True, w, y_in, cst_in, shifts, grad, st_out))
    weight_grad(direct, meta, dyt, act, field, shifts, wg)
    for j in range(8):
        wg[j, 18] = block


def final_kernel(direct, meta, d0, d1, y, cst, st0, st1, sums1, sums2, u0, u1, u2, u3, own, other, gs, norm, *scratch):
    sums, feat, stem, field, flat, dyt, gf, blocks = scratch
    load_inputs(meta, (u0, u1, u2, u3), feat, stem)
    grad_sums(meta, jnp.sum(st0[...] + st1[...], axis=0), sums)
    for j in range(NCH):
        rows = slice(CH * j, CH * (j + 1))
        _, z = normed(cst, y[rows], SLOT[j])
        v = (d0[rows].astype(F32) + d1[rows].astype(F32)) * slope(z) * mask_of(meta, j)
        field[rows] = input_grad(meta, v, y, cst, sums, j)
    flat[...] = jnp.zeros((CP, 128), F32)
    to_compact(meta, field, flat)
    dyt[...] = flat[...].T.astype(BF)
    c = meta[2]
    outs = ((own, c), (other, c ^ 2))

    @pl.when(meta[0] == 0)
    def _():
        gf[0:128, :] = dot(stem[:, 0:128], dyt[...], TN).astype(BF)
        blocks[0] = dot(dyt[...], feat[0:128, :], NT).astype(BF)
        for i in range(1, 6):
            blocks[i] = jnp.zeros((128, 128), BF)
        for out, s in outs:
            out[...] = gf[at32(s), :]

    @pl.when(meta[0] == 1)
    def _():
        gf[0:256, 0:MID] = dot(stem[:, 0:256], dyt[:, 0:MID], TN).astype(BF)
        gf[:, MID : MID + 128] = dot(stem[:, 256:768], dyt[:, MID : MID + 128], TN).astype(BF)
        for i in range(2):
            blocks[i] = dot(dyt[:, 0:MID], feat[128 * i : 128 * (i + 1), 0:MID], NT).astype(BF)
        for i in range(4):
            rows = slice(128 * i, 128 * (i + 1))
            blocks[2 + i] = dot(dyt[:, MID : MID + 128], feat[rows, MID : MID + 128], NT).astype(BF)
        for out, s in outs:
            out[...] = jnp.zeros((32, CP), BF)
            for i in range(2):
                at = pl.ds(pl.multiple_of(64 * s + 32 * i, 32), 32)
                out[:, MID * i : MID * (i + 1)] = gf[at, 0:MID]
            for i in range(4):
                at = pl.ds(pl.multiple_of(128 * s + 32 * i, 32), 32)
                out[:, 1024 + 128 * i : 1152 + 128 * i] = gf[at, MID : MID + 128]

    for i in range(3):
        block = blocks[3 * meta[1] + i]
        for j in range(8):
            gs[place_of(direct, j), i] = block[16 * j : 16 * (j + 1)]
    rest = jnp.zeros((4, 128), F32)
    norm[0] = jnp.concatenate([sums[0:4], sums1[0:4], sums2[0:4], rest], axis=0).astype(BF)


def sum_kernel(meta, got, total, st):
    n = total.shape[0]
    v = got[0].astype(F32)
    rows = from_parts(got[0, n])
    for d in range(1, got.shape[0]):
        v += got[d].astype(F32)
        rows += from_parts(got[d, n])
    total[...] = v[0:n].astype(BF)
    st[0] = jnp.concatenate([rows, jnp.zeros((4, 128), F32)], axis=0)


def source(meta, k):
    c = meta[4] ^ (k % 4)
    return c >> 1, c & 1, meta[5] ^ (k // 4)


def at16(h):
    return pl.ds(pl.multiple_of(16 * h, 16), 16)


def conv_out(meta, half, parts, out, room, sems):
    for k in range(4):
        group, branch, _ = source(meta, k)
        r = parts[k]
        for slot in range(2):

            @pl.when(group >= slot)
            def _():
                level = jnp.where(group == 0, 0, 1 + slot)
                for layer in range(2):
                    for t in range(9):
                        room[layer, level, branch, t] = r[18 * layer + 9 * slot + t].astype(F32)

    h = meta[5] ^ half
    copies = []
    for layer in range(2):
        for level in range(3):
            for branch in range(2):
                to = out.at[level, 2 * branch + layer, :, at16(h), :]
                copy = pltpu.make_async_copy(room.at[layer, level, branch], to, sems.at[layer, level, branch])
                copy.start()
                copies.append(copy)
    return copies


def near_out_kernel(meta, *refs):
    parts, (out, room, sems) = refs[:4], refs[4:]
    for copy in conv_out(meta, 0, parts, out, room, sems):
        copy.wait()


def far_out_kernel(meta, *refs):
    parts, (_, out, gcw, gcb, gbw, gbb, s0, s1, s2, gains, shifts, room, sems) = refs[:8], refs[8:]
    copies = conv_out(meta, 1, parts[4:], out, room, sems)
    c = meta[2]
    for k in range(8):
        group, branch, h = source(meta, k)
        r = parts[k]
        for group_id in range(2):
            slots = range(1 + group_id)

            @pl.when((group == group_id) & (branch == 0))
            def _():
                turned = r[38].astype(F32).T
                for half in range(2):
                    size = (16, 4)[half]

                    @pl.when(h == half)
                    def _():
                        for slot in slots:
                            level = group_id + slot
                            gcw[level, 16 * half : 16 * half + size, :] = r[36 + slot].astype(F32)[0:size]
                            gcb[level : level + 1, 16 * half : 16 * half + size] = turned[slot : slot + 1, 0:size]

            @pl.when((group == group_id) & (branch == 1))
            def _():
                bias = r[38, 0:16].astype(F32)
                for slot in slots:
                    level = group_id + slot
                    gbb[level : level + 1, :] = bias[0:1, 2 + 5 * slot : 7 + 5 * slot]
                    turned = r[36 + slot].astype(F32).T
                    for half in range(2):

                        @pl.when(h == half)
                        def _():
                            for i in range(5):
                                gbw[i, level : level + 1, 16 * half : 16 * half + 16] = turned[i : i + 1, 0:16]

        @pl.when((group == 0) & (branch == 0))
        def _():
            s0[at16(h), :] = r[39].astype(F32)

        @pl.when((group == 1) & (branch == 0))
        def _():
            for i in range(2):
                s1[at16(h), 128 * i : 128 * (i + 1)] = r[39 + i].astype(F32)
            s2[at16(h), 0:128] = r[41].astype(F32)

        @pl.when((group == 1) & (branch == 1))
        def _():
            for i in range(3):
                s2[at16(h), 128 * (i + 1) : 128 * (i + 2)] = r[39 + i].astype(F32)

    for k in range(4):
        group, branch, _ = source(meta, k)
        v = parts[k][42].astype(F32)
        mine = v[:, 0:32]
        for i in range(1, 4):
            mine = jnp.where(c == i, v[:, 32 * i : 32 * (i + 1)], mine)
        for layer in range(3):
            at = 0 if layer == 0 else layer + 2 * branch
            base = 4 * layer

            @pl.when(group == 0)
            def _():
                shifts[at, 0:1, :] = mine[base : base + 1]
                gains[at, 0:1, :] = mine[base + 2 : base + 3]

            @pl.when(group == 1)
            def _():
                shifts[at, 1:3, :] = mine[base : base + 2]
                gains[at, 1:3, :] = mine[base + 2 : base + 4]

    for copy in copies:
        copy.wait()


def class_out_kernel(sizes, meta, mine, near, far, far_near, class_out, box_out):
    n0, n1, n2 = sizes
    group, branch = meta[0], meta[1]

    def store(fine, rest):
        for out, src in ((class_out, 0), (box_out, 1)):
            n = out.shape[0]
            a, b = fine[src][0:n], rest[src][0:n]
            out[:, 0:n0] = a[:, 0:n0]
            out[:, n0 : n0 + n1] = b[:, 0:n1]
            out[:, n0 + n1 : n0 + n1 + n2] = b[:, MID : MID + n2]

    for b in range(2):

        @pl.when((group == 0) & (branch == b))
        def _():
            here, there = (mine, near), (far, far_near)
            store((here[b][b], here[1 - b][0]), (there[b][b], there[1 - b][0]))

        @pl.when((group == 1) & (branch == b))
        def _():
            here, there = (mine, near), (far, far_near)
            store((there[b][b], there[1 - b][0]), (here[b][b], here[1 - b][0]))


def feature_out_kernel(meta, own, received, fine, mid, coarse):
    def store(a, b):
        n1, n2 = mid.shape[1], coarse.shape[0]
        fine[...] = a[:, 0 : fine.shape[1]]
        for i in range(2):
            mid[32 * i : 32 * (i + 1), :] = b[:, MID * i : MID * i + n1]
        v = jnp.concatenate([b[:, 1024 + 128 * i : 1152 + 128 * i] for i in range(4)], axis=0)
        coarse[...] = v.astype(F32).T[0:n2].astype(BF)

    @pl.when(meta[0] == 0)
    def _():
        store(own, received)

    @pl.when(meta[0] == 1)
    def _():
        store(received, own)


def pack_kernel(f0, f1, f2, s0, s1, s2, gains, shifts, box, own, send, small):
    group = lax.axis_index("chan") // 2

    def fine(out):
        out[:, 0 : f0.shape[1]] = f0[...]
        out[:, f0.shape[1] : CP] = jnp.zeros((32, CP - f0.shape[1]), BF)
        out[:, CP : CP + 128] = s0[...]
        out[:, CP + 128 : PAR] = jnp.zeros((32, PAR - CP - 128), BF)

    def rest(out):
        n1, n2 = f1.shape[1], f2.shape[0]
        for i in range(2):
            out[:, MID * i : MID * i + n1] = f1[32 * i : 32 * (i + 1), :]
            out[:, MID * i + n1 : MID * (i + 1)] = jnp.zeros((32, MID - n1), BF)
        v = jnp.concatenate([f2[...].astype(F32), jnp.zeros((128 - n2, 128), F32)], axis=0).T.astype(BF)
        for i in range(4):
            out[:, 1024 + 128 * i : 1152 + 128 * i] = v[32 * i : 32 * (i + 1)]
        out[:, STEM : STEM + 256] = s1[...]
        out[:, STEM + 256 : PAR] = s2[...]

    @pl.when(group == 0)
    def _():
        fine(own)
        rest(send)

    @pl.when(group == 1)
    def _():
        rest(own)
        fine(send)

    small[...] = jnp.zeros((64, 32), F32)
    for base, v in ((0, gains), (16, shifts), (32, box)):
        for k in range(5):
            small[base + 3 * k : base + 3 * k + 3] = v[k].astype(F32)
    for i in range(2):
        v = small[32 * i : 32 * (i + 1)]
        high = v.astype(BF).astype(F32)
        mid = (v - high).astype(BF).astype(F32)
        block = jnp.concatenate([high, mid, v - high - mid, jnp.zeros((32, 32), F32)], axis=1).astype(BF)
        for out in (own, send):
            out[:, PAR + 128 * i : PAR + 128 * (i + 1)] = block


def pred_kernel(sizes, meta, ccot, cw, cb, bcot, bb, own, send, box):
    n0, n1, n2 = sizes
    lane = lax.broadcasted_iota(jnp.int32, (32, 128), 1)

    def biases(b, level):
        block = jnp.concatenate([b[...], jnp.zeros((3, 128 - b.shape[1]), F32)], axis=1)
        block = jnp.concatenate([block, jnp.zeros((5, 128), F32)], axis=0)
        col = block.T[0:32, level : level + 1]
        high = col.astype(BF).astype(F32)
        mid = (col - high).astype(BF).astype(F32)
        low = col - high - mid
        v = jnp.where(lane == 0, high, jnp.where(lane == 1, mid, jnp.where(lane == 2, low, 0.0)))
        return v.astype(BF)

    def fill(out, cot, b, fine, weights):
        n = cot.shape[0]
        out[...] = jnp.zeros((32, CLS), BF)
        if fine:
            out[0:n, 0:n0] = cot[:, 0:n0]
        else:
            out[0:n, 0:n1] = cot[:, n0 : n0 + n1]
            out[0:n, MID : MID + n2] = cot[:, n0 + n1 : n0 + n1 + n2]
        for slot in range(2):
            level = 0 if fine else 1 + slot
            at = CP + 256 * slot
            if weights:
                out[0:n, at : at + 128] = cw[level]
            out[:, at + 128 : at + 256] = biases(b, level)

    for group in range(2):

        @pl.when(meta[0] == group)
        def _():
            fill(own, ccot, cb, group == 0, True)
            fill(box, bcot, bb, group == 0, False)

        @pl.when(meta[0] != group)
        def _():
            fill(send, ccot, cb, group == 0, True)


def call(body, outs, scratch, args, last=False, limit=VMEM):
    place = jax.ShapeDtypeStruct if last else pltpu.VMEM
    specs = [pl.BlockSpec(memory_space=pltpu.SMEM if a.dtype == jnp.int32 else pltpu.VMEM) for a in args]
    return pl.pallas_call(
        body,
        out_shape=[place(s, d) for s, d in outs],
        in_specs=specs,
        out_specs=[pl.BlockSpec(memory_space=pltpu.VMEM)] * len(outs),
        scratch_shapes=[pltpu.VMEM(s, d) for s, d in scratch],
        compiler_params=pltpu.CompilerParams(vmem_limit_bytes=limit),
        cost_estimate=pl.CostEstimate(flops=10**6, bytes_accessed=10**4, transcendentals=0),
    )(*args)


def shards(f0, f1, f2, units, s0, s1, s2, conv, gains, shifts, cw, cb, bw, bb, ccot, bcot):
    dp = lax.axis_size("dp")
    c = lax.axis_index("chan")
    group, branch = c // 2, c % 2
    fine = group == 0
    direct = dp == 8
    place = lax.axis_index("dp") if direct else 0
    meta = jnp.stack([group, branch, c, units[0], place // 2, place % 2]).astype(jnp.int32)
    n0, n1, n2 = f0.shape[2], f1.shape[2], f2.shape[2]

    def across(v):
        return lax.ppermute(v, "chan", [(i, i ^ 2) for i in range(4)])

    def beside(v, pairs=((0, 1), (1, 0), (2, 3), (3, 2))):
        return lax.ppermute(v, "chan", list(pairs))

    def exchange(st, *hold):
        st, *hold = lax.optimization_barrier((st, *hold))
        st = lax.all_to_all(st, "dp", 0, 0, tiled=True)
        return lax.optimization_barrier((st, *hold)) if hold else st

    def add_up(st, between=None):
        if not direct:
            st = exchange(st)
            return (st, between(st)[1]) if between else st
        st = st[:1]
        for k in (2, 4):
            st = st + lax.ppermute(st, "dp", [(i, i ^ k) for i in range(8)])
        if between:
            st, got = between(st)
        st = st + lax.ppermute(st, "dp", [(i, i ^ 1) for i in range(8)])
        return (st, got) if between else st

    def after(v, *others):
        return lax.optimization_barrier((v, *others))[0]

    def over_z(v):
        if not direct:
            return v
        parts = []
        for k in range(4):
            pairs = [
                (8 * z + 4 * y + i, 8 * (i ^ k) + 4 * y + OWNER[z]) for z in range(4) for y in range(2) for i in range(4)
            ]
            parts.append(lax.ppermute(v, ("dp", "chan"), pairs))
        return parts

    def everywhere(parts, joined):
        if direct:
            parts = [jnp.stack(parts)] if joined else parts
            return parts + [over_y(p) for p in parts]
        v = lax.all_to_all(parts.reshape(4, 2, *parts.shape[1:]), "chan", 0, 0, tiled=True)
        return [v[:, 0], v[:, 1]] if joined else [v[k % 4, k // 4] for k in range(8)]

    def joined(*parts):
        return jnp.concatenate(parts, axis=-3)

    def over_y(v):
        return lax.ppermute(v, "dp", [(i, i ^ 1) for i in range(8)])

    def reduce(v, st=None):
        if not direct:
            v = lax.optimization_barrier(lax.psum(v.astype(F32), "dp")).astype(BF)
            return (v[:, :-1], exchange(st)) if st is not None else v
        v = exchange(v)
        if st is None:
            return jnp.sum(v.astype(F32), axis=0).astype(BF)
        return call(sum_kernel, [((v.shape[1] - 1, 16, 128), BF), ((1, 8, 128), F32)], [], (meta, v))

    own, send = call(
        pack_kernel,
        [((32, WIDE), BF), ((32, WIDE), BF)],
        [((64, 32), F32)],
        (f0[0], f1[0], f2[0].T, s0, s1, s2, gains.transpose(1, 0, 2), shifts.transpose(1, 0, 2), bw.transpose(1, 0, 2)),
        limit=WHOLE,
    )
    far_u = across(send)
    own_pred, send_pred, box_pred = call(
        functools.partial(pred_kernel, (n0, n1, n2)),
        [((32, CLS), BF)] * 3,
        [],
        (meta, ccot[0], cw, cb, bcot[0], after(bb, own)),
        limit=WHOLE,
    )
    u = (after(own, send_pred), far_u, beside(own), beside(far_u))
    near = beside(conv)
    far_pred = across(send_pred)
    to_class = ((1, 0), (3, 2))
    near_pred, cross_pred = beside(own_pred, to_class), beside(far_pred, to_class)

    def weights_of(layer, far):
        return call(
            functools.partial(weight_kernel, layer),
            [((2, 128, 1152), BF), ((2, 1152, 128), BF)],
            [],
            (meta, conv, near, far, beside(far)),
        )

    canvas = (PX, 128)
    stat = (dp, 8, 128)
    moved = [((PX + 16, 128), F32), ((3, PX + 2 * ST, 128), BF)]
    y0, st, cnt, par = call(
        stem_kernel,
        [(canvas, F32), (stat, F32), ((8, 128), F32), ((64, 128), F32)],
        [((512, CP), BF), ((128, 768), BF), ((CP, 128), F32)],
        (meta, *u),
    )
    far1, far2 = (
        across(after(lax.dynamic_slice_in_dim(conv[:, layer::2], 1 - group, 2, 0), cnt, far_pred)) for layer in range(2)
    )
    st, far1 = add_up(st, lambda v: (after(v, near_pred, cross_pred), after(far1, v)))
    w1, w1_tall = weights_of(0, far1)
    forward_outs = [(canvas, BF), (canvas, F32), (stat, F32), ((16, 128), F32)]
    act0, y1, st, cst0 = call(functools.partial(forward_kernel, True), forward_outs, moved, (meta, y0, st, cnt, w1, par))
    w2, w2_tall = weights_of(1, after(far2, act0))
    pred = (own_pred, far_pred, near_pred, cross_pred, box_pred)
    st, w2, w2_tall, *pred = exchange(st, w2, w2_tall, *pred)
    act1, y2, st, cst1 = call(
        functools.partial(forward_kernel, False), forward_outs, moved, (meta, y1, st, cnt, w2, par)
    )
    st = exchange(st)
    dz2, st, cst2, x2, cot, wp = call(
        heads_kernel,
        [(canvas, F32), (stat, F32), ((16, 128), F32), ((CP, 256), BF), ((128, CP), BF), ((2, 128, 256), BF)],
        [(canvas, F32), ((CP, 128), F32)],
        (meta, y2, st, par, *pred),
    )
    st = exchange(st)
    gw, mine, far = call(
        logits_kernel,
        [((8, 3, 16, 128), BF), ((2, 32, CP), BF), ((2, 32, CP), BF)],
        [((128, CP), BF)],
        (meta, x2, cot, after(wp, st)),
    )
    far = across(far)
    near = beside(mine)
    back_scratch = moved + [((128, PX), BF)]
    dz1, st, sums2, wg2 = call(
        functools.partial(second_back_kernel, direct),
        [(canvas, F32), (stat, F32), ((8, 128), F32), ((8, 22, 16, 128), BF)],
        back_scratch,
        (meta, dz2, y2, cst2, st, w2_tall, act1, y1, cst1, gw),
    )
    wg2, near, far = lax.optimization_barrier((wg2, near, far))
    sum2, st = reduce(wg2, st)
    far = after(far, st)
    far_near = beside(far)
    d0, st, sums1, wg1 = call(
        functools.partial(first_back_kernel, direct),
        [(canvas, BF), (stat, F32), ((8, 128), F32), ((8, 19, 16, 128), BF)],
        back_scratch,
        (meta, dz1, y1, cst1, st, w1_tall, act0, y0, cst0),
    )
    d0_other = beside(d0)
    wg1, d0_other, far_near = lax.optimization_barrier((wg1, d0_other, far_near))
    sum1, st = reduce(wg1, st)
    st_other = beside(st)
    own, other, gs, norm = call(
        functools.partial(final_kernel, direct),
        [((32, CP), BF), ((32, CP), BF), ((8, 3, 16, 128), BF), ((1, 16, 128), BF)],
        [
            ((8, 128), F32),
            ((512, CP), BF),
            ((128, 768), BF),
            (canvas, F32),
            ((CP, 128), F32),
            ((128, CP), BF),
            ((512, CP), BF),
            ((6, 128, 128), BF),
        ],
        (meta, d0, d0_other, y0, cst0, st, st_other, sums1, sums2, *u),
    )
    received = across(other)
    gs = reduce(gs)
    norm = norm if direct else jnp.broadcast_to(norm[None], (8, *norm.shape))
    grads = everywhere(over_z(joined(sum1, sum2, gs, norm)), False)

    box_rows, class_rows = bcot.shape[1], ccot.shape[1]
    class_out, box_out = call(
        functools.partial(class_out_kernel, (n0, n1, n2)),
        [((class_rows, n0 + n1 + n2), BF), ((box_rows, n0 + n1 + n2), BF)],
        [],
        (meta, mine, near, far, far_near),
        True,
    )
    grad_fine, grad_mid, grad_coarse = call(
        feature_out_kernel, [(f0.shape[1:], BF), (f1.shape[1:], BF), ((n2, f2.shape[1]), BF)], [], (meta, own, received), True
    )

    any_space = pl.BlockSpec(memory_space=pl.ANY)
    vmem = pl.BlockSpec(memory_space=pltpu.VMEM)
    smem = pl.BlockSpec(memory_space=pltpu.SMEM)
    room = [pltpu.VMEM((2, 3, 2, conv.shape[2], 16, 128), F32), pltpu.SemaphoreType.DMA((2, 3, 2))]
    params = pltpu.CompilerParams(vmem_limit_bytes=VMEM)
    grad_conv = pl.pallas_call(
        near_out_kernel,
        out_shape=jax.ShapeDtypeStruct(conv.shape, F32),
        in_specs=[smem] + [vmem] * 4,
        out_specs=any_space,
        scratch_shapes=room,
        compiler_params=params,
    )(meta, *grads[:4])
    shapes = [conv.shape, cw.shape, cb.shape, (5, 3, 32), bb.shape, s0.shape, s1.shape, s2.shape, (5, 3, 32), (5, 3, 32)]
    grad_conv, grad_cw, grad_cb, grad_bw, grad_bb, grad_s0, grad_s1, grad_s2, grad_gains, grad_shifts = pl.pallas_call(
        far_out_kernel,
        out_shape=[jax.ShapeDtypeStruct(s, F32) for s in shapes],
        in_specs=[smem] + [vmem] * 8 + [any_space],
        out_specs=[any_space] + [vmem] * 9,
        scratch_shapes=room,
        input_output_aliases={9: 0},
        compiler_params=params,
    )(meta, *grads, grad_conv)
    return (
        class_out[None],
        box_out[None],
        grad_fine[None],
        grad_mid[None],
        grad_coarse.T[None],
        grad_s0,
        grad_s1,
        grad_s2,
        grad_conv,
        grad_gains.transpose(1, 0, 2),
        grad_shifts.transpose(1, 0, 2),
        grad_cw,
        grad_cb,
        grad_bw.transpose(1, 0, 2),
        grad_bb,
    )


def solution(mesh):
    placed = (
        P("dp", "chan", None),
        P("dp", "chan", None),
        P("dp", "chan", None),
        P("dp"),
        P("chan", None),
        P("chan", None),
        P("chan", None),
        P(None, None, None, "chan", None),
        P(None, None, "chan"),
        P(None, None, "chan"),
        P(None, "chan", None),
        P(None, "chan"),
        P(None, None, "chan"),
        P(),
        P("dp", "chan", None),
        P("dp", None, None),
    )
    return jax.shard_map(
        shards,
        mesh=mesh,
        in_specs=placed,
        out_specs=(
            P("dp", "chan", None),
            P("dp", None, None),
            P("dp", "chan", None),
            P("dp", "chan", None),
            P("dp", "chan", None),
            P("chan", None),
            P("chan", None),
            P("chan", None),
            P(None, None, None, "chan", None),
            P(None, None, "chan"),
            P(None, None, "chan"),
            P(None, "chan", None),
            P(None, "chan"),
            P(None, None, "chan"),
            P(),
        ),
        check_vma=False,
    )
```

```python
import functools

import jax
import jax.numpy as jnp
from jax import lax
from jax.experimental import pallas as pl
from jax.experimental.pallas import tpu as pltpu
from jax.sharding import PartitionSpec as P

BF = jnp.bfloat16
F32 = jnp.float32
EPS = 0.001
ST = 48
ROWS = 40
PX = ST * ROWS
CR = 8
CH = CR * ST
NCH = ROWS // CR
SLOT = (0, 0, 0, 1, 1)
CUT = 24 * ST
CP = 1664
MID = 512
E0, E1, E2 = 40, 20, 10
STEM = 1536
PAR = STEM + 768
WIDE = PAR + 256
CLS = CP // 128 + 4
TAPS = 36
VMEM = 12 * 2**20
WHOLE = 56 * 2**20
OWNER = (0, 2, 1, 3)
NT = (((1,), (1,)), ((), ()))
TN = (((0,), (0,)), ((), ()))


def dot(a, b, dims=(((1,), (0,)), ((), ()))):
    return lax.dot_general(a, b, dims, preferred_element_type=F32)


def limits(meta, slot):
    group, units = meta[0], meta[3]
    if slot == 0:
        edge = jnp.where(group == 0, 4 * units, 2 * units)
        return edge, edge
    return (
        jnp.where(group == 0, 4 * units, 24 + units),
        jnp.where(group == 0, 4 * units, units),
    )


def mask_of(meta, j):
    row_end, col_end = limits(meta, SLOT[j])
    row = lax.broadcasted_iota(jnp.int32, (CR, ST, 128), 0) + CR * j
    col = lax.broadcasted_iota(jnp.int32, (CR, ST, 128), 1)
    inside = (row < row_end) & (col < col_end)
    return jnp.where(inside, 1.0, 0.0).reshape(CH, 128)


def pick(meta, first, second):
    total = first + second
    return jnp.where(meta[0] == 0, total, first), jnp.where(meta[0] == 0, total, second)


def level_rows(meta, base, layer):
    fine = meta[0] == 0
    at = base + 3 * layer
    return at + jnp.where(fine, 0, 1), at + jnp.where(fine, 0, 2)


def norm_constants(meta, st, par, layer, cst):
    total = jnp.sum(st[...], axis=0)
    row = [total[i : i + 1] for i in range(6)]
    first = pick(meta, row[0], row[1])
    second = pick(meta, row[2], row[3])
    count = pick(meta, row[4], row[5])
    gain_at = level_rows(meta, 0, layer)
    shift_at = level_rows(meta, 16, layer)
    for s in range(2):
        rn = 1.0 / count[s]
        mean = first[s] * rn
        inv = lax.rsqrt(second[s] * rn - mean * mean + EPS)
        cst[s : s + 1] = mean
        cst[2 + s : 3 + s] = inv
        cst[4 + s : 5 + s] = par[pl.ds(gain_at[s], 1), :]
        cst[6 + s : 7 + s] = par[pl.ds(shift_at[s], 1), :]
        cst[8 + s : 9 + s] = rn
        cst[10 + s : 11 + s] = count[s]
    cst[12:16] = jnp.zeros((4, 128), F32)


def normed(cst, y, s):
    xhat = (y - cst[s : s + 1]) * cst[2 + s : 3 + s]
    return xhat, xhat * cst[4 + s : 5 + s] + cst[6 + s : 7 + s]


def sigmoid(z):
    return 0.5 * jnp.tanh(0.5 * z) + 0.5


def slope(z):
    s = sigmoid(z)
    return s * (1.0 + z * (1.0 - s))


def spread_out(st, rows):
    block = jnp.concatenate(rows + [jnp.zeros((8 - len(rows), 128), F32)], axis=0)
    st[...] = jnp.broadcast_to(block[None], st.shape)


def colsum(v):
    return jnp.sum(v, axis=0, keepdims=True)


def guard(field, shifts):
    field[0:8] = jnp.zeros((8, 128), F32)
    field[8 + PX : 16 + PX] = jnp.zeros((8, 128), F32)
    for k in range(3):
        shifts[k, 0:ST] = jnp.zeros((ST, 128), BF)
        shifts[k, ST + PX :] = jnp.zeros((ST, 128), BF)


def fill_shifts(field, shifts):
    for k in range(3):
        for j in range(NCH):
            at = 8 + CH * j + k - 1
            shifts[k, ST + CH * j : ST + CH * (j + 1)] = field[at : at + CH].astype(BF)


def taps(shifts, begin, size, back=False):
    parts = []
    for kr in range(3):
        for kc in range(3):
            k, r = (2 - kc, 1 - kr) if back else (kc, kr - 1)
            at = ST + begin + ST * r
            parts.append(shifts[k, at : at + size])
    return jnp.concatenate(parts, axis=1)


def slices_of(meta):
    c = meta[2]
    return (c, c ^ 2, c ^ 1, c ^ 3)


def at32(s, extra=0):
    return pl.ds(pl.multiple_of(32 * s + extra, 32), 32)


def weight_slot(meta, j):
    return jnp.where(meta[0] == 0, 0, SLOT[j])


def to_compact(meta, canvas, out):
    @pl.when(meta[0] == 0)
    def _():
        for r in range(E0):
            out[E0 * r : E0 * (r + 1)] = canvas[ST * r : ST * r + E0]

    @pl.when(meta[0] == 1)
    def _():
        for r in range(E1):
            out[E1 * r : E1 * (r + 1)] = canvas[ST * r : ST * r + E1]
        for r in range(E2):
            at = CUT + ST * r
            out[MID + E2 * r : MID + E2 * (r + 1)] = canvas[at : at + E2]


def to_canvas(meta, compact, out):
    @pl.when(meta[0] == 0)
    def _():
        for r in range(E0):
            out[ST * r : ST * r + E0] = compact[E0 * r : E0 * (r + 1)]

    @pl.when(meta[0] == 1)
    def _():
        for r in range(E1):
            out[ST * r : ST * r + E1] = compact[E1 * r : E1 * (r + 1)]
        for r in range(E2):
            at = CUT + ST * r
            out[at : at + E2] = compact[MID + E2 * r : MID + E2 * (r + 1)]


def load_inputs(meta, pieces, feat, stem):
    for s, u in zip(slices_of(meta), pieces):

        @pl.when(meta[0] == 0)
        def _():
            feat[at32(s), :] = u[:, 0:CP]
            stem[at32(s), 0:128] = u[:, CP : CP + 128]

        @pl.when(meta[0] == 1)
        def _():
            for i in range(2):
                at = pl.ds(pl.multiple_of(64 * s + 32 * i, 32), 32)
                feat[at, 0:MID] = u[:, MID * i : MID * (i + 1)]
            for i in range(4):
                at = pl.ds(pl.multiple_of(128 * s + 32 * i, 32), 32)
                feat[at, MID : MID + 128] = u[:, 1024 + 128 * i : 1152 + 128 * i]
            stem[at32(s), :] = u[:, STEM:PAR]


def stem_kernel(meta, u0, u1, u2, u3, y, st, cnt, par, feat, stem, flat):
    load_inputs(meta, (u0, u1, u2, u3), feat, stem)
    lane = lax.broadcasted_iota(jnp.int32, (32, 128), 1) // 32
    for i in range(2):
        total = jnp.zeros((32, 128), F32)
        for s, u in zip(slices_of(meta), (u0, u1, u2, u3)):
            v = u[:, PAR + 128 * i : PAR + 128 * (i + 1)].astype(F32)
            v = v[:, 0:32] + v[:, 32:64] + v[:, 64:96]
            total = jnp.where(lane == s, jnp.concatenate([v] * 4, axis=1), total)
        par[32 * i : 32 * (i + 1)] = total
    y[...] = jnp.zeros((PX, 128), F32)

    @pl.when(meta[0] == 0)
    def _():
        flat[...] = dot(stem[:, 0:128], feat[0:128, :]).T

    @pl.when(meta[0] == 1)
    def _():
        flat[0:MID] = dot(stem[:, 0:256], feat[0:256, 0:MID]).T
        flat[MID : MID + 128] = dot(stem[:, 256:768], feat[0:512, MID : MID + 128]).T

    to_canvas(meta, flat, y)
    sums = [jnp.zeros((1, 128), F32) for _ in range(6)]
    for j in range(NCH):
        m = mask_of(meta, j)
        v = y[CH * j : CH * (j + 1)] * m
        s = SLOT[j]
        sums[s] += colsum(v)
        sums[2 + s] += colsum(v * v)
        sums[4 + s] += colsum(m)
    spread_out(st, sums)
    cnt[...] = jnp.concatenate(sums[4:6] + [jnp.zeros((6, 128), F32)], axis=0)


def forward_kernel(first, meta, y, st, cnt, w, *refs):
    par, act, out, st_out, cst, field, shifts = refs
    layer = 0 if first else 1 + 2 * meta[1]
    norm_constants(meta, st, par, layer, cst)
    guard(field, shifts)
    for j in range(NCH):
        rows = slice(CH * j, CH * (j + 1))
        _, z = normed(cst, y[rows], SLOT[j])
        v = z * sigmoid(z) * mask_of(meta, j)
        act[rows] = v.astype(BF)
        field[8 + CH * j : 8 + CH * (j + 1)] = v
    fill_shifts(field, shifts)
    sums = [jnp.zeros((1, 128), F32) for _ in range(4)]
    for j in range(NCH):
        v = dot(taps(shifts, CH * j, CH), w[weight_slot(meta, j)], NT)
        out[CH * j : CH * (j + 1)] = v
        v = v * mask_of(meta, j)
        s = SLOT[j]
        sums[s] += colsum(v)
        sums[2 + s] += colsum(v * v)
    spread_out(st_out, sums + [cnt[0:1], cnt[1:2]])


def weight_kernel(layer, meta, mine, near, far, cross, flat, tall):
    group, branch, c = meta[0], meta[1], meta[2]
    conv = 2 * branch + layer
    for slot in range(2):
        level = group + slot
        for t in range(9):
            for s, piece in (
                (c, mine[level, conv, t]),
                (c ^ 1, near[level, conv, t]),
                (c ^ 2, far[9 * (2 * slot + branch) + t]),
                (c ^ 3, cross[9 * (2 * slot + branch) + t]),
            ):
                flat[slot, at32(s), 128 * t : 128 * (t + 1)] = piece
                tall[slot, at32(s, 128 * t), :] = piece


def heads_kernel(meta, y, st, par, k0, k1, k2, k3, box_pack, dz, st_out, cst, x2, cot, wp, field, flat):
    norm_constants(meta, st, par, 2 + 2 * meta[1], cst)
    cot[...] = jnp.zeros((128, CP), BF)
    wp[...] = jnp.zeros((2, 128, 256), BF)

    pixels = CP // 128

    @pl.when(meta[1] == 0)
    def _():
        for s, k, base in zip(slices_of(meta), (k0, k1, k2, k3), (0, TAPS, 0, TAPS)):
            for i in range(pixels):
                cot[at32(s), 128 * i : 128 * (i + 1)] = k[base + i]
            for slot in range(2):
                for i in range(2):
                    wp[slot, at32(s), 128 * i : 128 * (i + 1)] = k[base + pixels + 2 * slot + i]

    @pl.when(meta[1] == 1)
    def _():
        for i in range(pixels):
            cot[0:32, 128 * i : 128 * (i + 1)] = box_pack[i]
        fine = meta[0] == 0
        for slot in range(2):
            row = lax.broadcasted_iota(jnp.int32, (32, 128), 0)
            box = jnp.zeros((32, 128), F32)
            for i in range(5):
                at = 32 + 3 * i
                line = jnp.where(fine, par[at : at + 1], par[at + 1 + slot : at + 2 + slot])
                box = jnp.where(row == i, line, box)
            wp[slot, 0:32, 0:128] = box.astype(BF)
            wp[slot, 0:32, 128:256] = box_pack[pixels + 2 * slot + 1]

    for part in range(2):
        for j in range(NCH):
            m = mask_of(meta, j)
            if part == 0:
                _, z = normed(cst, y[CH * j : CH * (j + 1)], SLOT[j])
                m = z * sigmoid(z) * m
            field[CH * j : CH * (j + 1)] = m
        flat[...] = jnp.zeros((CP, 128), F32)
        to_compact(meta, field, flat)
        x2[:, 128 * part : 128 * (part + 1)] = flat[...].astype(BF)

    @pl.when(meta[0] == 0)
    def _():
        flat[...] = dot(cot[...], wp[0, :, 0:128], TN)

    @pl.when(meta[0] == 1)
    def _():
        for slot, a, b in ((0, 0, MID), (1, MID, MID + 128)):
            flat[a:b] = dot(cot[:, a:b], wp[slot, :, 0:128], TN)

    field[...] = jnp.zeros((PX, 128), F32)
    to_canvas(meta, flat, field)
    sums = [jnp.zeros((1, 128), F32) for _ in range(4)]
    for j in range(NCH):
        rows = slice(CH * j, CH * (j + 1))
        s = SLOT[j]
        xhat, z = normed(cst, y[rows], s)
        v = field[rows] * slope(z) * mask_of(meta, j)
        dz[rows] = v
        sums[s] += colsum(v)
        sums[2 + s] += colsum(v * xhat)
    spread_out(st_out, sums)


def logits_kernel(meta, x2, cot, wp, gw, mine, far, logits):
    def store(slot, v):
        bias = v[:, 128:256]

        @pl.when(meta[1] == 0)
        def _():
            gw_block(gw, slot, v[:, 0:128])

        @pl.when(meta[1] == 1)
        def _():
            gw_block(gw, slot, v[:, 0:128].T)

        return bias

    def finish(first, second):
        lane = lax.broadcasted_iota(jnp.int32, (128, 128), 1)
        cls = jnp.where(lane == 0, first, jnp.where(lane == 1, second, 0.0))
        a, b = first.T, second.T
        box = jnp.where((lane >= 7) & (lane < 12), pltpu.roll(b, 7, 1), 0.0)
        box = jnp.where((lane >= 2) & (lane < 7), pltpu.roll(a, 2, 1), box)
        gw_block(gw, 2, jnp.where(meta[1] == 0, cls, box))

    @pl.when(meta[0] == 0)
    def _():
        logits[...] = dot(wp[0], x2[...], NT).astype(BF)
        first = store(0, dot(cot[...], x2[...]))
        gw_block(gw, 1, jnp.zeros((128, 128), F32))
        finish(first, jnp.zeros((128, 128), F32))

    @pl.when(meta[0] == 1)
    def _():
        logits[...] = jnp.zeros((128, CP), BF)
        bias = []
        for slot, a, b in ((0, 0, MID), (1, MID, MID + 128)):
            logits[:, a:b] = dot(wp[slot], x2[a:b], NT).astype(BF)
            bias.append(store(slot, dot(cot[:, a:b], x2[a:b])))
        finish(*bias)

    for out, group in ((mine, meta[0]), (far, 1 - meta[0])):
        for i in range(2):
            out[i] = logits[at32(jnp.where(meta[1] == 0, 2 * group + i, 0)), :]


def gw_block(gw, i, v):
    for j in range(8):
        gw[j, i] = v[16 * j : 16 * (j + 1)].astype(BF)


def stat_total(st):
    if st.dtype == F32:
        return jnp.sum(st[...], axis=0)
    n = st.shape[1] - 1
    rows = from_parts(st[0, n])
    for d in range(1, st.shape[0]):
        rows += from_parts(st[d, n])
    return rows


def grad_sums(meta, total, sums):
    shift = pick(meta, total[0:1], total[1:2])
    gain = pick(meta, total[2:3], total[3:4])
    sums[...] = jnp.concatenate(list(shift) + list(gain) + [jnp.zeros((4, 128), F32)], axis=0)


def input_grad(meta, dz, y, cst, sums, j):
    s = SLOT[j]
    xhat, _ = normed(cst, y[CH * j : CH * (j + 1)], s)
    factor = cst[4 + s : 5 + s] * cst[2 + s : 3 + s]
    mean = (sums[s : s + 1] + xhat * sums[2 + s : 3 + s]) * cst[8 + s : 9 + s]
    return mask_of(meta, j) * factor * (dz - mean)


def out_grad(meta, dz, y, cst, st, sums, field, dyt):
    grad_sums(meta, stat_total(st), sums)
    for j in range(NCH):
        rows = slice(CH * j, CH * (j + 1))
        v = input_grad(meta, dz[rows], y, cst, sums, j)
        field[8 + CH * j : 8 + CH * (j + 1)] = v
        dyt[:, rows] = v.T.astype(BF)


def conv_back(meta, last, w, y_in, cst_in, shifts, grad, st_out):
    total = [jnp.zeros((1, 128), F32) for _ in range(4)]
    for j in range(NCH):
        rows = slice(CH * j, CH * (j + 1))
        s = SLOT[j]
        v = dot(taps(shifts, CH * j, CH, True), w[weight_slot(meta, j)])
        xhat, z = normed(cst_in, y_in[rows], s)
        d = v * slope(z) * mask_of(meta, j)
        grad[rows] = v.astype(BF) if last else d
        total[s] += colsum(d)
        total[2 + s] += colsum(d * xhat)
    spread_out(st_out, total)
    return total


def as_parts(rows):
    v = jnp.concatenate(rows, axis=0)
    high = v.astype(BF).astype(F32)
    mid = (v - high).astype(BF).astype(F32)
    return jnp.concatenate([high, mid, v - high - mid, jnp.zeros((4, 128), F32)], axis=0).astype(BF)


def from_parts(block):
    v = block.astype(F32)
    return v[0:4] + v[4:8] + v[8:12]


def place_of(direct, j):
    return 2 * OWNER[j // 2] + j % 2 if direct else j


def weight_grad(direct, meta, dyt, act, field, shifts, wg):
    for j in range(NCH):
        field[8 + CH * j : 8 + CH * (j + 1)] = act[CH * j : CH * (j + 1)].astype(F32)
    fill_shifts(field, shifts)

    def store(slot, v):
        for t in range(9):
            for j in range(8):
                block = v[16 * j : 16 * (j + 1), 128 * t : 128 * (t + 1)].astype(BF)
                wg[place_of(direct, j), 9 * slot + t] = block

    @pl.when(meta[0] == 0)
    def _():
        store(0, dot(dyt[...], taps(shifts, 0, PX)))
        store(1, jnp.zeros((128, 1152), F32))

    @pl.when(meta[0] == 1)
    def _():
        store(0, dot(dyt[:, 0:CUT], taps(shifts, 0, CUT)))
        store(1, dot(dyt[:, CUT:PX], taps(shifts, CUT, PX - CUT)))


def second_back_kernel(direct, meta, dz, y, cst, st, w, act, y_in, cst_in, gw, grad, st_out, sums, wg, field, shifts, dyt):
    guard(field, shifts)
    out_grad(meta, dz, y, cst, st, sums, field, dyt)
    fill_shifts(field, shifts)
    block = as_parts(conv_back(meta, False, w, y_in, cst_in, shifts, grad, st_out))
    weight_grad(direct, meta, dyt, act, field, shifts, wg)
    for j in range(8):
        for i in range(3):
            wg[place_of(direct, j), 18 + i] = gw[j, i]
        wg[j, 21] = block


def first_back_kernel(direct, meta, dz, y, cst, st, w, act, y_in, cst_in, grad, st_out, sums, wg, field, shifts, dyt):
    guard(field, shifts)
    out_grad(meta, dz, y, cst, st, sums, field, dyt)
    fill_shifts(field, shifts)
    block = as_parts(conv_back(meta, True, w, y_in, cst_in, shifts, grad, st_out))
    weight_grad(direct, meta, dyt, act, field, shifts, wg)
    for j in range(8):
        wg[j, 18] = block


def final_kernel(direct, meta, d0, d1, y, cst, st, sums1, sums2, u0, u1, u2, u3, own, other, gs, norm, *scratch):
    sums, feat, stem, field, flat, dyt, gf, blocks = scratch
    load_inputs(meta, (u0, u1, u2, u3), feat, stem)
    grad_sums(meta, stat_total(st), sums)
    for j in range(NCH):
        rows = slice(CH * j, CH * (j + 1))
        _, z = normed(cst, y[rows], SLOT[j])
        v = (d0[rows].astype(F32) + d1[rows].astype(F32)) * slope(z) * mask_of(meta, j)
        field[rows] = input_grad(meta, v, y, cst, sums, j)
    flat[...] = jnp.zeros((CP, 128), F32)
    to_compact(meta, field, flat)
    dyt[...] = flat[...].T.astype(BF)
    c = meta[2]
    outs = ((own, c), (other, c ^ 2))

    @pl.when(meta[0] == 0)
    def _():
        gf[0:128, :] = dot(stem[:, 0:128], dyt[...], TN).astype(BF)
        blocks[0] = dot(dyt[...], feat[0:128, :], NT).astype(BF)
        for i in range(1, 6):
            blocks[i] = jnp.zeros((128, 128), BF)
        for out, s in outs:
            out[...] = gf[at32(s), :]

    @pl.when(meta[0] == 1)
    def _():
        gf[0:256, 0:MID] = dot(stem[:, 0:256], dyt[:, 0:MID], TN).astype(BF)
        gf[:, MID : MID + 128] = dot(stem[:, 256:768], dyt[:, MID : MID + 128], TN).astype(BF)
        for i in range(2):
            blocks[i] = dot(dyt[:, 0:MID], feat[128 * i : 128 * (i + 1), 0:MID], NT).astype(BF)
        for i in range(4):
            rows = slice(128 * i, 128 * (i + 1))
            blocks[2 + i] = dot(dyt[:, MID : MID + 128], feat[rows, MID : MID + 128], NT).astype(BF)
        for out, s in outs:
            out[...] = jnp.zeros((32, CP), BF)
            for i in range(2):
                at = pl.ds(pl.multiple_of(64 * s + 32 * i, 32), 32)
                out[:, MID * i : MID * (i + 1)] = gf[at, 0:MID]
            for i in range(4):
                at = pl.ds(pl.multiple_of(128 * s + 32 * i, 32), 32)
                out[:, 1024 + 128 * i : 1152 + 128 * i] = gf[at, MID : MID + 128]

    for i in range(3):
        block = blocks[3 * meta[1] + i]
        for j in range(8):
            gs[place_of(direct, j), i] = block[16 * j : 16 * (j + 1)]
    rest = jnp.zeros((4, 128), F32)
    norm[0] = jnp.concatenate([sums[0:4], sums1[0:4], sums2[0:4], rest], axis=0).astype(BF)


def patch_kernel(wg, other, out):
    n = wg.shape[1] - 1
    block = as_parts([from_parts(wg[0, n]) + other[0, 0:4]])
    for j in range(8):
        out[j, n] = block


def summed(v, begin, end):
    total = v[0, begin:end].astype(F32)
    for d in range(1, v.shape[0]):
        total += v[d, begin:end].astype(F32)
    return total.astype(BF)


def sum_kernel(meta, second, total, extra):
    total[0:9] = summed(second, 0, 9)
    total[9:12] = summed(second, 18, 21)
    extra[...] = summed(second, 9, 18)


def join_kernel(meta, first, total, extra, gs, norm, out):
    out[0:9] = summed(first, 0, 9)
    out[9:18] = total[0:9]
    out[27:30] = total[9:12]

    @pl.when(meta[0] == 0)
    def _():
        out[18:27] = extra[...]

    @pl.when(meta[0] == 1)
    def _():
        out[18:27] = summed(first, 9, 18)

    out[30:33] = summed(gs, 0, 3)
    out[33:34] = norm[...]


def source(meta, k):
    c = meta[4] ^ (k % 4)
    return c >> 1, c & 1, meta[5] ^ (k // 4)


def at16(h):
    return pl.ds(pl.multiple_of(16 * h, 16), 16)


def conv_out(meta, half, parts, out, room, sems):
    for k in range(4):
        group, branch, _ = source(meta, k)
        r = parts[k]
        for i in range(3):
            layer = i if i < 2 else 1 - group
            level = group if i < 2 else 2
            for t in range(9):
                room[layer, level, branch, t] = r[9 * i + t].astype(F32)

    h = meta[5] ^ half
    copies = []
    for layer in range(2):
        for level in range(3):
            for branch in range(2):
                to = out.at[level, 2 * branch + layer, :, at16(h), :]
                copy = pltpu.make_async_copy(room.at[layer, level, branch], to, sems.at[layer, level, branch])
                copy.start()
                copies.append(copy)
    return copies


def row_outs(meta, half, parts, gcw, gcb, gbw, s0, s1, s2):
    h = meta[5] ^ half
    for k in range(4):
        group, branch, _ = source(meta, k)
        r = parts[k]
        for group_id in range(2):
            slots = range(1 + group_id)

            @pl.when((group == group_id) & (branch == 0))
            def _():
                turned = r[29].astype(F32).T
                for half_id in range(2):
                    size = (16, 4)[half_id]

                    @pl.when(h == half_id)
                    def _():
                        for slot in slots:
                            level = group_id + slot
                            gcw[level, 16 * half_id : 16 * half_id + size, :] = r[27 + slot].astype(F32)[0:size]
                            gcb[level : level + 1, 16 * half_id : 16 * half_id + size] = turned[slot : slot + 1, 0:size]

            @pl.when((group == group_id) & (branch == 1))
            def _():
                for slot in slots:
                    turned = r[27 + slot].astype(F32).T
                    for half_id in range(2):

                        @pl.when(h == half_id)
                        def _():
                            for i in range(5):
                                at = 16 * half_id
                                gbw[i, group_id + slot : group_id + slot + 1, at : at + 16] = turned[i : i + 1, 0:16]

        @pl.when((group == 0) & (branch == 0))
        def _():
            s0[at16(h), :] = r[30].astype(F32)

        @pl.when((group == 1) & (branch == 0))
        def _():
            for i in range(2):
                s1[at16(h), 128 * i : 128 * (i + 1)] = r[30 + i].astype(F32)
            s2[at16(h), 0:128] = r[32].astype(F32)

        @pl.when((group == 1) & (branch == 1))
        def _():
            for i in range(3):
                s2[at16(h), 128 * (i + 1) : 128 * (i + 2)] = r[30 + i].astype(F32)


def near_out_kernel(meta, *refs):
    parts, (out, gcw, gcb, gbw, s0, s1, s2, gbb, gains, shifts, room, sems) = refs[:4], refs[4:]
    copies = conv_out(meta, 0, parts, out, room, sems)
    row_outs(meta, 0, parts, gcw, gcb, gbw, s0, s1, s2)
    c = meta[2]
    for k in range(4):
        group, branch, _ = source(meta, k)
        r = parts[k]
        for group_id in range(2):

            @pl.when((group == group_id) & (branch == 1))
            def _():
                bias = r[29].astype(F32)
                for slot in range(1 + group_id):
                    level = group_id + slot
                    gbb[level : level + 1, :] = bias[0:1, 2 + 5 * slot : 7 + 5 * slot]

        v = r[33].astype(F32)
        mine = v[:, 0:32]
        for i in range(1, 4):
            mine = jnp.where(c == i, v[:, 32 * i : 32 * (i + 1)], mine)
        for layer in range(3):
            at = 0 if layer == 0 else layer + 2 * branch
            base = 4 * layer

            @pl.when(group == 0)
            def _():
                shifts[at, 0:1, :] = mine[base : base + 1]
                gains[at, 0:1, :] = mine[base + 2 : base + 3]

            @pl.when(group == 1)
            def _():
                shifts[at, 1:3, :] = mine[base : base + 2]
                gains[at, 1:3, :] = mine[base + 2 : base + 4]

    for copy in copies:
        copy.wait()


def far_out_kernel(meta, *refs):
    parts, earlier, (out, gcw, gcb, gbw, s0, s1, s2, room, sems) = refs[:4], refs[5:11], refs[11:]
    copies = conv_out(meta, 1, parts, out, room, sems)
    outs = (gcw, gcb, gbw, s0, s1, s2)
    for old, new in zip(earlier, outs):
        new[...] = old[...]
    row_outs(meta, 1, parts, *outs)
    for copy in copies:
        copy.wait()


def class_out_kernel(sizes, meta, mine, near, far, far_near, class_out, box_out):
    n0, n1, n2 = sizes
    group, branch = meta[0], meta[1]

    def store(fine, rest):
        for out, src in ((class_out, 0), (box_out, 1)):
            n = out.shape[0]
            a, b = fine[src][0:n], rest[src][0:n]
            out[:, 0:n0] = a[:, 0:n0]
            out[:, n0 : n0 + n1] = b[:, 0:n1]
            out[:, n0 + n1 : n0 + n1 + n2] = b[:, MID : MID + n2]

    for b in range(2):

        @pl.when((group == 0) & (branch == b))
        def _():
            here, there = (mine, near), (far, far_near)
            store((here[b][b], here[1 - b][0]), (there[b][b], there[1 - b][0]))

        @pl.when((group == 1) & (branch == b))
        def _():
            here, there = (mine, near), (far, far_near)
            store((there[b][b], there[1 - b][0]), (here[b][b], here[1 - b][0]))


def feature_out_kernel(meta, own, received, fine, mid, coarse):
    def store(a, b):
        n1, n2 = mid.shape[1], coarse.shape[0]
        fine[...] = a[:, 0 : fine.shape[1]]
        for i in range(2):
            mid[32 * i : 32 * (i + 1), :] = b[:, MID * i : MID * i + n1]
        v = jnp.concatenate([b[:, 1024 + 128 * i : 1152 + 128 * i] for i in range(4)], axis=0)
        coarse[...] = v.astype(F32).T[0:n2].astype(BF)

    @pl.when(meta[0] == 0)
    def _():
        store(own, received)

    @pl.when(meta[0] == 1)
    def _():
        store(received, own)


def pack_kernel(f0, f1, f2, s0, s1, s2, gains, shifts, box, own, send, small):
    group = lax.axis_index("chan") // 2

    def fine(out):
        out[:, 0 : f0.shape[1]] = f0[...]
        out[:, f0.shape[1] : CP] = jnp.zeros((32, CP - f0.shape[1]), BF)
        out[:, CP : CP + 128] = s0[...]
        out[:, CP + 128 : PAR] = jnp.zeros((32, PAR - CP - 128), BF)

    def rest(out):
        n1, n2 = f1.shape[1], f2.shape[0]
        for i in range(2):
            out[:, MID * i : MID * i + n1] = f1[32 * i : 32 * (i + 1), :]
            out[:, MID * i + n1 : MID * (i + 1)] = jnp.zeros((32, MID - n1), BF)
        v = jnp.concatenate([f2[...].astype(F32), jnp.zeros((128 - n2, 128), F32)], axis=0).T.astype(BF)
        for i in range(4):
            out[:, 1024 + 128 * i : 1152 + 128 * i] = v[32 * i : 32 * (i + 1)]
        out[:, STEM : STEM + 256] = s1[...]
        out[:, STEM + 256 : PAR] = s2[...]

    @pl.when(group == 0)
    def _():
        fine(own)
        rest(send)

    @pl.when(group == 1)
    def _():
        rest(own)
        fine(send)

    small[...] = jnp.zeros((64, 32), F32)
    for base, v in ((0, gains), (16, shifts), (32, box)):
        for k in range(5):
            small[base + 3 * k : base + 3 * k + 3] = v[k].astype(F32)
    for i in range(2):
        v = small[32 * i : 32 * (i + 1)]
        high = v.astype(BF).astype(F32)
        mid = (v - high).astype(BF).astype(F32)
        block = jnp.concatenate([high, mid, v - high - mid, jnp.zeros((32, 32), F32)], axis=1).astype(BF)
        for out in (own, send):
            out[:, PAR + 128 * i : PAR + 128 * (i + 1)] = block


def pred_kernel(sizes, meta, ccot, cw, cb, bcot, bb, conv, own, box, first, second, room, sems):
    n0, n1, n2 = sizes
    copies = []
    for layer, out in enumerate((first, second)):
        for slot in range(2):
            for branch in range(2):
                taken = conv.at[1 - meta[0] + slot, 2 * branch + layer]
                to = out.at[pl.ds(9 * (2 * slot + branch), 9)]
                copy = pltpu.make_async_copy(taken, to, sems.at[layer, slot, branch])
                copy.start()
                copies.append(copy)
    lane = lax.broadcasted_iota(jnp.int32, (32, 128), 1)

    def biases(b, level):
        block = jnp.concatenate([b[...], jnp.zeros((3, 128 - b.shape[1]), F32)], axis=1)
        block = jnp.concatenate([block, jnp.zeros((5, 128), F32)], axis=0)
        col = block.T[0:32, level : level + 1]
        high = col.astype(BF).astype(F32)
        mid = (col - high).astype(BF).astype(F32)
        low = col - high - mid
        v = jnp.where(lane == 0, high, jnp.where(lane == 1, mid, jnp.where(lane == 2, low, 0.0)))
        return v.astype(BF)

    def fill(out, base, cot, b, fine, weights):
        n = cot.shape[0]
        room[...] = jnp.zeros((32, CP), BF)
        if fine:
            room[0:n, 0:n0] = cot[:, 0:n0]
        else:
            room[0:n, 0:n1] = cot[:, n0 : n0 + n1]
            room[0:n, MID : MID + n2] = cot[:, n0 + n1 : n0 + n1 + n2]
        for i in range(CP // 128):
            out[base + i] = room[:, 128 * i : 128 * (i + 1)]
        for slot in range(2):
            level = 0 if fine else 1 + slot
            at = base + CP // 128 + 2 * slot
            out[at] = jnp.zeros((32, 128), BF)
            if weights:
                out[at, 0:n] = cw[level]
            out[at + 1] = biases(b, level)

    for group in range(2):

        @pl.when(meta[0] == group)
        def _():
            fill(own, 0, ccot, cb, group == 0, True)
            fill(box, 0, bcot, bb, group == 0, False)

        @pl.when(meta[0] != group)
        def _():
            fill(second, TAPS, ccot, cb, group == 0, True)

    for copy in copies:
        copy.wait()


def call(body, outs, scratch, args, last=False, limit=VMEM, in_place=(), aliases={}, flops=10**6):
    place = jax.ShapeDtypeStruct if last else pltpu.VMEM

    def space(i, dtype):
        if i in in_place:
            return pl.BlockSpec(memory_space=pl.ANY)
        return pl.BlockSpec(memory_space=pltpu.SMEM if dtype == jnp.int32 else pltpu.VMEM)

    return pl.pallas_call(
        body,
        out_shape=[place(s, d) for s, d in outs],
        in_specs=[space(i, a.dtype) for i, a in enumerate(args)],
        out_specs=[space(len(args) + i, d) for i, (_, d) in enumerate(outs)],
        scratch_shapes=[s if callable(getattr(s, "get_ref_aval", None)) else pltpu.VMEM(*s) for s in scratch],
        input_output_aliases=aliases,
        compiler_params=pltpu.CompilerParams(vmem_limit_bytes=limit),
        cost_estimate=pl.CostEstimate(flops=flops, bytes_accessed=10**4, transcendentals=0),
    )(*args)


def shards(f0, f1, f2, units, s0, s1, s2, conv, gains, shifts, cw, cb, bw, bb, ccot, bcot):
    dp = lax.axis_size("dp")
    c = lax.axis_index("chan")
    group, branch = c // 2, c % 2
    fine = group == 0
    direct = dp == 8
    place = lax.axis_index("dp") if direct else 0
    meta = jnp.stack([group, branch, c, units[0], place // 2, place % 2]).astype(jnp.int32)
    n0, n1, n2 = f0.shape[2], f1.shape[2], f2.shape[2]

    def across(v):
        return lax.ppermute(v, "chan", [(i, i ^ 2) for i in range(4)])

    def beside(v, pairs=((0, 1), (1, 0), (2, 3), (3, 2))):
        return lax.ppermute(v, "chan", list(pairs))

    def exchange(st, *hold):
        st, *hold = lax.optimization_barrier((st, *hold))
        st = lax.all_to_all(st, "dp", 0, 0, tiled=True)
        return lax.optimization_barrier((st, *hold)) if hold else st

    def add_up(st, between=None):
        if not direct:
            st = exchange(st)
            return (st, between(st)[1]) if between else st
        st = st[:1]
        for k in (2, 4):
            st = st + lax.ppermute(st, "dp", [(i, i ^ k) for i in range(8)])
        if between:
            st, got = between(st)
        st = st + lax.ppermute(st, "dp", [(i, i ^ 1) for i in range(8)])
        return (st, got) if between else st

    def after(v, *others):
        return lax.optimization_barrier((v, *others))[0]

    def over_z(v):
        if not direct:
            return v
        parts = []
        for k in range(4):
            pairs = [
                (8 * z + 4 * y + i, 8 * (i ^ k) + 4 * y + OWNER[z]) for z in range(4) for y in range(2) for i in range(4)
            ]
            parts.append(lax.ppermute(v, ("dp", "chan"), pairs))
        return parts

    def everywhere(parts):
        if direct:
            return parts + [over_y(p) for p in parts]
        v = lax.all_to_all(parts.reshape(4, 2, *parts.shape[1:]), "chan", 0, 0, tiled=True)
        return [v[k % 4, k // 4] for k in range(8)]

    def joined(*parts):
        return jnp.concatenate(parts, axis=-3)

    def over_y(v):
        return lax.ppermute(v, "dp", [(i, i ^ 1) for i in range(8)])

    def reduce(v):
        return lax.optimization_barrier(lax.psum(v.astype(F32), "dp")).astype(BF)

    own, send = call(
        pack_kernel,
        [((32, WIDE), BF), ((32, WIDE), BF)],
        [((64, 32), F32)],
        (f0[0], f1[0], f2[0].T, s0, s1, s2, gains.transpose(1, 0, 2), shifts.transpose(1, 0, 2), bw.transpose(1, 0, 2)),
        limit=WHOLE,
    )
    far_u = across(send)
    own_pred, box_pred, send1, send2 = call(
        functools.partial(pred_kernel, (n0, n1, n2)),
        [((CLS, 32, 128), BF)] * 2 + [((TAPS, 32, 128), BF), ((TAPS + CLS, 32, 128), BF)],
        [((32, CP), BF), pltpu.SemaphoreType.DMA((2, 2, 2))],
        (meta, ccot[0], cw, cb, bcot[0], after(bb, own), conv),
        limit=WHOLE,
        in_place=(6,),
        flops=2 * 10**9,
    )
    near = beside(after(conv, own))
    far_u = after(far_u, near, send2)
    u = (own, far_u, beside(own), beside(far_u))
    to_class = ((1, 0), (3, 2))
    near_pred = beside(own_pred, to_class)

    def weights_of(layer, far, cross):
        return call(
            functools.partial(weight_kernel, layer),
            [((2, 128, 1152), BF), ((2, 1152, 128), BF)],
            [],
            (meta, conv, near, far, cross),
        )

    canvas = (PX, 128)
    stat = (dp, 8, 128)
    moved = [((PX + 16, 128), F32), ((3, PX + 2 * ST, 128), BF)]
    y0, st, cnt, par = call(
        stem_kernel,
        [(canvas, F32), (stat, F32), ((8, 128), F32), ((64, 128), F32)],
        [((512, CP), BF), ((128, 768), BF), ((CP, 128), F32)],
        (meta, *u),
    )
    far1 = across(after(send1, far_u))
    st, near_pred = exchange(st, near_pred)
    far1 = after(far1, st)
    far2 = across(after(send2, far1))
    w1, w1_tall = weights_of(0, far1, beside(far1))
    forward_outs = [(canvas, BF), (canvas, F32), (stat, F32), ((16, 128), F32)]
    act0, y1, st, cst0 = call(functools.partial(forward_kernel, True), forward_outs, moved, (meta, y0, st, cnt, w1, par))
    st = exchange(st)
    far2 = after(far2, st)
    cross2 = beside(far2)
    w2, w2_tall = weights_of(1, far2, cross2)
    act1, y2, st, cst1 = call(
        functools.partial(forward_kernel, False), forward_outs, moved, (meta, y1, st, cnt, w2, par)
    )
    st = exchange(st)
    dz2, st, cst2, x2, cot, wp = call(
        heads_kernel,
        [(canvas, F32), (stat, F32), ((16, 128), F32), ((CP, 256), BF), ((128, CP), BF), ((2, 128, 256), BF)],
        [(canvas, F32), ((CP, 128), F32)],
        (meta, y2, st, par, own_pred, far2, near_pred, cross2, box_pred),
    )
    st = exchange(st)
    gw, mine, far = call(
        logits_kernel,
        [((8, 3, 16, 128), BF), ((2, 32, CP), BF), ((2, 32, CP), BF)],
        [((128, CP), BF)],
        (meta, x2, cot, after(wp, st)),
    )
    far = across(far)
    near = beside(mine)
    back_scratch = moved + [((128, PX), BF)]
    dz1, st, sums2, wg2 = call(
        functools.partial(second_back_kernel, direct),
        [(canvas, F32), (stat, F32), ((8, 128), F32), ((8, 22, 16, 128), BF)],
        back_scratch,
        (meta, dz2, y2, cst2, st, w2_tall, act1, y1, cst1, gw),
    )
    wg2, near, far = lax.optimization_barrier((wg2, near, far))
    got2 = exchange(wg2) if direct else reduce(wg2)
    st = got2 if direct else exchange(st)
    far = after(far, st)
    far_near = beside(far)
    d0, st, sums1, wg1 = call(
        functools.partial(first_back_kernel, direct),
        [(canvas, BF), (stat, F32), ((8, 128), F32), ((8, 19, 16, 128), BF)],
        back_scratch,
        (meta, dz1, y1, cst1, st, w1_tall, act0, y0, cst0),
    )
    d0_other = beside(d0)
    st_other = beside(st[:1])
    if direct:
        (wg1,) = call(patch_kernel, [(wg1.shape, BF)], [], (wg1, st_other), aliases={0: 0})
        total, extra = call(sum_kernel, [((12, 16, 128), BF), ((9, 16, 128), BF)], [], (meta, after(got2, d0)))
        extra = lax.ppermute(extra, "chan", [(2, 0), (3, 1)])
        wg1 = after(wg1, total)
        wg1, d0_other, far_near = lax.optimization_barrier((wg1, d0_other, far_near))
        got1 = st = exchange(wg1)
    else:
        got1 = reduce(wg1)
        st = exchange(st + st_other)
    own, other, gs, norm = call(
        functools.partial(final_kernel, direct),
        [((32, CP), BF), ((32, CP), BF), ((8, 3, 16, 128), BF), ((1, 16, 128), BF)],
        [
            ((8, 128), F32),
            ((512, CP), BF),
            ((128, 768), BF),
            (canvas, F32),
            ((CP, 128), F32),
            ((128, CP), BF),
            ((512, CP), BF),
            ((6, 128, 128), BF),
        ],
        (meta, d0, d0_other, y0, cst0, st, sums1, sums2, *u),
    )
    received = across(other)
    if direct:
        gs, extra, received = lax.optimization_barrier((exchange(gs), extra, received))
        (grads,) = call(join_kernel, [((34, 16, 128), BF)], [], (meta, got1, total, extra, gs, norm))
    else:
        extra = lax.ppermute(got2[:, 9:18], "chan", [(2, 0), (3, 1)])
        third = jnp.where(fine, extra, got1[:, 9:18])
        norm = jnp.broadcast_to(norm[None], (8, *norm.shape))
        grads = joined(got1[:, :9], got2[:, :9], third, got2[:, 18:21], reduce(gs), norm)
    grads = everywhere(over_z(grads))

    room = [((2, 3, 2, conv.shape[2], 16, 128), F32), pltpu.SemaphoreType.DMA((2, 3, 2))]
    rows = [(cw.shape, F32), (cb.shape, F32), ((5, 3, 32), F32), (s0.shape, F32), (s1.shape, F32), (s2.shape, F32)]
    wholes = [(bb.shape, F32), ((5, 3, 32), F32), ((5, 3, 32), F32)]
    grad_conv, *half, grad_bb, grad_gains, grad_shifts = call(
        near_out_kernel, [(conv.shape, F32)] + rows + wholes, room, (meta, *grads[:4]), True, in_place=(5,)
    )
    mine, own = after((mine, own), *half)
    box_rows, class_rows = bcot.shape[1], ccot.shape[1]
    class_out, box_out = call(
        functools.partial(class_out_kernel, (n0, n1, n2)),
        [((class_rows, n0 + n1 + n2), BF), ((box_rows, n0 + n1 + n2), BF)],
        [],
        (meta, mine, near, far, far_near),
        True,
    )
    grad_fine, grad_mid, grad_coarse = call(
        feature_out_kernel, [(f0.shape[1:], BF), (f1.shape[1:], BF), ((n2, f2.shape[1]), BF)], [], (meta, own, received), True
    )

    grad_conv, grad_cw, grad_cb, grad_bw, grad_s0, grad_s1, grad_s2 = call(
        far_out_kernel,
        [(conv.shape, F32)] + rows,
        room,
        (meta, *grads[4:], grad_conv, *half),
        True,
        in_place=(5, 12),
        aliases={5: 0},
    )
    return (
        class_out[None],
        box_out[None],
        grad_fine[None],
        grad_mid[None],
        grad_coarse.T[None],
        grad_s0,
        grad_s1,
        grad_s2,
        grad_conv,
        grad_gains.transpose(1, 0, 2),
        grad_shifts.transpose(1, 0, 2),
        grad_cw,
        grad_cb,
        grad_bw.transpose(1, 0, 2),
        grad_bb,
    )


def solution(mesh):
    placed = (
        P("dp", "chan", None),
        P("dp", "chan", None),
        P("dp", "chan", None),
        P("dp"),
        P("chan", None),
        P("chan", None),
        P("chan", None),
        P(None, None, None, "chan", None),
        P(None, None, "chan"),
        P(None, None, "chan"),
        P(None, "chan", None),
        P(None, "chan"),
        P(None, None, "chan"),
        P(),
        P("dp", "chan", None),
        P("dp", None, None),
    )
    return jax.shard_map(
        shards,
        mesh=mesh,
        in_specs=placed,
        out_specs=(
            P("dp", "chan", None),
            P("dp", None, None),
            P("dp", "chan", None),
            P("dp", "chan", None),
            P("dp", "chan", None),
            P("chan", None),
            P("chan", None),
            P("chan", None),
            P(None, None, None, "chan", None),
            P(None, None, "chan"),
            P(None, None, "chan"),
            P(None, "chan", None),
            P(None, "chan"),
            P(None, None, "chan"),
            P(),
        ),
        check_vma=False,
    )
```

```python
import functools

import jax
import jax.numpy as jnp
from jax import lax
from jax.experimental import pallas as pl
from jax.experimental.pallas import tpu as pltpu
from jax.sharding import PartitionSpec as P

BF = jnp.bfloat16
F32 = jnp.float32
EPS = 0.001
ST = 48
ROWS = 40
PX = ST * ROWS
CR = 8
CH = CR * ST
NCH = ROWS // CR
SLOT = (0, 0, 0, 1, 1)
CUT = 24 * ST
CP = 1664
MID = 512
E0, E1, E2 = 40, 20, 10
STEM = 1536
PAR = STEM + 768
WIDE = PAR + 256
CLS = CP // 128 + 4
TAPS = 18
SENT = 50
VMEM = 12 * 2**20
WHOLE = 56 * 2**20
NT = (((1,), (1,)), ((), ()))
TN = (((0,), (0,)), ((), ()))


def dot(a, b, dims=(((1,), (0,)), ((), ()))):
    return lax.dot_general(a, b, dims, preferred_element_type=F32)


def limits(meta, slot):
    group, units = meta[0], meta[3]
    if slot == 0:
        edge = jnp.where(group == 0, 4 * units, 2 * units)
        return edge, edge
    return (
        jnp.where(group == 0, 4 * units, 24 + units),
        jnp.where(group == 0, 4 * units, units),
    )


def mask_of(meta, j):
    row_end, col_end = limits(meta, SLOT[j])
    row = lax.broadcasted_iota(jnp.int32, (CR, ST, 128), 0) + CR * j
    col = lax.broadcasted_iota(jnp.int32, (CR, ST, 128), 1)
    inside = (row < row_end) & (col < col_end)
    return jnp.where(inside, 1.0, 0.0).reshape(CH, 128)


def pick(meta, first, second):
    total = first + second
    return jnp.where(meta[0] == 0, total, first), jnp.where(meta[0] == 0, total, second)


def level_rows(meta, base, layer):
    fine = meta[0] == 0
    at = base + 3 * layer
    return at + jnp.where(fine, 0, 1), at + jnp.where(fine, 0, 2)


def norm_constants(meta, st, par, layer, cst):
    total = jnp.sum(st[...], axis=0)
    row = [total[i : i + 1] for i in range(6)]
    first = pick(meta, row[0], row[1])
    second = pick(meta, row[2], row[3])
    count = pick(meta, row[4], row[5])
    gain_at = level_rows(meta, 0, layer)
    shift_at = level_rows(meta, 16, layer)
    for s in range(2):
        rn = 1.0 / count[s]
        mean = first[s] * rn
        inv = lax.rsqrt(second[s] * rn - mean * mean + EPS)
        cst[s : s + 1] = mean
        cst[2 + s : 3 + s] = inv
        cst[4 + s : 5 + s] = par[pl.ds(gain_at[s], 1), :]
        cst[6 + s : 7 + s] = par[pl.ds(shift_at[s], 1), :]
        cst[8 + s : 9 + s] = rn
        cst[10 + s : 11 + s] = count[s]
    cst[12:16] = jnp.zeros((4, 128), F32)


def normed(cst, y, s):
    xhat = (y - cst[s : s + 1]) * cst[2 + s : 3 + s]
    return xhat, xhat * cst[4 + s : 5 + s] + cst[6 + s : 7 + s]


def sigmoid(z):
    return 0.5 * jnp.tanh(0.5 * z) + 0.5


def slope(z):
    s = sigmoid(z)
    return s * (1.0 + z * (1.0 - s))


def spread_out(st, rows):
    block = jnp.concatenate(rows + [jnp.zeros((8 - len(rows), 128), F32)], axis=0)
    st[...] = jnp.broadcast_to(block[None], st.shape)


def colsum(v):
    return jnp.sum(v, axis=0, keepdims=True)


def guard(field, shifts):
    field[0:8] = jnp.zeros((8, 128), F32)
    field[8 + PX : 16 + PX] = jnp.zeros((8, 128), F32)
    for k in range(3):
        shifts[k, 0:ST] = jnp.zeros((ST, 128), BF)
        shifts[k, ST + PX :] = jnp.zeros((ST, 128), BF)


def fill_shifts(field, shifts):
    for k in range(3):
        for j in range(NCH):
            at = 8 + CH * j + k - 1
            shifts[k, ST + CH * j : ST + CH * (j + 1)] = field[at : at + CH].astype(BF)


def taps(shifts, begin, size, back=False):
    parts = []
    for kr in range(3):
        for kc in range(3):
            k, r = (2 - kc, 1 - kr) if back else (kc, kr - 1)
            at = ST + begin + ST * r
            parts.append(shifts[k, at : at + size])
    return jnp.concatenate(parts, axis=1)


def slices_of(meta):
    c = meta[2]
    return (c, c ^ 2, c ^ 1, c ^ 3)


def at32(s, extra=0):
    return pl.ds(pl.multiple_of(32 * s + extra, 32), 32)


def weight_slot(meta, j):
    return jnp.where(meta[0] == 0, 0, SLOT[j])


def to_compact(meta, canvas, out):
    @pl.when(meta[0] == 0)
    def _():
        for r in range(E0):
            out[E0 * r : E0 * (r + 1)] = canvas[ST * r : ST * r + E0]

    @pl.when(meta[0] == 1)
    def _():
        for r in range(E1):
            out[E1 * r : E1 * (r + 1)] = canvas[ST * r : ST * r + E1]
        for r in range(E2):
            at = CUT + ST * r
            out[MID + E2 * r : MID + E2 * (r + 1)] = canvas[at : at + E2]


def to_canvas(meta, compact, out):
    @pl.when(meta[0] == 0)
    def _():
        for r in range(E0):
            out[ST * r : ST * r + E0] = compact[E0 * r : E0 * (r + 1)]

    @pl.when(meta[0] == 1)
    def _():
        for r in range(E1):
            out[ST * r : ST * r + E1] = compact[E1 * r : E1 * (r + 1)]
        for r in range(E2):
            at = CUT + ST * r
            out[at : at + E2] = compact[MID + E2 * r : MID + E2 * (r + 1)]


def load_inputs(meta, pieces, feat, stem):
    for s, u in zip(slices_of(meta), pieces):

        @pl.when(meta[0] == 0)
        def _():
            feat[at32(s), :] = u[:, 0:CP]
            stem[at32(s), 0:128] = u[:, CP : CP + 128]

        @pl.when(meta[0] == 1)
        def _():
            for i in range(2):
                at = pl.ds(pl.multiple_of(64 * s + 32 * i, 32), 32)
                feat[at, 0:MID] = u[:, MID * i : MID * (i + 1)]
            for i in range(4):
                at = pl.ds(pl.multiple_of(128 * s + 32 * i, 32), 32)
                feat[at, MID : MID + 128] = u[:, 1024 + 128 * i : 1152 + 128 * i]
            stem[at32(s), :] = u[:, STEM:PAR]


def stem_kernel(meta, u0, u1, u2, u3, y, st, cnt, par, feat, stem, flat):
    load_inputs(meta, (u0, u1, u2, u3), feat, stem)
    lane = lax.broadcasted_iota(jnp.int32, (32, 128), 1) // 32
    for i in range(2):
        total = jnp.zeros((32, 128), F32)
        for s, u in zip(slices_of(meta), (u0, u1, u2, u3)):
            v = u[:, PAR + 128 * i : PAR + 128 * (i + 1)].astype(F32)
            v = v[:, 0:32] + v[:, 32:64] + v[:, 64:96]
            total = jnp.where(lane == s, jnp.concatenate([v] * 4, axis=1), total)
        par[32 * i : 32 * (i + 1)] = total
    y[...] = jnp.zeros((PX, 128), F32)

    @pl.when(meta[0] == 0)
    def _():
        flat[...] = dot(stem[:, 0:128], feat[0:128, :]).T

    @pl.when(meta[0] == 1)
    def _():
        flat[0:MID] = dot(stem[:, 0:256], feat[0:256, 0:MID]).T
        flat[MID : MID + 128] = dot(stem[:, 256:768], feat[0:512, MID : MID + 128]).T

    to_canvas(meta, flat, y)
    sums = [jnp.zeros((1, 128), F32) for _ in range(6)]
    for j in range(NCH):
        m = mask_of(meta, j)
        v = y[CH * j : CH * (j + 1)] * m
        s = SLOT[j]
        sums[s] += colsum(v)
        sums[2 + s] += colsum(v * v)
        sums[4 + s] += colsum(m)
    spread_out(st, sums)
    cnt[...] = jnp.concatenate(sums[4:6] + [jnp.zeros((6, 128), F32)], axis=0)


def forward_kernel(first, meta, y, st, cnt, w, *refs):
    par, act, out, st_out, cst, field, shifts = refs
    layer = 0 if first else 1 + 2 * meta[1]
    norm_constants(meta, st, par, layer, cst)
    guard(field, shifts)
    for j in range(NCH):
        rows = slice(CH * j, CH * (j + 1))
        _, z = normed(cst, y[rows], SLOT[j])
        v = z * sigmoid(z) * mask_of(meta, j)
        act[rows] = v.astype(BF)
        field[8 + CH * j : 8 + CH * (j + 1)] = v
    fill_shifts(field, shifts)
    sums = [jnp.zeros((1, 128), F32) for _ in range(4)]
    for j in range(NCH):
        v = dot(taps(shifts, CH * j, CH), w[weight_slot(meta, j)], NT)
        out[CH * j : CH * (j + 1)] = v
        v = v * mask_of(meta, j)
        s = SLOT[j]
        sums[s] += colsum(v)
        sums[2 + s] += colsum(v * v)
    spread_out(st_out, sums + [cnt[0:1], cnt[1:2]])


def weight_kernel(layer, meta, mine, near, far, cross, flat, tall):
    group, branch, c = meta[0], meta[1], meta[2]
    conv = 2 * branch + layer
    for slot in range(2):
        level = group + slot
        for t in range(9):
            for s, piece in (
                (c, mine[level, conv, t]),
                (c ^ 1, near[level, conv, t]),
                (c ^ 2, far[9 * slot + t]),
                (c ^ 3, cross[9 * slot + t]),
            ):
                flat[slot, at32(s), 128 * t : 128 * (t + 1)] = piece
                tall[slot, at32(s, 128 * t), :] = piece


def heads_kernel(meta, y, st, par, k0, k1, k2, k3, box_pack, dz, st_out, cst, x2, cot, wp, field, flat):
    norm_constants(meta, st, par, 2 + 2 * meta[1], cst)
    cot[...] = jnp.zeros((128, CP), BF)
    wp[...] = jnp.zeros((2, 128, 256), BF)

    pixels = CP // 128

    @pl.when(meta[1] == 0)
    def _():
        for s, k, base in zip(slices_of(meta), (k0, k1, k2, k3), (0, TAPS, 0, TAPS)):
            for i in range(pixels):
                cot[at32(s), 128 * i : 128 * (i + 1)] = k[base + i]
            for slot in range(2):
                for i in range(2):
                    wp[slot, at32(s), 128 * i : 128 * (i + 1)] = k[base + pixels + 2 * slot + i]

    @pl.when(meta[1] == 1)
    def _():
        for i in range(pixels):
            cot[0:32, 128 * i : 128 * (i + 1)] = box_pack[i]
        fine = meta[0] == 0
        for slot in range(2):
            row = lax.broadcasted_iota(jnp.int32, (32, 128), 0)
            box = jnp.zeros((32, 128), F32)
            for i in range(5):
                at = 32 + 3 * i
                line = jnp.where(fine, par[at : at + 1], par[at + 1 + slot : at + 2 + slot])
                box = jnp.where(row == i, line, box)
            wp[slot, 0:32, 0:128] = box.astype(BF)
            wp[slot, 0:32, 128:256] = box_pack[pixels + 2 * slot + 1]

    for part in range(2):
        for j in range(NCH):
            m = mask_of(meta, j)
            if part == 0:
                _, z = normed(cst, y[CH * j : CH * (j + 1)], SLOT[j])
                m = z * sigmoid(z) * m
            field[CH * j : CH * (j + 1)] = m
        flat[...] = jnp.zeros((CP, 128), F32)
        to_compact(meta, field, flat)
        x2[:, 128 * part : 128 * (part + 1)] = flat[...].astype(BF)

    @pl.when(meta[0] == 0)
    def _():
        flat[...] = dot(cot[...], wp[0, :, 0:128], TN)

    @pl.when(meta[0] == 1)
    def _():
        for slot, a, b in ((0, 0, MID), (1, MID, MID + 128)):
            flat[a:b] = dot(cot[:, a:b], wp[slot, :, 0:128], TN)

    field[...] = jnp.zeros((PX, 128), F32)
    to_canvas(meta, flat, field)
    sums = [jnp.zeros((1, 128), F32) for _ in range(4)]
    for j in range(NCH):
        rows = slice(CH * j, CH * (j + 1))
        s = SLOT[j]
        xhat, z = normed(cst, y[rows], s)
        v = field[rows] * slope(z) * mask_of(meta, j)
        dz[rows] = v
        sums[s] += colsum(v)
        sums[2 + s] += colsum(v * xhat)
    spread_out(st_out, sums)


def logits_kernel(meta, x2, cot, wp, gw, mine, near, far, cross, logits):
    def store(slot, v):
        bias = v[:, 128:256]

        @pl.when(meta[1] == 0)
        def _():
            gw_block(gw, slot, v[:, 0:128])

        @pl.when(meta[1] == 1)
        def _():
            gw_block(gw, slot, v[:, 0:128].T)

        return bias

    def finish(first, second):
        lane = lax.broadcasted_iota(jnp.int32, (128, 128), 1)
        cls = jnp.where(lane == 0, first, jnp.where(lane == 1, second, 0.0))
        a, b = first.T, second.T
        box = jnp.where((lane >= 7) & (lane < 12), pltpu.roll(b, 7, 1), 0.0)
        box = jnp.where((lane >= 2) & (lane < 7), pltpu.roll(a, 2, 1), box)
        gw_block(gw, 2, jnp.where(meta[1] == 0, cls, box))

    @pl.when(meta[0] == 0)
    def _():
        logits[...] = dot(wp[0], x2[...], NT).astype(BF)
        first = store(0, dot(cot[...], x2[...]))
        gw_block(gw, 1, jnp.zeros((128, 128), F32))
        finish(first, jnp.zeros((128, 128), F32))

    @pl.when(meta[0] == 1)
    def _():
        logits[...] = jnp.zeros((128, CP), BF)
        bias = []
        for slot, a, b in ((0, 0, MID), (1, MID, MID + 128)):
            logits[:, a:b] = dot(wp[slot], x2[a:b], NT).astype(BF)
            bias.append(store(slot, dot(cot[:, a:b], x2[a:b])))
        finish(*bias)

    for out, c in ((mine, 0), (near, 1), (far, 2), (cross, 3)):
        out[...] = logits[at32(jnp.where(meta[1] == 0, meta[2] ^ c, 0)), :]


def gw_block(gw, i, v):
    for j in range(8):
        gw[j, i] = v[16 * j : 16 * (j + 1)].astype(BF)


def stat_total(st):
    if st.dtype == F32:
        return jnp.sum(st[...], axis=0)
    n = st.shape[1] - 1
    rows = from_parts(st[0, n])
    for d in range(1, st.shape[0]):
        rows += from_parts(st[d, n])
    return rows


def grad_sums(meta, total, sums):
    shift = pick(meta, total[0:1], total[1:2])
    gain = pick(meta, total[2:3], total[3:4])
    sums[...] = jnp.concatenate(list(shift) + list(gain) + [jnp.zeros((4, 128), F32)], axis=0)


def input_grad(meta, dz, y, cst, sums, j):
    s = SLOT[j]
    xhat, _ = normed(cst, y[CH * j : CH * (j + 1)], s)
    factor = cst[4 + s : 5 + s] * cst[2 + s : 3 + s]
    mean = (sums[s : s + 1] + xhat * sums[2 + s : 3 + s]) * cst[8 + s : 9 + s]
    return mask_of(meta, j) * factor * (dz - mean)


def out_grad(meta, dz, y, cst, st, sums, field, dyt):
    grad_sums(meta, stat_total(st), sums)
    for j in range(NCH):
        rows = slice(CH * j, CH * (j + 1))
        v = input_grad(meta, dz[rows], y, cst, sums, j)
        field[8 + CH * j : 8 + CH * (j + 1)] = v
        dyt[:, rows] = v.T.astype(BF)


def conv_back(meta, last, w, y_in, cst_in, shifts, grad, st_out):
    total = [jnp.zeros((1, 128), F32) for _ in range(4)]
    for j in range(NCH):
        rows = slice(CH * j, CH * (j + 1))
        s = SLOT[j]
        v = dot(taps(shifts, CH * j, CH, True), w[weight_slot(meta, j)])
        xhat, z = normed(cst_in, y_in[rows], s)
        d = v * slope(z) * mask_of(meta, j)
        grad[rows] = v.astype(BF) if last else d
        total[s] += colsum(d)
        total[2 + s] += colsum(d * xhat)
    spread_out(st_out, total)
    return total


def as_parts(rows):
    v = jnp.concatenate(rows, axis=0)
    high = v.astype(BF).astype(F32)
    mid = (v - high).astype(BF).astype(F32)
    return jnp.concatenate([high, mid, v - high - mid, jnp.zeros((4, 128), F32)], axis=0).astype(BF)


def from_parts(block):
    v = block.astype(F32)
    return v[0:4] + v[4:8] + v[8:12]


def weight_grad(meta, dyt, act, field, shifts, wg):
    for j in range(NCH):
        field[8 + CH * j : 8 + CH * (j + 1)] = act[CH * j : CH * (j + 1)].astype(F32)
    fill_shifts(field, shifts)

    def store(slot, v):
        for t in range(9):
            for j in range(8):
                block = v[16 * j : 16 * (j + 1), 128 * t : 128 * (t + 1)].astype(BF)
                wg[j, 9 * slot + t] = block

    @pl.when(meta[0] == 0)
    def _():
        store(0, dot(dyt[...], taps(shifts, 0, PX)))
        store(1, jnp.zeros((128, 1152), F32))

    @pl.when(meta[0] == 1)
    def _():
        store(0, dot(dyt[:, 0:CUT], taps(shifts, 0, CUT)))
        store(1, dot(dyt[:, CUT:PX], taps(shifts, CUT, PX - CUT)))


def second_back_kernel(meta, dz, y, cst, st, w, act, y_in, cst_in, gw, grad, st_out, sums, wg, field, shifts, dyt):
    guard(field, shifts)
    out_grad(meta, dz, y, cst, st, sums, field, dyt)
    fill_shifts(field, shifts)
    block = as_parts(conv_back(meta, False, w, y_in, cst_in, shifts, grad, st_out))
    weight_grad(meta, dyt, act, field, shifts, wg)
    for j in range(8):
        for i in range(3):
            wg[j, 18 + i] = gw[j, i]
        wg[j, 21] = block


def first_back_kernel(meta, dz, y, cst, st, w, act, y_in, cst_in, grad, st_out, sums, wg, field, shifts, dyt):
    guard(field, shifts)
    out_grad(meta, dz, y, cst, st, sums, field, dyt)
    fill_shifts(field, shifts)
    block = as_parts(conv_back(meta, True, w, y_in, cst_in, shifts, grad, st_out))
    weight_grad(meta, dyt, act, field, shifts, wg)
    for j in range(8):
        wg[j, 18] = block


def final_kernel(meta, d0, d1, y, cst, st, sums1, sums2, u0, u1, u2, u3, extra, own, send, gs, norm, *scratch):
    sums, feat, stem, field, flat, dyt, gf, blocks, other = scratch
    load_inputs(meta, (u0, u1, u2, u3), feat, stem)
    grad_sums(meta, stat_total(st), sums)
    for j in range(NCH):
        rows = slice(CH * j, CH * (j + 1))
        _, z = normed(cst, y[rows], SLOT[j])
        v = (d0[rows].astype(F32) + d1[rows].astype(F32)) * slope(z) * mask_of(meta, j)
        field[rows] = input_grad(meta, v, y, cst, sums, j)
    flat[...] = jnp.zeros((CP, 128), F32)
    to_compact(meta, field, flat)
    dyt[...] = flat[...].T.astype(BF)
    c = meta[2]
    outs = ((own, c), (other, c ^ 2))

    @pl.when(meta[0] == 0)
    def _():
        gf[0:128, :] = dot(stem[:, 0:128], dyt[...], TN).astype(BF)
        blocks[0] = dot(dyt[...], feat[0:128, :], NT).astype(BF)
        for i in range(1, 6):
            blocks[i] = jnp.zeros((128, 128), BF)
        for out, s in outs:
            out[...] = gf[at32(s), :]

    @pl.when(meta[0] == 1)
    def _():
        gf[0:256, 0:MID] = dot(stem[:, 0:256], dyt[:, 0:MID], TN).astype(BF)
        gf[:, MID : MID + 128] = dot(stem[:, 256:768], dyt[:, MID : MID + 128], TN).astype(BF)
        for i in range(2):
            blocks[i] = dot(dyt[:, 0:MID], feat[128 * i : 128 * (i + 1), 0:MID], NT).astype(BF)
        for i in range(4):
            rows = slice(128 * i, 128 * (i + 1))
            blocks[2 + i] = dot(dyt[:, MID : MID + 128], feat[rows, MID : MID + 128], NT).astype(BF)
        for out, s in outs:
            out[...] = jnp.zeros((32, CP), BF)
            for i in range(2):
                at = pl.ds(pl.multiple_of(64 * s + 32 * i, 32), 32)
                out[:, MID * i : MID * (i + 1)] = gf[at, 0:MID]
            for i in range(4):
                at = pl.ds(pl.multiple_of(128 * s + 32 * i, 32), 32)
                out[:, 1024 + 128 * i : 1152 + 128 * i] = gf[at, MID : MID + 128]

    for i in range(CP // 128):
        for h in range(2):
            send[2 * i + h] = other[16 * h : 16 * (h + 1), 128 * i : 128 * (i + 1)]
    send[2 * (CP // 128) : 2 * (CP // 128) + 9] = extra[...]
    for i in range(3):
        block = blocks[3 * meta[1] + i]
        for j in range(8):
            gs[j, i] = block[16 * j : 16 * (j + 1)]
    rest = jnp.zeros((4, 128), F32)
    norm[0] = jnp.concatenate([sums[0:4], sums1[0:4], sums2[0:4], rest], axis=0).astype(BF)


def patch_kernel(wg, other, out):
    n = wg.shape[1] - 1
    block = as_parts([from_parts(wg[0, n]) + other[0, 0:4]])
    for j in range(8):
        out[j, n] = block


def summed(v, begin, end):
    total = v[0, begin:end].astype(F32)
    for d in range(1, v.shape[0]):
        total += v[d, begin:end].astype(F32)
    return total.astype(BF)


def sum_kernel(meta, second, total, extra):
    total[0:9] = summed(second, 0, 9)
    total[9:12] = summed(second, 18, 21)
    extra[...] = summed(second, 9, 18)


def join_kernel(meta, first, total, extra, gs, norm, out):
    out[0:9] = summed(first, 0, 9)
    out[9:18] = total[0:9]
    out[27:30] = total[9:12]

    @pl.when(meta[0] == 0)
    def _():
        out[18:27] = extra[2 * (CP // 128) : 2 * (CP // 128) + 9]

    @pl.when(meta[0] == 1)
    def _():
        out[18:27] = summed(first, 9, 18)

    out[30:33] = summed(gs, 0, 3)
    out[33:34] = norm[...]


def source(meta, k):
    c = meta[4] ^ (k % 4)
    return c >> 1, c & 1, meta[5] ^ (k // 4)


def at16(h):
    return pl.ds(pl.multiple_of(16 * h, 16), 16)


def conv_out(meta, half, parts, out, room, sems):
    for k in range(4):
        group, branch, _ = source(meta, k)
        r = parts[k]
        for i in range(3):
            layer = i if i < 2 else 1 - group
            level = group if i < 2 else 2
            for t in range(9):
                room[layer, level, branch, t] = r[9 * i + t].astype(F32)

    h = meta[5] ^ half
    copies = []
    for layer in range(2):
        for level in range(3):
            for branch in range(2):
                to = out.at[level, 2 * branch + layer, :, at16(h), :]
                copy = pltpu.make_async_copy(room.at[layer, level, branch], to, sems.at[layer, level, branch])
                copy.start()
                copies.append(copy)
    return copies


def row_outs(meta, half, parts, gcw, gcb, gbw, s0, s1, s2):
    h = meta[5] ^ half
    for k in range(4):
        group, branch, _ = source(meta, k)
        r = parts[k]
        for group_id in range(2):
            slots = range(1 + group_id)

            @pl.when((group == group_id) & (branch == 0))
            def _():
                turned = r[29].astype(F32).T
                for half_id in range(2):
                    size = (16, 4)[half_id]

                    @pl.when(h == half_id)
                    def _():
                        for slot in slots:
                            level = group_id + slot
                            gcw[level, 16 * half_id : 16 * half_id + size, :] = r[27 + slot].astype(F32)[0:size]
                            gcb[level : level + 1, 16 * half_id : 16 * half_id + size] = turned[slot : slot + 1, 0:size]

            @pl.when((group == group_id) & (branch == 1))
            def _():
                for slot in slots:
                    turned = r[27 + slot].astype(F32).T
                    for half_id in range(2):

                        @pl.when(h == half_id)
                        def _():
                            for i in range(5):
                                at = 16 * half_id
                                gbw[i, group_id + slot : group_id + slot + 1, at : at + 16] = turned[i : i + 1, 0:16]

        @pl.when((group == 0) & (branch == 0))
        def _():
            s0[at16(h), :] = r[30].astype(F32)

        @pl.when((group == 1) & (branch == 0))
        def _():
            for i in range(2):
                s1[at16(h), 128 * i : 128 * (i + 1)] = r[30 + i].astype(F32)
            s2[at16(h), 0:128] = r[32].astype(F32)

        @pl.when((group == 1) & (branch == 1))
        def _():
            for i in range(3):
                s2[at16(h), 128 * (i + 1) : 128 * (i + 2)] = r[30 + i].astype(F32)


def near_out_kernel(meta, *refs):
    parts, (out, gcw, gcb, gbw, s0, s1, s2, gbb, gains, shifts, room, sems) = refs[:4], refs[4:]
    copies = conv_out(meta, 0, parts, out, room, sems)
    row_outs(meta, 0, parts, gcw, gcb, gbw, s0, s1, s2)
    c = meta[2]
    for k in range(4):
        group, branch, _ = source(meta, k)
        r = parts[k]
        for group_id in range(2):

            @pl.when((group == group_id) & (branch == 1))
            def _():
                bias = r[29].astype(F32)
                for slot in range(1 + group_id):
                    level = group_id + slot
                    gbb[level : level + 1, :] = bias[0:1, 2 + 5 * slot : 7 + 5 * slot]

        v = r[33].astype(F32)
        mine = v[:, 0:32]
        for i in range(1, 4):
            mine = jnp.where(c == i, v[:, 32 * i : 32 * (i + 1)], mine)
        for layer in range(3):
            at = 0 if layer == 0 else layer + 2 * branch
            base = 4 * layer

            @pl.when(group == 0)
            def _():
                shifts[at, 0:1, :] = mine[base : base + 1]
                gains[at, 0:1, :] = mine[base + 2 : base + 3]

            @pl.when(group == 1)
            def _():
                shifts[at, 1:3, :] = mine[base : base + 2]
                gains[at, 1:3, :] = mine[base + 2 : base + 4]

    for copy in copies:
        copy.wait()


def far_out_kernel(meta, *refs):
    parts, earlier, (out, gcw, gcb, gbw, s0, s1, s2, room, sems) = refs[:4], refs[5:11], refs[11:]
    copies = conv_out(meta, 1, parts, out, room, sems)
    outs = (gcw, gcb, gbw, s0, s1, s2)
    for old, new in zip(earlier, outs):
        new[...] = old[...]
    row_outs(meta, 1, parts, *outs)
    for copy in copies:
        copy.wait()


def class_out_kernel(sizes, meta, mine, near, far, cross, class_out, box_out):
    n0, n1, n2 = sizes

    def store(out, fine, rest):
        n = out.shape[0]
        out[:, 0:n0] = fine[0:n, 0:n0]
        out[:, n0 : n0 + n1] = rest[0:n, 0:n1]
        out[:, n0 + n1 : n0 + n1 + n2] = rest[0:n, MID : MID + n2]

    for group in range(2):
        for branch in range(2):

            @pl.when((meta[0] == group) & (meta[1] == branch))
            def _():
                here, there = (mine, near), (far, cross)
                for i, out in enumerate((class_out, box_out)):
                    pair = (here[branch ^ i], there[branch ^ i])
                    store(out, pair[group], pair[1 - group])


def feature_out_kernel(meta, own, received, fine, mid, coarse, other):
    for i in range(CP // 128):
        for h in range(2):
            other[16 * h : 16 * (h + 1), 128 * i : 128 * (i + 1)] = received[2 * i + h]

    def store(a, b):
        n1, n2 = mid.shape[1], coarse.shape[0]
        fine[...] = a[:, 0 : fine.shape[1]]
        for i in range(2):
            mid[32 * i : 32 * (i + 1), :] = b[:, MID * i : MID * i + n1]
        v = jnp.concatenate([b[:, 1024 + 128 * i : 1152 + 128 * i] for i in range(4)], axis=0)
        coarse[...] = v.astype(F32).T[0:n2].astype(BF)

    @pl.when(meta[0] == 0)
    def _():
        store(own, other)

    @pl.when(meta[0] == 1)
    def _():
        store(other, own)


def pack_kernel(f0, f1, f2, s0, s1, s2, gains, shifts, box, own, send, small):
    group = lax.axis_index("chan") // 2

    def fine(out):
        out[:, 0 : f0.shape[1]] = f0[...]
        out[:, f0.shape[1] : CP] = jnp.zeros((32, CP - f0.shape[1]), BF)
        out[:, CP : CP + 128] = s0[...]
        out[:, CP + 128 : PAR] = jnp.zeros((32, PAR - CP - 128), BF)

    def rest(out):
        n1, n2 = f1.shape[1], f2.shape[0]
        for i in range(2):
            out[:, MID * i : MID * i + n1] = f1[32 * i : 32 * (i + 1), :]
            out[:, MID * i + n1 : MID * (i + 1)] = jnp.zeros((32, MID - n1), BF)
        v = jnp.concatenate([f2[...].astype(F32), jnp.zeros((128 - n2, 128), F32)], axis=0).T.astype(BF)
        for i in range(4):
            out[:, 1024 + 128 * i : 1152 + 128 * i] = v[32 * i : 32 * (i + 1)]
        out[:, STEM : STEM + 256] = s1[...]
        out[:, STEM + 256 : PAR] = s2[...]

    @pl.when(group == 0)
    def _():
        fine(own)
        rest(send)

    @pl.when(group == 1)
    def _():
        rest(own)
        fine(send)

    small[...] = jnp.zeros((64, 32), F32)
    for base, v in ((0, gains), (16, shifts), (32, box)):
        for k in range(5):
            small[base + 3 * k : base + 3 * k + 3] = v[k].astype(F32)
    for i in range(2):
        v = small[32 * i : 32 * (i + 1)]
        high = v.astype(BF).astype(F32)
        mid = (v - high).astype(BF).astype(F32)
        block = jnp.concatenate([high, mid, v - high - mid, jnp.zeros((32, 32), F32)], axis=1).astype(BF)
        for out in (own, send):
            out[:, PAR + 128 * i : PAR + 128 * (i + 1)] = block


def pred_kernel(sizes, meta, ccot, cw, cb, bcot, bb, conv, own, box, first, first_cross, second, second_cross, room, sems):
    n0, n1, n2 = sizes
    copies = []
    for layer, outs in enumerate(((first, first_cross), (second, second_cross))):
        for i, out in enumerate(outs):
            for slot in range(2):
                taken = conv.at[1 - meta[0] + slot, 2 * (meta[1] ^ i) + layer]
                copy = pltpu.make_async_copy(taken, out.at[pl.ds(9 * slot, 9)], sems.at[layer, i, slot])
                copy.start()
                copies.append(copy)
    lane = lax.broadcasted_iota(jnp.int32, (32, 128), 1)

    def biases(b, level):
        block = jnp.concatenate([b[...], jnp.zeros((3, 128 - b.shape[1]), F32)], axis=1)
        block = jnp.concatenate([block, jnp.zeros((5, 128), F32)], axis=0)
        col = block.T[0:32, level : level + 1]
        high = col.astype(BF).astype(F32)
        mid = (col - high).astype(BF).astype(F32)
        low = col - high - mid
        v = jnp.where(lane == 0, high, jnp.where(lane == 1, mid, jnp.where(lane == 2, low, 0.0)))
        return v.astype(BF)

    def fill(out, base, cot, b, fine, weights):
        n = cot.shape[0]
        room[...] = jnp.zeros((32, CP), BF)
        if fine:
            room[0:n, 0:n0] = cot[:, 0:n0]
        else:
            room[0:n, 0:n1] = cot[:, n0 : n0 + n1]
            room[0:n, MID : MID + n2] = cot[:, n0 + n1 : n0 + n1 + n2]
        for i in range(CP // 128):
            out[base + i] = room[:, 128 * i : 128 * (i + 1)]
        for slot in range(2):
            level = 0 if fine else 1 + slot
            at = base + CP // 128 + 2 * slot
            out[at] = jnp.zeros((32, 128), BF)
            if weights:
                out[at, 0:n] = cw[level]
            out[at + 1] = biases(b, level)

    for group in range(2):

        @pl.when(meta[0] == group)
        def _():
            fill(own, 0, ccot, cb, group == 0, True)
            fill(box, 0, bcot, bb, group == 0, False)

        @pl.when(meta[0] != group)
        def _():
            fill(second, TAPS, ccot, cb, group == 0, True)
            second_cross[TAPS:] = second[TAPS:]

    for copy in copies:
        copy.wait()


def call(body, outs, scratch, args, last=False, limit=VMEM, in_place=(), aliases={}, flops=10**6):
    place = jax.ShapeDtypeStruct if last else pltpu.VMEM

    def space(i, dtype):
        if i in in_place:
            return pl.BlockSpec(memory_space=pl.ANY)
        return pl.BlockSpec(memory_space=pltpu.SMEM if dtype == jnp.int32 else pltpu.VMEM)

    return pl.pallas_call(
        body,
        out_shape=[place(s, d) for s, d in outs],
        in_specs=[space(i, a.dtype) for i, a in enumerate(args)],
        out_specs=[space(len(args) + i, d) for i, (_, d) in enumerate(outs)],
        scratch_shapes=[s if callable(getattr(s, "get_ref_aval", None)) else pltpu.VMEM(*s) for s in scratch],
        input_output_aliases=aliases,
        compiler_params=pltpu.CompilerParams(vmem_limit_bytes=limit),
        cost_estimate=pl.CostEstimate(flops=flops, bytes_accessed=10**4, transcendentals=0),
    )(*args)


def shards(f0, f1, f2, units, s0, s1, s2, conv, gains, shifts, cw, cb, bw, bb, ccot, bcot):
    dp = lax.axis_size("dp")
    c = lax.axis_index("chan")
    group, branch = c // 2, c % 2
    fine = group == 0
    direct = dp == 8
    place = lax.axis_index("dp") if direct else 0
    meta = jnp.stack([group, branch, c, units[0], place // 2, place % 2]).astype(jnp.int32)
    n0, n1, n2 = f0.shape[2], f1.shape[2], f2.shape[2]

    def across(v):
        return lax.ppermute(v, "chan", [(i, i ^ 2) for i in range(4)])

    def diagonal(v):
        return lax.ppermute(v, "chan", [(i, i ^ 3) for i in range(4)])

    def beside(v, pairs=((0, 1), (1, 0), (2, 3), (3, 2))):
        return lax.ppermute(v, "chan", list(pairs))

    def exchange(st, *hold):
        st, *hold = lax.optimization_barrier((st, *hold))
        st = lax.all_to_all(st, "dp", 0, 0, tiled=True)
        return lax.optimization_barrier((st, *hold)) if hold else st

    def after(v, *others):
        return lax.optimization_barrier((v, *others))[0]

    def over_z(v):
        if not direct:
            return v
        parts = []
        for k in range(4):
            pairs = [
                (8 * z + 4 * y + i, 8 * (i ^ k) + 4 * y + z) for z in range(4) for y in range(2) for i in range(4)
            ]
            parts.append(lax.ppermute(v, ("dp", "chan"), pairs))
        return parts

    def everywhere(parts):
        if direct:
            return parts + [over_y(p) for p in parts]
        v = lax.all_to_all(parts.reshape(4, 2, *parts.shape[1:]), "chan", 0, 0, tiled=True)
        return [v[k % 4, k // 4] for k in range(8)]

    def joined(*parts):
        return jnp.concatenate(parts, axis=-3)

    def over_y(v):
        return lax.ppermute(v, "dp", [(i, i ^ 1) for i in range(8)])

    def reduce(v):
        return lax.optimization_barrier(lax.psum(v.astype(F32), "dp")).astype(BF)

    own, send = call(
        pack_kernel,
        [((32, WIDE), BF), ((32, WIDE), BF)],
        [((64, 32), F32)],
        (f0[0], f1[0], f2[0].T, s0, s1, s2, gains.transpose(1, 0, 2), shifts.transpose(1, 0, 2), bw.transpose(1, 0, 2)),
        limit=WHOLE,
    )
    far_u = across(send)
    own_pred, box_pred, send1, send1_cross, send2, send2_cross = call(
        functools.partial(pred_kernel, (n0, n1, n2)),
        [((CLS, 32, 128), BF)] * 2 + [((TAPS, 32, 128), BF)] * 2 + [((TAPS + CLS, 32, 128), BF)] * 2,
        [((32, CP), BF), pltpu.SemaphoreType.DMA((2, 2, 2))],
        (meta, ccot[0], cw, cb, bcot[0], after(bb, own), conv),
        limit=WHOLE,
        in_place=(6,),
        flops=2 * 10**9,
    )
    near = beside(after(conv, own))
    far_u = after(far_u, near, send2)
    u = (own, far_u, beside(own), beside(far_u))
    to_class = ((1, 0), (3, 2))
    near_pred = beside(own_pred, to_class)

    def weights_of(layer, far, cross):
        return call(
            functools.partial(weight_kernel, layer),
            [((2, 128, 1152), BF), ((2, 1152, 128), BF)],
            [],
            (meta, conv, near, far, cross),
        )

    canvas = (PX, 128)
    stat = (dp, 8, 128)
    moved = [((PX + 16, 128), F32), ((3, PX + 2 * ST, 128), BF)]
    y0, st, cnt, par = call(
        stem_kernel,
        [(canvas, F32), (stat, F32), ((8, 128), F32), ((64, 128), F32)],
        [((512, CP), BF), ((128, 768), BF), ((CP, 128), F32)],
        (meta, *u),
    )
    far1, cross1 = across(after(send1, far_u)), diagonal(after(send1_cross, far_u))
    st, near_pred = exchange(st, near_pred)
    far1, cross1 = after((far1, cross1), st)
    far2, cross2 = across(after(send2, far1)), diagonal(after(send2_cross, cross1))
    w1, w1_tall = weights_of(0, far1, cross1)
    forward_outs = [(canvas, BF), (canvas, F32), (stat, F32), ((16, 128), F32)]
    act0, y1, st, cst0 = call(functools.partial(forward_kernel, True), forward_outs, moved, (meta, y0, st, cnt, w1, par))
    st = exchange(st)
    far2, cross2 = after((far2, cross2), st)
    w2, w2_tall = weights_of(1, far2, cross2)
    act1, y2, st, cst1 = call(
        functools.partial(forward_kernel, False), forward_outs, moved, (meta, y1, st, cnt, w2, par)
    )
    st = exchange(st)
    dz2, st, cst2, x2, cot, wp = call(
        heads_kernel,
        [(canvas, F32), (stat, F32), ((16, 128), F32), ((CP, 256), BF), ((128, CP), BF), ((2, 128, 256), BF)],
        [(canvas, F32), ((CP, 128), F32)],
        (meta, y2, st, par, own_pred, far2, near_pred, cross2, box_pred),
    )
    gw, mine, near, far, cross = call(
        logits_kernel, [((8, 3, 16, 128), BF)] + [((32, CP), BF)] * 4, [((128, CP), BF)], (meta, x2, cot, wp)
    )
    near, far, cross = beside(near), across(far), diagonal(cross)
    st = exchange(after(st, gw))
    st, near, far, cross = lax.optimization_barrier((st, near, far, cross))
    back_scratch = moved + [((128, PX), BF)]
    dz1, st, sums2, wg2 = call(
        second_back_kernel,
        [(canvas, F32), (stat, F32), ((8, 128), F32), ((8, 22, 16, 128), BF)],
        back_scratch,
        (meta, dz2, y2, cst2, st, w2_tall, act1, y1, cst1, gw),
    )
    got2 = exchange(wg2) if direct else reduce(wg2)
    st = got2 if direct else exchange(st)
    d0, st, sums1, wg1 = call(
        first_back_kernel,
        [(canvas, BF), (stat, F32), ((8, 128), F32), ((8, 19, 16, 128), BF)],
        back_scratch,
        (meta, dz1, y1, cst1, st, w1_tall, act0, y0, cst0),
        flops=6 * 10**9,
    )
    d0_other = beside(d0)
    st_other = beside(st[:1])
    if direct:
        (wg1,) = call(patch_kernel, [(wg1.shape, BF)], [], (wg1, st_other), aliases={0: 0})
        total, extra = call(sum_kernel, [((12, 16, 128), BF), ((9, 16, 128), BF)], [], (meta, after(got2, d0)))
        wg1, d0_other, total = lax.optimization_barrier((wg1, d0_other, total))
        got1 = st = exchange(wg1)
    else:
        got1 = reduce(wg1)
        st = exchange(st + st_other)
    if not direct:
        extra = jnp.zeros((9, 16, 128), BF)
    own, send, gs, norm = call(
        final_kernel,
        [((32, CP), BF), ((SENT, 16, 128), BF), ((8, 3, 16, 128), BF), ((1, 16, 128), BF)],
        [
            ((8, 128), F32),
            ((512, CP), BF),
            ((128, 768), BF),
            (canvas, F32),
            ((CP, 128), F32),
            ((128, CP), BF),
            ((512, CP), BF),
            ((6, 128, 128), BF),
            ((32, CP), BF),
        ],
        (meta, d0, d0_other, y0, cst0, st, sums1, sums2, *u, extra),
    )
    received = across(send)
    if direct:
        gs, received = lax.optimization_barrier((exchange(gs), received))
        (grads,) = call(join_kernel, [((34, 16, 128), BF)], [], (meta, got1, total, received, gs, norm))
    else:
        extra = lax.ppermute(got2[:, 9:18], "chan", [(2, 0), (3, 1)])
        third = jnp.where(fine, extra, got1[:, 9:18])
        norm = jnp.broadcast_to(norm[None], (8, *norm.shape))
        grads = joined(got1[:, :9], got2[:, :9], third, got2[:, 18:21], reduce(gs), norm)
    grads = everywhere(over_z(grads))

    room = [((2, 3, 2, conv.shape[2], 16, 128), F32), pltpu.SemaphoreType.DMA((2, 3, 2))]
    rows = [(cw.shape, F32), (cb.shape, F32), ((5, 3, 32), F32), (s0.shape, F32), (s1.shape, F32), (s2.shape, F32)]
    wholes = [(bb.shape, F32), ((5, 3, 32), F32), ((5, 3, 32), F32)]
    grad_conv, *half, grad_bb, grad_gains, grad_shifts = call(
        near_out_kernel, [(conv.shape, F32)] + rows + wholes, room, (meta, *grads[:4]), True, in_place=(5,)
    )
    mine, own = after((mine, own), *half)
    box_rows, class_rows = bcot.shape[1], ccot.shape[1]
    class_out, box_out = call(
        functools.partial(class_out_kernel, (n0, n1, n2)),
        [((class_rows, n0 + n1 + n2), BF), ((box_rows, n0 + n1 + n2), BF)],
        [],
        (meta, mine, near, far, cross),
        True,
    )
    grad_fine, grad_mid, grad_coarse = call(
        feature_out_kernel,
        [(f0.shape[1:], BF), (f1.shape[1:], BF), ((n2, f2.shape[1]), BF)],
        [((32, CP), BF)],
        (meta, own, received),
        True,
    )

    grad_conv, grad_cw, grad_cb, grad_bw, grad_s0, grad_s1, grad_s2 = call(
        far_out_kernel,
        [(conv.shape, F32)] + rows,
        room,
        (meta, *grads[4:], grad_conv, *half),
        True,
        in_place=(5, 12),
        aliases={5: 0},
    )
    return (
        class_out[None],
        box_out[None],
        grad_fine[None],
        grad_mid[None],
        grad_coarse.T[None],
        grad_s0,
        grad_s1,
        grad_s2,
        grad_conv,
        grad_gains.transpose(1, 0, 2),
        grad_shifts.transpose(1, 0, 2),
        grad_cw,
        grad_cb,
        grad_bw.transpose(1, 0, 2),
        grad_bb,
    )


def solution(mesh):
    placed = (
        P("dp", "chan", None),
        P("dp", "chan", None),
        P("dp", "chan", None),
        P("dp"),
        P("chan", None),
        P("chan", None),
        P("chan", None),
        P(None, None, None, "chan", None),
        P(None, None, "chan"),
        P(None, None, "chan"),
        P(None, "chan", None),
        P(None, "chan"),
        P(None, None, "chan"),
        P(),
        P("dp", "chan", None),
        P("dp", None, None),
    )
    return jax.shard_map(
        shards,
        mesh=mesh,
        in_specs=placed,
        out_specs=(
            P("dp", "chan", None),
            P("dp", None, None),
            P("dp", "chan", None),
            P("dp", "chan", None),
            P("dp", "chan", None),
            P("chan", None),
            P("chan", None),
            P("chan", None),
            P(None, None, None, "chan", None),
            P(None, None, "chan"),
            P(None, None, "chan"),
            P(None, "chan", None),
            P(None, "chan"),
            P(None, None, "chan"),
            P(),
        ),
        check_vma=False,
    )
```

```python
import functools

import jax
import jax.numpy as jnp
from jax import lax
from jax.experimental import pallas as pl
from jax.experimental.pallas import tpu as pltpu
from jax.sharding import PartitionSpec as P

BF = jnp.bfloat16
F32 = jnp.float32
EPS = 0.001
ST = 48
ROWS = 40
PX = ST * ROWS
CR = 8
CH = CR * ST
NCH = ROWS // CR
SLOT = (0, 0, 0, 1, 1)
CUT = 24 * ST
CP = 1664
MID = 512
E0, E1, E2 = 40, 20, 10
STEM = 1536
PAR = STEM + 768
WIDE = PAR + 256
CLS = CP // 128 + 4
TAPS = 18
SENT = 2 * (CP // 128) + 9
VMEM = 12 * 2**20
WHOLE = 56 * 2**20
NT = (((1,), (1,)), ((), ()))
TN = (((0,), (0,)), ((), ()))


def dot(a, b, dims=(((1,), (0,)), ((), ()))):
    return lax.dot_general(a, b, dims, preferred_element_type=F32)


def limits(meta, slot):
    group, units = meta[0], meta[3]
    if slot == 0:
        edge = jnp.where(group == 0, 4 * units, 2 * units)
        return edge, edge
    return (
        jnp.where(group == 0, 4 * units, 24 + units),
        jnp.where(group == 0, 4 * units, units),
    )


def mask_of(meta, j):
    row_end, col_end = limits(meta, SLOT[j])
    row = lax.broadcasted_iota(jnp.int32, (CR, ST, 128), 0) + CR * j
    col = lax.broadcasted_iota(jnp.int32, (CR, ST, 128), 1)
    inside = (row < row_end) & (col < col_end)
    return jnp.where(inside, 1.0, 0.0).reshape(CH, 128)


def pick(meta, first, second):
    total = first + second
    return jnp.where(meta[0] == 0, total, first), jnp.where(meta[0] == 0, total, second)


def level_rows(meta, base, layer):
    fine = meta[0] == 0
    at = base + 3 * layer
    return at + jnp.where(fine, 0, 1), at + jnp.where(fine, 0, 2)


def norm_constants(meta, st, par, layer, cst):
    total = jnp.sum(st[...], axis=0)
    row = [total[i : i + 1] for i in range(6)]
    first = pick(meta, row[0], row[1])
    second = pick(meta, row[2], row[3])
    count = pick(meta, row[4], row[5])
    gain_at = level_rows(meta, 0, layer)
    shift_at = level_rows(meta, 16, layer)
    for s in range(2):
        rn = 1.0 / count[s]
        mean = first[s] * rn
        inv = lax.rsqrt(second[s] * rn - mean * mean + EPS)
        cst[s : s + 1] = mean
        cst[2 + s : 3 + s] = inv
        cst[4 + s : 5 + s] = par[pl.ds(gain_at[s], 1), :]
        cst[6 + s : 7 + s] = par[pl.ds(shift_at[s], 1), :]
        cst[8 + s : 9 + s] = rn
        cst[10 + s : 11 + s] = count[s]
    cst[12:16] = jnp.zeros((4, 128), F32)


def normed(cst, y, s):
    xhat = (y - cst[s : s + 1]) * cst[2 + s : 3 + s]
    return xhat, xhat * cst[4 + s : 5 + s] + cst[6 + s : 7 + s]


def sigmoid(z):
    return 0.5 * jnp.tanh(0.5 * z) + 0.5


def slope(z):
    s = sigmoid(z)
    return s * (1.0 + z * (1.0 - s))


def spread_out(st, rows):
    block = jnp.concatenate(rows + [jnp.zeros((8 - len(rows), 128), F32)], axis=0)
    st[...] = jnp.broadcast_to(block[None], st.shape)


def colsum(v):
    return jnp.sum(v, axis=0, keepdims=True)


def guard(field, shifts):
    field[0:8] = jnp.zeros((8, 128), F32)
    field[8 + PX : 16 + PX] = jnp.zeros((8, 128), F32)
    for k in range(3):
        shifts[k, 0:ST] = jnp.zeros((ST, 128), BF)
        shifts[k, ST + PX :] = jnp.zeros((ST, 128), BF)


def fill_shifts(field, shifts):
    for k in range(3):
        for j in range(NCH):
            at = 8 + CH * j + k - 1
            shifts[k, ST + CH * j : ST + CH * (j + 1)] = field[at : at + CH].astype(BF)


def taps(shifts, begin, size, back=False):
    parts = []
    for kr in range(3):
        for kc in range(3):
            k, r = (2 - kc, 1 - kr) if back else (kc, kr - 1)
            at = ST + begin + ST * r
            parts.append(shifts[k, at : at + size])
    return jnp.concatenate(parts, axis=1)


def slices_of(meta):
    c = meta[2]
    return (c, c ^ 2, c ^ 1, c ^ 3)


def at32(s, extra=0):
    return pl.ds(pl.multiple_of(32 * s + extra, 32), 32)


def weight_slot(meta, j):
    return jnp.where(meta[0] == 0, 0, SLOT[j])


def to_compact(meta, canvas, out):
    @pl.when(meta[0] == 0)
    def _():
        for r in range(E0):
            out[E0 * r : E0 * (r + 1)] = canvas[ST * r : ST * r + E0]

    @pl.when(meta[0] == 1)
    def _():
        for r in range(E1):
            out[E1 * r : E1 * (r + 1)] = canvas[ST * r : ST * r + E1]
        for r in range(E2):
            at = CUT + ST * r
            out[MID + E2 * r : MID + E2 * (r + 1)] = canvas[at : at + E2]


def to_canvas(meta, compact, out):
    @pl.when(meta[0] == 0)
    def _():
        for r in range(E0):
            out[ST * r : ST * r + E0] = compact[E0 * r : E0 * (r + 1)]

    @pl.when(meta[0] == 1)
    def _():
        for r in range(E1):
            out[ST * r : ST * r + E1] = compact[E1 * r : E1 * (r + 1)]
        for r in range(E2):
            at = CUT + ST * r
            out[at : at + E2] = compact[MID + E2 * r : MID + E2 * (r + 1)]


def load_inputs(meta, pieces, feat, stem):
    for s, u in zip(slices_of(meta), pieces):

        @pl.when(meta[0] == 0)
        def _():
            feat[at32(s), :] = u[:, 0:CP]
            stem[at32(s), 0:128] = u[:, CP : CP + 128]

        @pl.when(meta[0] == 1)
        def _():
            for i in range(2):
                at = pl.ds(pl.multiple_of(64 * s + 32 * i, 32), 32)
                feat[at, 0:MID] = u[:, MID * i : MID * (i + 1)]
            for i in range(4):
                at = pl.ds(pl.multiple_of(128 * s + 32 * i, 32), 32)
                feat[at, MID : MID + 128] = u[:, 1024 + 128 * i : 1152 + 128 * i]
            stem[at32(s), :] = u[:, STEM:PAR]


def stem_kernel(meta, u0, u1, u2, u3, y, st, cnt, par, feat, stem, flat):
    load_inputs(meta, (u0, u1, u2, u3), feat, stem)
    lane = lax.broadcasted_iota(jnp.int32, (32, 128), 1) // 32
    for i in range(2):
        total = jnp.zeros((32, 128), F32)
        for s, u in zip(slices_of(meta), (u0, u1, u2, u3)):
            v = u[:, PAR + 128 * i : PAR + 128 * (i + 1)].astype(F32)
            v = v[:, 0:32] + v[:, 32:64] + v[:, 64:96]
            total = jnp.where(lane == s, jnp.concatenate([v] * 4, axis=1), total)
        par[32 * i : 32 * (i + 1)] = total
    y[...] = jnp.zeros((PX, 128), F32)

    @pl.when(meta[0] == 0)
    def _():
        flat[...] = dot(stem[:, 0:128], feat[0:128, :]).T

    @pl.when(meta[0] == 1)
    def _():
        flat[0:MID] = dot(stem[:, 0:256], feat[0:256, 0:MID]).T
        flat[MID : MID + 128] = dot(stem[:, 256:768], feat[0:512, MID : MID + 128]).T

    to_canvas(meta, flat, y)
    sums = [jnp.zeros((1, 128), F32) for _ in range(6)]
    for j in range(NCH):
        m = mask_of(meta, j)
        v = y[CH * j : CH * (j + 1)] * m
        s = SLOT[j]
        sums[s] += colsum(v)
        sums[2 + s] += colsum(v * v)
        sums[4 + s] += colsum(m)
    spread_out(st, sums)
    cnt[...] = jnp.concatenate(sums[4:6] + [jnp.zeros((6, 128), F32)], axis=0)


def forward_kernel(first, meta, y, st, cnt, w, *refs):
    par, act, out, st_out, cst, field, shifts = refs
    layer = 0 if first else 1 + 2 * meta[1]
    norm_constants(meta, st, par, layer, cst)
    guard(field, shifts)
    for j in range(NCH):
        rows = slice(CH * j, CH * (j + 1))
        _, z = normed(cst, y[rows], SLOT[j])
        v = z * sigmoid(z) * mask_of(meta, j)
        act[rows] = v.astype(BF)
        field[8 + CH * j : 8 + CH * (j + 1)] = v
    fill_shifts(field, shifts)
    sums = [jnp.zeros((1, 128), F32) for _ in range(4)]
    for j in range(NCH):
        v = dot(taps(shifts, CH * j, CH), w[weight_slot(meta, j)], NT)
        out[CH * j : CH * (j + 1)] = v
        v = v * mask_of(meta, j)
        s = SLOT[j]
        sums[s] += colsum(v)
        sums[2 + s] += colsum(v * v)
    spread_out(st_out, sums + [cnt[0:1], cnt[1:2]])


def weight_kernel(layer, meta, mine, near, far, cross, flat, tall):
    group, branch, c = meta[0], meta[1], meta[2]
    conv = 2 * branch + layer
    for slot in range(2):
        level = group + slot
        for t in range(9):
            for s, piece in (
                (c, mine[level, conv, t]),
                (c ^ 1, near[level, conv, t]),
                (c ^ 2, far[9 * slot + t]),
                (c ^ 3, cross[9 * slot + t]),
            ):
                flat[slot, at32(s), 128 * t : 128 * (t + 1)] = piece
                tall[slot, at32(s, 128 * t), :] = piece


def heads_kernel(meta, y, st, par, k0, k1, k2, k3, box_pack, dz, st_out, cst, x2, cot, wp, field, flat):
    norm_constants(meta, st, par, 2 + 2 * meta[1], cst)
    cot[...] = jnp.zeros((128, CP), BF)
    wp[...] = jnp.zeros((2, 128, 256), BF)

    pixels = CP // 128

    @pl.when(meta[1] == 0)
    def _():
        for s, k, base in zip(slices_of(meta), (k0, k1, k2, k3), (0, TAPS, 0, TAPS)):
            for i in range(pixels):
                cot[at32(s), 128 * i : 128 * (i + 1)] = k[base + i]
            for slot in range(2):
                for i in range(2):
                    wp[slot, at32(s), 128 * i : 128 * (i + 1)] = k[base + pixels + 2 * slot + i]

    @pl.when(meta[1] == 1)
    def _():
        for i in range(pixels):
            cot[0:32, 128 * i : 128 * (i + 1)] = box_pack[i]
        fine = meta[0] == 0
        for slot in range(2):
            row = lax.broadcasted_iota(jnp.int32, (32, 128), 0)
            box = jnp.zeros((32, 128), F32)
            for i in range(5):
                at = 32 + 3 * i
                line = jnp.where(fine, par[at : at + 1], par[at + 1 + slot : at + 2 + slot])
                box = jnp.where(row == i, line, box)
            wp[slot, 0:32, 0:128] = box.astype(BF)
            wp[slot, 0:32, 128:256] = box_pack[pixels + 2 * slot + 1]

    for part in range(2):
        for j in range(NCH):
            m = mask_of(meta, j)
            if part == 0:
                _, z = normed(cst, y[CH * j : CH * (j + 1)], SLOT[j])
                m = z * sigmoid(z) * m
            field[CH * j : CH * (j + 1)] = m
        flat[...] = jnp.zeros((CP, 128), F32)
        to_compact(meta, field, flat)
        x2[:, 128 * part : 128 * (part + 1)] = flat[...].astype(BF)

    @pl.when(meta[0] == 0)
    def _():
        flat[...] = dot(cot[...], wp[0, :, 0:128], TN)

    @pl.when(meta[0] == 1)
    def _():
        for slot, a, b in ((0, 0, MID), (1, MID, MID + 128)):
            flat[a:b] = dot(cot[:, a:b], wp[slot, :, 0:128], TN)

    field[...] = jnp.zeros((PX, 128), F32)
    to_canvas(meta, flat, field)
    sums = [jnp.zeros((1, 128), F32) for _ in range(4)]
    for j in range(NCH):
        rows = slice(CH * j, CH * (j + 1))
        s = SLOT[j]
        xhat, z = normed(cst, y[rows], s)
        v = field[rows] * slope(z) * mask_of(meta, j)
        dz[rows] = v
        sums[s] += colsum(v)
        sums[2 + s] += colsum(v * xhat)
    spread_out(st_out, sums)


def logits_kernel(meta, x2, cot, wp, gw, mine, near, far, cross, logits):
    def store(slot, v):
        bias = v[:, 128:256]

        @pl.when(meta[1] == 0)
        def _():
            gw_block(gw, slot, v[:, 0:128])

        @pl.when(meta[1] == 1)
        def _():
            gw_block(gw, slot, v[:, 0:128].T)

        return bias

    def finish(first, second):
        lane = lax.broadcasted_iota(jnp.int32, (128, 128), 1)
        cls = jnp.where(lane == 0, first, jnp.where(lane == 1, second, 0.0))
        a, b = first.T, second.T
        box = jnp.where((lane >= 7) & (lane < 12), pltpu.roll(b, 7, 1), 0.0)
        box = jnp.where((lane >= 2) & (lane < 7), pltpu.roll(a, 2, 1), box)
        gw_block(gw, 2, jnp.where(meta[1] == 0, cls, box))

    @pl.when(meta[0] == 0)
    def _():
        logits[...] = dot(wp[0], x2[...], NT).astype(BF)
        first = store(0, dot(cot[...], x2[...]))
        gw_block(gw, 1, jnp.zeros((128, 128), F32))
        finish(first, jnp.zeros((128, 128), F32))

    @pl.when(meta[0] == 1)
    def _():
        logits[...] = jnp.zeros((128, CP), BF)
        bias = []
        for slot, a, b in ((0, 0, MID), (1, MID, MID + 128)):
            logits[:, a:b] = dot(wp[slot], x2[a:b], NT).astype(BF)
            bias.append(store(slot, dot(cot[:, a:b], x2[a:b])))
        finish(*bias)

    for out, c in ((mine, 0), (near, 1), (far, 2), (cross, 3)):
        out[...] = logits[at32(jnp.where(meta[1] == 0, meta[2] ^ c, 0)), :]


def gw_block(gw, i, v):
    for j in range(8):
        gw[j, i] = v[16 * j : 16 * (j + 1)].astype(BF)


def grad_sums(meta, total, sums):
    shift = pick(meta, total[0:1], total[1:2])
    gain = pick(meta, total[2:3], total[3:4])
    sums[...] = jnp.concatenate(list(shift) + list(gain) + [jnp.zeros((4, 128), F32)], axis=0)


def input_grad(meta, dz, y, cst, sums, j):
    s = SLOT[j]
    xhat, _ = normed(cst, y[CH * j : CH * (j + 1)], s)
    factor = cst[4 + s : 5 + s] * cst[2 + s : 3 + s]
    mean = (sums[s : s + 1] + xhat * sums[2 + s : 3 + s]) * cst[8 + s : 9 + s]
    return mask_of(meta, j) * factor * (dz - mean)


def out_grad(meta, dz, y, cst, st, sums, field, dyt):
    grad_sums(meta, jnp.sum(st[...], axis=0), sums)
    for j in range(NCH):
        rows = slice(CH * j, CH * (j + 1))
        v = input_grad(meta, dz[rows], y, cst, sums, j)
        field[8 + CH * j : 8 + CH * (j + 1)] = v
        dyt[:, rows] = v.T.astype(BF)


def conv_back(meta, last, w, y_in, cst_in, shifts, grad, st_out):
    total = [jnp.zeros((1, 128), F32) for _ in range(4)]
    for j in range(NCH):
        rows = slice(CH * j, CH * (j + 1))
        s = SLOT[j]
        v = dot(taps(shifts, CH * j, CH, True), w[weight_slot(meta, j)])
        xhat, z = normed(cst_in, y_in[rows], s)
        d = v * slope(z) * mask_of(meta, j)
        grad[rows] = v.astype(BF) if last else d
        total[s] += colsum(d)
        total[2 + s] += colsum(d * xhat)
    spread_out(st_out, total)


def weight_grad(meta, dyt, act, field, shifts, wg):
    for j in range(NCH):
        field[8 + CH * j : 8 + CH * (j + 1)] = act[CH * j : CH * (j + 1)].astype(F32)
    fill_shifts(field, shifts)

    def store(slot, v):
        for t in range(9):
            for j in range(8):
                block = v[16 * j : 16 * (j + 1), 128 * t : 128 * (t + 1)].astype(BF)
                wg[j, 9 * slot + t] = block

    @pl.when(meta[0] == 0)
    def _():
        store(0, dot(dyt[...], taps(shifts, 0, PX)))
        store(1, jnp.zeros((128, 1152), F32))

    @pl.when(meta[0] == 1)
    def _():
        store(0, dot(dyt[:, 0:CUT], taps(shifts, 0, CUT)))
        store(1, dot(dyt[:, CUT:PX], taps(shifts, CUT, PX - CUT)))


def part_out(meta, wg, send):
    for z in range(4):
        send[z] = wg[2 * z + 1 - meta[5]]


def second_back_kernel(meta, dz, y, cst, st, w, act, y_in, cst_in, gw, grad, st_out, sums, wg, send, field, shifts, dyt):
    guard(field, shifts)
    out_grad(meta, dz, y, cst, st, sums, field, dyt)
    fill_shifts(field, shifts)
    conv_back(meta, False, w, y_in, cst_in, shifts, grad, st_out)
    weight_grad(meta, dyt, act, field, shifts, wg)
    for j in range(8):
        for i in range(3):
            wg[j, 18 + i] = gw[j, i]
    part_out(meta, wg, send)


def first_back_kernel(meta, dz, y, cst, st, w, act, y_in, cst_in, grad, st_out, sums, wg, send, field, shifts, dyt):
    guard(field, shifts)
    out_grad(meta, dz, y, cst, st, sums, field, dyt)
    fill_shifts(field, shifts)
    conv_back(meta, True, w, y_in, cst_in, shifts, grad, st_out)
    weight_grad(meta, dyt, act, field, shifts, wg)
    part_out(meta, wg, send)


def final_kernel(meta, d0, d1, y, cst, st, sums1, sums2, u0, u1, u2, u3, extra, own, send, gs, gs_send, norm, *scratch):
    sums, feat, stem, field, flat, dyt, gf, blocks, other = scratch
    load_inputs(meta, (u0, u1, u2, u3), feat, stem)
    grad_sums(meta, jnp.sum(st[...], axis=0), sums)
    for j in range(NCH):
        rows = slice(CH * j, CH * (j + 1))
        _, z = normed(cst, y[rows], SLOT[j])
        v = (d0[rows].astype(F32) + d1[rows].astype(F32)) * slope(z) * mask_of(meta, j)
        field[rows] = input_grad(meta, v, y, cst, sums, j)
    flat[...] = jnp.zeros((CP, 128), F32)
    to_compact(meta, field, flat)
    dyt[...] = flat[...].T.astype(BF)
    c = meta[2]
    outs = ((own, c), (other, c ^ 2))

    @pl.when(meta[0] == 0)
    def _():
        gf[0:128, :] = dot(stem[:, 0:128], dyt[...], TN).astype(BF)
        blocks[0] = dot(dyt[...], feat[0:128, :], NT).astype(BF)
        for i in range(1, 6):
            blocks[i] = jnp.zeros((128, 128), BF)
        for out, s in outs:
            out[...] = gf[at32(s), :]

    @pl.when(meta[0] == 1)
    def _():
        gf[0:256, 0:MID] = dot(stem[:, 0:256], dyt[:, 0:MID], TN).astype(BF)
        gf[:, MID : MID + 128] = dot(stem[:, 256:768], dyt[:, MID : MID + 128], TN).astype(BF)
        for i in range(2):
            blocks[i] = dot(dyt[:, 0:MID], feat[128 * i : 128 * (i + 1), 0:MID], NT).astype(BF)
        for i in range(4):
            rows = slice(128 * i, 128 * (i + 1))
            blocks[2 + i] = dot(dyt[:, MID : MID + 128], feat[rows, MID : MID + 128], NT).astype(BF)
        for out, s in outs:
            out[...] = jnp.zeros((32, CP), BF)
            for i in range(2):
                at = pl.ds(pl.multiple_of(64 * s + 32 * i, 32), 32)
                out[:, MID * i : MID * (i + 1)] = gf[at, 0:MID]
            for i in range(4):
                at = pl.ds(pl.multiple_of(128 * s + 32 * i, 32), 32)
                out[:, 1024 + 128 * i : 1152 + 128 * i] = gf[at, MID : MID + 128]

    for i in range(CP // 128):
        for h in range(2):
            send[2 * i + h] = other[16 * h : 16 * (h + 1), 128 * i : 128 * (i + 1)]
    send[2 * (CP // 128) : 2 * (CP // 128) + 9] = extra[...]
    for i in range(3):
        block = blocks[3 * meta[1] + i]
        for j in range(8):
            gs[j, i] = block[16 * j : 16 * (j + 1)]
    part_out(meta, gs, gs_send)
    rest = jnp.zeros((4, 128), F32)
    norm[0] = jnp.concatenate([sums[0:4], sums1[0:4], sums2[0:4], rest], axis=0).astype(BF)


def total_kernel(st, out):
    out[0] = jnp.sum(st[...], axis=0)


def add_kernel(count, meta, *refs):
    kept, got, outs = refs[:count], refs[count : 2 * count], refs[2 * count :]
    for k, out in enumerate(outs):
        z = meta[4] ^ k
        at = 0
        for a, b in zip(kept, got):
            n = a.shape[1]
            out[at : at + n] = (a[2 * z + meta[5]].astype(F32) + b[z].astype(F32)).astype(out.dtype)
            at += n


def summed(refs, begin, end):
    total = refs[0][begin:end].astype(F32)
    for r in refs[1:]:
        total += r[begin:end].astype(F32)
    return total.astype(BF)


def sum_kernel(meta, *refs):
    parts, (total, extra) = refs[:4], refs[4:]
    total[0:9] = summed(parts, 0, 9)
    total[9:12] = summed(parts, 18, 21)
    extra[...] = summed(parts, 9, 18)


def join_kernel(meta, *refs):
    parts, (total, received, norm, out) = refs[:4], refs[4:]
    out[0:9] = summed(parts, 0, 9)
    out[9:18] = total[0:9]
    out[27:30] = total[9:12]

    @pl.when(meta[0] == 0)
    def _():
        at = 2 * (CP // 128)
        out[18:27] = received[at : at + 9]

    @pl.when(meta[0] == 1)
    def _():
        out[18:27] = summed(parts, 9, 18)

    out[30:33] = summed(parts, 18, 21)
    out[33:34] = norm[...]


def source(meta, k):
    c = meta[4] ^ (k % 4)
    return c >> 1, c & 1, meta[5] ^ (k // 4)


def at16(h):
    return pl.ds(pl.multiple_of(16 * h, 16), 16)


def conv_out(meta, half, parts, out, room, sems):
    for k in range(4):
        group, branch, _ = source(meta, k)
        r = parts[k]
        for i in range(3):
            layer = i if i < 2 else 1 - group
            level = group if i < 2 else 2
            for t in range(9):
                room[layer, level, branch, t] = r[9 * i + t].astype(F32)

    h = meta[5] ^ half
    copies = []
    for layer in range(2):
        for level in range(3):
            for branch in range(2):
                to = out.at[level, 2 * branch + layer, :, at16(h), :]
                copy = pltpu.make_async_copy(room.at[layer, level, branch], to, sems.at[layer, level, branch])
                copy.start()
                copies.append(copy)
    return copies


def row_outs(meta, half, parts, gcw, gcb, gbw, s0, s1, s2):
    h = meta[5] ^ half
    for k in range(4):
        group, branch, _ = source(meta, k)
        r = parts[k]
        for group_id in range(2):
            slots = range(1 + group_id)

            @pl.when((group == group_id) & (branch == 0))
            def _():
                turned = r[29].astype(F32).T
                for half_id in range(2):
                    size = (16, 4)[half_id]

                    @pl.when(h == half_id)
                    def _():
                        for slot in slots:
                            level = group_id + slot
                            gcw[level, 16 * half_id : 16 * half_id + size, :] = r[27 + slot].astype(F32)[0:size]
                            gcb[level : level + 1, 16 * half_id : 16 * half_id + size] = turned[slot : slot + 1, 0:size]

            @pl.when((group == group_id) & (branch == 1))
            def _():
                for slot in slots:
                    turned = r[27 + slot].astype(F32).T
                    for half_id in range(2):

                        @pl.when(h == half_id)
                        def _():
                            for i in range(5):
                                at = 16 * half_id
                                gbw[i, group_id + slot : group_id + slot + 1, at : at + 16] = turned[i : i + 1, 0:16]

        @pl.when((group == 0) & (branch == 0))
        def _():
            s0[at16(h), :] = r[30].astype(F32)

        @pl.when((group == 1) & (branch == 0))
        def _():
            for i in range(2):
                s1[at16(h), 128 * i : 128 * (i + 1)] = r[30 + i].astype(F32)
            s2[at16(h), 0:128] = r[32].astype(F32)

        @pl.when((group == 1) & (branch == 1))
        def _():
            for i in range(3):
                s2[at16(h), 128 * (i + 1) : 128 * (i + 2)] = r[30 + i].astype(F32)


def near_out_kernel(meta, *refs):
    parts, (out, gcw, gcb, gbw, s0, s1, s2, gbb, gains, shifts, room, sems) = refs[:4], refs[4:]
    copies = conv_out(meta, 0, parts, out, room, sems)
    row_outs(meta, 0, parts, gcw, gcb, gbw, s0, s1, s2)
    c = meta[2]
    for k in range(4):
        group, branch, _ = source(meta, k)
        r = parts[k]
        for group_id in range(2):

            @pl.when((group == group_id) & (branch == 1))
            def _():
                bias = r[29].astype(F32)
                for slot in range(1 + group_id):
                    level = group_id + slot
                    gbb[level : level + 1, :] = bias[0:1, 2 + 5 * slot : 7 + 5 * slot]

        v = r[33].astype(F32)
        mine = v[:, 0:32]
        for i in range(1, 4):
            mine = jnp.where(c == i, v[:, 32 * i : 32 * (i + 1)], mine)
        for layer in range(3):
            at = 0 if layer == 0 else layer + 2 * branch
            base = 4 * layer

            @pl.when(group == 0)
            def _():
                shifts[at, 0:1, :] = mine[base : base + 1]
                gains[at, 0:1, :] = mine[base + 2 : base + 3]

            @pl.when(group == 1)
            def _():
                shifts[at, 1:3, :] = mine[base : base + 2]
                gains[at, 1:3, :] = mine[base + 2 : base + 4]

    for copy in copies:
        copy.wait()


def far_out_kernel(meta, *refs):
    parts, earlier, (out, gcw, gcb, gbw, s0, s1, s2, room, sems) = refs[:4], refs[5:11], refs[11:]
    copies = conv_out(meta, 1, parts, out, room, sems)
    outs = (gcw, gcb, gbw, s0, s1, s2)
    for old, new in zip(earlier, outs):
        new[...] = old[...]
    row_outs(meta, 1, parts, *outs)
    for copy in copies:
        copy.wait()


def class_out_kernel(sizes, meta, mine, near, far, cross, class_out, box_out):
    n0, n1, n2 = sizes

    def store(out, fine, rest):
        n = out.shape[0]
        out[:, 0:n0] = fine[0:n, 0:n0]
        out[:, n0 : n0 + n1] = rest[0:n, 0:n1]
        out[:, n0 + n1 : n0 + n1 + n2] = rest[0:n, MID : MID + n2]

    for group in range(2):
        for branch in range(2):

            @pl.when((meta[0] == group) & (meta[1] == branch))
            def _():
                here, there = (mine, near), (far, cross)
                for i, out in enumerate((class_out, box_out)):
                    pair = (here[branch ^ i], there[branch ^ i])
                    store(out, pair[group], pair[1 - group])


def feature_out_kernel(meta, own, received, fine, mid, coarse, other):
    for i in range(CP // 128):
        for h in range(2):
            other[16 * h : 16 * (h + 1), 128 * i : 128 * (i + 1)] = received[2 * i + h]

    def store(a, b):
        n1, n2 = mid.shape[1], coarse.shape[0]
        fine[...] = a[:, 0 : fine.shape[1]]
        for i in range(2):
            mid[32 * i : 32 * (i + 1), :] = b[:, MID * i : MID * i + n1]
        v = jnp.concatenate([b[:, 1024 + 128 * i : 1152 + 128 * i] for i in range(4)], axis=0)
        coarse[...] = v.astype(F32).T[0:n2].astype(BF)

    @pl.when(meta[0] == 0)
    def _():
        store(own, other)

    @pl.when(meta[0] == 1)
    def _():
        store(other, own)


def pack_kernel(f0, f1, f2, s0, s1, s2, gains, shifts, box, own, send, small):
    group = lax.axis_index("chan") // 2

    def fine(out):
        out[:, 0 : f0.shape[1]] = f0[...]
        out[:, f0.shape[1] : CP] = jnp.zeros((32, CP - f0.shape[1]), BF)
        out[:, CP : CP + 128] = s0[...]
        out[:, CP + 128 : PAR] = jnp.zeros((32, PAR - CP - 128), BF)

    def rest(out):
        n1, n2 = f1.shape[1], f2.shape[0]
        for i in range(2):
            out[:, MID * i : MID * i + n1] = f1[32 * i : 32 * (i + 1), :]
            out[:, MID * i + n1 : MID * (i + 1)] = jnp.zeros((32, MID - n1), BF)
        v = jnp.concatenate([f2[...].astype(F32), jnp.zeros((128 - n2, 128), F32)], axis=0).T.astype(BF)
        for i in range(4):
            out[:, 1024 + 128 * i : 1152 + 128 * i] = v[32 * i : 32 * (i + 1)]
        out[:, STEM : STEM + 256] = s1[...]
        out[:, STEM + 256 : PAR] = s2[...]

    @pl.when(group == 0)
    def _():
        fine(own)
        rest(send)

    @pl.when(group == 1)
    def _():
        rest(own)
        fine(send)

    small[...] = jnp.zeros((64, 32), F32)
    for base, v in ((0, gains), (16, shifts), (32, box)):
        for k in range(5):
            small[base + 3 * k : base + 3 * k + 3] = v[k].astype(F32)
    for i in range(2):
        v = small[32 * i : 32 * (i + 1)]
        high = v.astype(BF).astype(F32)
        mid = (v - high).astype(BF).astype(F32)
        block = jnp.concatenate([high, mid, v - high - mid, jnp.zeros((32, 32), F32)], axis=1).astype(BF)
        for out in (own, send):
            out[:, PAR + 128 * i : PAR + 128 * (i + 1)] = block


def pred_kernel(sizes, meta, ccot, cw, cb, bcot, bb, conv, own, box, first, first_cross, second, second_cross, room, sems):
    n0, n1, n2 = sizes
    copies = []
    for layer, outs in enumerate(((first, first_cross), (second, second_cross))):
        for i, out in enumerate(outs):
            for slot in range(2):
                taken = conv.at[1 - meta[0] + slot, 2 * (meta[1] ^ i) + layer]
                copy = pltpu.make_async_copy(taken, out.at[pl.ds(9 * slot, 9)], sems.at[layer, i, slot])
                copy.start()
                copies.append(copy)
    lane = lax.broadcasted_iota(jnp.int32, (32, 128), 1)

    def biases(b, level):
        block = jnp.concatenate([b[...], jnp.zeros((3, 128 - b.shape[1]), F32)], axis=1)
        block = jnp.concatenate([block, jnp.zeros((5, 128), F32)], axis=0)
        col = block.T[0:32, level : level + 1]
        high = col.astype(BF).astype(F32)
        mid = (col - high).astype(BF).astype(F32)
        low = col - high - mid
        v = jnp.where(lane == 0, high, jnp.where(lane == 1, mid, jnp.where(lane == 2, low, 0.0)))
        return v.astype(BF)

    def fill(out, base, cot, b, fine, weights):
        n = cot.shape[0]
        room[...] = jnp.zeros((32, CP), BF)
        if fine:
            room[0:n, 0:n0] = cot[:, 0:n0]
        else:
            room[0:n, 0:n1] = cot[:, n0 : n0 + n1]
            room[0:n, MID : MID + n2] = cot[:, n0 + n1 : n0 + n1 + n2]
        for i in range(CP // 128):
            out[base + i] = room[:, 128 * i : 128 * (i + 1)]
        for slot in range(2):
            level = 0 if fine else 1 + slot
            at = base + CP // 128 + 2 * slot
            out[at] = jnp.zeros((32, 128), BF)
            if weights:
                out[at, 0:n] = cw[level]
            out[at + 1] = biases(b, level)

    for group in range(2):

        @pl.when(meta[0] == group)
        def _():
            fill(own, 0, ccot, cb, group == 0, True)
            fill(box, 0, bcot, bb, group == 0, False)

        @pl.when(meta[0] != group)
        def _():
            fill(second, TAPS, ccot, cb, group == 0, True)
            second_cross[TAPS:] = second[TAPS:]

    for copy in copies:
        copy.wait()


def call(body, outs, scratch, args, last=False, limit=VMEM, in_place=(), aliases={}, flops=10**6):
    place = jax.ShapeDtypeStruct if last else pltpu.VMEM

    def space(i, dtype):
        if i in in_place:
            return pl.BlockSpec(memory_space=pl.ANY)
        return pl.BlockSpec(memory_space=pltpu.SMEM if dtype == jnp.int32 else pltpu.VMEM)

    return pl.pallas_call(
        body,
        out_shape=[place(s, d) for s, d in outs],
        in_specs=[space(i, a.dtype) for i, a in enumerate(args)],
        out_specs=[space(len(args) + i, d) for i, (_, d) in enumerate(outs)],
        scratch_shapes=[s if callable(getattr(s, "get_ref_aval", None)) else pltpu.VMEM(*s) for s in scratch],
        input_output_aliases=aliases,
        compiler_params=pltpu.CompilerParams(vmem_limit_bytes=limit),
        cost_estimate=pl.CostEstimate(flops=flops, bytes_accessed=10**4, transcendentals=0),
    )(*args)


def shards(f0, f1, f2, units, s0, s1, s2, conv, gains, shifts, cw, cb, bw, bb, ccot, bcot):
    dp = lax.axis_size("dp")
    c = lax.axis_index("chan")
    group, branch = c // 2, c % 2
    fine = group == 0
    direct = dp == 8
    place = lax.axis_index("dp") if direct else 0
    meta = jnp.stack([group, branch, c, units[0], place // 2, place % 2]).astype(jnp.int32)
    n0, n1, n2 = f0.shape[2], f1.shape[2], f2.shape[2]

    def across(v):
        return lax.ppermute(v, "chan", [(i, i ^ 2) for i in range(4)])

    def diagonal(v):
        return lax.ppermute(v, "chan", [(i, i ^ 3) for i in range(4)])

    def beside(v, pairs=((0, 1), (1, 0), (2, 3), (3, 2))):
        return lax.ppermute(v, "chan", list(pairs))

    def exchange(st, *hold):
        st, *hold = lax.optimization_barrier((st, *hold))
        st = lax.all_to_all(st, "dp", 0, 0, tiled=True)
        return lax.optimization_barrier((st, *hold)) if hold else st

    def after(v, *others):
        return lax.optimization_barrier((v, *others))[0]

    def over_z(v):
        if not direct:
            return v
        parts = []
        for k in range(4):
            pairs = [
                (8 * z + 4 * y + i, 8 * (i ^ k) + 4 * y + z) for z in range(4) for y in range(2) for i in range(4)
            ]
            parts.append(lax.ppermute(v, ("dp", "chan"), pairs))
        return parts

    def everywhere(parts):
        if direct:
            return parts + [over_y(p) for p in parts]
        v = lax.all_to_all(parts.reshape(4, 2, *parts.shape[1:]), "chan", 0, 0, tiled=True)
        return [v[k % 4, k // 4] for k in range(8)]

    def joined(*parts):
        return jnp.concatenate(parts, axis=-3)

    def over_y(v):
        return lax.ppermute(v, "dp", [(i, i ^ 1) for i in range(8)])

    def along_z(kept, got):
        shape = (sum(v.shape[1] for v in kept), 16, 128)
        outs = [(shape, F32)] + [(shape, BF)] * 3
        own, *rest = call(functools.partial(add_kernel, len(kept)), outs, [], (meta, *kept, *got))
        return [own] + [lax.ppermute(v, "dp", [(i, i ^ (2 * k + 2)) for i in range(8)]) for k, v in enumerate(rest)]

    def reduce(v):
        return lax.optimization_barrier(lax.psum(v.astype(F32), "dp")).astype(BF)

    own, send = call(
        pack_kernel,
        [((32, WIDE), BF), ((32, WIDE), BF)],
        [((64, 32), F32)],
        (f0[0], f1[0], f2[0].T, s0, s1, s2, gains.transpose(1, 0, 2), shifts.transpose(1, 0, 2), bw.transpose(1, 0, 2)),
        limit=WHOLE,
    )
    far_u = across(send)
    own_pred, box_pred, send1, send1_cross, send2, send2_cross = call(
        functools.partial(pred_kernel, (n0, n1, n2)),
        [((CLS, 32, 128), BF)] * 2 + [((TAPS, 32, 128), BF)] * 2 + [((TAPS + CLS, 32, 128), BF)] * 2,
        [((32, CP), BF), pltpu.SemaphoreType.DMA((2, 2, 2))],
        (meta, ccot[0], cw, cb, bcot[0], after(bb, own), conv),
        limit=WHOLE,
        in_place=(6,),
        flops=2 * 10**9,
    )
    near = beside(after(conv, own))
    far_u = after(far_u, near, send2)
    u = (own, far_u, beside(own), beside(far_u))
    to_class = ((1, 0), (3, 2))
    near_pred = beside(own_pred, to_class)

    def weights_of(layer, far, cross):
        return call(
            functools.partial(weight_kernel, layer),
            [((2, 128, 1152), BF), ((2, 1152, 128), BF)],
            [],
            (meta, conv, near, far, cross),
        )

    canvas = (PX, 128)
    stat = (dp, 8, 128)
    moved = [((PX + 16, 128), F32), ((3, PX + 2 * ST, 128), BF)]
    y0, st, cnt, par = call(
        stem_kernel,
        [(canvas, F32), (stat, F32), ((8, 128), F32), ((64, 128), F32)],
        [((512, CP), BF), ((128, 768), BF), ((CP, 128), F32)],
        (meta, *u),
    )
    far1, cross1 = across(after(send1, far_u)), diagonal(after(send1_cross, far_u))
    st, near_pred = exchange(st, near_pred)
    far1, cross1 = after((far1, cross1), st)
    far2, cross2 = across(after(send2, far1)), diagonal(after(send2_cross, cross1))
    w1, w1_tall = weights_of(0, far1, cross1)
    forward_outs = [(canvas, BF), (canvas, F32), (stat, F32), ((16, 128), F32)]
    act0, y1, st, cst0 = call(functools.partial(forward_kernel, True), forward_outs, moved, (meta, y0, st, cnt, w1, par))
    st = exchange(st)
    far2, cross2 = after((far2, cross2), st)
    w2, w2_tall = weights_of(1, far2, cross2)
    act1, y2, st, cst1 = call(
        functools.partial(forward_kernel, False), forward_outs, moved, (meta, y1, st, cnt, w2, par)
    )
    st = exchange(st)
    dz2, st, cst2, x2, cot, wp = call(
        heads_kernel,
        [(canvas, F32), (stat, F32), ((16, 128), F32), ((CP, 256), BF), ((128, CP), BF), ((2, 128, 256), BF)],
        [(canvas, F32), ((CP, 128), F32)],
        (meta, y2, st, par, own_pred, far2, near_pred, cross2, box_pred),
    )
    gw, mine, near, far, cross = call(
        logits_kernel, [((8, 3, 16, 128), BF)] + [((32, CP), BF)] * 4, [((128, CP), BF)], (meta, x2, cot, wp)
    )
    near, far, cross = beside(near), across(far), diagonal(cross)
    st = exchange(after(st, gw))
    st, near, far, cross = lax.optimization_barrier((st, near, far, cross))
    back_scratch = moved + [((128, PX), BF)]
    dz1, st, sums2, wg2, send2 = call(
        second_back_kernel,
        [(canvas, F32), (stat, F32), ((8, 128), F32), ((8, 21, 16, 128), BF), ((4, 21, 16, 128), BF)],
        back_scratch,
        (meta, dz2, y2, cst2, st, w2_tall, act1, y1, cst1, gw),
    )
    got2 = over_y(send2) if direct else reduce(wg2)
    st, got2 = lax.optimization_barrier((exchange(after(st, send2)), got2))
    d0, st, sums1, wg1, send1 = call(
        first_back_kernel,
        [(canvas, BF), (stat, F32), ((8, 128), F32), ((8, 18, 16, 128), BF), ((4, 18, 16, 128), BF)],
        back_scratch,
        (meta, dz1, y1, cst1, st, w1_tall, act0, y0, cst0),
    )
    got1 = over_y(send1) if direct else reduce(wg1)
    d0_other, st_other = beside(d0), beside(st)
    st = st + st_other
    if direct:
        parts2 = along_z([wg2], [after(got2, d0)])
        st = after(st, d0_other, *parts2[:1])
        (st,) = call(total_kernel, [((1, 8, 128), F32)], [], (exchange(st),))
        st, got1, *parts2 = lax.optimization_barrier((st, got1, *parts2))
        total, extra = call(sum_kernel, [((12, 16, 128), BF), ((9, 16, 128), BF)], [], (meta, *parts2))
    else:
        st = exchange(st)
        extra = jnp.zeros((9, 16, 128), BF)
    own, send, gs, gs_send, norm = call(
        final_kernel,
        [((32, CP), BF), ((SENT, 16, 128), BF), ((8, 3, 16, 128), BF), ((4, 3, 16, 128), BF), ((1, 16, 128), BF)],
        [
            ((8, 128), F32),
            ((512, CP), BF),
            ((128, 768), BF),
            (canvas, F32),
            ((CP, 128), F32),
            ((128, CP), BF),
            ((512, CP), BF),
            ((6, 128, 128), BF),
            ((32, CP), BF),
        ],
        (meta, d0, d0_other, y0, cst0, st, sums1, sums2, *u, extra),
    )
    received = across(send)
    if direct:
        parts1 = along_z([wg1, gs], [got1, over_y(gs_send)])
        (grads,) = call(join_kernel, [((34, 16, 128), BF)], [], (meta, *parts1, total, received, norm))
    else:
        extra = lax.ppermute(got2[:, 9:18], "chan", [(2, 0), (3, 1)])
        third = jnp.where(fine, extra, got1[:, 9:18])
        norm = jnp.broadcast_to(norm[None], (8, *norm.shape))
        grads = joined(got1[:, :9], got2[:, :9], third, got2[:, 18:21], reduce(gs), norm)
    grads = everywhere(over_z(grads))

    room = [((2, 3, 2, conv.shape[2], 16, 128), F32), pltpu.SemaphoreType.DMA((2, 3, 2))]
    rows = [(cw.shape, F32), (cb.shape, F32), ((5, 3, 32), F32), (s0.shape, F32), (s1.shape, F32), (s2.shape, F32)]
    wholes = [(bb.shape, F32), ((5, 3, 32), F32), ((5, 3, 32), F32)]
    grad_conv, *half, grad_bb, grad_gains, grad_shifts = call(
        near_out_kernel, [(conv.shape, F32)] + rows + wholes, room, (meta, *grads[:4]), True, in_place=(5,)
    )
    mine, own = after((mine, own), *half)
    box_rows, class_rows = bcot.shape[1], ccot.shape[1]
    class_out, box_out = call(
        functools.partial(class_out_kernel, (n0, n1, n2)),
        [((class_rows, n0 + n1 + n2), BF), ((box_rows, n0 + n1 + n2), BF)],
        [],
        (meta, mine, near, far, cross),
        True,
    )
    grad_fine, grad_mid, grad_coarse = call(
        feature_out_kernel,
        [(f0.shape[1:], BF), (f1.shape[1:], BF), ((n2, f2.shape[1]), BF)],
        [((32, CP), BF)],
        (meta, own, received),
        True,
    )

    grad_conv, grad_cw, grad_cb, grad_bw, grad_s0, grad_s1, grad_s2 = call(
        far_out_kernel,
        [(conv.shape, F32)] + rows,
        room,
        (meta, *grads[4:], grad_conv, *half),
        True,
        in_place=(5, 12),
        aliases={5: 0},
    )
    return (
        class_out[None],
        box_out[None],
        grad_fine[None],
        grad_mid[None],
        grad_coarse.T[None],
        grad_s0,
        grad_s1,
        grad_s2,
        grad_conv,
        grad_gains.transpose(1, 0, 2),
        grad_shifts.transpose(1, 0, 2),
        grad_cw,
        grad_cb,
        grad_bw.transpose(1, 0, 2),
        grad_bb,
    )


def solution(mesh):
    placed = (
        P("dp", "chan", None),
        P("dp", "chan", None),
        P("dp", "chan", None),
        P("dp"),
        P("chan", None),
        P("chan", None),
        P("chan", None),
        P(None, None, None, "chan", None),
        P(None, None, "chan"),
        P(None, None, "chan"),
        P(None, "chan", None),
        P(None, "chan"),
        P(None, None, "chan"),
        P(),
        P("dp", "chan", None),
        P("dp", None, None),
    )
    return jax.shard_map(
        shards,
        mesh=mesh,
        in_specs=placed,
        out_specs=(
            P("dp", "chan", None),
            P("dp", None, None),
            P("dp", "chan", None),
            P("dp", "chan", None),
            P("dp", "chan", None),
            P("chan", None),
            P("chan", None),
            P("chan", None),
            P(None, None, None, "chan", None),
            P(None, None, "chan"),
            P(None, None, "chan"),
            P(None, "chan", None),
            P(None, "chan"),
            P(None, None, "chan"),
            P(),
        ),
        check_vma=False,
    )
```

```python
import functools

import jax
import jax.numpy as jnp
from jax import lax
from jax.experimental import pallas as pl
from jax.experimental.pallas import tpu as pltpu
from jax.sharding import PartitionSpec as P

BF = jnp.bfloat16
F32 = jnp.float32
EPS = 0.001
ST = 48
ROWS = 40
PX = ST * ROWS
CR = 8
CH = CR * ST
NCH = ROWS // CR
SLOT = (0, 0, 0, 1, 1)
CUT = 24 * ST
CP = 1664
MID = 512
E0, E1, E2 = 40, 20, 10
STEM = 1536
PAR = STEM + 768
WIDE = PAR + 256
CLS = CP // 128 + 4
TAPS = 18
LOW = (MID + 128) // 128
SECOND = TAPS + LOW + 4
SENT = 2 * (CP // 128) + 9
VMEM = 12 * 2**20
WHOLE = 56 * 2**20
NT = (((1,), (1,)), ((), ()))
TN = (((0,), (0,)), ((), ()))


def dot(a, b, dims=(((1,), (0,)), ((), ()))):
    return lax.dot_general(a, b, dims, preferred_element_type=F32)


def limits(meta, slot):
    group, units = meta[0], meta[3]
    if slot == 0:
        edge = jnp.where(group == 0, 4 * units, 2 * units)
        return edge, edge
    return (
        jnp.where(group == 0, 4 * units, 24 + units),
        jnp.where(group == 0, 4 * units, units),
    )


def mask_of(meta, j):
    row_end, col_end = limits(meta, SLOT[j])
    row = lax.broadcasted_iota(jnp.int32, (CR, ST, 128), 0) + CR * j
    col = lax.broadcasted_iota(jnp.int32, (CR, ST, 128), 1)
    inside = (row < row_end) & (col < col_end)
    return jnp.where(inside, 1.0, 0.0).reshape(CH, 128)


def pick(meta, first, second):
    total = first + second
    return jnp.where(meta[0] == 0, total, first), jnp.where(meta[0] == 0, total, second)


def level_rows(meta, base, layer):
    fine = meta[0] == 0
    at = base + 3 * layer
    return at + jnp.where(fine, 0, 1), at + jnp.where(fine, 0, 2)


def norm_constants(meta, st, par, layer, cst):
    total = jnp.sum(st[...], axis=0)
    row = [total[i : i + 1] for i in range(6)]
    first = pick(meta, row[0], row[1])
    second = pick(meta, row[2], row[3])
    count = pick(meta, row[4], row[5])
    gain_at = level_rows(meta, 0, layer)
    shift_at = level_rows(meta, 16, layer)
    for s in range(2):
        rn = 1.0 / count[s]
        mean = first[s] * rn
        inv = lax.rsqrt(second[s] * rn - mean * mean + EPS)
        cst[s : s + 1] = mean
        cst[2 + s : 3 + s] = inv
        cst[4 + s : 5 + s] = par[pl.ds(gain_at[s], 1), :]
        cst[6 + s : 7 + s] = par[pl.ds(shift_at[s], 1), :]
        cst[8 + s : 9 + s] = rn
        cst[10 + s : 11 + s] = count[s]
    cst[12:16] = jnp.zeros((4, 128), F32)


def normed(cst, y, s):
    xhat = (y - cst[s : s + 1]) * cst[2 + s : 3 + s]
    return xhat, xhat * cst[4 + s : 5 + s] + cst[6 + s : 7 + s]


def sigmoid(z):
    return 0.5 * jnp.tanh(0.5 * z) + 0.5


def slope(z):
    s = sigmoid(z)
    return s * (1.0 + z * (1.0 - s))


def spread_out(st, rows):
    block = jnp.concatenate(rows + [jnp.zeros((8 - len(rows), 128), F32)], axis=0)
    st[...] = jnp.broadcast_to(block[None], st.shape)


def colsum(v):
    return jnp.sum(v, axis=0, keepdims=True)


def guard(field, shifts):
    field[0:8] = jnp.zeros((8, 128), F32)
    field[8 + PX : 16 + PX] = jnp.zeros((8, 128), F32)
    for k in range(3):
        shifts[k, 0:ST] = jnp.zeros((ST, 128), BF)
        shifts[k, ST + PX :] = jnp.zeros((ST, 128), BF)


def fill_shifts(field, shifts):
    for k in range(3):
        for j in range(NCH):
            at = 8 + CH * j + k - 1
            shifts[k, ST + CH * j : ST + CH * (j + 1)] = field[at : at + CH].astype(BF)


def taps(shifts, begin, size, back=False):
    parts = []
    for kr in range(3):
        for kc in range(3):
            k, r = (2 - kc, 1 - kr) if back else (kc, kr - 1)
            at = ST + begin + ST * r
            parts.append(shifts[k, at : at + size])
    return jnp.concatenate(parts, axis=1)


def slices_of(meta):
    c = meta[2]
    return (c, c ^ 2, c ^ 1, c ^ 3)


def at32(s, extra=0):
    return pl.ds(pl.multiple_of(32 * s + extra, 32), 32)


def weight_slot(meta, j):
    return jnp.where(meta[0] == 0, 0, SLOT[j])


def to_compact(meta, canvas, out):
    @pl.when(meta[0] == 0)
    def _():
        for r in range(E0):
            out[E0 * r : E0 * (r + 1)] = canvas[ST * r : ST * r + E0]

    @pl.when(meta[0] == 1)
    def _():
        for r in range(E1):
            out[E1 * r : E1 * (r + 1)] = canvas[ST * r : ST * r + E1]
        for r in range(E2):
            at = CUT + ST * r
            out[MID + E2 * r : MID + E2 * (r + 1)] = canvas[at : at + E2]


def to_canvas(meta, compact, out):
    @pl.when(meta[0] == 0)
    def _():
        for r in range(E0):
            out[ST * r : ST * r + E0] = compact[E0 * r : E0 * (r + 1)]

    @pl.when(meta[0] == 1)
    def _():
        for r in range(E1):
            out[ST * r : ST * r + E1] = compact[E1 * r : E1 * (r + 1)]
        for r in range(E2):
            at = CUT + ST * r
            out[at : at + E2] = compact[MID + E2 * r : MID + E2 * (r + 1)]


def load_inputs(meta, pieces, feat, stem):
    for s, u in zip(slices_of(meta), pieces):

        @pl.when(meta[0] == 0)
        def _():
            feat[at32(s), :] = u[:, 0:CP]
            stem[at32(s), 0:128] = u[:, CP : CP + 128]

        @pl.when(meta[0] == 1)
        def _():
            for i in range(2):
                at = pl.ds(pl.multiple_of(64 * s + 32 * i, 32), 32)
                feat[at, 0:MID] = u[:, MID * i : MID * (i + 1)]
            for i in range(4):
                at = pl.ds(pl.multiple_of(128 * s + 32 * i, 32), 32)
                feat[at, MID : MID + 128] = u[:, 1024 + 128 * i : 1152 + 128 * i]
            stem[at32(s), :] = u[:, STEM:PAR]


def stem_kernel(meta, u0, u1, u2, u3, y, st, cnt, par, feat, stem, flat):
    load_inputs(meta, (u0, u1, u2, u3), feat, stem)
    lane = lax.broadcasted_iota(jnp.int32, (32, 128), 1) // 32
    for i in range(2):
        total = jnp.zeros((32, 128), F32)
        for s, u in zip(slices_of(meta), (u0, u1, u2, u3)):
            v = u[:, PAR + 128 * i : PAR + 128 * (i + 1)].astype(F32)
            v = v[:, 0:32] + v[:, 32:64] + v[:, 64:96]
            total = jnp.where(lane == s, jnp.concatenate([v] * 4, axis=1), total)
        par[32 * i : 32 * (i + 1)] = total
    y[...] = jnp.zeros((PX, 128), F32)

    @pl.when(meta[0] == 0)
    def _():
        flat[...] = dot(stem[:, 0:128], feat[0:128, :]).T

    @pl.when(meta[0] == 1)
    def _():
        flat[0:MID] = dot(stem[:, 0:256], feat[0:256, 0:MID]).T
        flat[MID : MID + 128] = dot(stem[:, 256:768], feat[0:512, MID : MID + 128]).T

    to_canvas(meta, flat, y)
    sums = [jnp.zeros((1, 128), F32) for _ in range(6)]
    for j in range(NCH):
        m = mask_of(meta, j)
        v = y[CH * j : CH * (j + 1)] * m
        s = SLOT[j]
        sums[s] += colsum(v)
        sums[2 + s] += colsum(v * v)
        sums[4 + s] += colsum(m)
    spread_out(st, sums)
    cnt[...] = jnp.concatenate(sums[4:6] + [jnp.zeros((6, 128), F32)], axis=0)


def forward_kernel(first, meta, y, st, cnt, w, *refs):
    par, act, out, st_out, cst, field, shifts = refs
    layer = 0 if first else 1 + 2 * meta[1]
    norm_constants(meta, st, par, layer, cst)
    guard(field, shifts)
    for j in range(NCH):
        rows = slice(CH * j, CH * (j + 1))
        _, z = normed(cst, y[rows], SLOT[j])
        v = z * sigmoid(z) * mask_of(meta, j)
        act[rows] = v.astype(BF)
        field[8 + CH * j : 8 + CH * (j + 1)] = v
    fill_shifts(field, shifts)
    sums = [jnp.zeros((1, 128), F32) for _ in range(4)]
    for j in range(NCH):
        v = dot(taps(shifts, CH * j, CH), w[weight_slot(meta, j)], NT)
        out[CH * j : CH * (j + 1)] = v
        v = v * mask_of(meta, j)
        s = SLOT[j]
        sums[s] += colsum(v)
        sums[2 + s] += colsum(v * v)
    spread_out(st_out, sums + [cnt[0:1], cnt[1:2]])


def weight_kernel(layer, meta, mine, near, far, cross, flat, tall):
    group, branch, c = meta[0], meta[1], meta[2]
    conv = 2 * branch + layer
    for slot in range(2):
        level = group + slot
        for t in range(9):
            for s, piece in (
                (c, mine[level, conv, t]),
                (c ^ 1, near[level, conv, t]),
                (c ^ 2, far[9 * slot + t]),
                (c ^ 3, cross[9 * slot + t]),
            ):
                flat[slot, at32(s), 128 * t : 128 * (t + 1)] = piece
                tall[slot, at32(s, 128 * t), :] = piece


def heads_kernel(meta, y, st, par, k0, k1, k2, k3, box_pack, dz, st_out, cst, x2, cot, wp, field, flat):
    norm_constants(meta, st, par, 2 + 2 * meta[1], cst)
    cot[...] = jnp.zeros((128, CP), BF)
    wp[...] = jnp.zeros((2, 128, 256), BF)

    pixels = CP // 128

    @pl.when(meta[1] == 0)
    def _():
        for s, k, sent in zip(slices_of(meta), (k0, k1, k2, k3), (False, True, False, True)):
            for i in range(pixels):
                if not sent or i < LOW:
                    cot[at32(s), 128 * i : 128 * (i + 1)] = k[TAPS + i if sent else i]
            for slot in range(2):
                for i in range(2):
                    at = (TAPS + LOW if sent else pixels) + 2 * slot + i
                    wp[slot, at32(s), 128 * i : 128 * (i + 1)] = k[at]

    @pl.when((meta[1] == 0) & (meta[0] == 0))
    def _():
        for s, k in zip(slices_of(meta)[1::2], (k1, k3)):
            for i in range(LOW, pixels):
                cot[at32(s), 128 * i : 128 * (i + 1)] = k[9 + i - LOW]

    @pl.when(meta[1] == 1)
    def _():
        for i in range(pixels):
            cot[0:32, 128 * i : 128 * (i + 1)] = box_pack[i]
        fine = meta[0] == 0
        for slot in range(2):
            row = lax.broadcasted_iota(jnp.int32, (32, 128), 0)
            box = jnp.zeros((32, 128), F32)
            for i in range(5):
                at = 32 + 3 * i
                line = jnp.where(fine, par[at : at + 1], par[at + 1 + slot : at + 2 + slot])
                box = jnp.where(row == i, line, box)
            wp[slot, 0:32, 0:128] = box.astype(BF)
            wp[slot, 0:32, 128:256] = box_pack[pixels + 2 * slot + 1]

    for part in range(2):
        for j in range(NCH):
            m = mask_of(meta, j)
            if part == 0:
                _, z = normed(cst, y[CH * j : CH * (j + 1)], SLOT[j])
                m = z * sigmoid(z) * m
            field[CH * j : CH * (j + 1)] = m
        flat[...] = jnp.zeros((CP, 128), F32)
        to_compact(meta, field, flat)
        x2[:, 128 * part : 128 * (part + 1)] = flat[...].astype(BF)

    @pl.when(meta[0] == 0)
    def _():
        flat[...] = dot(cot[...], wp[0, :, 0:128], TN)

    @pl.when(meta[0] == 1)
    def _():
        for slot, a, b in ((0, 0, MID), (1, MID, MID + 128)):
            flat[a:b] = dot(cot[:, a:b], wp[slot, :, 0:128], TN)

    field[...] = jnp.zeros((PX, 128), F32)
    to_canvas(meta, flat, field)
    sums = [jnp.zeros((1, 128), F32) for _ in range(4)]
    for j in range(NCH):
        rows = slice(CH * j, CH * (j + 1))
        s = SLOT[j]
        xhat, z = normed(cst, y[rows], s)
        v = field[rows] * slope(z) * mask_of(meta, j)
        dz[rows] = v
        sums[s] += colsum(v)
        sums[2 + s] += colsum(v * xhat)
    spread_out(st_out, sums)


def logits_kernel(meta, x2, cot, wp, gw, mine, near, far, cross, logits):
    def store(slot, v):
        bias = v[:, 128:256]

        @pl.when(meta[1] == 0)
        def _():
            gw_block(gw, slot, v[:, 0:128])

        @pl.when(meta[1] == 1)
        def _():
            gw_block(gw, slot, v[:, 0:128].T)

        return bias

    def finish(first, second):
        lane = lax.broadcasted_iota(jnp.int32, (128, 128), 1)
        cls = jnp.where(lane == 0, first, jnp.where(lane == 1, second, 0.0))
        a, b = first.T, second.T
        box = jnp.where((lane >= 7) & (lane < 12), pltpu.roll(b, 7, 1), 0.0)
        box = jnp.where((lane >= 2) & (lane < 7), pltpu.roll(a, 2, 1), box)
        gw_block(gw, 2, jnp.where(meta[1] == 0, cls, box))

    @pl.when(meta[0] == 0)
    def _():
        logits[...] = dot(wp[0], x2[...], NT).astype(BF)
        first = store(0, dot(cot[...], x2[...]))
        gw_block(gw, 1, jnp.zeros((128, 128), F32))
        finish(first, jnp.zeros((128, 128), F32))

    @pl.when(meta[0] == 1)
    def _():
        logits[...] = jnp.zeros((128, CP), BF)
        bias = []
        for slot, a, b in ((0, 0, MID), (1, MID, MID + 128)):
            logits[:, a:b] = dot(wp[slot], x2[a:b], NT).astype(BF)
            bias.append(store(slot, dot(cot[:, a:b], x2[a:b])))
        finish(*bias)

    for out, c in ((mine, 0), (near, 1), (far, 2), (cross, 3)):
        out[...] = logits[at32(jnp.where(meta[1] == 0, meta[2] ^ c, 0)), :]


def gw_block(gw, i, v):
    for j in range(8):
        gw[j, i] = v[16 * j : 16 * (j + 1)].astype(BF)


def grad_sums(meta, total, sums):
    shift = pick(meta, total[0:1], total[1:2])
    gain = pick(meta, total[2:3], total[3:4])
    sums[...] = jnp.concatenate(list(shift) + list(gain) + [jnp.zeros((4, 128), F32)], axis=0)


def input_grad(meta, dz, y, cst, sums, j):
    s = SLOT[j]
    xhat, _ = normed(cst, y[CH * j : CH * (j + 1)], s)
    factor = cst[4 + s : 5 + s] * cst[2 + s : 3 + s]
    mean = (sums[s : s + 1] + xhat * sums[2 + s : 3 + s]) * cst[8 + s : 9 + s]
    return mask_of(meta, j) * factor * (dz - mean)


def out_grad(meta, dz, y, cst, st, sums, field, dyt):
    grad_sums(meta, jnp.sum(st[...], axis=0), sums)
    for j in range(NCH):
        rows = slice(CH * j, CH * (j + 1))
        v = input_grad(meta, dz[rows], y, cst, sums, j)
        field[8 + CH * j : 8 + CH * (j + 1)] = v
        dyt[:, rows] = v.T.astype(BF)


def conv_back(meta, last, w, y_in, cst_in, shifts, grad, st_out):
    total = [jnp.zeros((1, 128), F32) for _ in range(4)]
    for j in range(NCH):
        rows = slice(CH * j, CH * (j + 1))
        s = SLOT[j]
        v = dot(taps(shifts, CH * j, CH, True), w[weight_slot(meta, j)])
        xhat, z = normed(cst_in, y_in[rows], s)
        d = v * slope(z) * mask_of(meta, j)
        grad[rows] = v.astype(BF) if last else d
        total[s] += colsum(d)
        total[2 + s] += colsum(d * xhat)
    spread_out(st_out, total)


def weight_grad(meta, dyt, act, field, shifts, wg):
    for j in range(NCH):
        field[8 + CH * j : 8 + CH * (j + 1)] = act[CH * j : CH * (j + 1)].astype(F32)
    fill_shifts(field, shifts)

    def store(slot, v):
        for t in range(9):
            for j in range(8):
                block = v[16 * j : 16 * (j + 1), 128 * t : 128 * (t + 1)].astype(BF)
                wg[j, 9 * slot + t] = block

    @pl.when(meta[0] == 0)
    def _():
        store(0, dot(dyt[...], taps(shifts, 0, PX)))
        store(1, jnp.zeros((128, 1152), F32))

    @pl.when(meta[0] == 1)
    def _():
        store(0, dot(dyt[:, 0:CUT], taps(shifts, 0, CUT)))
        store(1, dot(dyt[:, CUT:PX], taps(shifts, CUT, PX - CUT)))


def part_out(meta, wg, send):
    for z in range(4):
        send[z] = wg[2 * z + 1 - meta[5]]


def second_back_kernel(meta, dz, y, cst, st, w, act, y_in, cst_in, gw, grad, st_out, sums, wg, send, field, shifts, dyt):
    guard(field, shifts)
    out_grad(meta, dz, y, cst, st, sums, field, dyt)
    fill_shifts(field, shifts)
    conv_back(meta, False, w, y_in, cst_in, shifts, grad, st_out)
    weight_grad(meta, dyt, act, field, shifts, wg)
    for j in range(8):
        for i in range(3):
            wg[j, 18 + i] = gw[j, i]
    part_out(meta, wg, send)


def first_back_kernel(meta, dz, y, cst, st, w, act, y_in, cst_in, grad, st_out, sums, wg, send, field, shifts, dyt):
    guard(field, shifts)
    out_grad(meta, dz, y, cst, st, sums, field, dyt)
    fill_shifts(field, shifts)
    conv_back(meta, True, w, y_in, cst_in, shifts, grad, st_out)
    weight_grad(meta, dyt, act, field, shifts, wg)
    part_out(meta, wg, send)


def final_kernel(meta, d0, d1, y, cst, st, sums1, sums2, u0, u1, u2, u3, own, other, gs, gs_send, norm, *scratch):
    sums, feat, stem, field, flat, dyt, gf, blocks = scratch
    load_inputs(meta, (u0, u1, u2, u3), feat, stem)
    grad_sums(meta, jnp.sum(st[...], axis=0), sums)
    for j in range(NCH):
        rows = slice(CH * j, CH * (j + 1))
        _, z = normed(cst, y[rows], SLOT[j])
        v = (d0[rows].astype(F32) + d1[rows].astype(F32)) * slope(z) * mask_of(meta, j)
        field[rows] = input_grad(meta, v, y, cst, sums, j)
    flat[...] = jnp.zeros((CP, 128), F32)
    to_compact(meta, field, flat)
    dyt[...] = flat[...].T.astype(BF)
    c = meta[2]
    outs = ((own, c), (other, c ^ 2))

    @pl.when(meta[0] == 0)
    def _():
        gf[0:128, :] = dot(stem[:, 0:128], dyt[...], TN).astype(BF)
        blocks[0] = dot(dyt[...], feat[0:128, :], NT).astype(BF)
        for i in range(1, 6):
            blocks[i] = jnp.zeros((128, 128), BF)
        for out, s in outs:
            out[...] = gf[at32(s), :]

    @pl.when(meta[0] == 1)
    def _():
        gf[0:256, 0:MID] = dot(stem[:, 0:256], dyt[:, 0:MID], TN).astype(BF)
        gf[:, MID : MID + 128] = dot(stem[:, 256:768], dyt[:, MID : MID + 128], TN).astype(BF)
        for i in range(2):
            blocks[i] = dot(dyt[:, 0:MID], feat[128 * i : 128 * (i + 1), 0:MID], NT).astype(BF)
        for i in range(4):
            rows = slice(128 * i, 128 * (i + 1))
            blocks[2 + i] = dot(dyt[:, MID : MID + 128], feat[rows, MID : MID + 128], NT).astype(BF)
        for out, s in outs:
            out[...] = jnp.zeros((32, CP), BF)
            for i in range(2):
                at = pl.ds(pl.multiple_of(64 * s + 32 * i, 32), 32)
                out[:, MID * i : MID * (i + 1)] = gf[at, 0:MID]
            for i in range(4):
                at = pl.ds(pl.multiple_of(128 * s + 32 * i, 32), 32)
                out[:, 1024 + 128 * i : 1152 + 128 * i] = gf[at, MID : MID + 128]

    for i in range(3):
        block = blocks[3 * meta[1] + i]
        for j in range(8):
            gs[j, i] = block[16 * j : 16 * (j + 1)]
    part_out(meta, gs, gs_send)
    rest = jnp.zeros((4, 128), F32)
    norm[0] = jnp.concatenate([sums[0:4], sums1[0:4], sums2[0:4], rest], axis=0).astype(BF)


def total_kernel(st, out):
    out[0] = jnp.sum(st[...], axis=0)


def add_kernel(count, meta, *refs):
    kept, got, outs = refs[:count], refs[count : 2 * count], refs[2 * count :]
    for k, out in enumerate(outs):
        z = meta[4] ^ k
        at = 0
        for a, b in zip(kept, got):
            n = a.shape[1]
            out[at : at + n] = (a[2 * z + meta[5]].astype(F32) + b[z].astype(F32)).astype(out.dtype)
            at += n


def halve_kernel(meta, kept, got, own, send):
    for k in range(4):
        z = meta[4] ^ k
        total = kept[2 * z + meta[5]].astype(F32) + got[z].astype(F32)
        if k % 2:
            send[k // 2] = total.astype(BF)
        else:
            own[k // 2] = total


def again_kernel(meta, own, got, mine, send):
    mine[...] = own[0] + got[0].astype(F32)
    send[...] = (own[1] + got[1].astype(F32)).astype(BF)


def summed(refs, begin, end):
    total = refs[0][begin:end].astype(F32)
    for r in refs[1:]:
        total += r[begin:end].astype(F32)
    return total.astype(BF)


def sum_kernel(meta, *refs):
    parts, (total, extra) = refs[:-2], refs[-2:]
    total[0:9] = summed(parts, 0, 9)
    total[9:12] = summed(parts, 18, 21)
    extra[...] = summed(parts, 9, 18)


def join_kernel(meta, *refs):
    parts, (total, extra, norm, out) = refs[:4], refs[4:]
    out[0:9] = summed(parts, 0, 9)
    out[9:18] = total[0:9]
    out[27:30] = total[9:12]

    @pl.when(meta[0] == 0)
    def _():
        out[18:27] = extra[...]

    @pl.when(meta[0] == 1)
    def _():
        out[18:27] = summed(parts, 9, 18)

    out[30:33] = summed(parts, 18, 21)
    out[33:34] = norm[...]


def source(meta, k):
    c = meta[4] ^ (k % 4)
    return c >> 1, c & 1, meta[5] ^ (k // 4)


def at16(h):
    return pl.ds(pl.multiple_of(16 * h, 16), 16)


def conv_out(meta, half, parts, out, room, sems):
    for k in range(4):
        group, branch, _ = source(meta, k)
        r = parts[k]
        for i in range(3):
            layer = i if i < 2 else 1 - group
            level = group if i < 2 else 2
            for t in range(9):
                room[layer, level, branch, t] = r[9 * i + t].astype(F32)

    h = meta[5] ^ half
    copies = []
    for layer in range(2):
        for level in range(3):
            for branch in range(2):
                to = out.at[level, 2 * branch + layer, :, at16(h), :]
                copy = pltpu.make_async_copy(room.at[layer, level, branch], to, sems.at[layer, level, branch])
                copy.start()
                copies.append(copy)
    return copies


def row_outs(meta, half, parts, gcw, gcb, gbw, s0, s1, s2):
    h = meta[5] ^ half
    for k in range(4):
        group, branch, _ = source(meta, k)
        r = parts[k]
        for group_id in range(2):
            slots = range(1 + group_id)

            @pl.when((group == group_id) & (branch == 0))
            def _():
                turned = r[29].astype(F32).T
                for half_id in range(2):
                    size = (16, 4)[half_id]

                    @pl.when(h == half_id)
                    def _():
                        for slot in slots:
                            level = group_id + slot
                            gcw[level, 16 * half_id : 16 * half_id + size, :] = r[27 + slot].astype(F32)[0:size]
                            gcb[level : level + 1, 16 * half_id : 16 * half_id + size] = turned[slot : slot + 1, 0:size]

            @pl.when((group == group_id) & (branch == 1))
            def _():
                for slot in slots:
                    turned = r[27 + slot].astype(F32).T
                    for half_id in range(2):

                        @pl.when(h == half_id)
                        def _():
                            for i in range(5):
                                at = 16 * half_id
                                gbw[i, group_id + slot : group_id + slot + 1, at : at + 16] = turned[i : i + 1, 0:16]

        @pl.when((group == 0) & (branch == 0))
        def _():
            s0[at16(h), :] = r[30].astype(F32)

        @pl.when((group == 1) & (branch == 0))
        def _():
            for i in range(2):
                s1[at16(h), 128 * i : 128 * (i + 1)] = r[30 + i].astype(F32)
            s2[at16(h), 0:128] = r[32].astype(F32)

        @pl.when((group == 1) & (branch == 1))
        def _():
            for i in range(3):
                s2[at16(h), 128 * (i + 1) : 128 * (i + 2)] = r[30 + i].astype(F32)


def near_out_kernel(meta, *refs):
    parts, (out, gcw, gcb, gbw, s0, s1, s2, gbb, gains, shifts, room, sems) = refs[:4], refs[4:]
    copies = conv_out(meta, 0, parts, out, room, sems)
    row_outs(meta, 0, parts, gcw, gcb, gbw, s0, s1, s2)
    c = meta[2]
    for k in range(4):
        group, branch, _ = source(meta, k)
        r = parts[k]
        for group_id in range(2):

            @pl.when((group == group_id) & (branch == 1))
            def _():
                bias = r[29].astype(F32)
                for slot in range(1 + group_id):
                    level = group_id + slot
                    gbb[level : level + 1, :] = bias[0:1, 2 + 5 * slot : 7 + 5 * slot]

        v = r[33].astype(F32)
        mine = v[:, 0:32]
        for i in range(1, 4):
            mine = jnp.where(c == i, v[:, 32 * i : 32 * (i + 1)], mine)
        for layer in range(3):
            at = 0 if layer == 0 else layer + 2 * branch
            base = 4 * layer

            @pl.when(group == 0)
            def _():
                shifts[at, 0:1, :] = mine[base : base + 1]
                gains[at, 0:1, :] = mine[base + 2 : base + 3]

            @pl.when(group == 1)
            def _():
                shifts[at, 1:3, :] = mine[base : base + 2]
                gains[at, 1:3, :] = mine[base + 2 : base + 4]

    for copy in copies:
        copy.wait()


def far_out_kernel(meta, *refs):
    parts, earlier, (out, gcw, gcb, gbw, s0, s1, s2, room, sems) = refs[:4], refs[5:11], refs[11:]
    copies = conv_out(meta, 1, parts, out, room, sems)
    outs = (gcw, gcb, gbw, s0, s1, s2)
    for old, new in zip(earlier, outs):
        new[...] = old[...]
    row_outs(meta, 1, parts, *outs)
    for copy in copies:
        copy.wait()


def class_out_kernel(sizes, meta, mine, near, far, cross, class_out, box_out):
    n0, n1, n2 = sizes

    def store(out, fine, rest):
        n = out.shape[0]
        out[:, 0:n0] = fine[0:n, 0:n0]
        out[:, n0 : n0 + n1] = rest[0:n, 0:n1]
        out[:, n0 + n1 : n0 + n1 + n2] = rest[0:n, MID : MID + n2]

    for group in range(2):
        for branch in range(2):

            @pl.when((meta[0] == group) & (meta[1] == branch))
            def _():
                here, there = (mine, near), (far, cross)
                for i, out in enumerate((class_out, box_out)):
                    pair = (here[branch ^ i], there[branch ^ i])
                    store(out, pair[group], pair[1 - group])


def feature_out_kernel(meta, own, received, fine, mid, coarse):
    def store(a, b):
        n1, n2 = mid.shape[1], coarse.shape[0]
        fine[...] = a[:, 0 : fine.shape[1]]
        for i in range(2):
            mid[32 * i : 32 * (i + 1), :] = b[:, MID * i : MID * i + n1]
        v = jnp.concatenate([b[:, 1024 + 128 * i : 1152 + 128 * i] for i in range(4)], axis=0)
        coarse[...] = v.astype(F32).T[0:n2].astype(BF)

    @pl.when(meta[0] == 0)
    def _():
        store(own, received)

    @pl.when(meta[0] == 1)
    def _():
        store(received, own)


def pack_kernel(f0, f1, f2, s0, s1, s2, gains, shifts, box, own, send, small):
    group = lax.axis_index("chan") // 2

    def fine(out):
        out[:, 0 : f0.shape[1]] = f0[...]
        out[:, f0.shape[1] : CP] = jnp.zeros((32, CP - f0.shape[1]), BF)
        out[:, CP : CP + 128] = s0[...]
        out[:, CP + 128 : PAR] = jnp.zeros((32, PAR - CP - 128), BF)

    def rest(out):
        n1, n2 = f1.shape[1], f2.shape[0]
        for i in range(2):
            out[:, MID * i : MID * i + n1] = f1[32 * i : 32 * (i + 1), :]
            out[:, MID * i + n1 : MID * (i + 1)] = jnp.zeros((32, MID - n1), BF)
        v = jnp.concatenate([f2[...].astype(F32), jnp.zeros((128 - n2, 128), F32)], axis=0).T.astype(BF)
        for i in range(4):
            out[:, 1024 + 128 * i : 1152 + 128 * i] = v[32 * i : 32 * (i + 1)]
        out[:, STEM : STEM + 256] = s1[...]
        out[:, STEM + 256 : PAR] = s2[...]

    @pl.when(group == 0)
    def _():
        fine(own)
        rest(send)

    @pl.when(group == 1)
    def _():
        rest(own)
        fine(send)

    small[...] = jnp.zeros((64, 32), F32)
    for base, v in ((0, gains), (16, shifts), (32, box)):
        for k in range(5):
            small[base + 3 * k : base + 3 * k + 3] = v[k].astype(F32)
    for i in range(2):
        v = small[32 * i : 32 * (i + 1)]
        high = v.astype(BF).astype(F32)
        mid = (v - high).astype(BF).astype(F32)
        block = jnp.concatenate([high, mid, v - high - mid, jnp.zeros((32, 32), F32)], axis=1).astype(BF)
        for out in (own, send):
            out[:, PAR + 128 * i : PAR + 128 * (i + 1)] = block


def pred_kernel(sizes, meta, ccot, cw, cb, bcot, bb, conv, own, box, first, first_cross, second, second_cross, room, spare, sems):
    n0, n1, n2 = sizes
    copies = []
    for layer, outs in enumerate(((first, first_cross), (second, second_cross))):
        for i, out in enumerate(outs):
            for slot in range(2):
                taken = conv.at[1 - meta[0] + slot, 2 * (meta[1] ^ i) + layer]
                to = spare.at[i] if layer == 1 and slot == 1 else out.at[pl.ds(9 * slot, 9)]
                copy = pltpu.make_async_copy(taken, to, sems.at[layer, i, slot])
                copy.start()
                copies.append(copy)
    lane = lax.broadcasted_iota(jnp.int32, (32, 128), 1)

    def biases(b, level):
        block = jnp.concatenate([b[...], jnp.zeros((3, 128 - b.shape[1]), F32)], axis=1)
        block = jnp.concatenate([block, jnp.zeros((5, 128), F32)], axis=0)
        col = block.T[0:32, level : level + 1]
        high = col.astype(BF).astype(F32)
        mid = (col - high).astype(BF).astype(F32)
        low = col - high - mid
        v = jnp.where(lane == 0, high, jnp.where(lane == 1, mid, jnp.where(lane == 2, low, 0.0)))
        return v.astype(BF)

    def fill(outs, cot, b, fine, weights, sent=False):
        n = cot.shape[0]
        room[...] = jnp.zeros((32, CP), BF)
        if fine:
            room[0:n, 0:n0] = cot[:, 0:n0]
        else:
            room[0:n, 0:n1] = cot[:, n0 : n0 + n1]
            room[0:n, MID : MID + n2] = cot[:, n0 + n1 : n0 + n1 + n2]
        base = CP // 128
        if sent:
            base = TAPS + LOW
        for out in outs:
            for i in range(CP // 128 if fine else LOW):
                at = i
                if sent:
                    at = TAPS + i if i < LOW else 9 + i - LOW
                out[at] = room[:, 128 * i : 128 * (i + 1)]
            if not fine and not sent:
                out[LOW : CP // 128] = jnp.zeros((CP // 128 - LOW, 32, 128), BF)
            if fine and sent:
                out[9 + CP // 128 - LOW] = jnp.zeros((32, 128), BF)
            for slot in range(2):
                level = 0 if fine else 1 + slot
                out[base + 2 * slot] = jnp.zeros((32, 128), BF)
                if weights:
                    out[base + 2 * slot, 0:n] = cw[level]
                out[base + 2 * slot + 1] = biases(b, level)

    for group in range(2):

        @pl.when(meta[0] == group)
        def _():
            fill([own], ccot, cb, group == 0, True)
            fill([box], bcot, bb, group == 0, False)

        @pl.when(meta[0] != group)
        def _():
            fill([second, second_cross], ccot, cb, group == 0, True, True)

    for copy in copies:
        copy.wait()

    @pl.when(meta[0] == 0)
    def _():
        second[9:18] = spare[0]
        second_cross[9:18] = spare[1]


def call(body, outs, scratch, args, last=False, limit=VMEM, in_place=(), aliases={}, flops=10**6):
    place = jax.ShapeDtypeStruct if last else pltpu.VMEM

    def space(i, dtype):
        if i in in_place:
            return pl.BlockSpec(memory_space=pl.ANY)
        return pl.BlockSpec(memory_space=pltpu.SMEM if dtype == jnp.int32 else pltpu.VMEM)

    return pl.pallas_call(
        body,
        out_shape=[place(s, d) for s, d in outs],
        in_specs=[space(i, a.dtype) for i, a in enumerate(args)],
        out_specs=[space(len(args) + i, d) for i, (_, d) in enumerate(outs)],
        scratch_shapes=[s if callable(getattr(s, "get_ref_aval", None)) else pltpu.VMEM(*s) for s in scratch],
        input_output_aliases=aliases,
        compiler_params=pltpu.CompilerParams(vmem_limit_bytes=limit),
        cost_estimate=pl.CostEstimate(flops=flops, bytes_accessed=10**4, transcendentals=0),
    )(*args)


def shards(f0, f1, f2, units, s0, s1, s2, conv, gains, shifts, cw, cb, bw, bb, ccot, bcot):
    dp = lax.axis_size("dp")
    c = lax.axis_index("chan")
    group, branch = c // 2, c % 2
    fine = group == 0
    direct = dp == 8
    place = lax.axis_index("dp") if direct else 0
    meta = jnp.stack([group, branch, c, units[0], place // 2, place % 2]).astype(jnp.int32)
    n0, n1, n2 = f0.shape[2], f1.shape[2], f2.shape[2]

    def across(v):
        return lax.ppermute(v, "chan", [(i, i ^ 2) for i in range(4)])

    def diagonal(v):
        return lax.ppermute(v, "chan", [(i, i ^ 3) for i in range(4)])

    def beside(v, pairs=((0, 1), (1, 0), (2, 3), (3, 2))):
        return lax.ppermute(v, "chan", list(pairs))

    def exchange(st, *hold):
        st, *hold = lax.optimization_barrier((st, *hold))
        st = lax.all_to_all(st, "dp", 0, 0, tiled=True)
        return lax.optimization_barrier((st, *hold)) if hold else st

    def after(v, *others):
        return lax.optimization_barrier((v, *others))[0]

    def over_z(v):
        if not direct:
            return v
        parts = []
        for k in range(4):
            pairs = [
                (8 * z + 4 * y + i, 8 * (i ^ k) + 4 * y + z) for z in range(4) for y in range(2) for i in range(4)
            ]
            parts.append(lax.ppermute(v, ("dp", "chan"), pairs))
        return parts

    def everywhere(parts):
        if direct:
            return parts + [over_y(p) for p in parts]
        v = lax.all_to_all(parts.reshape(4, 2, *parts.shape[1:]), "chan", 0, 0, tiled=True)
        return [v[k % 4, k // 4] for k in range(8)]

    def joined(*parts):
        return jnp.concatenate(parts, axis=-3)

    def over_y(v):
        return lax.ppermute(v, "dp", [(i, i ^ 1) for i in range(8)])

    def along_z(kept, got):
        shape = (sum(v.shape[1] for v in kept), 16, 128)
        outs = [(shape, F32)] + [(shape, BF)] * 3
        own, *rest = call(functools.partial(add_kernel, len(kept)), outs, [], (meta, *kept, *got))
        return [own] + [lax.ppermute(v, "dp", [(i, i ^ (2 * k + 2)) for i in range(8)]) for k, v in enumerate(rest)]

    def reduce(v):
        return lax.optimization_barrier(lax.psum(v.astype(F32), "dp")).astype(BF)

    own, send = call(
        pack_kernel,
        [((32, WIDE), BF), ((32, WIDE), BF)],
        [((64, 32), F32)],
        (f0[0], f1[0], f2[0].T, s0, s1, s2, gains.transpose(1, 0, 2), shifts.transpose(1, 0, 2), bw.transpose(1, 0, 2)),
        limit=WHOLE,
    )
    far_u = across(send)
    own_pred, box_pred, send1, send1_cross, send2, send2_cross = call(
        functools.partial(pred_kernel, (n0, n1, n2)),
        [((CLS, 32, 128), BF)] * 2 + [((TAPS, 32, 128), BF)] * 2 + [((SECOND, 32, 128), BF)] * 2,
        [((32, CP), BF), ((2, 9, 32, 128), BF), pltpu.SemaphoreType.DMA((2, 2, 2))],
        (meta, ccot[0], cw, cb, bcot[0], after(bb, own), conv),
        limit=WHOLE,
        in_place=(6,),
        flops=2 * 10**9,
    )
    near = beside(after(conv, own))
    far_u = after(far_u, near, send2)
    u = (own, far_u, beside(own), beside(far_u))
    to_class = ((1, 0), (3, 2))
    near_pred = beside(own_pred, to_class)

    def weights_of(layer, far, cross):
        return call(
            functools.partial(weight_kernel, layer),
            [((2, 128, 1152), BF), ((2, 1152, 128), BF)],
            [],
            (meta, conv, near, far, cross),
        )

    canvas = (PX, 128)
    stat = (dp, 8, 128)
    moved = [((PX + 16, 128), F32), ((3, PX + 2 * ST, 128), BF)]
    y0, st, cnt, par = call(
        stem_kernel,
        [(canvas, F32), (stat, F32), ((8, 128), F32), ((64, 128), F32)],
        [((512, CP), BF), ((128, 768), BF), ((CP, 128), F32)],
        (meta, *u),
    )
    far1, cross1 = across(after(send1, far_u)), diagonal(after(send1_cross, far_u))
    st, near_pred = exchange(st, near_pred)
    far1, cross1 = after((far1, cross1), st)
    far2, cross2 = across(after(send2, far1)), diagonal(after(send2_cross, cross1))
    w1, w1_tall = weights_of(0, far1, cross1)
    forward_outs = [(canvas, BF), (canvas, F32), (stat, F32), ((16, 128), F32)]
    act0, y1, st, cst0 = call(functools.partial(forward_kernel, True), forward_outs, moved, (meta, y0, st, cnt, w1, par))
    st = exchange(st)
    far2, cross2 = after((far2, cross2), st)
    w2, w2_tall = weights_of(1, far2, cross2)
    act1, y2, st, cst1 = call(
        functools.partial(forward_kernel, False), forward_outs, moved, (meta, y1, st, cnt, w2, par)
    )
    st = exchange(st)
    dz2, st, cst2, x2, cot, wp = call(
        heads_kernel,
        [(canvas, F32), (stat, F32), ((16, 128), F32), ((CP, 256), BF), ((128, CP), BF), ((2, 128, 256), BF)],
        [(canvas, F32), ((CP, 128), F32)],
        (meta, y2, st, par, own_pred, far2, near_pred, cross2, box_pred),
    )
    gw, mine, near, far, cross = call(
        logits_kernel, [((8, 3, 16, 128), BF)] + [((32, CP), BF)] * 4, [((128, CP), BF)], (meta, x2, cot, wp)
    )
    near, far, cross = beside(near), across(far), diagonal(cross)
    st = exchange(after(st, gw))
    st, near, far, cross = lax.optimization_barrier((st, near, far, cross))
    back_scratch = moved + [((128, PX), BF)]
    dz1, st, sums2, wg2, send2 = call(
        second_back_kernel,
        [(canvas, F32), (stat, F32), ((8, 128), F32), ((8, 21, 16, 128), BF), ((4, 21, 16, 128), BF)],
        back_scratch,
        (meta, dz2, y2, cst2, st, w2_tall, act1, y1, cst1, gw),
    )
    got2 = over_y(send2) if direct else reduce(wg2)
    st, got2 = lax.optimization_barrier((exchange(after(st, send2)), got2))
    d0, st, sums1, wg1, send1 = call(
        first_back_kernel,
        [(canvas, BF), (stat, F32), ((8, 128), F32), ((8, 18, 16, 128), BF), ((4, 18, 16, 128), BF)],
        back_scratch,
        (meta, dz1, y1, cst1, st, w1_tall, act0, y0, cst0),
    )
    got1 = over_y(send1) if direct else reduce(wg1)
    d0_other, st_other = beside(d0), beside(st)
    st = st + st_other
    if direct:
        pair = (2, 21, 16, 128)
        own2, send2 = call(halve_kernel, [(pair, F32), (pair, BF)], [], (meta, wg2, after(got2, d0)))
        got2 = lax.ppermute(send2, "dp", [(i, i ^ 2) for i in range(8)])
        st = exchange(after(st, d0_other, own2))
        (st,) = call(total_kernel, [((1, 8, 128), F32)], [], (st,))
        st, got1, got2 = lax.optimization_barrier((st, got1, got2))
        own2, send2 = call(again_kernel, [(pair[1:], F32), (pair[1:], BF)], [], (meta, own2, got2))
        got2 = lax.ppermute(send2, "dp", [(i, i ^ 4) for i in range(8)])
    else:
        st = exchange(st)
    own, other, gs, gs_send, norm = call(
        final_kernel,
        [((32, CP), BF), ((32, CP), BF), ((8, 3, 16, 128), BF), ((4, 3, 16, 128), BF), ((1, 16, 128), BF)],
        [
            ((8, 128), F32),
            ((512, CP), BF),
            ((128, 768), BF),
            (canvas, F32),
            ((CP, 128), F32),
            ((128, CP), BF),
            ((512, CP), BF),
            ((6, 128, 128), BF),
        ],
        (meta, d0, d0_other, y0, cst0, st, sums1, sums2, *u),
    )
    received = across(other)
    if direct:
        parts1 = along_z([wg1, gs], [got1, over_y(gs_send)])
        total, extra = call(
            sum_kernel, [((12, 16, 128), BF), ((9, 16, 128), BF)], [], (meta, own2, after(got2, parts1[0]))
        )
        extra = lax.ppermute(extra, "chan", [(2, 0), (3, 1)])
        extra, received = lax.optimization_barrier((extra, received))
        (grads,) = call(join_kernel, [((34, 16, 128), BF)], [], (meta, *parts1, total, extra, norm))
    else:
        extra = lax.ppermute(got2[:, 9:18], "chan", [(2, 0), (3, 1)])
        third = jnp.where(fine, extra, got1[:, 9:18])
        norm = jnp.broadcast_to(norm[None], (8, *norm.shape))
        grads = joined(got1[:, :9], got2[:, :9], third, got2[:, 18:21], reduce(gs), norm)
    grads = everywhere(over_z(grads))

    room = [((2, 3, 2, conv.shape[2], 16, 128), F32), pltpu.SemaphoreType.DMA((2, 3, 2))]
    rows = [(cw.shape, F32), (cb.shape, F32), ((5, 3, 32), F32), (s0.shape, F32), (s1.shape, F32), (s2.shape, F32)]
    wholes = [(bb.shape, F32), ((5, 3, 32), F32), ((5, 3, 32), F32)]
    grad_conv, *half, grad_bb, grad_gains, grad_shifts = call(
        near_out_kernel, [(conv.shape, F32)] + rows + wholes, room, (meta, *grads[:4]), True, in_place=(5,)
    )
    mine, own = after((mine, own), *half)
    box_rows, class_rows = bcot.shape[1], ccot.shape[1]
    class_out, box_out = call(
        functools.partial(class_out_kernel, (n0, n1, n2)),
        [((class_rows, n0 + n1 + n2), BF), ((box_rows, n0 + n1 + n2), BF)],
        [],
        (meta, mine, near, far, cross),
        True,
    )
    grad_fine, grad_mid, grad_coarse = call(
        feature_out_kernel,
        [(f0.shape[1:], BF), (f1.shape[1:], BF), ((n2, f2.shape[1]), BF)],
        [],
        (meta, own, received),
        True,
    )

    grad_conv, grad_cw, grad_cb, grad_bw, grad_s0, grad_s1, grad_s2 = call(
        far_out_kernel,
        [(conv.shape, F32)] + rows,
        room,
        (meta, *grads[4:], grad_conv, *half),
        True,
        in_place=(5, 12),
        aliases={5: 0},
    )
    return (
        class_out[None],
        box_out[None],
        grad_fine[None],
        grad_mid[None],
        grad_coarse.T[None],
        grad_s0,
        grad_s1,
        grad_s2,
        grad_conv,
        grad_gains.transpose(1, 0, 2),
        grad_shifts.transpose(1, 0, 2),
        grad_cw,
        grad_cb,
        grad_bw.transpose(1, 0, 2),
        grad_bb,
    )


def solution(mesh):
    placed = (
        P("dp", "chan", None),
        P("dp", "chan", None),
        P("dp", "chan", None),
        P("dp"),
        P("chan", None),
        P("chan", None),
        P("chan", None),
        P(None, None, None, "chan", None),
        P(None, None, "chan"),
        P(None, None, "chan"),
        P(None, "chan", None),
        P(None, "chan"),
        P(None, None, "chan"),
        P(),
        P("dp", "chan", None),
        P("dp", None, None),
    )
    return jax.shard_map(
        shards,
        mesh=mesh,
        in_specs=placed,
        out_specs=(
            P("dp", "chan", None),
            P("dp", None, None),
            P("dp", "chan", None),
            P("dp", "chan", None),
            P("dp", "chan", None),
            P("chan", None),
            P("chan", None),
            P("chan", None),
            P(None, None, None, "chan", None),
            P(None, None, "chan"),
            P(None, None, "chan"),
            P(None, "chan", None),
            P(None, "chan"),
            P(None, None, "chan"),
            P(),
        ),
        check_vma=False,
    )
```

```python
import functools

import jax
import jax.numpy as jnp
from jax import lax
from jax.experimental import pallas as pl
from jax.experimental.pallas import tpu as pltpu
from jax.sharding import PartitionSpec as P

BF = jnp.bfloat16
F32 = jnp.float32
EPS = 0.001
ST = 48
ROWS = 40
PX = ST * ROWS
CR = 8
CH = CR * ST
NCH = ROWS // CR
SLOT = (0, 0, 0, 1, 1)
CUT = 24 * ST
CP = 1664
MID = 512
E0, E1, E2 = 40, 20, 10
STEM = 1536
PAR = STEM + 768
WIDE = PAR + 256
CLS = CP // 128 + 4
TAPS = 18
LOW = (MID + 128) // 128
SECOND = TAPS + LOW + 4
SENT = 2 * (CP // 128) + 9
VMEM = 12 * 2**20
WHOLE = 56 * 2**20
NT = (((1,), (1,)), ((), ()))
TN = (((0,), (0,)), ((), ()))


def dot(a, b, dims=(((1,), (0,)), ((), ()))):
    return lax.dot_general(a, b, dims, preferred_element_type=F32)


def position(units):
    c = lax.axis_index("chan")
    place = lax.axis_index("dp") if lax.axis_size("dp") == 8 else jnp.int32(0)
    return c >> 1, c & 1, c, units[0:1, :], place >> 1, place & 1


def limits(meta, slot):
    group, units = meta[0], meta[3]
    if slot == 0:
        edge = jnp.where(group == 0, 4 * units, 2 * units)
        return edge, edge
    return (
        jnp.where(group == 0, 4 * units, 24 + units),
        jnp.where(group == 0, 4 * units, units),
    )


def mask_of(meta, j):
    row_end, col_end = (v.reshape(1, 1, 128) for v in limits(meta, SLOT[j]))
    row = lax.broadcasted_iota(jnp.int32, (CR, ST, 128), 0) + CR * j
    col = lax.broadcasted_iota(jnp.int32, (CR, ST, 128), 1)
    inside = (row < row_end) & (col < col_end)
    return jnp.where(inside, 1.0, 0.0).reshape(CH, 128)


def pick(meta, first, second):
    total = first + second
    return jnp.where(meta[0] == 0, total, first), jnp.where(meta[0] == 0, total, second)


def level_rows(meta, base, layer):
    fine = meta[0] == 0
    at = base + 3 * layer
    return at + jnp.where(fine, 0, 1), at + jnp.where(fine, 0, 2)


def norm_constants(meta, st, par, layer, cst):
    total = jnp.sum(st[...], axis=0)
    row = [total[i : i + 1] for i in range(6)]
    first = pick(meta, row[0], row[1])
    second = pick(meta, row[2], row[3])
    count = pick(meta, row[4], row[5])
    gain_at = level_rows(meta, 0, layer)
    shift_at = level_rows(meta, 16, layer)
    for s in range(2):
        rn = 1.0 / count[s]
        mean = first[s] * rn
        inv = lax.rsqrt(second[s] * rn - mean * mean + EPS)
        cst[s : s + 1] = mean
        cst[2 + s : 3 + s] = inv
        cst[4 + s : 5 + s] = par[pl.ds(gain_at[s], 1), :]
        cst[6 + s : 7 + s] = par[pl.ds(shift_at[s], 1), :]
        cst[8 + s : 9 + s] = rn
        cst[10 + s : 11 + s] = count[s]
    cst[12:16] = jnp.zeros((4, 128), F32)


def normed(cst, y, s):
    xhat = (y - cst[s : s + 1]) * cst[2 + s : 3 + s]
    return xhat, xhat * cst[4 + s : 5 + s] + cst[6 + s : 7 + s]


def sigmoid(z):
    return 0.5 * jnp.tanh(0.5 * z) + 0.5


def slope(z):
    s = sigmoid(z)
    return s * (1.0 + z * (1.0 - s))


def spread_out(st, rows):
    block = jnp.concatenate(rows + [jnp.zeros((8 - len(rows), 128), F32)], axis=0)
    st[...] = jnp.broadcast_to(block[None], st.shape)


def colsum(v):
    return jnp.sum(v, axis=0, keepdims=True)


def guard(field, shifts):
    field[0:8] = jnp.zeros((8, 128), F32)
    field[8 + PX : 16 + PX] = jnp.zeros((8, 128), F32)
    for k in range(3):
        shifts[k, 0:ST] = jnp.zeros((ST, 128), BF)
        shifts[k, ST + PX :] = jnp.zeros((ST, 128), BF)


def fill_shifts(field, shifts):
    for k in range(3):
        for j in range(NCH):
            at = 8 + CH * j + k - 1
            shifts[k, ST + CH * j : ST + CH * (j + 1)] = field[at : at + CH].astype(BF)


def taps(shifts, begin, size, back=False):
    parts = []
    for kr in range(3):
        for kc in range(3):
            k, r = (2 - kc, 1 - kr) if back else (kc, kr - 1)
            at = ST + begin + ST * r
            parts.append(shifts[k, at : at + size])
    return jnp.concatenate(parts, axis=1)


def slices_of(meta):
    c = meta[2]
    return (c, c ^ 2, c ^ 1, c ^ 3)


def at32(s, extra=0):
    return pl.ds(pl.multiple_of(32 * s + extra, 32), 32)


def weight_slot(meta, j):
    return jnp.where(meta[0] == 0, 0, SLOT[j])


def to_compact(meta, canvas, out):
    @pl.when(meta[0] == 0)
    def _():
        for r in range(E0):
            out[E0 * r : E0 * (r + 1)] = canvas[ST * r : ST * r + E0]

    @pl.when(meta[0] == 1)
    def _():
        for r in range(E1):
            out[E1 * r : E1 * (r + 1)] = canvas[ST * r : ST * r + E1]
        for r in range(E2):
            at = CUT + ST * r
            out[MID + E2 * r : MID + E2 * (r + 1)] = canvas[at : at + E2]


def to_canvas(meta, compact, out):
    @pl.when(meta[0] == 0)
    def _():
        for r in range(E0):
            out[ST * r : ST * r + E0] = compact[E0 * r : E0 * (r + 1)]

    @pl.when(meta[0] == 1)
    def _():
        for r in range(E1):
            out[ST * r : ST * r + E1] = compact[E1 * r : E1 * (r + 1)]
        for r in range(E2):
            at = CUT + ST * r
            out[at : at + E2] = compact[MID + E2 * r : MID + E2 * (r + 1)]


def load_inputs(meta, pieces, feat, stem):
    for s, u in zip(slices_of(meta), pieces):

        @pl.when(meta[0] == 0)
        def _():
            feat[at32(s), :] = u[:, 0:CP]
            stem[at32(s), 0:128] = u[:, CP : CP + 128]

        @pl.when(meta[0] == 1)
        def _():
            for i in range(2):
                at = pl.ds(pl.multiple_of(64 * s + 32 * i, 32), 32)
                feat[at, 0:MID] = u[:, MID * i : MID * (i + 1)]
            for i in range(4):
                at = pl.ds(pl.multiple_of(128 * s + 32 * i, 32), 32)
                feat[at, MID : MID + 128] = u[:, 1024 + 128 * i : 1152 + 128 * i]
            stem[at32(s), :] = u[:, STEM:PAR]


def stem_kernel(meta, u0, u1, u2, u3, y, st, cnt, par, feat, stem, flat):
    load_inputs(meta, (u0, u1, u2, u3), feat, stem)
    lane = lax.broadcasted_iota(jnp.int32, (32, 128), 1) // 32
    for i in range(2):
        total = jnp.zeros((32, 128), F32)
        for s, u in zip(slices_of(meta), (u0, u1, u2, u3)):
            v = u[:, PAR + 128 * i : PAR + 128 * (i + 1)].astype(F32)
            v = v[:, 0:32] + v[:, 32:64] + v[:, 64:96]
            total = jnp.where(lane == s, jnp.concatenate([v] * 4, axis=1), total)
        par[32 * i : 32 * (i + 1)] = total
    y[...] = jnp.zeros((PX, 128), F32)

    @pl.when(meta[0] == 0)
    def _():
        flat[...] = dot(stem[:, 0:128], feat[0:128, :]).T

    @pl.when(meta[0] == 1)
    def _():
        flat[0:MID] = dot(stem[:, 0:256], feat[0:256, 0:MID]).T
        flat[MID : MID + 128] = dot(stem[:, 256:768], feat[0:512, MID : MID + 128]).T

    to_canvas(meta, flat, y)
    sums = [jnp.zeros((1, 128), F32) for _ in range(6)]
    for j in range(NCH):
        m = mask_of(meta, j)
        v = y[CH * j : CH * (j + 1)] * m
        s = SLOT[j]
        sums[s] += colsum(v)
        sums[2 + s] += colsum(v * v)
        sums[4 + s] += colsum(m)
    spread_out(st, sums)
    cnt[...] = jnp.concatenate(sums[4:6] + [jnp.zeros((6, 128), F32)], axis=0)


def forward_kernel(first, meta, y, st, cnt, w, *refs):
    par, act, out, st_out, cst, field, shifts = refs
    layer = 0 if first else 1 + 2 * meta[1]
    norm_constants(meta, st, par, layer, cst)
    guard(field, shifts)
    for j in range(NCH):
        rows = slice(CH * j, CH * (j + 1))
        _, z = normed(cst, y[rows], SLOT[j])
        v = z * sigmoid(z) * mask_of(meta, j)
        act[rows] = v.astype(BF)
        field[8 + CH * j : 8 + CH * (j + 1)] = v
    fill_shifts(field, shifts)
    sums = [jnp.zeros((1, 128), F32) for _ in range(4)]
    for j in range(NCH):
        v = dot(taps(shifts, CH * j, CH), w[weight_slot(meta, j)], NT)
        out[CH * j : CH * (j + 1)] = v
        v = v * mask_of(meta, j)
        s = SLOT[j]
        sums[s] += colsum(v)
        sums[2 + s] += colsum(v * v)
    spread_out(st_out, sums + [cnt[0:1], cnt[1:2]])


def weight_kernel(layer, meta, mine, near, far, cross, flat, tall):
    group, branch, c = meta[0], meta[1], meta[2]
    conv = 2 * branch + layer
    for slot in range(2):
        level = group + slot
        for t in range(9):
            for s, piece in (
                (c, mine[level, conv, t]),
                (c ^ 1, near[level, conv, t]),
                (c ^ 2, far[9 * slot + t]),
                (c ^ 3, cross[9 * slot + t]),
            ):
                flat[slot, at32(s), 128 * t : 128 * (t + 1)] = piece
                tall[slot, at32(s, 128 * t), :] = piece


def heads_kernel(meta, y, st, par, k0, k1, k2, k3, box_pack, dz, st_out, cst, x2, cot, wp, field, flat):
    norm_constants(meta, st, par, 2 + 2 * meta[1], cst)
    cot[...] = jnp.zeros((128, CP), BF)
    wp[...] = jnp.zeros((2, 128, 256), BF)

    pixels = CP // 128

    @pl.when(meta[1] == 0)
    def _():
        for s, k, sent in zip(slices_of(meta), (k0, k1, k2, k3), (False, True, False, True)):
            for i in range(pixels):
                if not sent or i < LOW:
                    cot[at32(s), 128 * i : 128 * (i + 1)] = k[TAPS + i if sent else i]
            for slot in range(2):
                for i in range(2):
                    at = (TAPS + LOW if sent else pixels) + 2 * slot + i
                    wp[slot, at32(s), 128 * i : 128 * (i + 1)] = k[at]

    @pl.when((meta[1] == 0) & (meta[0] == 0))
    def _():
        for s, k in zip(slices_of(meta)[1::2], (k1, k3)):
            for i in range(LOW, pixels):
                cot[at32(s), 128 * i : 128 * (i + 1)] = k[9 + i - LOW]

    @pl.when(meta[1] == 1)
    def _():
        for i in range(pixels):
            cot[0:32, 128 * i : 128 * (i + 1)] = box_pack[i]
        fine = meta[0] == 0
        for slot in range(2):
            row = lax.broadcasted_iota(jnp.int32, (32, 128), 0)
            box = jnp.zeros((32, 128), F32)
            for i in range(5):
                at = 32 + 3 * i
                line = jnp.where(fine, par[at : at + 1], par[at + 1 + slot : at + 2 + slot])
                box = jnp.where(row == i, line, box)
            wp[slot, 0:32, 0:128] = box.astype(BF)
            wp[slot, 0:32, 128:256] = box_pack[pixels + 2 * slot + 1]

    for part in range(2):
        for j in range(NCH):
            m = mask_of(meta, j)
            if part == 0:
                _, z = normed(cst, y[CH * j : CH * (j + 1)], SLOT[j])
                m = z * sigmoid(z) * m
            field[CH * j : CH * (j + 1)] = m
        flat[...] = jnp.zeros((CP, 128), F32)
        to_compact(meta, field, flat)
        x2[:, 128 * part : 128 * (part + 1)] = flat[...].astype(BF)

    @pl.when(meta[0] == 0)
    def _():
        flat[...] = dot(cot[...], wp[0, :, 0:128], TN)

    @pl.when(meta[0] == 1)
    def _():
        for slot, a, b in ((0, 0, MID), (1, MID, MID + 128)):
            flat[a:b] = dot(cot[:, a:b], wp[slot, :, 0:128], TN)

    field[...] = jnp.zeros((PX, 128), F32)
    to_canvas(meta, flat, field)
    sums = [jnp.zeros((1, 128), F32) for _ in range(4)]
    for j in range(NCH):
        rows = slice(CH * j, CH * (j + 1))
        s = SLOT[j]
        xhat, z = normed(cst, y[rows], s)
        v = field[rows] * slope(z) * mask_of(meta, j)
        dz[rows] = v
        sums[s] += colsum(v)
        sums[2 + s] += colsum(v * xhat)
    spread_out(st_out, sums)


def logits_kernel(meta, x2, cot, wp, gw, mine, near, far, cross, logits):
    def store(slot, v):
        bias = v[:, 128:256]

        @pl.when(meta[1] == 0)
        def _():
            gw_block(gw, slot, v[:, 0:128])

        @pl.when(meta[1] == 1)
        def _():
            gw_block(gw, slot, v[:, 0:128].T)

        return bias

    def finish(first, second):
        lane = lax.broadcasted_iota(jnp.int32, (128, 128), 1)
        cls = jnp.where(lane == 0, first, jnp.where(lane == 1, second, 0.0))
        a, b = first.T, second.T
        box = jnp.where((lane >= 7) & (lane < 12), pltpu.roll(b, 7, 1), 0.0)
        box = jnp.where((lane >= 2) & (lane < 7), pltpu.roll(a, 2, 1), box)
        gw_block(gw, 2, jnp.where(meta[1] == 0, cls, box))

    @pl.when(meta[0] == 0)
    def _():
        logits[...] = dot(wp[0], x2[...], NT).astype(BF)
        first = store(0, dot(cot[...], x2[...]))
        gw_block(gw, 1, jnp.zeros((128, 128), F32))
        finish(first, jnp.zeros((128, 128), F32))

    @pl.when(meta[0] == 1)
    def _():
        logits[...] = jnp.zeros((128, CP), BF)
        bias = []
        for slot, a, b in ((0, 0, MID), (1, MID, MID + 128)):
            logits[:, a:b] = dot(wp[slot], x2[a:b], NT).astype(BF)
            bias.append(store(slot, dot(cot[:, a:b], x2[a:b])))
        finish(*bias)

    for out, c in ((mine, 0), (near, 1), (far, 2), (cross, 3)):
        out[...] = logits[at32(jnp.where(meta[1] == 0, meta[2] ^ c, 0)), :]


def gw_block(gw, i, v):
    for j in range(8):
        gw[j, i] = v[16 * j : 16 * (j + 1)].astype(BF)


def grad_sums(meta, total, sums):
    shift = pick(meta, total[0:1], total[1:2])
    gain = pick(meta, total[2:3], total[3:4])
    sums[...] = jnp.concatenate(list(shift) + list(gain) + [jnp.zeros((4, 128), F32)], axis=0)


def input_grad(meta, dz, y, cst, sums, j):
    s = SLOT[j]
    xhat, _ = normed(cst, y[CH * j : CH * (j + 1)], s)
    factor = cst[4 + s : 5 + s] * cst[2 + s : 3 + s]
    mean = (sums[s : s + 1] + xhat * sums[2 + s : 3 + s]) * cst[8 + s : 9 + s]
    return mask_of(meta, j) * factor * (dz - mean)


def out_grad(meta, dz, y, cst, st, sums, field, dyt):
    grad_sums(meta, jnp.sum(st[...], axis=0), sums)
    for j in range(NCH):
        rows = slice(CH * j, CH * (j + 1))
        v = input_grad(meta, dz[rows], y, cst, sums, j)
        field[8 + CH * j : 8 + CH * (j + 1)] = v
        dyt[:, rows] = v.T.astype(BF)


def conv_back(meta, last, w, y_in, cst_in, shifts, grad, st_out):
    total = [jnp.zeros((1, 128), F32) for _ in range(4)]
    for j in range(NCH):
        rows = slice(CH * j, CH * (j + 1))
        s = SLOT[j]
        v = dot(taps(shifts, CH * j, CH, True), w[weight_slot(meta, j)])
        xhat, z = normed(cst_in, y_in[rows], s)
        d = v * slope(z) * mask_of(meta, j)
        grad[rows] = v.astype(BF) if last else d
        total[s] += colsum(d)
        total[2 + s] += colsum(d * xhat)
    spread_out(st_out, total)


def as_parts(st):
    high = st.astype(BF).astype(F32)
    mid = (st - high).astype(BF).astype(F32)
    return jnp.concatenate([high, mid, st - high - mid, jnp.zeros((8, 128), F32)], axis=0).astype(BF)


def weight_grad(meta, dyt, act, field, shifts, wg):
    for j in range(NCH):
        field[8 + CH * j : 8 + CH * (j + 1)] = act[CH * j : CH * (j + 1)].astype(F32)
    fill_shifts(field, shifts)

    def store(slot, v):
        for t in range(9):
            for j in range(8):
                block = v[16 * j : 16 * (j + 1), 128 * t : 128 * (t + 1)].astype(BF)
                wg[j, 9 * slot + t] = block

    @pl.when(meta[0] == 0)
    def _():
        store(0, dot(dyt[...], taps(shifts, 0, PX)))
        store(1, jnp.zeros((128, 1152), F32))

    @pl.when(meta[0] == 1)
    def _():
        store(0, dot(dyt[:, 0:CUT], taps(shifts, 0, CUT)))
        store(1, dot(dyt[:, CUT:PX], taps(shifts, CUT, PX - CUT)))


def part_out(meta, wg, send):
    for z in range(4):
        send[z] = wg[2 * z + 1 - meta[5]]


def second_back_kernel(meta, dz, y, cst, st, w, act, y_in, cst_in, gw, grad, st_out, sums, wg, send, field, shifts, dyt):
    guard(field, shifts)
    out_grad(meta, dz, y, cst, st, sums, field, dyt)
    fill_shifts(field, shifts)
    conv_back(meta, False, w, y_in, cst_in, shifts, grad, st_out)
    weight_grad(meta, dyt, act, field, shifts, wg)
    for j in range(8):
        for i in range(3):
            wg[j, 18 + i] = gw[j, i]
    part_out(meta, wg, send)


def first_back_kernel(meta, dz, y, cst, st, w, act, y_in, cst_in, grad, st_out, sums, wg, send, field, shifts, dyt):
    guard(field, shifts)
    out_grad(meta, dz, y, cst, st, sums, field, dyt)
    fill_shifts(field, shifts)
    conv_back(meta, True, w, y_in, cst_in, shifts, grad, st_out)
    grad[PX:] = as_parts(st_out[0])
    weight_grad(meta, dyt, act, field, shifts, wg)
    part_out(meta, wg, send)


def final_kernel(meta, d0, d1, y, cst, st, sums1, sums2, u0, u1, u2, u3, own, other, gs, gs_send, norm, *scratch):
    sums, feat, stem, field, flat, dyt, gf, blocks = scratch
    load_inputs(meta, (u0, u1, u2, u3), feat, stem)
    grad_sums(meta, jnp.sum(st[...], axis=0), sums)
    for j in range(NCH):
        rows = slice(CH * j, CH * (j + 1))
        _, z = normed(cst, y[rows], SLOT[j])
        v = (d0[rows].astype(F32) + d1[rows].astype(F32)) * slope(z) * mask_of(meta, j)
        field[rows] = input_grad(meta, v, y, cst, sums, j)
    flat[...] = jnp.zeros((CP, 128), F32)
    to_compact(meta, field, flat)
    dyt[...] = flat[...].T.astype(BF)
    c = meta[2]
    outs = ((own, c), (other, c ^ 2))

    @pl.when(meta[0] == 0)
    def _():
        gf[0:128, :] = dot(stem[:, 0:128], dyt[...], TN).astype(BF)
        blocks[0] = dot(dyt[...], feat[0:128, :], NT).astype(BF)
        for i in range(1, 6):
            blocks[i] = jnp.zeros((128, 128), BF)
        for out, s in outs:
            out[...] = gf[at32(s), :]

    @pl.when(meta[0] == 1)
    def _():
        gf[0:256, 0:MID] = dot(stem[:, 0:256], dyt[:, 0:MID], TN).astype(BF)
        gf[:, MID : MID + 128] = dot(stem[:, 256:768], dyt[:, MID : MID + 128], TN).astype(BF)
        for i in range(2):
            blocks[i] = dot(dyt[:, 0:MID], feat[128 * i : 128 * (i + 1), 0:MID], NT).astype(BF)
        for i in range(4):
            rows = slice(128 * i, 128 * (i + 1))
            blocks[2 + i] = dot(dyt[:, MID : MID + 128], feat[rows, MID : MID + 128], NT).astype(BF)
        for out, s in outs:
            out[...] = jnp.zeros((32, CP), BF)
            for i in range(2):
                at = pl.ds(pl.multiple_of(64 * s + 32 * i, 32), 32)
                out[:, MID * i : MID * (i + 1)] = gf[at, 0:MID]
            for i in range(4):
                at = pl.ds(pl.multiple_of(128 * s + 32 * i, 32), 32)
                out[:, 1024 + 128 * i : 1152 + 128 * i] = gf[at, MID : MID + 128]

    for i in range(3):
        block = blocks[3 * meta[1] + i]
        for j in range(8):
            gs[j, i] = block[16 * j : 16 * (j + 1)]
    part_out(meta, gs, gs_send)
    rest = jnp.zeros((4, 128), F32)
    norm[0] = jnp.concatenate([sums[0:4], sums1[0:4], sums2[0:4], rest], axis=0).astype(BF)


def both_kernel(st, other, out):
    v = other[PX:].astype(F32)
    out[...] = st[...] + (v[0:8] + v[8:16] + v[16:24])[None]


def total_kernel(st, out):
    out[0] = jnp.sum(st[...], axis=0)


def add_kernel(count, meta, *refs):
    kept, got, outs = refs[:count], refs[count : 2 * count], refs[2 * count :]
    for k, out in enumerate(outs):
        z = meta[4] ^ k
        at = 0
        for a, b in zip(kept, got):
            n = a.shape[1]
            out[at : at + n] = (a[2 * z + meta[5]].astype(F32) + b[z].astype(F32)).astype(out.dtype)
            at += n


def halve_kernel(meta, kept, got, own, send):
    for k in range(4):
        z = meta[4] ^ k
        total = kept[2 * z + meta[5]].astype(F32) + got[z].astype(F32)
        if k % 2:
            send[k // 2] = total.astype(BF)
        else:
            own[k // 2] = total


def again_kernel(meta, own, got, mine, send):
    mine[...] = own[0] + got[0].astype(F32)
    send[...] = (own[1] + got[1].astype(F32)).astype(BF)


def summed(refs, begin, end):
    total = refs[0][begin:end].astype(F32)
    for r in refs[1:]:
        total += r[begin:end].astype(F32)
    return total.astype(BF)


def sum_kernel(meta, *refs):
    parts, (total, extra) = refs[:-2], refs[-2:]
    total[0:9] = summed(parts, 0, 9)
    total[9:12] = summed(parts, 18, 21)
    extra[...] = summed(parts, 9, 18)


def join_kernel(meta, *refs):
    parts, (total, extra, norm, out) = refs[:4], refs[4:]
    out[0:9] = summed(parts, 0, 9)
    out[9:18] = total[0:9]
    out[27:30] = total[9:12]

    @pl.when(meta[0] == 0)
    def _():
        out[18:27] = extra[...]

    @pl.when(meta[0] == 1)
    def _():
        out[18:27] = summed(parts, 9, 18)

    out[30:33] = summed(parts, 18, 21)
    out[33:34] = norm[...]


def source(meta, k):
    c = meta[4] ^ (k % 4)
    return c >> 1, c & 1, meta[5] ^ (k // 4)


def at16(h):
    return pl.ds(pl.multiple_of(16 * h, 16), 16)


def conv_out(meta, half, parts, out, room, sems):
    for k in range(4):
        group, branch, _ = source(meta, k)
        r = parts[k]
        for i in range(3):
            layer = i if i < 2 else 1 - group
            level = group if i < 2 else 2
            for t in range(9):
                room[layer, level, branch, t] = r[9 * i + t].astype(F32)

    h = meta[5] ^ half
    copies = []
    for layer in range(2):
        for level in range(3):
            for branch in range(2):
                to = out.at[level, 2 * branch + layer, :, at16(h), :]
                copy = pltpu.make_async_copy(room.at[layer, level, branch], to, sems.at[layer, level, branch])
                copy.start()
                copies.append(copy)
    return copies


def row_outs(meta, half, parts, gcw, gcb, gbw, s0, s1, s2):
    h = meta[5] ^ half
    for k in range(4):
        group, branch, _ = source(meta, k)
        r = parts[k]
        for group_id in range(2):
            slots = range(1 + group_id)

            @pl.when((group == group_id) & (branch == 0))
            def _():
                turned = r[29].astype(F32).T
                for half_id in range(2):
                    size = (16, 4)[half_id]

                    @pl.when(h == half_id)
                    def _():
                        for slot in slots:
                            level = group_id + slot
                            gcw[level, 16 * half_id : 16 * half_id + size, :] = r[27 + slot].astype(F32)[0:size]
                            gcb[level : level + 1, 16 * half_id : 16 * half_id + size] = turned[slot : slot + 1, 0:size]

            @pl.when((group == group_id) & (branch == 1))
            def _():
                for slot in slots:
                    turned = r[27 + slot].astype(F32).T
                    for half_id in range(2):

                        @pl.when(h == half_id)
                        def _():
                            for i in range(5):
                                at = 16 * half_id
                                gbw[i, group_id + slot : group_id + slot + 1, at : at + 16] = turned[i : i + 1, 0:16]

        @pl.when((group == 0) & (branch == 0))
        def _():
            s0[at16(h), :] = r[30].astype(F32)

        @pl.when((group == 1) & (branch == 0))
        def _():
            for i in range(2):
                s1[at16(h), 128 * i : 128 * (i + 1)] = r[30 + i].astype(F32)
            s2[at16(h), 0:128] = r[32].astype(F32)

        @pl.when((group == 1) & (branch == 1))
        def _():
            for i in range(3):
                s2[at16(h), 128 * (i + 1) : 128 * (i + 2)] = r[30 + i].astype(F32)


def near_out_kernel(meta, *refs):
    parts, (out, gcw, gcb, gbw, s0, s1, s2, gbb, gains, shifts, room, sems) = refs[:4], refs[4:]
    copies = conv_out(meta, 0, parts, out, room, sems)
    row_outs(meta, 0, parts, gcw, gcb, gbw, s0, s1, s2)
    c = meta[2]
    for k in range(4):
        group, branch, _ = source(meta, k)
        r = parts[k]
        for group_id in range(2):

            @pl.when((group == group_id) & (branch == 1))
            def _():
                bias = r[29].astype(F32)
                for slot in range(1 + group_id):
                    level = group_id + slot
                    gbb[level : level + 1, :] = bias[0:1, 2 + 5 * slot : 7 + 5 * slot]

        v = r[33].astype(F32)
        mine = v[:, 0:32]
        for i in range(1, 4):
            mine = jnp.where(c == i, v[:, 32 * i : 32 * (i + 1)], mine)
        for layer in range(3):
            at = 0 if layer == 0 else layer + 2 * branch
            base = 4 * layer

            @pl.when(group == 0)
            def _():
                shifts[at, 0:1, :] = mine[base : base + 1]
                gains[at, 0:1, :] = mine[base + 2 : base + 3]

            @pl.when(group == 1)
            def _():
                shifts[at, 1:3, :] = mine[base : base + 2]
                gains[at, 1:3, :] = mine[base + 2 : base + 4]

    for copy in copies:
        copy.wait()


def far_out_kernel(meta, *refs):
    parts, earlier, (out, gcw, gcb, gbw, s0, s1, s2, room, sems) = refs[:4], refs[5:11], refs[11:]
    copies = conv_out(meta, 1, parts, out, room, sems)
    outs = (gcw, gcb, gbw, s0, s1, s2)
    for old, new in zip(earlier, outs):
        new[...] = old[...]
    row_outs(meta, 1, parts, *outs)
    for copy in copies:
        copy.wait()


def class_out_kernel(sizes, meta, mine, near, far, cross, class_out, box_out):
    n0, n1, n2 = sizes

    def store(out, fine, rest):
        n = out.shape[0]
        out[:, 0:n0] = fine[0:n, 0:n0]
        out[:, n0 : n0 + n1] = rest[0:n, 0:n1]
        out[:, n0 + n1 : n0 + n1 + n2] = rest[0:n, MID : MID + n2]

    for group in range(2):
        for branch in range(2):

            @pl.when((meta[0] == group) & (meta[1] == branch))
            def _():
                here, there = (mine, near), (far, cross)
                for i, out in enumerate((class_out, box_out)):
                    pair = (here[branch ^ i], there[branch ^ i])
                    store(out, pair[group], pair[1 - group])


def feature_out_kernel(meta, own, received, fine, mid, coarse):
    def store(a, b):
        n1, n2 = mid.shape[1], coarse.shape[0]
        fine[...] = a[:, 0 : fine.shape[1]]
        for i in range(2):
            mid[32 * i : 32 * (i + 1), :] = b[:, MID * i : MID * i + n1]
        v = jnp.concatenate([b[:, 1024 + 128 * i : 1152 + 128 * i] for i in range(4)], axis=0)
        coarse[...] = v.astype(F32).T[0:n2].astype(BF)

    @pl.when(meta[0] == 0)
    def _():
        store(own, received)

    @pl.when(meta[0] == 1)
    def _():
        store(received, own)


def pack_kernel(f0, f1, f2, s0, s1, s2, gains, shifts, box, own, send, small):
    group = lax.axis_index("chan") // 2

    def fine(out):
        out[:, 0 : f0.shape[1]] = f0[...]
        out[:, f0.shape[1] : CP] = jnp.zeros((32, CP - f0.shape[1]), BF)
        out[:, CP : CP + 128] = s0[...]
        out[:, CP + 128 : PAR] = jnp.zeros((32, PAR - CP - 128), BF)

    def rest(out):
        n1, n2 = f1.shape[1], f2.shape[0]
        for i in range(2):
            out[:, MID * i : MID * i + n1] = f1[32 * i : 32 * (i + 1), :]
            out[:, MID * i + n1 : MID * (i + 1)] = jnp.zeros((32, MID - n1), BF)
        v = jnp.concatenate([f2[...].astype(F32), jnp.zeros((128 - n2, 128), F32)], axis=0).T.astype(BF)
        for i in range(4):
            out[:, 1024 + 128 * i : 1152 + 128 * i] = v[32 * i : 32 * (i + 1)]
        out[:, STEM : STEM + 256] = s1[...]
        out[:, STEM + 256 : PAR] = s2[...]

    @pl.when(group == 0)
    def _():
        fine(own)
        rest(send)

    @pl.when(group == 1)
    def _():
        rest(own)
        fine(send)

    small[...] = jnp.zeros((64, 32), F32)
    for base, v in ((0, gains), (16, shifts), (32, box)):
        for k in range(5):
            small[base + 3 * k : base + 3 * k + 3] = v[k].astype(F32)
    for i in range(2):
        v = small[32 * i : 32 * (i + 1)]
        high = v.astype(BF).astype(F32)
        mid = (v - high).astype(BF).astype(F32)
        block = jnp.concatenate([high, mid, v - high - mid, jnp.zeros((32, 32), F32)], axis=1).astype(BF)
        for out in (own, send):
            out[:, PAR + 128 * i : PAR + 128 * (i + 1)] = block


def pred_kernel(sizes, meta, ccot, cw, cb, bcot, bb, conv, own, box, first, first_cross, second, second_cross, room, spare, sems):
    n0, n1, n2 = sizes
    copies = []
    for layer, outs in enumerate(((first, first_cross), (second, second_cross))):
        for i, out in enumerate(outs):
            for slot in range(2):
                taken = conv.at[1 - meta[0] + slot, 2 * (meta[1] ^ i) + layer]
                to = spare.at[i] if layer == 1 and slot == 1 else out.at[pl.ds(9 * slot, 9)]
                copy = pltpu.make_async_copy(taken, to, sems.at[layer, i, slot])
                copy.start()
                copies.append(copy)
    lane = lax.broadcasted_iota(jnp.int32, (32, 128), 1)

    def biases(b, level):
        block = jnp.concatenate([b[...], jnp.zeros((3, 128 - b.shape[1]), F32)], axis=1)
        block = jnp.concatenate([block, jnp.zeros((5, 128), F32)], axis=0)
        col = block.T[0:32, level : level + 1]
        high = col.astype(BF).astype(F32)
        mid = (col - high).astype(BF).astype(F32)
        low = col - high - mid
        v = jnp.where(lane == 0, high, jnp.where(lane == 1, mid, jnp.where(lane == 2, low, 0.0)))
        return v.astype(BF)

    def fill(outs, cot, b, fine, weights, sent=False):
        n = cot.shape[0]
        room[...] = jnp.zeros((32, CP), BF)
        if fine:
            room[0:n, 0:n0] = cot[:, 0:n0]
        else:
            room[0:n, 0:n1] = cot[:, n0 : n0 + n1]
            room[0:n, MID : MID + n2] = cot[:, n0 + n1 : n0 + n1 + n2]
        base = CP // 128
        if sent:
            base = TAPS + LOW
        for out in outs:
            for i in range(CP // 128 if fine else LOW):
                at = i
                if sent:
                    at = TAPS + i if i < LOW else 9 + i - LOW
                out[at] = room[:, 128 * i : 128 * (i + 1)]
            if not fine and not sent:
                out[LOW : CP // 128] = jnp.zeros((CP // 128 - LOW, 32, 128), BF)
            if fine and sent:
                out[9 + CP // 128 - LOW] = jnp.zeros((32, 128), BF)
            for slot in range(2):
                level = 0 if fine else 1 + slot
                out[base + 2 * slot] = jnp.zeros((32, 128), BF)
                if weights:
                    out[base + 2 * slot, 0:n] = cw[level]
                out[base + 2 * slot + 1] = biases(b, level)

    for group in range(2):

        @pl.when(meta[0] == group)
        def _():
            fill([own], ccot, cb, group == 0, True)
            fill([box], bcot, bb, group == 0, False)

        @pl.when(meta[0] != group)
        def _():
            fill([second, second_cross], ccot, cb, group == 0, True, True)

    for copy in copies:
        copy.wait()

    @pl.when(meta[0] == 0)
    def _():
        second[9:18] = spare[0]
        second_cross[9:18] = spare[1]


def call(body, outs, scratch, args, last=False, limit=VMEM, in_place=(), aliases={}, flops=10**6):
    place = jax.ShapeDtypeStruct if last else pltpu.VMEM

    def space(i):
        return pl.BlockSpec(memory_space=pl.ANY if i in in_place else pltpu.VMEM)

    def placed(units, *refs):
        body(position(units), *refs)

    return pl.pallas_call(
        placed if args[0].dtype == jnp.int32 else body,
        out_shape=[place(s, d) for s, d in outs],
        in_specs=[space(i) for i in range(len(args))],
        out_specs=[space(len(args) + i) for i in range(len(outs))],
        scratch_shapes=[s if callable(getattr(s, "get_ref_aval", None)) else pltpu.VMEM(*s) for s in scratch],
        input_output_aliases=aliases,
        compiler_params=pltpu.CompilerParams(vmem_limit_bytes=limit),
        cost_estimate=pl.CostEstimate(flops=flops, bytes_accessed=10**4, transcendentals=0),
    )(*args)


def shards(f0, f1, f2, units, s0, s1, s2, conv, gains, shifts, cw, cb, bw, bb, ccot, bcot):
    dp = lax.axis_size("dp")
    c = lax.axis_index("chan")
    group, branch = c // 2, c % 2
    fine = group == 0
    direct = dp == 8
    meta = jnp.broadcast_to(units, (8, 128))
    n0, n1, n2 = f0.shape[2], f1.shape[2], f2.shape[2]

    def across(v):
        return lax.ppermute(v, "chan", [(i, i ^ 2) for i in range(4)])

    def diagonal(v):
        return lax.ppermute(v, "chan", [(i, i ^ 3) for i in range(4)])

    def beside(v, pairs=((0, 1), (1, 0), (2, 3), (3, 2))):
        return lax.ppermute(v, "chan", list(pairs))

    def exchange(st, *hold):
        st, *hold = lax.optimization_barrier((st, *hold))
        st = lax.all_to_all(st, "dp", 0, 0, tiled=True)
        return lax.optimization_barrier((st, *hold)) if hold else st

    def after(v, *others):
        return lax.optimization_barrier((v, *others))[0]

    def over_z(v):
        if not direct:
            return v
        parts = []
        for k in range(4):
            pairs = [
                (8 * z + 4 * y + i, 8 * (i ^ k) + 4 * y + z) for z in range(4) for y in range(2) for i in range(4)
            ]
            parts.append(lax.ppermute(v, ("dp", "chan"), pairs))
        return parts

    def everywhere(parts):
        if direct:
            return parts + [over_y(p) for p in parts]
        v = lax.all_to_all(parts.reshape(4, 2, *parts.shape[1:]), "chan", 0, 0, tiled=True)
        return [v[k % 4, k // 4] for k in range(8)]

    def joined(*parts):
        return jnp.concatenate(parts, axis=-3)

    def over_y(v):
        return lax.ppermute(v, "dp", [(i, i ^ 1) for i in range(8)])

    def along_z(kept, got):
        shape = (sum(v.shape[1] for v in kept), 16, 128)
        outs = [(shape, F32)] + [(shape, BF)] * 3
        own, *rest = call(functools.partial(add_kernel, len(kept)), outs, [], (meta, *kept, *got))
        return [own] + [lax.ppermute(v, "dp", [(i, i ^ (2 * k + 2)) for i in range(8)]) for k, v in enumerate(rest)]

    def reduce(v):
        return lax.optimization_barrier(lax.psum(v.astype(F32), "dp")).astype(BF)

    own, send = call(
        pack_kernel,
        [((32, WIDE), BF), ((32, WIDE), BF)],
        [((64, 32), F32)],
        (f0[0], f1[0], f2[0].T, s0, s1, s2, gains.transpose(1, 0, 2), shifts.transpose(1, 0, 2), bw.transpose(1, 0, 2)),
        limit=WHOLE,
    )
    far_u = across(send)
    own_pred, box_pred, send1, send1_cross, send2, send2_cross = call(
        functools.partial(pred_kernel, (n0, n1, n2)),
        [((CLS, 32, 128), BF)] * 2 + [((TAPS, 32, 128), BF)] * 2 + [((SECOND, 32, 128), BF)] * 2,
        [((32, CP), BF), ((2, 9, 32, 128), BF), pltpu.SemaphoreType.DMA((2, 2, 2))],
        (meta, ccot[0], cw, cb, bcot[0], after(bb, own), conv),
        limit=WHOLE,
        in_place=(6,),
        flops=2 * 10**9,
    )
    near = beside(after(conv, own))
    far_u = after(far_u, near, send2)
    u = (own, far_u, beside(own), beside(far_u))
    to_class = ((1, 0), (3, 2))
    near_pred = beside(own_pred, to_class)

    def weights_of(layer, far, cross):
        return call(
            functools.partial(weight_kernel, layer),
            [((2, 128, 1152), BF), ((2, 1152, 128), BF)],
            [],
            (meta, conv, near, far, cross),
        )

    canvas = (PX, 128)
    stat = (dp, 8, 128)
    moved = [((PX + 16, 128), F32), ((3, PX + 2 * ST, 128), BF)]
    y0, st, cnt, par = call(
        stem_kernel,
        [(canvas, F32), (stat, F32), ((8, 128), F32), ((64, 128), F32)],
        [((512, CP), BF), ((128, 768), BF), ((CP, 128), F32)],
        (meta, *u),
    )
    far1, cross1 = across(after(send1, far_u)), diagonal(after(send1_cross, far_u))
    st, near_pred = exchange(st, near_pred)
    far1, cross1 = after((far1, cross1), st)
    far2, cross2 = across(after(send2, far1)), diagonal(after(send2_cross, cross1))
    w1, w1_tall = weights_of(0, far1, cross1)
    forward_outs = [(canvas, BF), (canvas, F32), (stat, F32), ((16, 128), F32)]
    act0, y1, st, cst0 = call(functools.partial(forward_kernel, True), forward_outs, moved, (meta, y0, st, cnt, w1, par))
    st = exchange(st)
    far2, cross2 = after((far2, cross2), st)
    w2, w2_tall = weights_of(1, far2, cross2)
    act1, y2, st, cst1 = call(
        functools.partial(forward_kernel, False), forward_outs, moved, (meta, y1, st, cnt, w2, par)
    )
    st = exchange(st)
    dz2, st, cst2, x2, cot, wp = call(
        heads_kernel,
        [(canvas, F32), (stat, F32), ((16, 128), F32), ((CP, 256), BF), ((128, CP), BF), ((2, 128, 256), BF)],
        [(canvas, F32), ((CP, 128), F32)],
        (meta, y2, st, par, own_pred, far2, near_pred, cross2, box_pred),
    )
    gw, mine, near, far, cross = call(
        logits_kernel, [((8, 3, 16, 128), BF)] + [((32, CP), BF)] * 4, [((128, CP), BF)], (meta, x2, cot, wp)
    )
    near, far, cross = beside(near), across(far), diagonal(cross)
    st = exchange(after(st, gw))
    st, near, far, cross = lax.optimization_barrier((st, near, far, cross))
    back_scratch = moved + [((128, PX), BF)]
    dz1, st, sums2, wg2, send2 = call(
        second_back_kernel,
        [(canvas, F32), (stat, F32), ((8, 128), F32), ((8, 21, 16, 128), BF), ((4, 21, 16, 128), BF)],
        back_scratch,
        (meta, dz2, y2, cst2, st, w2_tall, act1, y1, cst1, gw),
    )
    got2 = over_y(send2) if direct else reduce(wg2)
    st, got2 = lax.optimization_barrier((exchange(after(st, send2)), got2))
    d0, st, sums1, wg1, send1 = call(
        first_back_kernel,
        [((PX + 32, 128), BF), (stat, F32), ((8, 128), F32), ((8, 18, 16, 128), BF), ((4, 18, 16, 128), BF)],
        back_scratch,
        (meta, dz1, y1, cst1, st, w1_tall, act0, y0, cst0),
    )
    got1 = over_y(send1) if direct else reduce(wg1)
    d0_other = beside(d0)
    if direct:
        pair = (2, 21, 16, 128)
        own2, send2 = call(halve_kernel, [(pair, F32), (pair, BF)], [], (meta, wg2, after(got2, d0)))
        got2 = lax.ppermute(send2, "dp", [(i, i ^ 2) for i in range(8)])
        (st,) = call(both_kernel, [(stat, F32)], [], (after(st, own2), d0_other))
        st = exchange(st)
        (st,) = call(total_kernel, [((1, 8, 128), F32)], [], (st,))
        st, got1, got2 = lax.optimization_barrier((st, got1, got2))
        own2, send2 = call(again_kernel, [(pair[1:], F32), (pair[1:], BF)], [], (meta, own2, got2))
        got2 = lax.ppermute(send2, "dp", [(i, i ^ 4) for i in range(8)])
    else:
        (st,) = call(both_kernel, [(stat, F32)], [], (st, d0_other))
        st = exchange(st)
    own, other, gs, gs_send, norm = call(
        final_kernel,
        [((32, CP), BF), ((32, CP), BF), ((8, 3, 16, 128), BF), ((4, 3, 16, 128), BF), ((1, 16, 128), BF)],
        [
            ((8, 128), F32),
            ((512, CP), BF),
            ((128, 768), BF),
            (canvas, F32),
            ((CP, 128), F32),
            ((128, CP), BF),
            ((512, CP), BF),
            ((6, 128, 128), BF),
        ],
        (meta, d0, d0_other, y0, cst0, st, sums1, sums2, *u),
    )
    received = across(other)
    if direct:
        parts1 = along_z([wg1, gs], [got1, over_y(gs_send)])
        total, extra = call(
            sum_kernel, [((12, 16, 128), BF), ((9, 16, 128), BF)], [], (meta, own2, after(got2, parts1[0]))
        )
        extra = lax.ppermute(extra, "chan", [(2, 0), (3, 1)])
        extra, received = lax.optimization_barrier((extra, received))
        (grads,) = call(join_kernel, [((34, 16, 128), BF)], [], (meta, *parts1, total, extra, norm))
    else:
        extra = lax.ppermute(got2[:, 9:18], "chan", [(2, 0), (3, 1)])
        third = jnp.where(fine, extra, got1[:, 9:18])
        norm = jnp.broadcast_to(norm[None], (8, *norm.shape))
        grads = joined(got1[:, :9], got2[:, :9], third, got2[:, 18:21], reduce(gs), norm)
    grads = everywhere(over_z(grads))

    room = [((2, 3, 2, conv.shape[2], 16, 128), F32), pltpu.SemaphoreType.DMA((2, 3, 2))]
    rows = [(cw.shape, F32), (cb.shape, F32), ((5, 3, 32), F32), (s0.shape, F32), (s1.shape, F32), (s2.shape, F32)]
    wholes = [(bb.shape, F32), ((5, 3, 32), F32), ((5, 3, 32), F32)]
    grad_conv, *half, grad_bb, grad_gains, grad_shifts = call(
        near_out_kernel, [(conv.shape, F32)] + rows + wholes, room, (meta, *grads[:4]), True, in_place=(5,)
    )
    mine, own = after((mine, own), *half)
    box_rows, class_rows = bcot.shape[1], ccot.shape[1]
    class_out, box_out = call(
        functools.partial(class_out_kernel, (n0, n1, n2)),
        [((class_rows, n0 + n1 + n2), BF), ((box_rows, n0 + n1 + n2), BF)],
        [],
        (meta, mine, near, far, cross),
        True,
    )
    grad_fine, grad_mid, grad_coarse = call(
        feature_out_kernel,
        [(f0.shape[1:], BF), (f1.shape[1:], BF), ((n2, f2.shape[1]), BF)],
        [],
        (meta, own, received),
        True,
    )

    grad_conv, grad_cw, grad_cb, grad_bw, grad_s0, grad_s1, grad_s2 = call(
        far_out_kernel,
        [(conv.shape, F32)] + rows,
        room,
        (meta, *grads[4:], grad_conv, *half),
        True,
        in_place=(5, 12),
        aliases={5: 0},
    )
    return (
        class_out[None],
        box_out[None],
        grad_fine[None],
        grad_mid[None],
        grad_coarse.T[None],
        grad_s0,
        grad_s1,
        grad_s2,
        grad_conv,
        grad_gains.transpose(1, 0, 2),
        grad_shifts.transpose(1, 0, 2),
        grad_cw,
        grad_cb,
        grad_bw.transpose(1, 0, 2),
        grad_bb,
    )


def solution(mesh):
    placed = (
        P("dp", "chan", None),
        P("dp", "chan", None),
        P("dp", "chan", None),
        P("dp"),
        P("chan", None),
        P("chan", None),
        P("chan", None),
        P(None, None, None, "chan", None),
        P(None, None, "chan"),
        P(None, None, "chan"),
        P(None, "chan", None),
        P(None, "chan"),
        P(None, None, "chan"),
        P(),
        P("dp", "chan", None),
        P("dp", None, None),
    )
    return jax.shard_map(
        shards,
        mesh=mesh,
        in_specs=placed,
        out_specs=(
            P("dp", "chan", None),
            P("dp", None, None),
            P("dp", "chan", None),
            P("dp", "chan", None),
            P("dp", "chan", None),
            P("chan", None),
            P("chan", None),
            P("chan", None),
            P(None, None, None, "chan", None),
            P(None, None, "chan"),
            P(None, None, "chan"),
            P(None, "chan", None),
            P(None, "chan"),
            P(None, None, "chan"),
            P(),
        ),
        check_vma=False,
    )
```

```python
import functools

import jax
import jax.numpy as jnp
from jax import lax
from jax.experimental import pallas as pl
from jax.experimental.pallas import tpu as pltpu
from jax.sharding import PartitionSpec as P

BF = jnp.bfloat16
F32 = jnp.float32
EPS = 0.001
ST = 48
ROWS = 40
PX = ST * ROWS
CR = 8
CH = CR * ST
NCH = ROWS // CR
SLOT = (0, 0, 0, 1, 1)
CUT = 24 * ST
CP = 1664
MID = 512
E0, E1, E2 = 40, 20, 10
STEM = 1536
PAR = STEM + 768
WIDE = PAR + 256
CLS = CP // 128 + 4
TAPS = 18
LOW = (MID + 128) // 128
SECOND = TAPS + LOW + 4
SENT = 2 * (CP // 128) + 9
VMEM = 12 * 2**20
WHOLE = 56 * 2**20
NT = (((1,), (1,)), ((), ()))
TN = (((0,), (0,)), ((), ()))


def dot(a, b, dims=(((1,), (0,)), ((), ()))):
    return lax.dot_general(a, b, dims, preferred_element_type=F32)


def position(units):
    c = lax.axis_index("chan")
    place = lax.axis_index("dp") if lax.axis_size("dp") == 8 else jnp.int32(0)
    return c >> 1, c & 1, c, units[0:1, :], place >> 1, place & 1


def limits(meta, slot):
    group, units = meta[0], meta[3]
    if slot == 0:
        edge = jnp.where(group == 0, 4 * units, 2 * units)
        return edge, edge
    return (
        jnp.where(group == 0, 4 * units, 24 + units),
        jnp.where(group == 0, 4 * units, units),
    )


def mask_of(meta, j):
    row_end, col_end = (v.reshape(1, 1, 128) for v in limits(meta, SLOT[j]))
    row = lax.broadcasted_iota(jnp.int32, (CR, ST, 128), 0) + CR * j
    col = lax.broadcasted_iota(jnp.int32, (CR, ST, 128), 1)
    inside = (row < row_end) & (col < col_end)
    return jnp.where(inside, 1.0, 0.0).reshape(CH, 128)


def pick(meta, first, second):
    total = first + second
    return jnp.where(meta[0] == 0, total, first), jnp.where(meta[0] == 0, total, second)


def level_rows(meta, base, layer):
    fine = meta[0] == 0
    at = base + 3 * layer
    return at + jnp.where(fine, 0, 1), at + jnp.where(fine, 0, 2)


def norm_constants(meta, st, par, layer, cst):
    total = jnp.sum(st[...], axis=0)
    row = [total[i : i + 1] for i in range(6)]
    first = pick(meta, row[0], row[1])
    second = pick(meta, row[2], row[3])
    count = pick(meta, row[4], row[5])
    gain_at = level_rows(meta, 0, layer)
    shift_at = level_rows(meta, 16, layer)
    for s in range(2):
        rn = 1.0 / count[s]
        mean = first[s] * rn
        inv = lax.rsqrt(second[s] * rn - mean * mean + EPS)
        cst[s : s + 1] = mean
        cst[2 + s : 3 + s] = inv
        cst[4 + s : 5 + s] = par[pl.ds(gain_at[s], 1), :]
        cst[6 + s : 7 + s] = par[pl.ds(shift_at[s], 1), :]
        cst[8 + s : 9 + s] = rn
        cst[10 + s : 11 + s] = count[s]
    cst[12:16] = jnp.zeros((4, 128), F32)


def normed(cst, y, s):
    xhat = (y - cst[s : s + 1]) * cst[2 + s : 3 + s]
    return xhat, xhat * cst[4 + s : 5 + s] + cst[6 + s : 7 + s]


def sigmoid(z):
    return 0.5 * jnp.tanh(0.5 * z) + 0.5


def slope(z):
    s = sigmoid(z)
    return s * (1.0 + z * (1.0 - s))


def spread_out(st, rows):
    block = jnp.concatenate(rows + [jnp.zeros((8 - len(rows), 128), F32)], axis=0)
    st[...] = jnp.broadcast_to(block[None], st.shape)


def colsum(v):
    return jnp.sum(v, axis=0, keepdims=True)


def guard(field, shifts):
    field[0:8] = jnp.zeros((8, 128), F32)
    field[8 + PX : 16 + PX] = jnp.zeros((8, 128), F32)
    for k in range(3):
        shifts[k, 0:ST] = jnp.zeros((ST, 128), BF)
        shifts[k, ST + PX :] = jnp.zeros((ST, 128), BF)


def fill_shifts(field, shifts):
    for k in range(3):
        for j in range(NCH):
            at = 8 + CH * j + k - 1
            shifts[k, ST + CH * j : ST + CH * (j + 1)] = field[at : at + CH].astype(BF)


def taps(shifts, begin, size, back=False):
    parts = []
    for kr in range(3):
        for kc in range(3):
            k, r = (2 - kc, 1 - kr) if back else (kc, kr - 1)
            at = ST + begin + ST * r
            parts.append(shifts[k, at : at + size])
    return jnp.concatenate(parts, axis=1)


def slices_of(meta):
    c = meta[2]
    return (c, c ^ 2, c ^ 1, c ^ 3)


def at32(s, extra=0):
    return pl.ds(pl.multiple_of(32 * s + extra, 32), 32)


def weight_slot(meta, j):
    return jnp.where(meta[0] == 0, 0, SLOT[j])


def to_compact(meta, canvas, out):
    @pl.when(meta[0] == 0)
    def _():
        for r in range(E0):
            out[E0 * r : E0 * (r + 1)] = canvas[ST * r : ST * r + E0]

    @pl.when(meta[0] == 1)
    def _():
        for r in range(E1):
            out[E1 * r : E1 * (r + 1)] = canvas[ST * r : ST * r + E1]
        for r in range(E2):
            at = CUT + ST * r
            out[MID + E2 * r : MID + E2 * (r + 1)] = canvas[at : at + E2]


def to_canvas(meta, compact, out):
    @pl.when(meta[0] == 0)
    def _():
        for r in range(E0):
            out[ST * r : ST * r + E0] = compact[E0 * r : E0 * (r + 1)]

    @pl.when(meta[0] == 1)
    def _():
        for r in range(E1):
            out[ST * r : ST * r + E1] = compact[E1 * r : E1 * (r + 1)]
        for r in range(E2):
            at = CUT + ST * r
            out[at : at + E2] = compact[MID + E2 * r : MID + E2 * (r + 1)]


def load_inputs(meta, pieces, feat, stem):
    for s, u in zip(slices_of(meta), pieces):

        @pl.when(meta[0] == 0)
        def _():
            feat[at32(s), :] = u[:, 0:CP]
            stem[at32(s), 0:128] = u[:, CP : CP + 128]

        @pl.when(meta[0] == 1)
        def _():
            for i in range(2):
                at = pl.ds(pl.multiple_of(64 * s + 32 * i, 32), 32)
                feat[at, 0:MID] = u[:, MID * i : MID * (i + 1)]
            for i in range(4):
                at = pl.ds(pl.multiple_of(128 * s + 32 * i, 32), 32)
                feat[at, MID : MID + 128] = u[:, 1024 + 128 * i : 1152 + 128 * i]
            stem[at32(s), :] = u[:, STEM:PAR]


def stem_kernel(meta, u0, u1, u2, u3, y, st, cnt, par, feat, stem, flat):
    load_inputs(meta, (u0, u1, u2, u3), feat, stem)
    lane = lax.broadcasted_iota(jnp.int32, (32, 128), 1) // 32
    for i in range(2):
        total = jnp.zeros((32, 128), F32)
        for s, u in zip(slices_of(meta), (u0, u1, u2, u3)):
            v = u[:, PAR + 128 * i : PAR + 128 * (i + 1)].astype(F32)
            v = v[:, 0:32] + v[:, 32:64] + v[:, 64:96]
            total = jnp.where(lane == s, jnp.concatenate([v] * 4, axis=1), total)
        par[32 * i : 32 * (i + 1)] = total
    y[...] = jnp.zeros((PX, 128), F32)

    @pl.when(meta[0] == 0)
    def _():
        flat[...] = dot(stem[:, 0:128], feat[0:128, :]).T

    @pl.when(meta[0] == 1)
    def _():
        flat[0:MID] = dot(stem[:, 0:256], feat[0:256, 0:MID]).T
        flat[MID : MID + 128] = dot(stem[:, 256:768], feat[0:512, MID : MID + 128]).T

    to_canvas(meta, flat, y)
    sums = [jnp.zeros((1, 128), F32) for _ in range(6)]
    for j in range(NCH):
        m = mask_of(meta, j)
        v = y[CH * j : CH * (j + 1)] * m
        s = SLOT[j]
        sums[s] += colsum(v)
        sums[2 + s] += colsum(v * v)
        sums[4 + s] += colsum(m)
    spread_out(st, sums)
    cnt[...] = jnp.concatenate(sums[4:6] + [jnp.zeros((6, 128), F32)], axis=0)


def forward_kernel(first, meta, y, st, cnt, w, *refs):
    par, act, out, st_out, cst, field, shifts = refs
    layer = 0 if first else 1 + 2 * meta[1]
    norm_constants(meta, st, par, layer, cst)
    guard(field, shifts)
    for j in range(NCH):
        rows = slice(CH * j, CH * (j + 1))
        _, z = normed(cst, y[rows], SLOT[j])
        v = z * sigmoid(z) * mask_of(meta, j)
        act[rows] = v.astype(BF)
        field[8 + CH * j : 8 + CH * (j + 1)] = v
    fill_shifts(field, shifts)
    sums = [jnp.zeros((1, 128), F32) for _ in range(4)]
    for j in range(NCH):
        v = dot(taps(shifts, CH * j, CH), w[weight_slot(meta, j)], NT)
        out[CH * j : CH * (j + 1)] = v
        v = v * mask_of(meta, j)
        s = SLOT[j]
        sums[s] += colsum(v)
        sums[2 + s] += colsum(v * v)
    spread_out(st_out, sums + [cnt[0:1], cnt[1:2]])


def weight_kernel(layer, meta, mine, near, far, cross, flat, tall):
    group, branch, c = meta[0], meta[1], meta[2]
    conv = 2 * branch + layer
    for slot in range(2):
        level = group + slot
        for t in range(9):
            for s, piece in (
                (c, mine[level, conv, t]),
                (c ^ 1, near[level, conv, t]),
                (c ^ 2, far[9 * slot + t]),
                (c ^ 3, cross[9 * slot + t]),
            ):
                flat[slot, at32(s), 128 * t : 128 * (t + 1)] = piece
                tall[slot, at32(s, 128 * t), :] = piece


def heads_kernel(meta, y, st, par, k0, k1, k2, k3, box_pack, dz, st_out, cst, x2, cot, wp, field, flat):
    norm_constants(meta, st, par, 2 + 2 * meta[1], cst)
    cot[...] = jnp.zeros((128, CP), BF)
    wp[...] = jnp.zeros((2, 128, 256), BF)

    pixels = CP // 128

    @pl.when(meta[1] == 0)
    def _():
        for s, k, sent in zip(slices_of(meta), (k0, k1, k2, k3), (False, True, False, True)):
            for i in range(pixels):
                if not sent or i < LOW:
                    cot[at32(s), 128 * i : 128 * (i + 1)] = k[TAPS + i if sent else i]
            for slot in range(2):
                for i in range(2):
                    at = (TAPS + LOW if sent else pixels) + 2 * slot + i
                    wp[slot, at32(s), 128 * i : 128 * (i + 1)] = k[at]

    @pl.when((meta[1] == 0) & (meta[0] == 0))
    def _():
        for s, k in zip(slices_of(meta)[1::2], (k1, k3)):
            for i in range(LOW, pixels):
                cot[at32(s), 128 * i : 128 * (i + 1)] = k[9 + i - LOW]

    @pl.when(meta[1] == 1)
    def _():
        for i in range(pixels):
            cot[0:32, 128 * i : 128 * (i + 1)] = box_pack[i]
        fine = meta[0] == 0
        for slot in range(2):
            row = lax.broadcasted_iota(jnp.int32, (32, 128), 0)
            box = jnp.zeros((32, 128), F32)
            for i in range(5):
                at = 32 + 3 * i
                line = jnp.where(fine, par[at : at + 1], par[at + 1 + slot : at + 2 + slot])
                box = jnp.where(row == i, line, box)
            wp[slot, 0:32, 0:128] = box.astype(BF)
            wp[slot, 0:32, 128:256] = box_pack[pixels + 2 * slot + 1]

    for part in range(2):
        for j in range(NCH):
            m = mask_of(meta, j)
            if part == 0:
                _, z = normed(cst, y[CH * j : CH * (j + 1)], SLOT[j])
                m = z * sigmoid(z) * m
            field[CH * j : CH * (j + 1)] = m
        flat[...] = jnp.zeros((CP, 128), F32)
        to_compact(meta, field, flat)
        x2[:, 128 * part : 128 * (part + 1)] = flat[...].astype(BF)

    @pl.when(meta[0] == 0)
    def _():
        flat[...] = dot(cot[...], wp[0, :, 0:128], TN)

    @pl.when(meta[0] == 1)
    def _():
        for slot, a, b in ((0, 0, MID), (1, MID, MID + 128)):
            flat[a:b] = dot(cot[:, a:b], wp[slot, :, 0:128], TN)

    field[...] = jnp.zeros((PX, 128), F32)
    to_canvas(meta, flat, field)
    sums = [jnp.zeros((1, 128), F32) for _ in range(4)]
    for j in range(NCH):
        rows = slice(CH * j, CH * (j + 1))
        s = SLOT[j]
        xhat, z = normed(cst, y[rows], s)
        v = field[rows] * slope(z) * mask_of(meta, j)
        dz[rows] = v
        sums[s] += colsum(v)
        sums[2 + s] += colsum(v * xhat)
    spread_out(st_out, sums)


def logits_kernel(meta, x2, cot, wp, gw, mine, near, far, cross, logits):
    def store(slot, v):
        bias = v[:, 128:256]

        @pl.when(meta[1] == 0)
        def _():
            gw_block(gw, slot, v[:, 0:128])

        @pl.when(meta[1] == 1)
        def _():
            gw_block(gw, slot, v[:, 0:128].T)

        return bias

    def finish(first, second):
        lane = lax.broadcasted_iota(jnp.int32, (128, 128), 1)
        cls = jnp.where(lane == 0, first, jnp.where(lane == 1, second, 0.0))
        a, b = first.T, second.T
        box = jnp.where((lane >= 7) & (lane < 12), pltpu.roll(b, 7, 1), 0.0)
        box = jnp.where((lane >= 2) & (lane < 7), pltpu.roll(a, 2, 1), box)
        gw_block(gw, 2, jnp.where(meta[1] == 0, cls, box))

    @pl.when(meta[0] == 0)
    def _():
        logits[...] = dot(wp[0], x2[...], NT).astype(BF)
        first = store(0, dot(cot[...], x2[...]))
        gw_block(gw, 1, jnp.zeros((128, 128), F32))
        finish(first, jnp.zeros((128, 128), F32))

    @pl.when(meta[0] == 1)
    def _():
        logits[...] = jnp.zeros((128, CP), BF)
        bias = []
        for slot, a, b in ((0, 0, MID), (1, MID, MID + 128)):
            logits[:, a:b] = dot(wp[slot], x2[a:b], NT).astype(BF)
            bias.append(store(slot, dot(cot[:, a:b], x2[a:b])))
        finish(*bias)

    for out, c in ((mine, 0), (near, 1), (far, 2), (cross, 3)):
        out[...] = logits[at32(jnp.where(meta[1] == 0, meta[2] ^ c, 0)), :]


def gw_block(gw, i, v):
    for j in range(8):
        gw[j, i] = v[16 * j : 16 * (j + 1)].astype(BF)


def grad_sums(meta, total, sums):
    shift = pick(meta, total[0:1], total[1:2])
    gain = pick(meta, total[2:3], total[3:4])
    sums[...] = jnp.concatenate(list(shift) + list(gain) + [jnp.zeros((4, 128), F32)], axis=0)


def input_grad(meta, dz, y, cst, sums, j):
    s = SLOT[j]
    xhat, _ = normed(cst, y[CH * j : CH * (j + 1)], s)
    factor = cst[4 + s : 5 + s] * cst[2 + s : 3 + s]
    mean = (sums[s : s + 1] + xhat * sums[2 + s : 3 + s]) * cst[8 + s : 9 + s]
    return mask_of(meta, j) * factor * (dz - mean)


def out_grad(meta, dz, y, cst, st, sums, field, dyt):
    grad_sums(meta, jnp.sum(st[...], axis=0), sums)
    for j in range(NCH):
        rows = slice(CH * j, CH * (j + 1))
        v = input_grad(meta, dz[rows], y, cst, sums, j)
        field[8 + CH * j : 8 + CH * (j + 1)] = v
        dyt[:, rows] = v.T.astype(BF)


def conv_back(meta, last, w, y_in, cst_in, shifts, grad, st_out):
    total = [jnp.zeros((1, 128), F32) for _ in range(4)]
    for j in range(NCH):
        rows = slice(CH * j, CH * (j + 1))
        s = SLOT[j]
        v = dot(taps(shifts, CH * j, CH, True), w[weight_slot(meta, j)])
        xhat, z = normed(cst_in, y_in[rows], s)
        d = v * slope(z) * mask_of(meta, j)
        grad[rows] = v.astype(BF) if last else d
        total[s] += colsum(d)
        total[2 + s] += colsum(d * xhat)
    spread_out(st_out, total)


def as_parts(st):
    high = st.astype(BF).astype(F32)
    mid = (st - high).astype(BF).astype(F32)
    return jnp.concatenate([high, mid, st - high - mid, jnp.zeros((8, 128), F32)], axis=0).astype(BF)


def weight_grad(meta, dyt, act, field, shifts, wg):
    for j in range(NCH):
        field[8 + CH * j : 8 + CH * (j + 1)] = act[CH * j : CH * (j + 1)].astype(F32)
    fill_shifts(field, shifts)

    def store(slot, v):
        for t in range(9):
            for j in range(8):
                block = v[16 * j : 16 * (j + 1), 128 * t : 128 * (t + 1)].astype(BF)
                wg[j, 9 * slot + t] = block

    @pl.when(meta[0] == 0)
    def _():
        store(0, dot(dyt[...], taps(shifts, 0, PX)))
        store(1, jnp.zeros((128, 1152), F32))

    @pl.when(meta[0] == 1)
    def _():
        store(0, dot(dyt[:, 0:CUT], taps(shifts, 0, CUT)))
        store(1, dot(dyt[:, CUT:PX], taps(shifts, CUT, PX - CUT)))


def part_out(meta, wg, send):
    for z in range(4):
        send[z] = wg[2 * z + 1 - meta[5]]


def second_back_kernel(meta, dz, y, cst, st, w, act, y_in, cst_in, gw, grad, st_out, sums, wg, send, field, shifts, dyt):
    guard(field, shifts)
    out_grad(meta, dz, y, cst, st, sums, field, dyt)
    fill_shifts(field, shifts)
    conv_back(meta, False, w, y_in, cst_in, shifts, grad, st_out)
    weight_grad(meta, dyt, act, field, shifts, wg)
    for j in range(8):
        for i in range(3):
            wg[j, 18 + i] = gw[j, i]
    part_out(meta, wg, send)


def first_back_kernel(meta, dz, y, cst, st, w, act, y_in, cst_in, grad, st_out, sums, wg, send, field, shifts, dyt):
    guard(field, shifts)
    out_grad(meta, dz, y, cst, st, sums, field, dyt)
    fill_shifts(field, shifts)
    conv_back(meta, True, w, y_in, cst_in, shifts, grad, st_out)
    grad[PX:] = as_parts(st_out[0])
    weight_grad(meta, dyt, act, field, shifts, wg)
    part_out(meta, wg, send)


def final_kernel(meta, d0, d1, y, cst, st, sums1, sums2, u0, u1, u2, u3, own, other, gs, gs_send, norm, *scratch):
    sums, feat, stem, field, flat, dyt, gf, blocks = scratch
    load_inputs(meta, (u0, u1, u2, u3), feat, stem)
    grad_sums(meta, jnp.sum(st[...], axis=0), sums)
    for j in range(NCH):
        rows = slice(CH * j, CH * (j + 1))
        _, z = normed(cst, y[rows], SLOT[j])
        v = (d0[rows].astype(F32) + d1[rows].astype(F32)) * slope(z) * mask_of(meta, j)
        field[rows] = input_grad(meta, v, y, cst, sums, j)
    flat[...] = jnp.zeros((CP, 128), F32)
    to_compact(meta, field, flat)
    dyt[...] = flat[...].T.astype(BF)
    c = meta[2]
    outs = ((own, c), (other, c ^ 2))

    @pl.when(meta[0] == 0)
    def _():
        gf[0:128, :] = dot(stem[:, 0:128], dyt[...], TN).astype(BF)
        blocks[0] = dot(dyt[...], feat[0:128, :], NT).astype(BF)
        for i in range(1, 6):
            blocks[i] = jnp.zeros((128, 128), BF)
        for out, s in outs:
            out[...] = gf[at32(s), :]

    @pl.when(meta[0] == 1)
    def _():
        gf[0:256, 0:MID] = dot(stem[:, 0:256], dyt[:, 0:MID], TN).astype(BF)
        gf[:, MID : MID + 128] = dot(stem[:, 256:768], dyt[:, MID : MID + 128], TN).astype(BF)
        for i in range(2):
            blocks[i] = dot(dyt[:, 0:MID], feat[128 * i : 128 * (i + 1), 0:MID], NT).astype(BF)
        for i in range(4):
            rows = slice(128 * i, 128 * (i + 1))
            blocks[2 + i] = dot(dyt[:, MID : MID + 128], feat[rows, MID : MID + 128], NT).astype(BF)
        for out, s in outs:
            out[...] = jnp.zeros((32, CP), BF)
            for i in range(2):
                at = pl.ds(pl.multiple_of(64 * s + 32 * i, 32), 32)
                out[:, MID * i : MID * (i + 1)] = gf[at, 0:MID]
            for i in range(4):
                at = pl.ds(pl.multiple_of(128 * s + 32 * i, 32), 32)
                out[:, 1024 + 128 * i : 1152 + 128 * i] = gf[at, MID : MID + 128]

    for i in range(3):
        block = blocks[3 * meta[1] + i]
        for j in range(8):
            gs[j, i] = block[16 * j : 16 * (j + 1)]
    part_out(meta, gs, gs_send)
    rest = jnp.zeros((4, 128), F32)
    norm[0] = jnp.concatenate([sums[0:4], sums1[0:4], sums2[0:4], rest], axis=0).astype(BF)


def both_kernel(st, other, out):
    v = other[PX:].astype(F32)
    out[...] = st[...] + (v[0:8] + v[8:16] + v[16:24])[None]


def total_kernel(st, out):
    out[0] = jnp.sum(st[...], axis=0)


def add_kernel(count, meta, *refs):
    kept, got, outs = refs[:count], refs[count : 2 * count], refs[2 * count :]
    for k, out in enumerate(outs):
        z = meta[4] ^ k
        at = 0
        for a, b in zip(kept, got):
            n = a.shape[1]
            out[at : at + n] = (a[2 * z + meta[5]].astype(F32) + b[z].astype(F32)).astype(out.dtype)
            at += n


def halve_kernel(meta, kept, got, own, send):
    for k in range(4):
        z = meta[4] ^ k
        total = kept[2 * z + meta[5]].astype(F32) + got[z].astype(F32)
        if k % 2:
            send[k // 2] = total.astype(BF)
        else:
            own[k // 2] = total


def again_kernel(meta, own, got, mine, send):
    mine[...] = own[0] + got[0].astype(F32)
    send[...] = (own[1] + got[1].astype(F32)).astype(BF)


def summed(refs, begin, end):
    total = refs[0][begin:end].astype(F32)
    for r in refs[1:]:
        total += r[begin:end].astype(F32)
    return total.astype(BF)


def sum_kernel(meta, *refs):
    parts, (total, extra) = refs[:-2], refs[-2:]
    total[0:9] = summed(parts, 0, 9)
    total[9:12] = summed(parts, 18, 21)
    extra[...] = summed(parts, 9, 18)


def join_kernel(meta, *refs):
    parts, (total, extra, norm, out) = refs[:4], refs[4:]
    out[0:9] = summed(parts, 0, 9)
    out[9:18] = total[0:9]
    out[27:30] = total[9:12]

    @pl.when(meta[0] == 0)
    def _():
        out[18:27] = extra[...]

    @pl.when(meta[0] == 1)
    def _():
        out[18:27] = summed(parts, 9, 18)

    out[30:33] = summed(parts, 18, 21)
    out[33:34] = norm[...]


def source(meta, k):
    c = meta[4] ^ (k % 4)
    return c >> 1, c & 1, meta[5] ^ (k // 4)


def at16(h):
    return pl.ds(pl.multiple_of(16 * h, 16), 16)


def conv_out(meta, half, parts, out, room, sems):
    for k in range(4):
        group, branch, _ = source(meta, k)
        r = parts[k]
        for i in range(3):
            layer = i if i < 2 else 1 - group
            level = group if i < 2 else 2
            for t in range(9):
                room[layer, level, branch, t] = r[9 * i + t].astype(F32)

    h = meta[5] ^ half
    copies = []
    for layer in range(2):
        for level in range(3):
            for branch in range(2):
                to = out.at[level, 2 * branch + layer, :, at16(h), :]
                copy = pltpu.make_async_copy(room.at[layer, level, branch], to, sems.at[layer, level, branch])
                copy.start()
                copies.append(copy)
    return copies


def row_outs(meta, half, parts, gcw, gcb, gbw, s0, s1, s2):
    h = meta[5] ^ half
    for k in range(4):
        group, branch, _ = source(meta, k)
        r = parts[k]
        for group_id in range(2):
            slots = range(1 + group_id)

            @pl.when((group == group_id) & (branch == 0))
            def _():
                turned = r[29].astype(F32).T
                for half_id in range(2):
                    size = (16, 4)[half_id]

                    @pl.when(h == half_id)
                    def _():
                        for slot in slots:
                            level = group_id + slot
                            gcw[level, 16 * half_id : 16 * half_id + size, :] = r[27 + slot].astype(F32)[0:size]
                            gcb[level : level + 1, 16 * half_id : 16 * half_id + size] = turned[slot : slot + 1, 0:size]

            @pl.when((group == group_id) & (branch == 1))
            def _():
                for slot in slots:
                    turned = r[27 + slot].astype(F32).T
                    for half_id in range(2):

                        @pl.when(h == half_id)
                        def _():
                            for i in range(5):
                                at = 16 * half_id
                                gbw[i, group_id + slot : group_id + slot + 1, at : at + 16] = turned[i : i + 1, 0:16]

        @pl.when((group == 0) & (branch == 0))
        def _():
            s0[at16(h), :] = r[30].astype(F32)

        @pl.when((group == 1) & (branch == 0))
        def _():
            for i in range(2):
                s1[at16(h), 128 * i : 128 * (i + 1)] = r[30 + i].astype(F32)
            s2[at16(h), 0:128] = r[32].astype(F32)

        @pl.when((group == 1) & (branch == 1))
        def _():
            for i in range(3):
                s2[at16(h), 128 * (i + 1) : 128 * (i + 2)] = r[30 + i].astype(F32)


def near_out_kernel(meta, *refs):
    parts, (out, gcw, gcb, gbw, s0, s1, s2, gbb, gains, shifts, room, sems) = refs[:4], refs[4:]
    copies = conv_out(meta, 0, parts, out, room, sems)
    row_outs(meta, 0, parts, gcw, gcb, gbw, s0, s1, s2)
    c = meta[2]
    for k in range(4):
        group, branch, _ = source(meta, k)
        r = parts[k]
        for group_id in range(2):

            @pl.when((group == group_id) & (branch == 1))
            def _():
                bias = r[29].astype(F32)
                for slot in range(1 + group_id):
                    level = group_id + slot
                    gbb[level : level + 1, :] = bias[0:1, 2 + 5 * slot : 7 + 5 * slot]

        v = r[33].astype(F32)
        mine = v[:, 0:32]
        for i in range(1, 4):
            mine = jnp.where(c == i, v[:, 32 * i : 32 * (i + 1)], mine)
        for layer in range(3):
            at = 0 if layer == 0 else layer + 2 * branch
            base = 4 * layer

            @pl.when(group == 0)
            def _():
                shifts[at, 0:1, :] = mine[base : base + 1]
                gains[at, 0:1, :] = mine[base + 2 : base + 3]

            @pl.when(group == 1)
            def _():
                shifts[at, 1:3, :] = mine[base : base + 2]
                gains[at, 1:3, :] = mine[base + 2 : base + 4]

    for copy in copies:
        copy.wait()


def far_out_kernel(meta, *refs):
    parts, earlier, (out, gcw, gcb, gbw, s0, s1, s2, room, sems) = refs[:4], refs[5:11], refs[11:]
    copies = conv_out(meta, 1, parts, out, room, sems)
    outs = (gcw, gcb, gbw, s0, s1, s2)
    for old, new in zip(earlier, outs):
        new[...] = old[...]
    row_outs(meta, 1, parts, *outs)
    for copy in copies:
        copy.wait()


def class_out_kernel(sizes, meta, mine, near, far, cross, class_out, box_out):
    n0, n1, n2 = sizes

    def store(out, fine, rest):
        n = out.shape[0]
        out[:, 0:n0] = fine[0:n, 0:n0]
        out[:, n0 : n0 + n1] = rest[0:n, 0:n1]
        out[:, n0 + n1 : n0 + n1 + n2] = rest[0:n, MID : MID + n2]

    for group in range(2):
        for branch in range(2):

            @pl.when((meta[0] == group) & (meta[1] == branch))
            def _():
                here, there = (mine, near), (far, cross)
                for i, out in enumerate((class_out, box_out)):
                    pair = (here[branch ^ i], there[branch ^ i])
                    store(out, pair[group], pair[1 - group])


def feature_out_kernel(meta, own, received, fine, mid, coarse):
    def store(a, b):
        n1, n2 = mid.shape[1], coarse.shape[0]
        fine[...] = a[:, 0 : fine.shape[1]]
        for i in range(2):
            mid[32 * i : 32 * (i + 1), :] = b[:, MID * i : MID * i + n1]
        v = jnp.concatenate([b[:, 1024 + 128 * i : 1152 + 128 * i] for i in range(4)], axis=0)
        coarse[...] = v.astype(F32).T[0:n2].astype(BF)

    @pl.when(meta[0] == 0)
    def _():
        store(own, received)

    @pl.when(meta[0] == 1)
    def _():
        store(received, own)


def pack_kernel(f0, f1, f2, s0, s1, s2, gains, shifts, box, own, send, small):
    group = lax.axis_index("chan") // 2

    def fine(out):
        out[:, 0 : f0.shape[1]] = f0[...]
        out[:, f0.shape[1] : CP] = jnp.zeros((32, CP - f0.shape[1]), BF)
        out[:, CP : CP + 128] = s0[...]
        out[:, CP + 128 : PAR] = jnp.zeros((32, PAR - CP - 128), BF)

    def rest(out):
        n1, n2 = f1.shape[1], f2.shape[0]
        for i in range(2):
            out[:, MID * i : MID * i + n1] = f1[32 * i : 32 * (i + 1), :]
            out[:, MID * i + n1 : MID * (i + 1)] = jnp.zeros((32, MID - n1), BF)
        v = jnp.concatenate([f2[...].astype(F32), jnp.zeros((128 - n2, 128), F32)], axis=0).T.astype(BF)
        for i in range(4):
            out[:, 1024 + 128 * i : 1152 + 128 * i] = v[32 * i : 32 * (i + 1)]
        out[:, STEM : STEM + 256] = s1[...]
        out[:, STEM + 256 : PAR] = s2[...]

    @pl.when(group == 0)
    def _():
        fine(own)
        rest(send)

    @pl.when(group == 1)
    def _():
        rest(own)
        fine(send)

    small[...] = jnp.zeros((64, 32), F32)
    for base, v in ((0, gains), (16, shifts), (32, box)):
        for k in range(5):
            small[base + 3 * k : base + 3 * k + 3] = v[k].astype(F32)
    for i in range(2):
        v = small[32 * i : 32 * (i + 1)]
        high = v.astype(BF).astype(F32)
        mid = (v - high).astype(BF).astype(F32)
        block = jnp.concatenate([high, mid, v - high - mid, jnp.zeros((32, 32), F32)], axis=1).astype(BF)
        for out in (own, send):
            out[:, PAR + 128 * i : PAR + 128 * (i + 1)] = block


def pred_kernel(sizes, meta, ccot, cw, cb, bcot, bb, conv, own, box, first, first_cross, second, second_cross, room, spare, sems):
    n0, n1, n2 = sizes
    copies = []
    for layer, outs in enumerate(((first, first_cross), (second, second_cross))):
        for i, out in enumerate(outs):
            for slot in range(2):
                taken = conv.at[1 - meta[0] + slot, 2 * (meta[1] ^ i) + layer]
                to = spare.at[i] if layer == 1 and slot == 1 else out.at[pl.ds(9 * slot, 9)]
                copy = pltpu.make_async_copy(taken, to, sems.at[layer, i, slot])
                copy.start()
                copies.append(copy)
    lane = lax.broadcasted_iota(jnp.int32, (32, 128), 1)

    def biases(b, level):
        block = jnp.concatenate([b[...], jnp.zeros((3, 128 - b.shape[1]), F32)], axis=1)
        block = jnp.concatenate([block, jnp.zeros((5, 128), F32)], axis=0)
        col = block.T[0:32, level : level + 1]
        high = col.astype(BF).astype(F32)
        mid = (col - high).astype(BF).astype(F32)
        low = col - high - mid
        v = jnp.where(lane == 0, high, jnp.where(lane == 1, mid, jnp.where(lane == 2, low, 0.0)))
        return v.astype(BF)

    def fill(outs, cot, b, fine, weights, sent=False):
        n = cot.shape[0]
        room[...] = jnp.zeros((32, CP), BF)
        if fine:
            room[0:n, 0:n0] = cot[:, 0:n0]
        else:
            room[0:n, 0:n1] = cot[:, n0 : n0 + n1]
            room[0:n, MID : MID + n2] = cot[:, n0 + n1 : n0 + n1 + n2]
        base = CP // 128
        if sent:
            base = TAPS + LOW
        for out in outs:
            for i in range(CP // 128 if fine else LOW):
                at = i
                if sent:
                    at = TAPS + i if i < LOW else 9 + i - LOW
                out[at] = room[:, 128 * i : 128 * (i + 1)]
            if not fine and not sent:
                out[LOW : CP // 128] = jnp.zeros((CP // 128 - LOW, 32, 128), BF)
            if fine and sent:
                out[9 + CP // 128 - LOW] = jnp.zeros((32, 128), BF)
            for slot in range(2):
                level = 0 if fine else 1 + slot
                out[base + 2 * slot] = jnp.zeros((32, 128), BF)
                if weights:
                    out[base + 2 * slot, 0:n] = cw[level]
                out[base + 2 * slot + 1] = biases(b, level)

    for group in range(2):

        @pl.when(meta[0] == group)
        def _():
            fill([own], ccot, cb, group == 0, True)
            fill([box], bcot, bb, group == 0, False)

        @pl.when(meta[0] != group)
        def _():
            fill([second, second_cross], ccot, cb, group == 0, True, True)

    for copy in copies:
        copy.wait()

    @pl.when(meta[0] == 0)
    def _():
        second[9:18] = spare[0]
        second_cross[9:18] = spare[1]


def call(body, outs, scratch, args, last=False, limit=VMEM, in_place=(), aliases={}, flops=10**6):
    final = range(len(outs)) if last is True else last or ()

    def space(i):
        return pl.BlockSpec(memory_space=pl.ANY if i in in_place else pltpu.VMEM)

    def placed(units, *refs):
        body(position(units), *refs)

    return pl.pallas_call(
        placed if args[0].dtype == jnp.int32 else body,
        out_shape=[(jax.ShapeDtypeStruct if i in final else pltpu.VMEM)(*o) for i, o in enumerate(outs)],
        in_specs=[space(i) for i in range(len(args))],
        out_specs=[space(len(args) + i) for i in range(len(outs))],
        scratch_shapes=[s if callable(getattr(s, "get_ref_aval", None)) else pltpu.VMEM(*s) for s in scratch],
        input_output_aliases=aliases,
        compiler_params=pltpu.CompilerParams(vmem_limit_bytes=limit),
        cost_estimate=pl.CostEstimate(flops=flops, bytes_accessed=10**4, transcendentals=0),
    )(*args)


def shards(f0, f1, f2, units, s0, s1, s2, conv, gains, shifts, cw, cb, bw, bb, ccot, bcot):
    dp = lax.axis_size("dp")
    c = lax.axis_index("chan")
    group, branch = c // 2, c % 2
    fine = group == 0
    direct = dp == 8
    meta = jnp.broadcast_to(units, (8, 128))
    n0, n1, n2 = f0.shape[2], f1.shape[2], f2.shape[2]

    def across(v):
        return lax.ppermute(v, "chan", [(i, i ^ 2) for i in range(4)])

    def diagonal(v):
        return lax.ppermute(v, "chan", [(i, i ^ 3) for i in range(4)])

    def beside(v, pairs=((0, 1), (1, 0), (2, 3), (3, 2))):
        return lax.ppermute(v, "chan", list(pairs))

    def exchange(st, *hold):
        st, *hold = lax.optimization_barrier((st, *hold))
        st = lax.all_to_all(st, "dp", 0, 0, tiled=True)
        return lax.optimization_barrier((st, *hold)) if hold else st

    def after(v, *others):
        return lax.optimization_barrier((v, *others))[0]

    def over_z(v):
        if not direct:
            return v
        parts = []
        for k in range(4):
            pairs = [
                (8 * z + 4 * y + i, 8 * (i ^ k) + 4 * y + z) for z in range(4) for y in range(2) for i in range(4)
            ]
            parts.append(lax.ppermute(v, ("dp", "chan"), pairs))
        return parts

    def everywhere(parts):
        if direct:
            return parts + [over_y(p) for p in parts]
        v = lax.all_to_all(parts.reshape(4, 2, *parts.shape[1:]), "chan", 0, 0, tiled=True)
        return [v[k % 4, k // 4] for k in range(8)]

    def joined(*parts):
        return jnp.concatenate(parts, axis=-3)

    def over_y(v):
        return lax.ppermute(v, "dp", [(i, i ^ 1) for i in range(8)])

    def along_z(kept, got):
        shape = (sum(v.shape[1] for v in kept), 16, 128)
        outs = [(shape, F32)] + [(shape, BF)] * 3
        own, *rest = call(functools.partial(add_kernel, len(kept)), outs, [], (meta, *kept, *got))
        return [own] + [lax.ppermute(v, "dp", [(i, i ^ (2 * k + 2)) for i in range(8)]) for k, v in enumerate(rest)]

    def reduce(v):
        return lax.optimization_barrier(lax.psum(v.astype(F32), "dp")).astype(BF)

    own, send = call(
        pack_kernel,
        [((32, WIDE), BF), ((32, WIDE), BF)],
        [((64, 32), F32)],
        (f0[0], f1[0], f2[0].T, s0, s1, s2, gains.transpose(1, 0, 2), shifts.transpose(1, 0, 2), bw.transpose(1, 0, 2)),
        limit=WHOLE,
    )
    far_u = across(send)
    own_pred, box_pred, send1, send1_cross, send2, send2_cross = call(
        functools.partial(pred_kernel, (n0, n1, n2)),
        [((CLS, 32, 128), BF)] * 2 + [((TAPS, 32, 128), BF)] * 2 + [((SECOND, 32, 128), BF)] * 2,
        [((32, CP), BF), ((2, 9, 32, 128), BF), pltpu.SemaphoreType.DMA((2, 2, 2))],
        (meta, ccot[0], cw, cb, bcot[0], after(bb, own), conv),
        limit=WHOLE,
        in_place=(6,),
        flops=2 * 10**9,
    )
    near = beside(after(conv, own))
    far_u = after(far_u, near, send2)
    u = (own, far_u, beside(own), beside(far_u))
    to_class = ((1, 0), (3, 2))
    near_pred = beside(own_pred, to_class)

    def weights_of(layer, far, cross):
        return call(
            functools.partial(weight_kernel, layer),
            [((2, 128, 1152), BF), ((2, 1152, 128), BF)],
            [],
            (meta, conv, near, far, cross),
        )

    canvas = (PX, 128)
    stat = (dp, 8, 128)
    moved = [((PX + 16, 128), F32), ((3, PX + 2 * ST, 128), BF)]
    y0, st, cnt, par = call(
        stem_kernel,
        [(canvas, F32), (stat, F32), ((8, 128), F32), ((64, 128), F32)],
        [((512, CP), BF), ((128, 768), BF), ((CP, 128), F32)],
        (meta, *u),
    )
    far1, cross1 = across(after(send1, far_u)), diagonal(after(send1_cross, far_u))
    st, near_pred = exchange(st, near_pred)
    far1, cross1 = after((far1, cross1), st)
    far2, cross2 = across(after(send2, far1)), diagonal(after(send2_cross, cross1))
    w1, w1_tall = weights_of(0, far1, cross1)
    forward_outs = [(canvas, BF), (canvas, F32), (stat, F32), ((16, 128), F32)]
    act0, y1, st, cst0 = call(functools.partial(forward_kernel, True), forward_outs, moved, (meta, y0, st, cnt, w1, par))
    st = exchange(st)
    far2, cross2 = after((far2, cross2), st)
    w2, w2_tall = weights_of(1, far2, cross2)
    act1, y2, st, cst1 = call(
        functools.partial(forward_kernel, False), forward_outs, moved, (meta, y1, st, cnt, w2, par)
    )
    st = exchange(st)
    dz2, st, cst2, x2, cot, wp = call(
        heads_kernel,
        [(canvas, F32), (stat, F32), ((16, 128), F32), ((CP, 256), BF), ((128, CP), BF), ((2, 128, 256), BF)],
        [(canvas, F32), ((CP, 128), F32)],
        (meta, y2, st, par, own_pred, far2, near_pred, cross2, box_pred),
    )
    gw, mine, near, far, cross = call(
        logits_kernel, [((8, 3, 16, 128), BF)] + [((32, CP), BF)] * 4, [((128, CP), BF)], (meta, x2, cot, wp)
    )
    near, far, cross = beside(near), across(far), diagonal(cross)
    st = exchange(after(st, gw))
    st, near, far, cross = lax.optimization_barrier((st, near, far, cross))
    back_scratch = moved + [((128, PX), BF)]
    dz1, st, sums2, wg2, send2 = call(
        second_back_kernel,
        [(canvas, F32), (stat, F32), ((8, 128), F32), ((8, 21, 16, 128), BF), ((4, 21, 16, 128), BF)],
        back_scratch,
        (meta, dz2, y2, cst2, st, w2_tall, act1, y1, cst1, gw),
    )
    got2 = over_y(send2) if direct else reduce(wg2)
    st, got2 = lax.optimization_barrier((exchange(after(st, send2)), got2))
    d0, st, sums1, wg1, send1 = call(
        first_back_kernel,
        [((PX + 32, 128), BF), (stat, F32), ((8, 128), F32), ((8, 18, 16, 128), BF), ((4, 18, 16, 128), BF)],
        back_scratch,
        (meta, dz1, y1, cst1, st, w1_tall, act0, y0, cst0),
    )
    got1 = over_y(send1) if direct else reduce(wg1)
    d0_other = beside(d0)
    if direct:
        pair = (2, 21, 16, 128)
        own2, send2 = call(halve_kernel, [(pair, F32), (pair, BF)], [], (meta, wg2, after(got2, d0)))
        got2 = lax.ppermute(send2, "dp", [(i, i ^ 2) for i in range(8)])
        (st,) = call(both_kernel, [(stat, F32)], [], (after(st, own2), d0_other))
        st = exchange(st)
        (st,) = call(total_kernel, [((1, 8, 128), F32)], [], (st,))
        st, got1, got2 = lax.optimization_barrier((st, got1, got2))
        own2, send2 = call(again_kernel, [(pair[1:], F32), (pair[1:], BF)], [], (meta, own2, got2))
        got2 = lax.ppermute(send2, "dp", [(i, i ^ 4) for i in range(8)])
    else:
        (st,) = call(both_kernel, [(stat, F32)], [], (st, d0_other))
        st = exchange(st)
    own, other, gs, gs_send, norm = call(
        final_kernel,
        [((32, CP), BF), ((32, CP), BF), ((8, 3, 16, 128), BF), ((4, 3, 16, 128), BF), ((1, 16, 128), BF)],
        [
            ((8, 128), F32),
            ((512, CP), BF),
            ((128, 768), BF),
            (canvas, F32),
            ((CP, 128), F32),
            ((128, CP), BF),
            ((512, CP), BF),
            ((6, 128, 128), BF),
        ],
        (meta, d0, d0_other, y0, cst0, st, sums1, sums2, *u),
    )
    if not direct:
        received = across(other)
    if direct:
        parts1 = along_z([wg1, gs], [got1, over_y(gs_send)])
        received = across(after(other, parts1[0]))
        total, extra = call(
            sum_kernel, [((12, 16, 128), BF), ((9, 16, 128), BF)], [], (meta, own2, after(got2, parts1[0]))
        )
        extra = lax.ppermute(extra, "chan", [(2, 0), (3, 1)])
        extra, received = lax.optimization_barrier((extra, received))
        (grads,) = call(join_kernel, [((34, 16, 128), BF)], [], (meta, *parts1, total, extra, norm))
    else:
        extra = lax.ppermute(got2[:, 9:18], "chan", [(2, 0), (3, 1)])
        third = jnp.where(fine, extra, got1[:, 9:18])
        norm = jnp.broadcast_to(norm[None], (8, *norm.shape))
        grads = joined(got1[:, :9], got2[:, :9], third, got2[:, 18:21], reduce(gs), norm)
    grads = everywhere(over_z(grads))

    room = [((2, 3, 2, conv.shape[2], 16, 128), F32), pltpu.SemaphoreType.DMA((2, 3, 2))]
    rows = [(cw.shape, F32), (cb.shape, F32), ((5, 3, 32), F32), (s0.shape, F32), (s1.shape, F32), (s2.shape, F32)]
    wholes = [(bb.shape, F32), ((5, 3, 32), F32), ((5, 3, 32), F32)]
    grad_conv, *half, grad_bb, grad_gains, grad_shifts = call(
        near_out_kernel, [(conv.shape, F32)] + rows + wholes, room, (meta, *grads[:4]), (0, 7, 8, 9), in_place=(5,)
    )
    mine, own = after((mine, own), *half)
    box_rows, class_rows = bcot.shape[1], ccot.shape[1]
    class_out, box_out = call(
        functools.partial(class_out_kernel, (n0, n1, n2)),
        [((class_rows, n0 + n1 + n2), BF), ((box_rows, n0 + n1 + n2), BF)],
        [],
        (meta, mine, near, far, cross),
        True,
    )
    grad_fine, grad_mid, grad_coarse = call(
        feature_out_kernel,
        [(f0.shape[1:], BF), (f1.shape[1:], BF), ((n2, f2.shape[1]), BF)],
        [],
        (meta, own, received),
        True,
    )

    grad_conv, grad_cw, grad_cb, grad_bw, grad_s0, grad_s1, grad_s2 = call(
        far_out_kernel,
        [(conv.shape, F32)] + rows,
        room,
        (meta, *grads[4:], grad_conv, *half),
        True,
        in_place=(5, 12),
        aliases={5: 0},
    )
    return (
        class_out[None],
        box_out[None],
        grad_fine[None],
        grad_mid[None],
        grad_coarse.T[None],
        grad_s0,
        grad_s1,
        grad_s2,
        grad_conv,
        grad_gains.transpose(1, 0, 2),
        grad_shifts.transpose(1, 0, 2),
        grad_cw,
        grad_cb,
        grad_bw.transpose(1, 0, 2),
        grad_bb,
    )


def solution(mesh):
    placed = (
        P("dp", "chan", None),
        P("dp", "chan", None),
        P("dp", "chan", None),
        P("dp"),
        P("chan", None),
        P("chan", None),
        P("chan", None),
        P(None, None, None, "chan", None),
        P(None, None, "chan"),
        P(None, None, "chan"),
        P(None, "chan", None),
        P(None, "chan"),
        P(None, None, "chan"),
        P(),
        P("dp", "chan", None),
        P("dp", None, None),
    )
    return jax.shard_map(
        shards,
        mesh=mesh,
        in_specs=placed,
        out_specs=(
            P("dp", "chan", None),
            P("dp", None, None),
            P("dp", "chan", None),
            P("dp", "chan", None),
            P("dp", "chan", None),
            P("chan", None),
            P("chan", None),
            P("chan", None),
            P(None, None, None, "chan", None),
            P(None, None, "chan"),
            P(None, None, "chan"),
            P(None, "chan", None),
            P(None, "chan"),
            P(None, None, "chan"),
            P(),
        ),
        check_vma=False,
    )
```

```python
import functools

import jax
import jax.numpy as jnp
from jax import lax
from jax.experimental import pallas as pl
from jax.experimental.pallas import tpu as pltpu
from jax.sharding import PartitionSpec as P

BF = jnp.bfloat16
F32 = jnp.float32
EPS = 0.001
ST = 48
ROWS = 40
PX = ST * ROWS
CR = 8
CH = CR * ST
NCH = ROWS // CR
SLOT = (0, 0, 0, 1, 1)
CUT = 24 * ST
CP = 1664
MID = 512
E0, E1, E2 = 40, 20, 10
STEM = 1536
PAR = STEM + 768
WIDE = PAR + 256
CLS = CP // 128 + 4
TAPS = 18
LOW = (MID + 128) // 128
SECOND = TAPS + LOW + 4
SENT = 2 * (CP // 128) + 9
VMEM = 12 * 2**20
WHOLE = 56 * 2**20
NT = (((1,), (1,)), ((), ()))
TN = (((0,), (0,)), ((), ()))


def dot(a, b, dims=(((1,), (0,)), ((), ()))):
    return lax.dot_general(a, b, dims, preferred_element_type=F32)


def position(units):
    c = lax.axis_index("chan")
    place = lax.axis_index("dp") if lax.axis_size("dp") == 8 else jnp.int32(0)
    return c >> 1, c & 1, c, units[0:1, :], place >> 1, place & 1


def limits(meta, slot):
    group, units = meta[0], meta[3]
    if slot == 0:
        edge = jnp.where(group == 0, 4 * units, 2 * units)
        return edge, edge
    return (
        jnp.where(group == 0, 4 * units, 24 + units),
        jnp.where(group == 0, 4 * units, units),
    )


def mask_of(meta, j):
    row_end, col_end = (v.reshape(1, 1, 128) for v in limits(meta, SLOT[j]))
    row = lax.broadcasted_iota(jnp.int32, (CR, ST, 128), 0) + CR * j
    col = lax.broadcasted_iota(jnp.int32, (CR, ST, 128), 1)
    inside = (row < row_end) & (col < col_end)
    return jnp.where(inside, 1.0, 0.0).reshape(CH, 128)


def pick(meta, first, second):
    total = first + second
    return jnp.where(meta[0] == 0, total, first), jnp.where(meta[0] == 0, total, second)


def level_rows(meta, base, layer):
    fine = meta[0] == 0
    at = base + 3 * layer
    return at + jnp.where(fine, 0, 1), at + jnp.where(fine, 0, 2)


def norm_constants(meta, st, par, layer, cst):
    total = jnp.sum(st[...], axis=0)
    row = [total[i : i + 1] for i in range(6)]
    first = pick(meta, row[0], row[1])
    second = pick(meta, row[2], row[3])
    count = pick(meta, row[4], row[5])
    gain_at = level_rows(meta, 0, layer)
    shift_at = level_rows(meta, 16, layer)
    for s in range(2):
        rn = 1.0 / count[s]
        mean = first[s] * rn
        inv = lax.rsqrt(second[s] * rn - mean * mean + EPS)
        cst[s : s + 1] = mean
        cst[2 + s : 3 + s] = inv
        cst[4 + s : 5 + s] = par[pl.ds(gain_at[s], 1), :]
        cst[6 + s : 7 + s] = par[pl.ds(shift_at[s], 1), :]
        cst[8 + s : 9 + s] = rn
        cst[10 + s : 11 + s] = count[s]
    cst[12:16] = jnp.zeros((4, 128), F32)


def normed(cst, y, s):
    xhat = (y - cst[s : s + 1]) * cst[2 + s : 3 + s]
    return xhat, xhat * cst[4 + s : 5 + s] + cst[6 + s : 7 + s]


def sigmoid(z):
    return 0.5 * jnp.tanh(0.5 * z) + 0.5


def slope(z):
    s = sigmoid(z)
    return s * (1.0 + z * (1.0 - s))


def spread_out(st, rows):
    block = jnp.concatenate(rows + [jnp.zeros((8 - len(rows), 128), F32)], axis=0)
    st[...] = jnp.broadcast_to(block[None], st.shape)


def colsum(v):
    return jnp.sum(v, axis=0, keepdims=True)


def guard(field, shifts):
    field[0:8] = jnp.zeros((8, 128), F32)
    field[8 + PX : 16 + PX] = jnp.zeros((8, 128), F32)
    for k in range(3):
        shifts[k, 0:ST] = jnp.zeros((ST, 128), BF)
        shifts[k, ST + PX :] = jnp.zeros((ST, 128), BF)


def fill_shifts(field, shifts):
    for k in range(3):
        for j in range(NCH):
            at = 8 + CH * j + k - 1
            shifts[k, ST + CH * j : ST + CH * (j + 1)] = field[at : at + CH].astype(BF)


def taps(shifts, begin, size, back=False):
    parts = []
    for kr in range(3):
        for kc in range(3):
            k, r = (2 - kc, 1 - kr) if back else (kc, kr - 1)
            at = ST + begin + ST * r
            parts.append(shifts[k, at : at + size])
    return jnp.concatenate(parts, axis=1)


def slices_of(meta):
    c = meta[2]
    return (c, c ^ 2, c ^ 1, c ^ 3)


def at32(s, extra=0):
    return pl.ds(pl.multiple_of(32 * s + extra, 32), 32)


def weight_slot(meta, j):
    return jnp.where(meta[0] == 0, 0, SLOT[j])


def to_compact(meta, canvas, out):
    @pl.when(meta[0] == 0)
    def _():
        for r in range(E0):
            out[E0 * r : E0 * (r + 1)] = canvas[ST * r : ST * r + E0]

    @pl.when(meta[0] == 1)
    def _():
        for r in range(E1):
            out[E1 * r : E1 * (r + 1)] = canvas[ST * r : ST * r + E1]
        for r in range(E2):
            at = CUT + ST * r
            out[MID + E2 * r : MID + E2 * (r + 1)] = canvas[at : at + E2]


def to_canvas(meta, compact, out):
    @pl.when(meta[0] == 0)
    def _():
        for r in range(E0):
            out[ST * r : ST * r + E0] = compact[E0 * r : E0 * (r + 1)]

    @pl.when(meta[0] == 1)
    def _():
        for r in range(E1):
            out[ST * r : ST * r + E1] = compact[E1 * r : E1 * (r + 1)]
        for r in range(E2):
            at = CUT + ST * r
            out[at : at + E2] = compact[MID + E2 * r : MID + E2 * (r + 1)]


def load_inputs(meta, pieces, feat, stem):
    for s, u in zip(slices_of(meta), pieces):

        @pl.when(meta[0] == 0)
        def _():
            feat[at32(s), :] = u[:, 0:CP]
            stem[at32(s), 0:128] = u[:, CP : CP + 128]

        @pl.when(meta[0] == 1)
        def _():
            for i in range(2):
                at = pl.ds(pl.multiple_of(64 * s + 32 * i, 32), 32)
                feat[at, 0:MID] = u[:, MID * i : MID * (i + 1)]
            for i in range(4):
                at = pl.ds(pl.multiple_of(128 * s + 32 * i, 32), 32)
                feat[at, MID : MID + 128] = u[:, 1024 + 128 * i : 1152 + 128 * i]
            stem[at32(s), :] = u[:, STEM:PAR]


def stem_kernel(meta, u0, u1, u2, u3, y, st, cnt, par, feat, stem, flat):
    load_inputs(meta, (u0, u1, u2, u3), feat, stem)
    lane = lax.broadcasted_iota(jnp.int32, (32, 128), 1) // 32
    for i in range(2):
        total = jnp.zeros((32, 128), F32)
        for s, u in zip(slices_of(meta), (u0, u1, u2, u3)):
            v = u[:, PAR + 128 * i : PAR + 128 * (i + 1)].astype(F32)
            v = v[:, 0:32] + v[:, 32:64] + v[:, 64:96]
            total = jnp.where(lane == s, jnp.concatenate([v] * 4, axis=1), total)
        par[32 * i : 32 * (i + 1)] = total
    y[...] = jnp.zeros((PX, 128), F32)

    @pl.when(meta[0] == 0)
    def _():
        flat[...] = dot(stem[:, 0:128], feat[0:128, :]).T

    @pl.when(meta[0] == 1)
    def _():
        flat[0:MID] = dot(stem[:, 0:256], feat[0:256, 0:MID]).T
        flat[MID : MID + 128] = dot(stem[:, 256:768], feat[0:512, MID : MID + 128]).T

    to_canvas(meta, flat, y)
    sums = [jnp.zeros((1, 128), F32) for _ in range(6)]
    for j in range(NCH):
        m = mask_of(meta, j)
        v = y[CH * j : CH * (j + 1)] * m
        s = SLOT[j]
        sums[s] += colsum(v)
        sums[2 + s] += colsum(v * v)
        sums[4 + s] += colsum(m)
    spread_out(st, sums)
    cnt[...] = jnp.concatenate(sums[4:6] + [jnp.zeros((6, 128), F32)], axis=0)


def forward_kernel(first, meta, y, st, cnt, w, *refs):
    par, act, out, st_out, cst, field, shifts = refs
    layer = 0 if first else 1 + 2 * meta[1]
    norm_constants(meta, st, par, layer, cst)
    guard(field, shifts)
    for j in range(NCH):
        rows = slice(CH * j, CH * (j + 1))
        _, z = normed(cst, y[rows], SLOT[j])
        v = z * sigmoid(z) * mask_of(meta, j)
        act[rows] = v.astype(BF)
        field[8 + CH * j : 8 + CH * (j + 1)] = v
    fill_shifts(field, shifts)
    sums = [jnp.zeros((1, 128), F32) for _ in range(4)]
    for j in range(NCH):
        v = dot(taps(shifts, CH * j, CH), w[weight_slot(meta, j)], NT)
        out[CH * j : CH * (j + 1)] = v
        v = v * mask_of(meta, j)
        s = SLOT[j]
        sums[s] += colsum(v)
        sums[2 + s] += colsum(v * v)
    spread_out(st_out, sums + [cnt[0:1], cnt[1:2]])


def weight_kernel(layer, meta, mine, near, far, cross, flat, tall):
    group, branch, c = meta[0], meta[1], meta[2]
    conv = 2 * branch + layer
    for slot in range(2):
        level = group + slot
        for t in range(9):
            for s, piece in (
                (c, mine[level, conv, t]),
                (c ^ 1, near[level, conv, t]),
                (c ^ 2, far[9 * slot + t]),
                (c ^ 3, cross[9 * slot + t]),
            ):
                flat[slot, at32(s), 128 * t : 128 * (t + 1)] = piece
                tall[slot, at32(s, 128 * t), :] = piece


def heads_kernel(meta, y, st, par, k0, k1, k2, k3, box_pack, dz, st_out, cst, x2, cot, wp, field, flat):
    norm_constants(meta, st, par, 2 + 2 * meta[1], cst)
    cot[...] = jnp.zeros((128, CP), BF)
    wp[...] = jnp.zeros((2, 128, 256), BF)

    pixels = CP // 128

    @pl.when(meta[1] == 0)
    def _():
        for s, k, sent in zip(slices_of(meta), (k0, k1, k2, k3), (False, True, False, True)):
            for i in range(pixels):
                if not sent or i < LOW:
                    cot[at32(s), 128 * i : 128 * (i + 1)] = k[TAPS + i if sent else i]
            for slot in range(2):
                for i in range(2):
                    at = (TAPS + LOW if sent else pixels) + 2 * slot + i
                    wp[slot, at32(s), 128 * i : 128 * (i + 1)] = k[at]

    @pl.when((meta[1] == 0) & (meta[0] == 0))
    def _():
        for s, k in zip(slices_of(meta)[1::2], (k1, k3)):
            for i in range(LOW, pixels):
                cot[at32(s), 128 * i : 128 * (i + 1)] = k[9 + i - LOW]

    @pl.when(meta[1] == 1)
    def _():
        for i in range(pixels):
            cot[0:32, 128 * i : 128 * (i + 1)] = box_pack[i]
        fine = meta[0] == 0
        for slot in range(2):
            row = lax.broadcasted_iota(jnp.int32, (32, 128), 0)
            box = jnp.zeros((32, 128), F32)
            for i in range(5):
                at = 32 + 3 * i
                line = jnp.where(fine, par[at : at + 1], par[at + 1 + slot : at + 2 + slot])
                box = jnp.where(row == i, line, box)
            wp[slot, 0:32, 0:128] = box.astype(BF)
            wp[slot, 0:32, 128:256] = box_pack[pixels + 2 * slot + 1]

    for part in range(2):
        for j in range(NCH):
            m = mask_of(meta, j)
            if part == 0:
                _, z = normed(cst, y[CH * j : CH * (j + 1)], SLOT[j])
                m = z * sigmoid(z) * m
            field[CH * j : CH * (j + 1)] = m
        flat[...] = jnp.zeros((CP, 128), F32)
        to_compact(meta, field, flat)
        x2[:, 128 * part : 128 * (part + 1)] = flat[...].astype(BF)

    @pl.when(meta[0] == 0)
    def _():
        flat[...] = dot(cot[...], wp[0, :, 0:128], TN)

    @pl.when(meta[0] == 1)
    def _():
        for slot, a, b in ((0, 0, MID), (1, MID, MID + 128)):
            flat[a:b] = dot(cot[:, a:b], wp[slot, :, 0:128], TN)

    field[...] = jnp.zeros((PX, 128), F32)
    to_canvas(meta, flat, field)
    sums = [jnp.zeros((1, 128), F32) for _ in range(4)]
    for j in range(NCH):
        rows = slice(CH * j, CH * (j + 1))
        s = SLOT[j]
        xhat, z = normed(cst, y[rows], s)
        v = field[rows] * slope(z) * mask_of(meta, j)
        dz[rows] = v
        sums[s] += colsum(v)
        sums[2 + s] += colsum(v * xhat)
    spread_out(st_out, sums)


def logits_kernel(meta, x2, cot, wp, gw, mine, near, far, cross, logits):
    def store(slot, v):
        bias = v[:, 128:256]

        @pl.when(meta[1] == 0)
        def _():
            gw_block(gw, slot, v[:, 0:128])

        @pl.when(meta[1] == 1)
        def _():
            gw_block(gw, slot, v[:, 0:128].T)

        return bias

    def finish(first, second):
        lane = lax.broadcasted_iota(jnp.int32, (128, 128), 1)
        cls = jnp.where(lane == 0, first, jnp.where(lane == 1, second, 0.0))
        a, b = first.T, second.T
        box = jnp.where((lane >= 7) & (lane < 12), pltpu.roll(b, 7, 1), 0.0)
        box = jnp.where((lane >= 2) & (lane < 7), pltpu.roll(a, 2, 1), box)
        gw_block(gw, 2, jnp.where(meta[1] == 0, cls, box))

    @pl.when(meta[0] == 0)
    def _():
        logits[...] = dot(wp[0], x2[...], NT).astype(BF)
        first = store(0, dot(cot[...], x2[...]))
        gw_block(gw, 1, jnp.zeros((128, 128), F32))
        finish(first, jnp.zeros((128, 128), F32))

    @pl.when(meta[0] == 1)
    def _():
        logits[...] = jnp.zeros((128, CP), BF)
        bias = []
        for slot, a, b in ((0, 0, MID), (1, MID, MID + 128)):
            logits[:, a:b] = dot(wp[slot], x2[a:b], NT).astype(BF)
            bias.append(store(slot, dot(cot[:, a:b], x2[a:b])))
        finish(*bias)

    for out, c in ((mine, 0), (near, 1), (far, 2), (cross, 3)):
        out[...] = logits[at32(jnp.where(meta[1] == 0, meta[2] ^ c, 0)), :]


def gw_block(gw, i, v):
    for j in range(8):
        gw[j, i] = v[16 * j : 16 * (j + 1)].astype(BF)


def grad_sums(meta, total, sums):
    shift = pick(meta, total[0:1], total[1:2])
    gain = pick(meta, total[2:3], total[3:4])
    sums[...] = jnp.concatenate(list(shift) + list(gain) + [jnp.zeros((4, 128), F32)], axis=0)


def input_grad(meta, dz, y, cst, sums, j):
    s = SLOT[j]
    xhat, _ = normed(cst, y[CH * j : CH * (j + 1)], s)
    factor = cst[4 + s : 5 + s] * cst[2 + s : 3 + s]
    mean = (sums[s : s + 1] + xhat * sums[2 + s : 3 + s]) * cst[8 + s : 9 + s]
    return mask_of(meta, j) * factor * (dz - mean)


def out_grad(meta, dz, y, cst, st, sums, field, dyt):
    grad_sums(meta, jnp.sum(st[...], axis=0), sums)
    for j in range(NCH):
        rows = slice(CH * j, CH * (j + 1))
        v = input_grad(meta, dz[rows], y, cst, sums, j)
        field[8 + CH * j : 8 + CH * (j + 1)] = v
        dyt[:, rows] = v.T.astype(BF)


def conv_back(meta, last, w, y_in, cst_in, shifts, grad, st_out):
    total = [jnp.zeros((1, 128), F32) for _ in range(4)]
    for j in range(NCH):
        rows = slice(CH * j, CH * (j + 1))
        s = SLOT[j]
        v = dot(taps(shifts, CH * j, CH, True), w[weight_slot(meta, j)])
        xhat, z = normed(cst_in, y_in[rows], s)
        d = v * slope(z) * mask_of(meta, j)
        grad[rows] = v.astype(BF) if last else d
        total[s] += colsum(d)
        total[2 + s] += colsum(d * xhat)
    spread_out(st_out, total)


def as_parts(st):
    high = st.astype(BF).astype(F32)
    mid = (st - high).astype(BF).astype(F32)
    return jnp.concatenate([high, mid, st - high - mid, jnp.zeros((8, 128), F32)], axis=0).astype(BF)


def weight_grad(meta, dyt, act, field, shifts, wg):
    for j in range(NCH):
        field[8 + CH * j : 8 + CH * (j + 1)] = act[CH * j : CH * (j + 1)].astype(F32)
    fill_shifts(field, shifts)

    def store(slot, v):
        for t in range(9):
            for j in range(8):
                block = v[16 * j : 16 * (j + 1), 128 * t : 128 * (t + 1)].astype(BF)
                wg[j, 9 * slot + t] = block

    @pl.when(meta[0] == 0)
    def _():
        store(0, dot(dyt[...], taps(shifts, 0, PX)))
        store(1, jnp.zeros((128, 1152), F32))

    @pl.when(meta[0] == 1)
    def _():
        store(0, dot(dyt[:, 0:CUT], taps(shifts, 0, CUT)))
        store(1, dot(dyt[:, CUT:PX], taps(shifts, CUT, PX - CUT)))


def part_out(meta, wg, send):
    for z in range(4):
        send[z] = wg[2 * z + 1 - meta[5]]


def second_back_kernel(meta, dz, y, cst, st, w, act, y_in, cst_in, gw, grad, st_out, sums, wg, send, field, shifts, dyt):
    guard(field, shifts)
    out_grad(meta, dz, y, cst, st, sums, field, dyt)
    fill_shifts(field, shifts)
    conv_back(meta, False, w, y_in, cst_in, shifts, grad, st_out)
    weight_grad(meta, dyt, act, field, shifts, wg)
    for j in range(8):
        for i in range(3):
            wg[j, 18 + i] = gw[j, i]
    part_out(meta, wg, send)


def first_back_kernel(meta, dz, y, cst, st, w, act, y_in, cst_in, grad, st_out, sums, wg, send, field, shifts, dyt):
    guard(field, shifts)
    out_grad(meta, dz, y, cst, st, sums, field, dyt)
    fill_shifts(field, shifts)
    conv_back(meta, True, w, y_in, cst_in, shifts, grad, st_out)
    grad[PX:] = as_parts(st_out[0])
    weight_grad(meta, dyt, act, field, shifts, wg)
    part_out(meta, wg, send)


def final_kernel(meta, d0, d1, y, cst, st, sums1, sums2, u0, u1, u2, u3, own, other, gs, gs_send, norm, *scratch):
    sums, feat, stem, field, flat, dyt, gf, blocks = scratch
    load_inputs(meta, (u0, u1, u2, u3), feat, stem)
    grad_sums(meta, jnp.sum(st[...], axis=0), sums)
    for j in range(NCH):
        rows = slice(CH * j, CH * (j + 1))
        _, z = normed(cst, y[rows], SLOT[j])
        v = (d0[rows].astype(F32) + d1[rows].astype(F32)) * slope(z) * mask_of(meta, j)
        field[rows] = input_grad(meta, v, y, cst, sums, j)
    flat[...] = jnp.zeros((CP, 128), F32)
    to_compact(meta, field, flat)
    dyt[...] = flat[...].T.astype(BF)
    c = meta[2]
    outs = ((own, c), (other, c ^ 2))

    @pl.when(meta[0] == 0)
    def _():
        gf[0:128, :] = dot(stem[:, 0:128], dyt[...], TN).astype(BF)
        blocks[0] = dot(dyt[...], feat[0:128, :], NT).astype(BF)
        for i in range(1, 6):
            blocks[i] = jnp.zeros((128, 128), BF)
        for out, s in outs:
            out[...] = gf[at32(s), :]

    @pl.when(meta[0] == 1)
    def _():
        gf[0:256, 0:MID] = dot(stem[:, 0:256], dyt[:, 0:MID], TN).astype(BF)
        gf[:, MID : MID + 128] = dot(stem[:, 256:768], dyt[:, MID : MID + 128], TN).astype(BF)
        for i in range(2):
            blocks[i] = dot(dyt[:, 0:MID], feat[128 * i : 128 * (i + 1), 0:MID], NT).astype(BF)
        for i in range(4):
            rows = slice(128 * i, 128 * (i + 1))
            blocks[2 + i] = dot(dyt[:, MID : MID + 128], feat[rows, MID : MID + 128], NT).astype(BF)
        for out, s in outs:
            out[...] = jnp.zeros((32, CP), BF)
            for i in range(2):
                at = pl.ds(pl.multiple_of(64 * s + 32 * i, 32), 32)
                out[:, MID * i : MID * (i + 1)] = gf[at, 0:MID]
            for i in range(4):
                at = pl.ds(pl.multiple_of(128 * s + 32 * i, 32), 32)
                out[:, 1024 + 128 * i : 1152 + 128 * i] = gf[at, MID : MID + 128]

    for i in range(3):
        block = blocks[3 * meta[1] + i]
        for j in range(8):
            gs[j, i] = block[16 * j : 16 * (j + 1)]
    part_out(meta, gs, gs_send)
    rest = jnp.zeros((4, 128), F32)
    norm[0] = jnp.concatenate([sums[0:4], sums1[0:4], sums2[0:4], rest], axis=0).astype(BF)


def both_kernel(st, other, out):
    v = other[PX:].astype(F32)
    out[...] = st[...] + (v[0:8] + v[8:16] + v[16:24])[None]


def total_kernel(st, out):
    out[0] = jnp.sum(st[...], axis=0)


def add_kernel(count, meta, *refs):
    kept, got, outs = refs[:count], refs[count : 2 * count], refs[2 * count :]
    for k, out in enumerate(outs):
        z = meta[4] ^ k
        at = 0
        for a, b in zip(kept, got):
            n = a.shape[1]
            out[at : at + n] = (a[2 * z + meta[5]].astype(F32) + b[z].astype(F32)).astype(out.dtype)
            at += n


def halve_kernel(meta, kept, got, own, send):
    for k in range(4):
        z = meta[4] ^ k
        total = kept[2 * z + meta[5]].astype(F32) + got[z].astype(F32)
        if k % 2:
            send[k // 2] = total.astype(BF)
        else:
            own[k // 2] = total


def again_kernel(meta, own, got, mine, send):
    mine[...] = own[0] + got[0].astype(F32)
    send[...] = (own[1] + got[1].astype(F32)).astype(BF)


def summed(refs, begin, end):
    total = refs[0][begin:end].astype(F32)
    for r in refs[1:]:
        total += r[begin:end].astype(F32)
    return total.astype(BF)


def sum_kernel(meta, *refs):
    parts, (total, extra) = refs[:-2], refs[-2:]
    total[0:9] = summed(parts, 0, 9)
    total[9:10] = summed(parts, 18, 19)
    total[10:11] = summed(parts, 20, 21)
    extra[0:9] = summed(parts, 9, 18)
    extra[9:10] = summed(parts, 19, 20)


def join_kernel(meta, *refs):
    parts, (total, extra, norm, out) = refs[:4], refs[4:]
    out[0:9] = summed(parts, 0, 9)
    out[9:18] = total[0:9]
    out[27:28] = total[9:10]
    out[28:31] = summed(parts, 18, 21)

    @pl.when(meta[0] == 0)
    def _():
        out[18:27] = extra[0:9]
        out[29:30] = extra[9:10]

    @pl.when(meta[0] == 1)
    def _():
        out[18:27] = summed(parts, 9, 18)

    bias = total[10].astype(F32)
    turned = jnp.concatenate([bias.T[0:2], jnp.zeros((2, 112), F32)], axis=1)
    row = lax.broadcasted_iota(jnp.int32, (16, 128), 0)
    block = norm[0].astype(F32)
    for i in range(2):
        line = jnp.where(meta[1] == 0, turned[i : i + 1], bias[0:1])
        block = jnp.where(row == 12 + i, line, block)
    out[31] = block.astype(BF)


def source(meta, k):
    c = meta[4] ^ (k % 4)
    return c >> 1, c & 1, meta[5] ^ (k // 4)


def at16(h):
    return pl.ds(pl.multiple_of(16 * h, 16), 16)


def conv_out(meta, half, first, parts, out, room, sems):
    h = meta[5] ^ half
    copies = []
    for j, r in enumerate(parts):
        group, branch, _ = source(meta, first + j)
        for i in range(3):
            layer = i if i < 2 else 1 - group
            level = group if i < 2 else 2
            for t in range(9):
                room[j, i, t] = r[9 * i + t].astype(F32)
            to = out.at[level, 2 * branch + layer, :, at16(h), :]
            copy = pltpu.make_async_copy(room.at[j, i], to, sems.at[j, i])
            copy.start()
            copies.append(copy)
    return copies


def row_outs(meta, half, first, parts, gcw, gcb, gbw, s0, s1, s2):
    h = meta[5] ^ half
    for j, r in enumerate(parts):
        group, branch, _ = source(meta, first + j)
        for group_id in range(2):
            heads = ((27, 0), (29, 2)) if group_id == 0 else ((27, 1),)
            biases = ((12, 0),) if group_id == 0 else ((12, 1), (13, 2))

            @pl.when((group == group_id) & (branch == 0))
            def _():
                rows = r[31].astype(F32)
                for half_id in range(2):
                    size = (16, 4)[half_id]
                    at = 16 * half_id

                    @pl.when(h == half_id)
                    def _():
                        for block, level in heads:
                            gcw[level, at : at + size, :] = r[block].astype(F32)[0:size]
                        for row, level in biases:
                            gcb[level : level + 1, at : at + size] = rows[row : row + 1, 0:size]

            @pl.when((group == group_id) & (branch == 1))
            def _():
                for block, level in heads:
                    turned = r[block].astype(F32).T
                    for half_id in range(2):

                        @pl.when(h == half_id)
                        def _():
                            for i in range(5):
                                at = 16 * half_id
                                gbw[i, level : level + 1, at : at + 16] = turned[i : i + 1, 0:16]

        @pl.when((group == 0) & (branch == 0))
        def _():
            s0[at16(h), :] = r[28].astype(F32)

        @pl.when((group == 1) & (branch == 0))
        def _():
            for i in range(2):
                s1[at16(h), 128 * i : 128 * (i + 1)] = r[28 + i].astype(F32)
            s2[at16(h), 0:128] = r[30].astype(F32)

        @pl.when((group == 1) & (branch == 1))
        def _():
            for i in range(3):
                s2[at16(h), 128 * (i + 1) : 128 * (i + 2)] = r[28 + i].astype(F32)


def near_out_kernel(meta, *refs):
    parts, (out, gcw, gcb, gbw, s0, s1, s2, gbb, gains, shifts, room, sems) = refs[:4], refs[4:]
    copies = conv_out(meta, 0, 0, parts, out, room, sems)
    row_outs(meta, 0, 0, parts, gcw, gcb, gbw, s0, s1, s2)
    c = meta[2]
    for k in range(4):
        group, branch, _ = source(meta, k)
        v = parts[k][31].astype(F32)

        @pl.when((group == 0) & (branch == 1))
        def _():
            gbb[0:1, :] = v[12:13, 2:7]

        @pl.when((group == 1) & (branch == 1))
        def _():
            gbb[1:2, :] = v[12:13, 2:7]
            gbb[2:3, :] = v[12:13, 7:12]

        mine = v[:, 0:32]
        for i in range(1, 4):
            mine = jnp.where(c == i, v[:, 32 * i : 32 * (i + 1)], mine)
        for layer in range(3):
            at = 0 if layer == 0 else layer + 2 * branch
            base = 4 * layer

            @pl.when(group == 0)
            def _():
                shifts[at, 0:1, :] = mine[base : base + 1]
                gains[at, 0:1, :] = mine[base + 2 : base + 3]

            @pl.when(group == 1)
            def _():
                shifts[at, 1:3, :] = mine[base : base + 2]
                gains[at, 1:3, :] = mine[base + 2 : base + 4]

    for copy in copies:
        copy.wait()


def far_out_kernel(meta, *refs):
    parts, earlier, (out, gcw, gcb, gbw, s0, s1, s2, room, sems) = refs[:4], refs[5:11], refs[11:]
    copies = conv_out(meta, 1, 0, parts, out, room, sems)
    outs = (gcw, gcb, gbw, s0, s1, s2)
    for old, new in zip(earlier, outs):
        new[...] = old[...]
    row_outs(meta, 1, 0, parts, *outs)
    for copy in copies:
        copy.wait()


def class_out_kernel(sizes, meta, mine, near, far, cross, class_out, box_out):
    n0, n1, n2 = sizes

    def store(out, fine, rest):
        n = out.shape[0]
        out[:, 0:n0] = fine[0:n, 0:n0]
        out[:, n0 : n0 + n1] = rest[0:n, 0:n1]
        out[:, n0 + n1 : n0 + n1 + n2] = rest[0:n, MID : MID + n2]

    for group in range(2):
        for branch in range(2):

            @pl.when((meta[0] == group) & (meta[1] == branch))
            def _():
                here, there = (mine, near), (far, cross)
                for i, out in enumerate((class_out, box_out)):
                    pair = (here[branch ^ i], there[branch ^ i])
                    store(out, pair[group], pair[1 - group])


def feature_out_kernel(meta, own, received, fine, mid, coarse):
    def store(a, b):
        n1, n2 = mid.shape[1], coarse.shape[0]
        fine[...] = a[:, 0 : fine.shape[1]]
        for i in range(2):
            mid[32 * i : 32 * (i + 1), :] = b[:, MID * i : MID * i + n1]
        v = jnp.concatenate([b[:, 1024 + 128 * i : 1152 + 128 * i] for i in range(4)], axis=0)
        coarse[...] = v.astype(F32).T[0:n2].astype(BF)

    @pl.when(meta[0] == 0)
    def _():
        store(own, received)

    @pl.when(meta[0] == 1)
    def _():
        store(received, own)


def pack_kernel(f0, f1, f2, s0, s1, s2, gains, shifts, box, own, send, small):
    group = lax.axis_index("chan") // 2

    def fine(out):
        out[:, 0 : f0.shape[1]] = f0[...]
        out[:, f0.shape[1] : CP] = jnp.zeros((32, CP - f0.shape[1]), BF)
        out[:, CP : CP + 128] = s0[...]
        out[:, CP + 128 : PAR] = jnp.zeros((32, PAR - CP - 128), BF)

    def rest(out):
        n1, n2 = f1.shape[1], f2.shape[0]
        for i in range(2):
            out[:, MID * i : MID * i + n1] = f1[32 * i : 32 * (i + 1), :]
            out[:, MID * i + n1 : MID * (i + 1)] = jnp.zeros((32, MID - n1), BF)
        v = jnp.concatenate([f2[...].astype(F32), jnp.zeros((128 - n2, 128), F32)], axis=0).T.astype(BF)
        for i in range(4):
            out[:, 1024 + 128 * i : 1152 + 128 * i] = v[32 * i : 32 * (i + 1)]
        out[:, STEM : STEM + 256] = s1[...]
        out[:, STEM + 256 : PAR] = s2[...]

    @pl.when(group == 0)
    def _():
        fine(own)
        rest(send)

    @pl.when(group == 1)
    def _():
        rest(own)
        fine(send)

    small[...] = jnp.zeros((64, 32), F32)
    for base, v in ((0, gains), (16, shifts), (32, box)):
        for k in range(5):
            small[base + 3 * k : base + 3 * k + 3] = v[k].astype(F32)
    for i in range(2):
        v = small[32 * i : 32 * (i + 1)]
        high = v.astype(BF).astype(F32)
        mid = (v - high).astype(BF).astype(F32)
        block = jnp.concatenate([high, mid, v - high - mid, jnp.zeros((32, 32), F32)], axis=1).astype(BF)
        for out in (own, send):
            out[:, PAR + 128 * i : PAR + 128 * (i + 1)] = block


def pred_kernel(sizes, meta, ccot, cw, cb, bcot, bb, conv, own, box, first, first_cross, second, second_cross, room, spare, sems):
    n0, n1, n2 = sizes
    copies = []
    for layer, outs in enumerate(((first, first_cross), (second, second_cross))):
        for i, out in enumerate(outs):
            for slot in range(2):
                taken = conv.at[1 - meta[0] + slot, 2 * (meta[1] ^ i) + layer]
                to = spare.at[i] if layer == 1 and slot == 1 else out.at[pl.ds(9 * slot, 9)]
                copy = pltpu.make_async_copy(taken, to, sems.at[layer, i, slot])
                copy.start()
                copies.append(copy)
    lane = lax.broadcasted_iota(jnp.int32, (32, 128), 1)

    def biases(b, level):
        block = jnp.concatenate([b[...], jnp.zeros((3, 128 - b.shape[1]), F32)], axis=1)
        block = jnp.concatenate([block, jnp.zeros((5, 128), F32)], axis=0)
        col = block.T[0:32, level : level + 1]
        high = col.astype(BF).astype(F32)
        mid = (col - high).astype(BF).astype(F32)
        low = col - high - mid
        v = jnp.where(lane == 0, high, jnp.where(lane == 1, mid, jnp.where(lane == 2, low, 0.0)))
        return v.astype(BF)

    def fill(outs, cot, b, fine, weights, sent=False):
        n = cot.shape[0]
        room[...] = jnp.zeros((32, CP), BF)
        if fine:
            room[0:n, 0:n0] = cot[:, 0:n0]
        else:
            room[0:n, 0:n1] = cot[:, n0 : n0 + n1]
            room[0:n, MID : MID + n2] = cot[:, n0 + n1 : n0 + n1 + n2]
        base = CP // 128
        if sent:
            base = TAPS + LOW
        for out in outs:
            for i in range(CP // 128 if fine else LOW):
                at = i
                if sent:
                    at = TAPS + i if i < LOW else 9 + i - LOW
                out[at] = room[:, 128 * i : 128 * (i + 1)]
            if not fine and not sent:
                out[LOW : CP // 128] = jnp.zeros((CP // 128 - LOW, 32, 128), BF)
            if fine and sent:
                out[9 + CP // 128 - LOW] = jnp.zeros((32, 128), BF)
            for slot in range(2):
                level = 0 if fine else 1 + slot
                out[base + 2 * slot] = jnp.zeros((32, 128), BF)
                if weights:
                    out[base + 2 * slot, 0:n] = cw[level]
                out[base + 2 * slot + 1] = biases(b, level)

    for group in range(2):

        @pl.when(meta[0] == group)
        def _():
            fill([own], ccot, cb, group == 0, True)
            fill([box], bcot, bb, group == 0, False)

        @pl.when(meta[0] != group)
        def _():
            fill([second, second_cross], ccot, cb, group == 0, True, True)

    for copy in copies:
        copy.wait()

    @pl.when(meta[0] == 0)
    def _():
        second[9:18] = spare[0]
        second_cross[9:18] = spare[1]


def call(body, outs, scratch, args, last=False, limit=VMEM, in_place=(), aliases={}, flops=10**6):
    final = range(len(outs)) if last is True else last or ()

    def space(i):
        return pl.BlockSpec(memory_space=pl.ANY if i in in_place else pltpu.VMEM)

    def placed(units, *refs):
        body(position(units), *refs)

    return pl.pallas_call(
        placed if args[0].dtype == jnp.int32 else body,
        out_shape=[(jax.ShapeDtypeStruct if i in final else pltpu.VMEM)(*o) for i, o in enumerate(outs)],
        in_specs=[space(i) for i in range(len(args))],
        out_specs=[space(len(args) + i) for i in range(len(outs))],
        scratch_shapes=[s if callable(getattr(s, "get_ref_aval", None)) else pltpu.VMEM(*s) for s in scratch],
        input_output_aliases=aliases,
        compiler_params=pltpu.CompilerParams(vmem_limit_bytes=limit),
        cost_estimate=pl.CostEstimate(flops=flops, bytes_accessed=10**4, transcendentals=0),
    )(*args)


def shards(f0, f1, f2, units, s0, s1, s2, conv, gains, shifts, cw, cb, bw, bb, ccot, bcot):
    dp = lax.axis_size("dp")
    c = lax.axis_index("chan")
    group, branch = c // 2, c % 2
    fine = group == 0
    direct = dp == 8
    meta = jnp.broadcast_to(units, (8, 128))
    n0, n1, n2 = f0.shape[2], f1.shape[2], f2.shape[2]

    def across(v):
        return lax.ppermute(v, "chan", [(i, i ^ 2) for i in range(4)])

    def diagonal(v):
        return lax.ppermute(v, "chan", [(i, i ^ 3) for i in range(4)])

    def beside(v, pairs=((0, 1), (1, 0), (2, 3), (3, 2))):
        return lax.ppermute(v, "chan", list(pairs))

    def exchange(st, *hold):
        st, *hold = lax.optimization_barrier((st, *hold))
        st = lax.all_to_all(st, "dp", 0, 0, tiled=True)
        return lax.optimization_barrier((st, *hold)) if hold else st

    def after(v, *others):
        return lax.optimization_barrier((v, *others))[0]

    def over_z(v):
        if not direct:
            return v
        parts = []
        for k in range(4):
            pairs = [
                (8 * z + 4 * y + i, 8 * (i ^ k) + 4 * y + z) for z in range(4) for y in range(2) for i in range(4)
            ]
            parts.append(lax.ppermute(v, ("dp", "chan"), pairs))
        return parts

    def everywhere(parts):
        if direct:
            return parts + [over_y(p) for p in parts]
        v = lax.all_to_all(parts.reshape(4, 2, *parts.shape[1:]), "chan", 0, 0, tiled=True)
        return [v[k % 4, k // 4] for k in range(8)]

    def joined(*parts):
        return jnp.concatenate(parts, axis=-3)

    def over_y(v):
        return lax.ppermute(v, "dp", [(i, i ^ 1) for i in range(8)])

    def along_z(kept, got):
        shape = (sum(v.shape[1] for v in kept), 16, 128)
        outs = [(shape, F32)] + [(shape, BF)] * 3
        own, *rest = call(functools.partial(add_kernel, len(kept)), outs, [], (meta, *kept, *got))
        return [own] + [lax.ppermute(v, "dp", [(i, i ^ (2 * k + 2)) for i in range(8)]) for k, v in enumerate(rest)]

    def reduce(v):
        return lax.optimization_barrier(lax.psum(v.astype(F32), "dp")).astype(BF)

    own, send = call(
        pack_kernel,
        [((32, WIDE), BF), ((32, WIDE), BF)],
        [((64, 32), F32)],
        (f0[0], f1[0], f2[0].T, s0, s1, s2, gains.transpose(1, 0, 2), shifts.transpose(1, 0, 2), bw.transpose(1, 0, 2)),
        limit=WHOLE,
    )
    far_u = across(send)
    own_pred, box_pred, send1, send1_cross, send2, send2_cross = call(
        functools.partial(pred_kernel, (n0, n1, n2)),
        [((CLS, 32, 128), BF)] * 2 + [((TAPS, 32, 128), BF)] * 2 + [((SECOND, 32, 128), BF)] * 2,
        [((32, CP), BF), ((2, 9, 32, 128), BF), pltpu.SemaphoreType.DMA((2, 2, 2))],
        (meta, ccot[0], cw, cb, bcot[0], after(bb, own), conv),
        limit=WHOLE,
        in_place=(6,),
        flops=2 * 10**9,
    )
    near = beside(after(conv, own))
    far_u = after(far_u, near, send2)
    u = (own, far_u, beside(own), beside(far_u))
    to_class = ((1, 0), (3, 2))
    near_pred = beside(own_pred, to_class)

    def weights_of(layer, far, cross):
        return call(
            functools.partial(weight_kernel, layer),
            [((2, 128, 1152), BF), ((2, 1152, 128), BF)],
            [],
            (meta, conv, near, far, cross),
        )

    canvas = (PX, 128)
    stat = (dp, 8, 128)
    moved = [((PX + 16, 128), F32), ((3, PX + 2 * ST, 128), BF)]
    y0, st, cnt, par = call(
        stem_kernel,
        [(canvas, F32), (stat, F32), ((8, 128), F32), ((64, 128), F32)],
        [((512, CP), BF), ((128, 768), BF), ((CP, 128), F32)],
        (meta, *u),
    )
    far1, cross1 = across(after(send1, far_u)), diagonal(after(send1_cross, far_u))
    st, near_pred = exchange(st, near_pred)
    far1, cross1 = after((far1, cross1), st)
    far2, cross2 = across(after(send2, far1)), diagonal(after(send2_cross, cross1))
    w1, w1_tall = weights_of(0, far1, cross1)
    forward_outs = [(canvas, BF), (canvas, F32), (stat, F32), ((16, 128), F32)]
    act0, y1, st, cst0 = call(functools.partial(forward_kernel, True), forward_outs, moved, (meta, y0, st, cnt, w1, par))
    st = exchange(st)
    far2, cross2 = after((far2, cross2), st)
    w2, w2_tall = weights_of(1, far2, cross2)
    act1, y2, st, cst1 = call(
        functools.partial(forward_kernel, False), forward_outs, moved, (meta, y1, st, cnt, w2, par)
    )
    st = exchange(st)
    dz2, st, cst2, x2, cot, wp = call(
        heads_kernel,
        [(canvas, F32), (stat, F32), ((16, 128), F32), ((CP, 256), BF), ((128, CP), BF), ((2, 128, 256), BF)],
        [(canvas, F32), ((CP, 128), F32)],
        (meta, y2, st, par, own_pred, far2, near_pred, cross2, box_pred),
    )
    gw, mine, near, far, cross = call(
        logits_kernel, [((8, 3, 16, 128), BF)] + [((32, CP), BF)] * 4, [((128, CP), BF)], (meta, x2, cot, wp)
    )
    near, far, cross = beside(near), across(far), diagonal(cross)
    st = exchange(after(st, gw))
    st, near, far, cross = lax.optimization_barrier((st, near, far, cross))
    back_scratch = moved + [((128, PX), BF)]
    dz1, st, sums2, wg2, send2 = call(
        second_back_kernel,
        [(canvas, F32), (stat, F32), ((8, 128), F32), ((8, 21, 16, 128), BF), ((4, 21, 16, 128), BF)],
        back_scratch,
        (meta, dz2, y2, cst2, st, w2_tall, act1, y1, cst1, gw),
    )
    got2 = over_y(send2) if direct else reduce(wg2)
    st, got2 = lax.optimization_barrier((exchange(after(st, send2)), got2))
    d0, st, sums1, wg1, send1 = call(
        first_back_kernel,
        [((PX + 32, 128), BF), (stat, F32), ((8, 128), F32), ((8, 18, 16, 128), BF), ((4, 18, 16, 128), BF)],
        back_scratch,
        (meta, dz1, y1, cst1, st, w1_tall, act0, y0, cst0),
    )
    got1 = over_y(send1) if direct else reduce(wg1)
    d0_other = beside(d0)
    if direct:
        pair = (2, 21, 16, 128)
        own2, send2 = call(halve_kernel, [(pair, F32), (pair, BF)], [], (meta, wg2, after(got2, d0)))
        got2 = lax.ppermute(send2, "dp", [(i, i ^ 2) for i in range(8)])
        (st,) = call(both_kernel, [(stat, F32)], [], (after(st, own2), d0_other))
        st = exchange(st)
        (st,) = call(total_kernel, [((1, 8, 128), F32)], [], (st,))
        st, got1, got2 = lax.optimization_barrier((st, got1, got2))
        own2, send2 = call(again_kernel, [(pair[1:], F32), (pair[1:], BF)], [], (meta, own2, got2))
        got2 = lax.ppermute(send2, "dp", [(i, i ^ 4) for i in range(8)])
    else:
        (st,) = call(both_kernel, [(stat, F32)], [], (st, d0_other))
        st = exchange(st)
    own, other, gs, gs_send, norm = call(
        final_kernel,
        [((32, CP), BF), ((32, CP), BF), ((8, 3, 16, 128), BF), ((4, 3, 16, 128), BF), ((1, 16, 128), BF)],
        [
            ((8, 128), F32),
            ((512, CP), BF),
            ((128, 768), BF),
            (canvas, F32),
            ((CP, 128), F32),
            ((128, CP), BF),
            ((512, CP), BF),
            ((6, 128, 128), BF),
        ],
        (meta, d0, d0_other, y0, cst0, st, sums1, sums2, *u),
    )
    if not direct:
        received = across(other)
    if direct:
        parts1 = along_z([wg1, gs], [got1, over_y(gs_send)])
        received = across(after(other, parts1[0]))
        total, extra = call(
            sum_kernel, [((11, 16, 128), BF), ((10, 16, 128), BF)], [], (meta, own2, after(got2, parts1[0]))
        )
        extra = lax.ppermute(extra, "chan", [(2, 0), (3, 1)])
        extra, received = lax.optimization_barrier((extra, received))
        (grads,) = call(join_kernel, [((32, 16, 128), BF)], [], (meta, *parts1, total, extra, norm))
    else:
        gs = reduce(gs)
        extra = lax.ppermute(got2[:, 9:20], "chan", [(2, 0), (3, 1)])
        third = jnp.where(fine, extra[:, :9], got1[:, 9:18])
        stems = jnp.where(fine, joined(gs[:, :1], extra[:, 10:], gs[:, 2:]), gs)
        bias = got2[:, 20]
        turned = jnp.pad(bias[:, :, :2].transpose(0, 2, 1), ((0, 0), (0, 0), (0, 112)))
        biases = jnp.where(branch == 0, turned, jnp.broadcast_to(bias[:, :1], turned.shape))
        norm = jnp.broadcast_to(norm, (8, 16, 128)).at[:, 12:14].set(biases)[:, None]
        grads = joined(got1[:, :9], got2[:, :9], third, got2[:, 18:19], stems, norm)
    grads = everywhere(over_z(grads))

    room = [((4, 3, conv.shape[2], 16, 128), F32), pltpu.SemaphoreType.DMA((4, 3))]
    rows = [(cw.shape, F32), (cb.shape, F32), ((5, 3, 32), F32), (s0.shape, F32), (s1.shape, F32), (s2.shape, F32)]
    wholes = [(bb.shape, F32), ((5, 3, 32), F32), ((5, 3, 32), F32)]
    grad_conv, *half, grad_bb, grad_gains, grad_shifts = call(
        near_out_kernel, [(conv.shape, F32)] + rows + wholes, room, (meta, *grads[:4]), (0, 7, 8, 9), in_place=(5,)
    )
    mine, own = after((mine, own), *half)
    box_rows, class_rows = bcot.shape[1], ccot.shape[1]
    class_out, box_out = call(
        functools.partial(class_out_kernel, (n0, n1, n2)),
        [((class_rows, n0 + n1 + n2), BF), ((box_rows, n0 + n1 + n2), BF)],
        [],
        (meta, mine, near, far, cross),
        True,
    )
    grad_fine, grad_mid, grad_coarse = call(
        feature_out_kernel,
        [(f0.shape[1:], BF), (f1.shape[1:], BF), ((n2, f2.shape[1]), BF)],
        [],
        (meta, own, received),
        True,
    )

    grad_conv, grad_cw, grad_cb, grad_bw, grad_s0, grad_s1, grad_s2 = call(
        far_out_kernel,
        [(conv.shape, F32)] + rows,
        room,
        (meta, *grads[4:], grad_conv, *half),
        True,
        in_place=(5, 12),
        aliases={5: 0},
    )
    return (
        class_out[None],
        box_out[None],
        grad_fine[None],
        grad_mid[None],
        grad_coarse.T[None],
        grad_s0,
        grad_s1,
        grad_s2,
        grad_conv,
        grad_gains.transpose(1, 0, 2),
        grad_shifts.transpose(1, 0, 2),
        grad_cw,
        grad_cb,
        grad_bw.transpose(1, 0, 2),
        grad_bb,
    )


def solution(mesh):
    placed = (
        P("dp", "chan", None),
        P("dp", "chan", None),
        P("dp", "chan", None),
        P("dp"),
        P("chan", None),
        P("chan", None),
        P("chan", None),
        P(None, None, None, "chan", None),
        P(None, None, "chan"),
        P(None, None, "chan"),
        P(None, "chan", None),
        P(None, "chan"),
        P(None, None, "chan"),
        P(),
        P("dp", "chan", None),
        P("dp", None, None),
    )
    return jax.shard_map(
        shards,
        mesh=mesh,
        in_specs=placed,
        out_specs=(
            P("dp", "chan", None),
            P("dp", None, None),
            P("dp", "chan", None),
            P("dp", "chan", None),
            P("dp", "chan", None),
            P("chan", None),
            P("chan", None),
            P("chan", None),
            P(None, None, None, "chan", None),
            P(None, None, "chan"),
            P(None, None, "chan"),
            P(None, "chan", None),
            P(None, "chan"),
            P(None, None, "chan"),
            P(),
        ),
        check_vma=False,
    )
```

```python
import functools

import jax
import jax.numpy as jnp
from jax import lax
from jax.experimental import pallas as pl
from jax.experimental.pallas import tpu as pltpu
from jax.sharding import PartitionSpec as P

BF = jnp.bfloat16
F32 = jnp.float32
EPS = 0.001
ST = 48
ROWS = 40
PX = ST * ROWS
CR = 8
CH = CR * ST
NCH = ROWS // CR
SLOT = (0, 0, 0, 1, 1)
CUT = 24 * ST
CP = 1664
MID = 512
E0, E1, E2 = 40, 20, 10
STEM = 1536
PAR = STEM + 768
WIDE = PAR + 256
CLS = CP // 128 + 4
TAPS = 18
LOW = (MID + 128) // 128
SECOND = TAPS + LOW + 4
SENT = 2 * (CP // 128) + 9
VMEM = 12 * 2**20
WHOLE = 56 * 2**20
NT = (((1,), (1,)), ((), ()))
TN = (((0,), (0,)), ((), ()))


def dot(a, b, dims=(((1,), (0,)), ((), ()))):
    return lax.dot_general(a, b, dims, preferred_element_type=F32)


def position(units):
    c = lax.axis_index("chan")
    place = lax.axis_index("dp") if lax.axis_size("dp") == 8 else jnp.int32(0)
    return c >> 1, c & 1, c, units[0:1, :], place >> 1, place & 1


def limits(meta, slot):
    group, units = meta[0], meta[3]
    if slot == 0:
        edge = jnp.where(group == 0, 4 * units, 2 * units)
        return edge, edge
    return (
        jnp.where(group == 0, 4 * units, 24 + units),
        jnp.where(group == 0, 4 * units, units),
    )


def mask_of(meta, j):
    row_end, col_end = (v.reshape(1, 1, 128) for v in limits(meta, SLOT[j]))
    row = lax.broadcasted_iota(jnp.int32, (CR, ST, 128), 0) + CR * j
    col = lax.broadcasted_iota(jnp.int32, (CR, ST, 128), 1)
    inside = (row < row_end) & (col < col_end)
    return jnp.where(inside, 1.0, 0.0).reshape(CH, 128)


def pick(meta, first, second):
    total = first + second
    return jnp.where(meta[0] == 0, total, first), jnp.where(meta[0] == 0, total, second)


def level_rows(meta, base, layer):
    fine = meta[0] == 0
    at = base + 3 * layer
    return at + jnp.where(fine, 0, 1), at + jnp.where(fine, 0, 2)


def norm_constants(meta, st, par, layer, cst):
    total = jnp.sum(st[...], axis=0)
    row = [total[i : i + 1] for i in range(6)]
    first = pick(meta, row[0], row[1])
    second = pick(meta, row[2], row[3])
    count = pick(meta, row[4], row[5])
    gain_at = level_rows(meta, 0, layer)
    shift_at = level_rows(meta, 16, layer)
    for s in range(2):
        rn = 1.0 / count[s]
        mean = first[s] * rn
        inv = lax.rsqrt(second[s] * rn - mean * mean + EPS)
        cst[s : s + 1] = mean
        cst[2 + s : 3 + s] = inv
        cst[4 + s : 5 + s] = par[pl.ds(gain_at[s], 1), :]
        cst[6 + s : 7 + s] = par[pl.ds(shift_at[s], 1), :]
        cst[8 + s : 9 + s] = rn
        cst[10 + s : 11 + s] = count[s]
    cst[12:16] = jnp.zeros((4, 128), F32)


def normed(cst, y, s):
    xhat = (y - cst[s : s + 1]) * cst[2 + s : 3 + s]
    return xhat, xhat * cst[4 + s : 5 + s] + cst[6 + s : 7 + s]


def sigmoid(z):
    return 0.5 * jnp.tanh(0.5 * z) + 0.5


def slope(z):
    s = sigmoid(z)
    return s * (1.0 + z * (1.0 - s))


def spread_out(st, rows):
    block = jnp.concatenate(rows + [jnp.zeros((8 - len(rows), 128), F32)], axis=0)
    st[...] = jnp.broadcast_to(block[None], st.shape)


def colsum(v):
    return jnp.sum(v, axis=0, keepdims=True)


def guard(field, shifts):
    field[0:8] = jnp.zeros((8, 128), F32)
    field[8 + PX : 16 + PX] = jnp.zeros((8, 128), F32)
    for k in range(3):
        shifts[k, 0:ST] = jnp.zeros((ST, 128), BF)
        shifts[k, ST + PX :] = jnp.zeros((ST, 128), BF)


def fill_shifts(field, shifts):
    for k in range(3):
        for j in range(NCH):
            at = 8 + CH * j + k - 1
            shifts[k, ST + CH * j : ST + CH * (j + 1)] = field[at : at + CH].astype(BF)


def taps(shifts, begin, size, back=False):
    parts = []
    for kr in range(3):
        for kc in range(3):
            k, r = (2 - kc, 1 - kr) if back else (kc, kr - 1)
            at = ST + begin + ST * r
            parts.append(shifts[k, at : at + size])
    return jnp.concatenate(parts, axis=1)


def slices_of(meta):
    c = meta[2]
    return (c, c ^ 2, c ^ 1, c ^ 3)


def at32(s, extra=0):
    return pl.ds(pl.multiple_of(32 * s + extra, 32), 32)


def weight_slot(meta, j):
    return jnp.where(meta[0] == 0, 0, SLOT[j])


def to_compact(meta, canvas, out):
    @pl.when(meta[0] == 0)
    def _():
        for r in range(E0):
            out[E0 * r : E0 * (r + 1)] = canvas[ST * r : ST * r + E0]

    @pl.when(meta[0] == 1)
    def _():
        for r in range(E1):
            out[E1 * r : E1 * (r + 1)] = canvas[ST * r : ST * r + E1]
        for r in range(E2):
            at = CUT + ST * r
            out[MID + E2 * r : MID + E2 * (r + 1)] = canvas[at : at + E2]


def to_canvas(meta, compact, out):
    @pl.when(meta[0] == 0)
    def _():
        for r in range(E0):
            out[ST * r : ST * r + E0] = compact[E0 * r : E0 * (r + 1)]

    @pl.when(meta[0] == 1)
    def _():
        for r in range(E1):
            out[ST * r : ST * r + E1] = compact[E1 * r : E1 * (r + 1)]
        for r in range(E2):
            at = CUT + ST * r
            out[at : at + E2] = compact[MID + E2 * r : MID + E2 * (r + 1)]


def load_inputs(meta, pieces, feat, stem):
    for s, u in zip(slices_of(meta), pieces):

        @pl.when(meta[0] == 0)
        def _():
            feat[at32(s), :] = u[:, 0:CP]
            stem[at32(s), 0:128] = u[:, CP : CP + 128]

        @pl.when(meta[0] == 1)
        def _():
            for i in range(2):
                at = pl.ds(pl.multiple_of(64 * s + 32 * i, 32), 32)
                feat[at, 0:MID] = u[:, MID * i : MID * (i + 1)]
            for i in range(4):
                at = pl.ds(pl.multiple_of(128 * s + 32 * i, 32), 32)
                feat[at, MID : MID + 128] = u[:, 1024 + 128 * i : 1152 + 128 * i]
            stem[at32(s), :] = u[:, STEM:PAR]


def stem_kernel(meta, u0, u1, u2, u3, y, st, cnt, par, feat, stem, flat):
    load_inputs(meta, (u0, u1, u2, u3), feat, stem)
    lane = lax.broadcasted_iota(jnp.int32, (32, 128), 1) // 32
    for i in range(2):
        total = jnp.zeros((32, 128), F32)
        for s, u in zip(slices_of(meta), (u0, u1, u2, u3)):
            v = u[:, PAR + 128 * i : PAR + 128 * (i + 1)].astype(F32)
            v = v[:, 0:32] + v[:, 32:64] + v[:, 64:96]
            total = jnp.where(lane == s, jnp.concatenate([v] * 4, axis=1), total)
        par[32 * i : 32 * (i + 1)] = total
    y[...] = jnp.zeros((PX, 128), F32)

    @pl.when(meta[0] == 0)
    def _():
        flat[...] = dot(stem[:, 0:128], feat[0:128, :]).T

    @pl.when(meta[0] == 1)
    def _():
        flat[0:MID] = dot(stem[:, 0:256], feat[0:256, 0:MID]).T
        flat[MID : MID + 128] = dot(stem[:, 256:768], feat[0:512, MID : MID + 128]).T

    to_canvas(meta, flat, y)
    sums = [jnp.zeros((1, 128), F32) for _ in range(6)]
    for j in range(NCH):
        m = mask_of(meta, j)
        v = y[CH * j : CH * (j + 1)] * m
        s = SLOT[j]
        sums[s] += colsum(v)
        sums[2 + s] += colsum(v * v)
        sums[4 + s] += colsum(m)
    spread_out(st, sums)
    cnt[...] = jnp.concatenate(sums[4:6] + [jnp.zeros((6, 128), F32)], axis=0)


def forward_kernel(first, meta, y, st, cnt, w, *refs):
    par, act, out, st_out, cst, field, shifts = refs
    layer = 0 if first else 1 + 2 * meta[1]
    norm_constants(meta, st, par, layer, cst)
    guard(field, shifts)
    for j in range(NCH):
        rows = slice(CH * j, CH * (j + 1))
        _, z = normed(cst, y[rows], SLOT[j])
        v = z * sigmoid(z) * mask_of(meta, j)
        act[rows] = v.astype(BF)
        field[8 + CH * j : 8 + CH * (j + 1)] = v
    fill_shifts(field, shifts)
    sums = [jnp.zeros((1, 128), F32) for _ in range(4)]
    for j in range(NCH):
        v = dot(taps(shifts, CH * j, CH), w[weight_slot(meta, j)], NT)
        out[CH * j : CH * (j + 1)] = v
        v = v * mask_of(meta, j)
        s = SLOT[j]
        sums[s] += colsum(v)
        sums[2 + s] += colsum(v * v)
    spread_out(st_out, sums + [cnt[0:1], cnt[1:2]])


def weight_kernel(layer, meta, mine, near, far, cross, flat, tall):
    group, branch, c = meta[0], meta[1], meta[2]
    conv = 2 * branch + layer
    for slot in range(2):
        level = group + slot
        for t in range(9):
            for s, piece in (
                (c, mine[level, conv, t]),
                (c ^ 1, near[level, conv, t]),
                (c ^ 2, far[9 * slot + t]),
                (c ^ 3, cross[9 * slot + t]),
            ):
                flat[slot, at32(s), 128 * t : 128 * (t + 1)] = piece
                tall[slot, at32(s, 128 * t), :] = piece


def heads_kernel(meta, y, st, par, k0, k1, k2, k3, box_pack, dz, st_out, cst, x2, cot, wp, field, flat):
    norm_constants(meta, st, par, 2 + 2 * meta[1], cst)
    cot[...] = jnp.zeros((128, CP), BF)
    wp[...] = jnp.zeros((2, 128, 256), BF)

    pixels = CP // 128

    @pl.when(meta[1] == 0)
    def _():
        for s, k, sent in zip(slices_of(meta), (k0, k1, k2, k3), (False, True, False, True)):
            for i in range(pixels):
                if not sent or i < LOW:
                    cot[at32(s), 128 * i : 128 * (i + 1)] = k[TAPS + i if sent else i]
            for slot in range(2):
                for i in range(2):
                    at = (TAPS + LOW if sent else pixels) + 2 * slot + i
                    wp[slot, at32(s), 128 * i : 128 * (i + 1)] = k[at]

    @pl.when((meta[1] == 0) & (meta[0] == 0))
    def _():
        for s, k in zip(slices_of(meta)[1::2], (k1, k3)):
            for i in range(LOW, pixels):
                cot[at32(s), 128 * i : 128 * (i + 1)] = k[9 + i - LOW]

    @pl.when(meta[1] == 1)
    def _():
        for i in range(pixels):
            cot[0:32, 128 * i : 128 * (i + 1)] = box_pack[i]
        fine = meta[0] == 0
        for slot in range(2):
            row = lax.broadcasted_iota(jnp.int32, (32, 128), 0)
            box = jnp.zeros((32, 128), F32)
            for i in range(5):
                at = 32 + 3 * i
                line = jnp.where(fine, par[at : at + 1], par[at + 1 + slot : at + 2 + slot])
                box = jnp.where(row == i, line, box)
            wp[slot, 0:32, 0:128] = box.astype(BF)
            wp[slot, 0:32, 128:256] = box_pack[pixels + 2 * slot + 1]

    for part in range(2):
        for j in range(NCH):
            m = mask_of(meta, j)
            if part == 0:
                _, z = normed(cst, y[CH * j : CH * (j + 1)], SLOT[j])
                m = z * sigmoid(z) * m
            field[CH * j : CH * (j + 1)] = m
        flat[...] = jnp.zeros((CP, 128), F32)
        to_compact(meta, field, flat)
        x2[:, 128 * part : 128 * (part + 1)] = flat[...].astype(BF)

    @pl.when(meta[0] == 0)
    def _():
        flat[...] = dot(cot[...], wp[0, :, 0:128], TN)

    @pl.when(meta[0] == 1)
    def _():
        for slot, a, b in ((0, 0, MID), (1, MID, MID + 128)):
            flat[a:b] = dot(cot[:, a:b], wp[slot, :, 0:128], TN)

    field[...] = jnp.zeros((PX, 128), F32)
    to_canvas(meta, flat, field)
    sums = [jnp.zeros((1, 128), F32) for _ in range(4)]
    for j in range(NCH):
        rows = slice(CH * j, CH * (j + 1))
        s = SLOT[j]
        xhat, z = normed(cst, y[rows], s)
        v = field[rows] * slope(z) * mask_of(meta, j)
        dz[rows] = v
        sums[s] += colsum(v)
        sums[2 + s] += colsum(v * xhat)
    spread_out(st_out, sums)


def logits_kernel(meta, x2, cot, wp, gw, mine, near, far, cross, logits):
    def store(slot, v):
        bias = v[:, 128:256]

        @pl.when(meta[1] == 0)
        def _():
            gw_block(gw, slot, v[:, 0:128])

        @pl.when(meta[1] == 1)
        def _():
            gw_block(gw, slot, v[:, 0:128].T)

        return bias

    def finish(first, second):
        lane = lax.broadcasted_iota(jnp.int32, (128, 128), 1)
        cls = jnp.where(lane == 0, first, jnp.where(lane == 1, second, 0.0))
        a, b = first.T, second.T
        box = jnp.where((lane >= 7) & (lane < 12), pltpu.roll(b, 7, 1), 0.0)
        box = jnp.where((lane >= 2) & (lane < 7), pltpu.roll(a, 2, 1), box)
        gw_block(gw, 2, jnp.where(meta[1] == 0, cls, box))

    @pl.when(meta[0] == 0)
    def _():
        logits[...] = dot(wp[0], x2[...], NT).astype(BF)
        first = store(0, dot(cot[...], x2[...]))
        gw_block(gw, 1, jnp.zeros((128, 128), F32))
        finish(first, jnp.zeros((128, 128), F32))

    @pl.when(meta[0] == 1)
    def _():
        logits[...] = jnp.zeros((128, CP), BF)
        bias = []
        for slot, a, b in ((0, 0, MID), (1, MID, MID + 128)):
            logits[:, a:b] = dot(wp[slot], x2[a:b], NT).astype(BF)
            bias.append(store(slot, dot(cot[:, a:b], x2[a:b])))
        finish(*bias)

    for out, c in ((mine, 0), (near, 1), (far, 2), (cross, 3)):
        out[...] = logits[at32(jnp.where(meta[1] == 0, meta[2] ^ c, 0)), :]


def gw_block(gw, i, v):
    for j in range(8):
        gw[j, i] = v[16 * j : 16 * (j + 1)].astype(BF)


def grad_sums(meta, total, sums):
    shift = pick(meta, total[0:1], total[1:2])
    gain = pick(meta, total[2:3], total[3:4])
    sums[...] = jnp.concatenate(list(shift) + list(gain) + [jnp.zeros((4, 128), F32)], axis=0)


def input_grad(meta, dz, y, cst, sums, j):
    s = SLOT[j]
    xhat, _ = normed(cst, y[CH * j : CH * (j + 1)], s)
    factor = cst[4 + s : 5 + s] * cst[2 + s : 3 + s]
    mean = (sums[s : s + 1] + xhat * sums[2 + s : 3 + s]) * cst[8 + s : 9 + s]
    return mask_of(meta, j) * factor * (dz - mean)


def out_grad(meta, dz, y, cst, st, sums, field, dyt):
    grad_sums(meta, jnp.sum(st[...], axis=0), sums)
    for j in range(NCH):
        rows = slice(CH * j, CH * (j + 1))
        v = input_grad(meta, dz[rows], y, cst, sums, j)
        field[8 + CH * j : 8 + CH * (j + 1)] = v
        dyt[:, rows] = v.T.astype(BF)


def conv_back(meta, last, w, y_in, cst_in, shifts, grad, st_out):
    total = [jnp.zeros((1, 128), F32) for _ in range(4)]
    for j in range(NCH):
        rows = slice(CH * j, CH * (j + 1))
        s = SLOT[j]
        v = dot(taps(shifts, CH * j, CH, True), w[weight_slot(meta, j)])
        xhat, z = normed(cst_in, y_in[rows], s)
        d = v * slope(z) * mask_of(meta, j)
        grad[rows] = v.astype(BF) if last else d
        total[s] += colsum(d)
        total[2 + s] += colsum(d * xhat)
    spread_out(st_out, total)


def as_parts(st):
    high = st.astype(BF).astype(F32)
    mid = (st - high).astype(BF).astype(F32)
    return jnp.concatenate([high, mid, st - high - mid, jnp.zeros((8, 128), F32)], axis=0).astype(BF)


def weight_grad(meta, dyt, act, field, shifts, wg):
    for j in range(NCH):
        field[8 + CH * j : 8 + CH * (j + 1)] = act[CH * j : CH * (j + 1)].astype(F32)
    fill_shifts(field, shifts)

    def store(slot, v):
        for t in range(9):
            for j in range(8):
                block = v[16 * j : 16 * (j + 1), 128 * t : 128 * (t + 1)].astype(BF)
                wg[j, 9 * slot + t] = block

    @pl.when(meta[0] == 0)
    def _():
        store(0, dot(dyt[...], taps(shifts, 0, PX)))
        store(1, jnp.zeros((128, 1152), F32))

    @pl.when(meta[0] == 1)
    def _():
        store(0, dot(dyt[:, 0:CUT], taps(shifts, 0, CUT)))
        store(1, dot(dyt[:, CUT:PX], taps(shifts, CUT, PX - CUT)))


def part_out(meta, wg, send):
    for z in range(4):
        send[z] = wg[2 * z + 1 - meta[5]]


def second_back_kernel(meta, dz, y, cst, st, w, act, y_in, cst_in, gw, grad, st_out, sums, wg, send, field, shifts, dyt):
    guard(field, shifts)
    out_grad(meta, dz, y, cst, st, sums, field, dyt)
    fill_shifts(field, shifts)
    conv_back(meta, False, w, y_in, cst_in, shifts, grad, st_out)
    weight_grad(meta, dyt, act, field, shifts, wg)
    for j in range(8):
        for i in range(3):
            wg[j, 18 + i] = gw[j, i]
    part_out(meta, wg, send)


def first_back_kernel(meta, dz, y, cst, st, w, act, y_in, cst_in, grad, st_out, sums, wg, send, field, shifts, dyt):
    guard(field, shifts)
    out_grad(meta, dz, y, cst, st, sums, field, dyt)
    fill_shifts(field, shifts)
    conv_back(meta, True, w, y_in, cst_in, shifts, grad, st_out)
    grad[PX:] = as_parts(st_out[0])
    weight_grad(meta, dyt, act, field, shifts, wg)
    part_out(meta, wg, send)


def final_kernel(meta, d0, d1, y, cst, st, sums1, sums2, u0, u1, u2, u3, own, other, gs, gs_send, norm, *scratch):
    sums, feat, stem, field, flat, dyt, gf, blocks = scratch
    load_inputs(meta, (u0, u1, u2, u3), feat, stem)
    grad_sums(meta, jnp.sum(st[...], axis=0), sums)
    for j in range(NCH):
        rows = slice(CH * j, CH * (j + 1))
        _, z = normed(cst, y[rows], SLOT[j])
        v = (d0[rows].astype(F32) + d1[rows].astype(F32)) * slope(z) * mask_of(meta, j)
        field[rows] = input_grad(meta, v, y, cst, sums, j)
    flat[...] = jnp.zeros((CP, 128), F32)
    to_compact(meta, field, flat)
    dyt[...] = flat[...].T.astype(BF)
    c = meta[2]
    outs = ((own, c), (other, c ^ 2))

    @pl.when(meta[0] == 0)
    def _():
        gf[0:128, :] = dot(stem[:, 0:128], dyt[...], TN).astype(BF)
        blocks[0] = dot(dyt[...], feat[0:128, :], NT).astype(BF)
        for i in range(1, 6):
            blocks[i] = jnp.zeros((128, 128), BF)
        for out, s in outs:
            out[...] = gf[at32(s), :]

    @pl.when(meta[0] == 1)
    def _():
        gf[0:256, 0:MID] = dot(stem[:, 0:256], dyt[:, 0:MID], TN).astype(BF)
        gf[:, MID : MID + 128] = dot(stem[:, 256:768], dyt[:, MID : MID + 128], TN).astype(BF)
        for i in range(2):
            blocks[i] = dot(dyt[:, 0:MID], feat[128 * i : 128 * (i + 1), 0:MID], NT).astype(BF)
        for i in range(4):
            rows = slice(128 * i, 128 * (i + 1))
            blocks[2 + i] = dot(dyt[:, MID : MID + 128], feat[rows, MID : MID + 128], NT).astype(BF)
        for out, s in outs:
            out[...] = jnp.zeros((32, CP), BF)
            for i in range(2):
                at = pl.ds(pl.multiple_of(64 * s + 32 * i, 32), 32)
                out[:, MID * i : MID * (i + 1)] = gf[at, 0:MID]
            for i in range(4):
                at = pl.ds(pl.multiple_of(128 * s + 32 * i, 32), 32)
                out[:, 1024 + 128 * i : 1152 + 128 * i] = gf[at, MID : MID + 128]

    for i in range(3):
        block = blocks[3 * meta[1] + i]
        for j in range(8):
            gs[j, i] = block[16 * j : 16 * (j + 1)]
    part_out(meta, gs, gs_send)
    rest = jnp.zeros((4, 128), F32)
    norm[0] = jnp.concatenate([sums[0:4], sums1[0:4], sums2[0:4], rest], axis=0).astype(BF)


def both_kernel(st, other, out):
    v = other[PX:].astype(F32)
    out[...] = st[...] + (v[0:8] + v[8:16] + v[16:24])[None]


def total_kernel(st, out):
    out[0] = jnp.sum(st[...], axis=0)


def add_kernel(count, meta, *refs):
    kept, got, outs = refs[:count], refs[count : 2 * count], refs[2 * count :]
    for k, out in enumerate(outs):
        z = meta[4] ^ k
        at = 0
        for a, b in zip(kept, got):
            n = a.shape[1]
            out[at : at + n] = (a[2 * z + meta[5]].astype(F32) + b[z].astype(F32)).astype(out.dtype)
            at += n


def halve_kernel(meta, kept, got, own, send):
    for k in range(4):
        z = meta[4] ^ k
        total = kept[2 * z + meta[5]].astype(F32) + got[z].astype(F32)
        if k % 2:
            send[k // 2] = total.astype(BF)
        else:
            own[k // 2] = total


def again_kernel(meta, own, got, mine, send):
    mine[...] = own[0] + got[0].astype(F32)
    send[...] = (own[1] + got[1].astype(F32)).astype(BF)


def summed(refs, begin, end):
    total = refs[0][begin:end].astype(F32)
    for r in refs[1:]:
        total += r[begin:end].astype(F32)
    return total.astype(BF)


def sum_kernel(meta, *refs):
    parts, (total, extra) = refs[:-2], refs[-2:]
    total[0:9] = summed(parts, 0, 9)
    total[9:10] = summed(parts, 18, 19)
    total[10:11] = summed(parts, 20, 21)
    extra[0:9] = summed(parts, 9, 18)
    extra[9:10] = summed(parts, 19, 20)


def join_kernel(meta, *refs):
    parts, (total, extra, norm, out) = refs[:4], refs[4:]
    out[0:9] = summed(parts, 0, 9)
    out[9:18] = total[0:9]
    out[27:28] = total[9:10]
    out[28:31] = summed(parts, 18, 21)

    @pl.when(meta[0] == 0)
    def _():
        out[18:27] = extra[0:9]
        out[29:30] = extra[9:10]

    @pl.when(meta[0] == 1)
    def _():
        out[18:27] = summed(parts, 9, 18)

    bias = total[10].astype(F32)
    turned = jnp.concatenate([bias.T[0:2], jnp.zeros((2, 112), F32)], axis=1)
    row = lax.broadcasted_iota(jnp.int32, (16, 128), 0)
    block = norm[0].astype(F32)
    for i in range(2):
        line = jnp.where(meta[1] == 0, turned[i : i + 1], bias[0:1])
        block = jnp.where(row == 12 + i, line, block)
    out[31] = block.astype(BF)


def source(meta, k):
    c = (meta[4] - (k % 4)) & 3
    return c >> 1, c & 1, meta[5] ^ (k // 4)


def at16(h):
    return pl.ds(pl.multiple_of(16 * h, 16), 16)


def conv_out(meta, half, first, parts, out, room, sems):
    h = meta[5] ^ half
    copies = []
    for j, r in enumerate(parts):
        group, branch, _ = source(meta, first + j)
        for i in range(3):
            layer = i if i < 2 else 1 - group
            level = group if i < 2 else 2
            for t in range(9):
                room[j, i, t] = r[9 * i + t].astype(F32)
            to = out.at[level, 2 * branch + layer, :, at16(h), :]
            copy = pltpu.make_async_copy(room.at[j, i], to, sems.at[j, i])
            copy.start()
            copies.append(copy)
    return copies


def row_outs(meta, half, first, parts, gcw, gcb, gbw, s0, s1, s2):
    h = meta[5] ^ half
    for j, r in enumerate(parts):
        group, branch, _ = source(meta, first + j)
        for group_id in range(2):
            heads = ((27, 0), (29, 2)) if group_id == 0 else ((27, 1),)
            biases = ((12, 0),) if group_id == 0 else ((12, 1), (13, 2))

            @pl.when((group == group_id) & (branch == 0))
            def _():
                rows = r[31].astype(F32)
                for half_id in range(2):
                    size = (16, 4)[half_id]
                    at = 16 * half_id

                    @pl.when(h == half_id)
                    def _():
                        for block, level in heads:
                            gcw[level, at : at + size, :] = r[block].astype(F32)[0:size]
                        for row, level in biases:
                            gcb[level : level + 1, at : at + size] = rows[row : row + 1, 0:size]

            @pl.when((group == group_id) & (branch == 1))
            def _():
                for block, level in heads:
                    turned = r[block].astype(F32).T
                    for half_id in range(2):

                        @pl.when(h == half_id)
                        def _():
                            for i in range(5):
                                at = 16 * half_id
                                gbw[i, level : level + 1, at : at + 16] = turned[i : i + 1, 0:16]

        @pl.when((group == 0) & (branch == 0))
        def _():
            s0[at16(h), :] = r[28].astype(F32)

        @pl.when((group == 1) & (branch == 0))
        def _():
            for i in range(2):
                s1[at16(h), 128 * i : 128 * (i + 1)] = r[28 + i].astype(F32)
            s2[at16(h), 0:128] = r[30].astype(F32)

        @pl.when((group == 1) & (branch == 1))
        def _():
            for i in range(3):
                s2[at16(h), 128 * (i + 1) : 128 * (i + 2)] = r[28 + i].astype(F32)


def near_out_kernel(meta, *refs):
    parts, (out, gcw, gcb, gbw, s0, s1, s2, gbb, gains, shifts, room, sems) = refs[:4], refs[4:]
    copies = conv_out(meta, 0, 0, parts, out, room, sems)
    row_outs(meta, 0, 0, parts, gcw, gcb, gbw, s0, s1, s2)
    c = meta[2]
    for k in range(4):
        group, branch, _ = source(meta, k)
        v = parts[k][31].astype(F32)

        @pl.when((group == 0) & (branch == 1))
        def _():
            gbb[0:1, :] = v[12:13, 2:7]

        @pl.when((group == 1) & (branch == 1))
        def _():
            gbb[1:2, :] = v[12:13, 2:7]
            gbb[2:3, :] = v[12:13, 7:12]

        mine = v[:, 0:32]
        for i in range(1, 4):
            mine = jnp.where(c == i, v[:, 32 * i : 32 * (i + 1)], mine)
        for layer in range(3):
            at = 0 if layer == 0 else layer + 2 * branch
            base = 4 * layer

            @pl.when(group == 0)
            def _():
                shifts[at, 0:1, :] = mine[base : base + 1]
                gains[at, 0:1, :] = mine[base + 2 : base + 3]

            @pl.when(group == 1)
            def _():
                shifts[at, 1:3, :] = mine[base : base + 2]
                gains[at, 1:3, :] = mine[base + 2 : base + 4]

    for copy in copies:
        copy.wait()


def far_out_kernel(meta, *refs):
    parts, earlier, (out, gcw, gcb, gbw, s0, s1, s2, room, sems) = refs[:4], refs[5:11], refs[11:]
    copies = conv_out(meta, 1, 0, parts, out, room, sems)
    outs = (gcw, gcb, gbw, s0, s1, s2)
    for old, new in zip(earlier, outs):
        new[...] = old[...]
    row_outs(meta, 1, 0, parts, *outs)
    for copy in copies:
        copy.wait()


def class_out_kernel(sizes, meta, mine, near, far, cross, class_out, box_out):
    n0, n1, n2 = sizes

    def store(out, fine, rest):
        n = out.shape[0]
        out[:, 0:n0] = fine[0:n, 0:n0]
        out[:, n0 : n0 + n1] = rest[0:n, 0:n1]
        out[:, n0 + n1 : n0 + n1 + n2] = rest[0:n, MID : MID + n2]

    for group in range(2):
        for branch in range(2):

            @pl.when((meta[0] == group) & (meta[1] == branch))
            def _():
                here, there = (mine, near), (far, cross)
                for i, out in enumerate((class_out, box_out)):
                    pair = (here[branch ^ i], there[branch ^ i])
                    store(out, pair[group], pair[1 - group])


def feature_out_kernel(meta, own, received, fine, mid, coarse):
    def store(a, b):
        n1, n2 = mid.shape[1], coarse.shape[0]
        fine[...] = a[:, 0 : fine.shape[1]]
        for i in range(2):
            mid[32 * i : 32 * (i + 1), :] = b[:, MID * i : MID * i + n1]
        v = jnp.concatenate([b[:, 1024 + 128 * i : 1152 + 128 * i] for i in range(4)], axis=0)
        coarse[...] = v.astype(F32).T[0:n2].astype(BF)

    @pl.when(meta[0] == 0)
    def _():
        store(own, received)

    @pl.when(meta[0] == 1)
    def _():
        store(received, own)


def pack_kernel(f0, f1, f2, s0, s1, s2, gains, shifts, box, own, send, small):
    group = lax.axis_index("chan") // 2

    def fine(out):
        out[:, 0 : f0.shape[1]] = f0[...]
        out[:, f0.shape[1] : CP] = jnp.zeros((32, CP - f0.shape[1]), BF)
        out[:, CP : CP + 128] = s0[...]
        out[:, CP + 128 : PAR] = jnp.zeros((32, PAR - CP - 128), BF)

    def rest(out):
        n1, n2 = f1.shape[1], f2.shape[0]
        for i in range(2):
            out[:, MID * i : MID * i + n1] = f1[32 * i : 32 * (i + 1), :]
            out[:, MID * i + n1 : MID * (i + 1)] = jnp.zeros((32, MID - n1), BF)
        v = jnp.concatenate([f2[...].astype(F32), jnp.zeros((128 - n2, 128), F32)], axis=0).T.astype(BF)
        for i in range(4):
            out[:, 1024 + 128 * i : 1152 + 128 * i] = v[32 * i : 32 * (i + 1)]
        out[:, STEM : STEM + 256] = s1[...]
        out[:, STEM + 256 : PAR] = s2[...]

    @pl.when(group == 0)
    def _():
        fine(own)
        rest(send)

    @pl.when(group == 1)
    def _():
        rest(own)
        fine(send)

    small[...] = jnp.zeros((64, 32), F32)
    for base, v in ((0, gains), (16, shifts), (32, box)):
        for k in range(5):
            small[base + 3 * k : base + 3 * k + 3] = v[k].astype(F32)
    for i in range(2):
        v = small[32 * i : 32 * (i + 1)]
        high = v.astype(BF).astype(F32)
        mid = (v - high).astype(BF).astype(F32)
        block = jnp.concatenate([high, mid, v - high - mid, jnp.zeros((32, 32), F32)], axis=1).astype(BF)
        for out in (own, send):
            out[:, PAR + 128 * i : PAR + 128 * (i + 1)] = block


def pred_kernel(sizes, meta, ccot, cw, cb, bcot, bb, conv, own, box, first, first_cross, second, second_cross, room, spare, sems):
    n0, n1, n2 = sizes
    copies = []
    for layer, outs in enumerate(((first, first_cross), (second, second_cross))):
        for i, out in enumerate(outs):
            for slot in range(2):
                taken = conv.at[1 - meta[0] + slot, 2 * (meta[1] ^ i) + layer]
                to = spare.at[i] if layer == 1 and slot == 1 else out.at[pl.ds(9 * slot, 9)]
                copy = pltpu.make_async_copy(taken, to, sems.at[layer, i, slot])
                copy.start()
                copies.append(copy)
    lane = lax.broadcasted_iota(jnp.int32, (32, 128), 1)

    def biases(b, level):
        block = jnp.concatenate([b[...], jnp.zeros((3, 128 - b.shape[1]), F32)], axis=1)
        block = jnp.concatenate([block, jnp.zeros((5, 128), F32)], axis=0)
        col = block.T[0:32, level : level + 1]
        high = col.astype(BF).astype(F32)
        mid = (col - high).astype(BF).astype(F32)
        low = col - high - mid
        v = jnp.where(lane == 0, high, jnp.where(lane == 1, mid, jnp.where(lane == 2, low, 0.0)))
        return v.astype(BF)

    def fill(outs, cot, b, fine, weights, sent=False):
        n = cot.shape[0]
        room[...] = jnp.zeros((32, CP), BF)
        if fine:
            room[0:n, 0:n0] = cot[:, 0:n0]
        else:
            room[0:n, 0:n1] = cot[:, n0 : n0 + n1]
            room[0:n, MID : MID + n2] = cot[:, n0 + n1 : n0 + n1 + n2]
        base = CP // 128
        if sent:
            base = TAPS + LOW
        for out in outs:
            for i in range(CP // 128 if fine else LOW):
                at = i
                if sent:
                    at = TAPS + i if i < LOW else 9 + i - LOW
                out[at] = room[:, 128 * i : 128 * (i + 1)]
            if not fine and not sent:
                out[LOW : CP // 128] = jnp.zeros((CP // 128 - LOW, 32, 128), BF)
            if fine and sent:
                out[9 + CP // 128 - LOW] = jnp.zeros((32, 128), BF)
            for slot in range(2):
                level = 0 if fine else 1 + slot
                out[base + 2 * slot] = jnp.zeros((32, 128), BF)
                if weights:
                    out[base + 2 * slot, 0:n] = cw[level]
                out[base + 2 * slot + 1] = biases(b, level)

    for group in range(2):

        @pl.when(meta[0] == group)
        def _():
            fill([own], ccot, cb, group == 0, True)
            fill([box], bcot, bb, group == 0, False)

        @pl.when(meta[0] != group)
        def _():
            fill([second, second_cross], ccot, cb, group == 0, True, True)

    for copy in copies:
        copy.wait()

    @pl.when(meta[0] == 0)
    def _():
        second[9:18] = spare[0]
        second_cross[9:18] = spare[1]


def call(body, outs, scratch, args, last=False, limit=VMEM, in_place=(), aliases={}, flops=10**6):
    final = range(len(outs)) if last is True else last or ()

    def space(i):
        return pl.BlockSpec(memory_space=pl.ANY if i in in_place else pltpu.VMEM)

    def placed(units, *refs):
        body(position(units), *refs)

    return pl.pallas_call(
        placed if args[0].dtype == jnp.int32 else body,
        out_shape=[(jax.ShapeDtypeStruct if i in final else pltpu.VMEM)(*o) for i, o in enumerate(outs)],
        in_specs=[space(i) for i in range(len(args))],
        out_specs=[space(len(args) + i) for i in range(len(outs))],
        scratch_shapes=[s if callable(getattr(s, "get_ref_aval", None)) else pltpu.VMEM(*s) for s in scratch],
        input_output_aliases=aliases,
        compiler_params=pltpu.CompilerParams(vmem_limit_bytes=limit),
        cost_estimate=pl.CostEstimate(flops=flops, bytes_accessed=10**4, transcendentals=0),
    )(*args)


def shards(f0, f1, f2, units, s0, s1, s2, conv, gains, shifts, cw, cb, bw, bb, ccot, bcot):
    dp = lax.axis_size("dp")
    c = lax.axis_index("chan")
    group, branch = c // 2, c % 2
    fine = group == 0
    direct = dp == 8
    meta = jnp.broadcast_to(units, (8, 128))
    n0, n1, n2 = f0.shape[2], f1.shape[2], f2.shape[2]

    def across(v):
        return lax.ppermute(v, "chan", [(i, i ^ 2) for i in range(4)])

    def diagonal(v):
        return lax.ppermute(v, "chan", [(i, i ^ 3) for i in range(4)])

    def beside(v, pairs=((0, 1), (1, 0), (2, 3), (3, 2))):
        return lax.ppermute(v, "chan", list(pairs))

    def exchange(st, *hold):
        st, *hold = lax.optimization_barrier((st, *hold))
        st = lax.all_to_all(st, "dp", 0, 0, tiled=True)
        return lax.optimization_barrier((st, *hold)) if hold else st

    def after(v, *others):
        return lax.optimization_barrier((v, *others))[0]

    def over_z(v):
        if not direct:
            return v
        parts = []
        for k in range(4):
            pairs = [
                (8 * z + 4 * y + i, 8 * ((i + k) % 4) + 4 * y + z) for z in range(4) for y in range(2) for i in range(4)
            ]
            parts.append(lax.ppermute(v, ("dp", "chan"), pairs))
        return parts

    def everywhere(parts):
        if direct:
            return parts + [over_y(p) for p in parts]
        v = lax.all_to_all(parts.reshape(4, 2, *parts.shape[1:]), "chan", 0, 0, tiled=True)
        return [v[-k % 4, k // 4] for k in range(8)]

    def joined(*parts):
        return jnp.concatenate(parts, axis=-3)

    def over_y(v):
        return lax.ppermute(v, "dp", [(i, i ^ 1) for i in range(8)])

    def along_z(kept, got):
        shape = (sum(v.shape[1] for v in kept), 16, 128)
        outs = [(shape, F32)] + [(shape, BF)] * 3
        own, *rest = call(functools.partial(add_kernel, len(kept)), outs, [], (meta, *kept, *got))
        return [own] + [lax.ppermute(v, "dp", [(i, i ^ (2 * k + 2)) for i in range(8)]) for k, v in enumerate(rest)]

    def reduce(v):
        return lax.optimization_barrier(lax.psum(v.astype(F32), "dp")).astype(BF)

    own, send = call(
        pack_kernel,
        [((32, WIDE), BF), ((32, WIDE), BF)],
        [((64, 32), F32)],
        (f0[0], f1[0], f2[0].T, s0, s1, s2, gains.transpose(1, 0, 2), shifts.transpose(1, 0, 2), bw.transpose(1, 0, 2)),
        limit=WHOLE,
    )
    far_u = across(send)
    own_pred, box_pred, send1, send1_cross, send2, send2_cross = call(
        functools.partial(pred_kernel, (n0, n1, n2)),
        [((CLS, 32, 128), BF)] * 2 + [((TAPS, 32, 128), BF)] * 2 + [((SECOND, 32, 128), BF)] * 2,
        [((32, CP), BF), ((2, 9, 32, 128), BF), pltpu.SemaphoreType.DMA((2, 2, 2))],
        (meta, ccot[0], cw, cb, bcot[0], after(bb, own), conv),
        limit=WHOLE,
        in_place=(6,),
        flops=2 * 10**9,
    )
    near = beside(after(conv, own))
    far_u = after(far_u, near, send2)
    u = (own, far_u, beside(own), beside(far_u))
    to_class = ((1, 0), (3, 2))
    near_pred = beside(own_pred, to_class)

    def weights_of(layer, far, cross):
        return call(
            functools.partial(weight_kernel, layer),
            [((2, 128, 1152), BF), ((2, 1152, 128), BF)],
            [],
            (meta, conv, near, far, cross),
        )

    canvas = (PX, 128)
    stat = (dp, 8, 128)
    moved = [((PX + 16, 128), F32), ((3, PX + 2 * ST, 128), BF)]
    y0, st, cnt, par = call(
        stem_kernel,
        [(canvas, F32), (stat, F32), ((8, 128), F32), ((64, 128), F32)],
        [((512, CP), BF), ((128, 768), BF), ((CP, 128), F32)],
        (meta, *u),
    )
    far1, cross1 = across(after(send1, far_u)), diagonal(after(send1_cross, far_u))
    st, near_pred = exchange(st, near_pred)
    far1, cross1 = after((far1, cross1), st)
    far2, cross2 = across(after(send2, far1)), diagonal(after(send2_cross, cross1))
    w1, w1_tall = weights_of(0, far1, cross1)
    forward_outs = [(canvas, BF), (canvas, F32), (stat, F32), ((16, 128), F32)]
    act0, y1, st, cst0 = call(functools.partial(forward_kernel, True), forward_outs, moved, (meta, y0, st, cnt, w1, par))
    st = exchange(st)
    far2, cross2 = after((far2, cross2), st)
    w2, w2_tall = weights_of(1, far2, cross2)
    act1, y2, st, cst1 = call(
        functools.partial(forward_kernel, False), forward_outs, moved, (meta, y1, st, cnt, w2, par)
    )
    st = exchange(st)
    dz2, st, cst2, x2, cot, wp = call(
        heads_kernel,
        [(canvas, F32), (stat, F32), ((16, 128), F32), ((CP, 256), BF), ((128, CP), BF), ((2, 128, 256), BF)],
        [(canvas, F32), ((CP, 128), F32)],
        (meta, y2, st, par, own_pred, far2, near_pred, cross2, box_pred),
    )
    gw, mine, near, far, cross = call(
        logits_kernel, [((8, 3, 16, 128), BF)] + [((32, CP), BF)] * 4, [((128, CP), BF)], (meta, x2, cot, wp)
    )
    near, far, cross = beside(near), across(far), diagonal(cross)
    st = exchange(after(st, gw))
    st, near, far, cross = lax.optimization_barrier((st, near, far, cross))
    back_scratch = moved + [((128, PX), BF)]
    dz1, st, sums2, wg2, send2 = call(
        second_back_kernel,
        [(canvas, F32), (stat, F32), ((8, 128), F32), ((8, 21, 16, 128), BF), ((4, 21, 16, 128), BF)],
        back_scratch,
        (meta, dz2, y2, cst2, st, w2_tall, act1, y1, cst1, gw),
    )
    got2 = over_y(send2) if direct else reduce(wg2)
    st, got2 = lax.optimization_barrier((exchange(after(st, send2)), got2))
    d0, st, sums1, wg1, send1 = call(
        first_back_kernel,
        [((PX + 32, 128), BF), (stat, F32), ((8, 128), F32), ((8, 18, 16, 128), BF), ((4, 18, 16, 128), BF)],
        back_scratch,
        (meta, dz1, y1, cst1, st, w1_tall, act0, y0, cst0),
    )
    got1 = over_y(send1) if direct else reduce(wg1)
    d0_other = beside(d0)
    if direct:
        pair = (2, 21, 16, 128)
        own2, send2 = call(halve_kernel, [(pair, F32), (pair, BF)], [], (meta, wg2, after(got2, d0)))
        got2 = lax.ppermute(send2, "dp", [(i, i ^ 2) for i in range(8)])
        (st,) = call(both_kernel, [(stat, F32)], [], (after(st, own2), d0_other))
        st = exchange(st)
        (st,) = call(total_kernel, [((1, 8, 128), F32)], [], (st,))
        st, got1, got2 = lax.optimization_barrier((st, got1, got2))
        own2, send2 = call(again_kernel, [(pair[1:], F32), (pair[1:], BF)], [], (meta, own2, got2))
        got2 = lax.ppermute(send2, "dp", [(i, i ^ 4) for i in range(8)])
    else:
        (st,) = call(both_kernel, [(stat, F32)], [], (st, d0_other))
        st = exchange(st)
    own, other, gs, gs_send, norm = call(
        final_kernel,
        [((32, CP), BF), ((32, CP), BF), ((8, 3, 16, 128), BF), ((4, 3, 16, 128), BF), ((1, 16, 128), BF)],
        [
            ((8, 128), F32),
            ((512, CP), BF),
            ((128, 768), BF),
            (canvas, F32),
            ((CP, 128), F32),
            ((128, CP), BF),
            ((512, CP), BF),
            ((6, 128, 128), BF),
        ],
        (meta, d0, d0_other, y0, cst0, st, sums1, sums2, *u),
    )
    if not direct:
        received = across(other)
    if direct:
        parts1 = along_z([wg1, gs], [got1, over_y(gs_send)])
        received = across(after(other, parts1[0]))
        total, extra = call(
            sum_kernel, [((11, 16, 128), BF), ((10, 16, 128), BF)], [], (meta, own2, after(got2, parts1[0]))
        )
        extra = lax.ppermute(extra, "chan", [(2, 0), (3, 1)])
        extra, received = lax.optimization_barrier((extra, received))
        (grads,) = call(join_kernel, [((32, 16, 128), BF)], [], (meta, *parts1, total, extra, norm))
    else:
        gs = reduce(gs)
        extra = lax.ppermute(got2[:, 9:20], "chan", [(2, 0), (3, 1)])
        third = jnp.where(fine, extra[:, :9], got1[:, 9:18])
        stems = jnp.where(fine, joined(gs[:, :1], extra[:, 10:], gs[:, 2:]), gs)
        bias = got2[:, 20]
        turned = jnp.pad(bias[:, :, :2].transpose(0, 2, 1), ((0, 0), (0, 0), (0, 112)))
        biases = jnp.where(branch == 0, turned, jnp.broadcast_to(bias[:, :1], turned.shape))
        norm = jnp.broadcast_to(norm, (8, 16, 128)).at[:, 12:14].set(biases)[:, None]
        grads = joined(got1[:, :9], got2[:, :9], third, got2[:, 18:19], stems, norm)
    grads = everywhere(over_z(grads))

    room = [((4, 3, conv.shape[2], 16, 128), F32), pltpu.SemaphoreType.DMA((4, 3))]
    rows = [(cw.shape, F32), (cb.shape, F32), ((5, 3, 32), F32), (s0.shape, F32), (s1.shape, F32), (s2.shape, F32)]
    wholes = [(bb.shape, F32), ((5, 3, 32), F32), ((5, 3, 32), F32)]
    grad_conv, *half, grad_bb, grad_gains, grad_shifts = call(
        near_out_kernel, [(conv.shape, F32)] + rows + wholes, room, (meta, *grads[:4]), (0, 7, 8, 9), in_place=(5,)
    )
    mine, own = after((mine, own), *half)
    box_rows, class_rows = bcot.shape[1], ccot.shape[1]
    class_out, box_out = call(
        functools.partial(class_out_kernel, (n0, n1, n2)),
        [((class_rows, n0 + n1 + n2), BF), ((box_rows, n0 + n1 + n2), BF)],
        [],
        (meta, mine, near, far, cross),
        True,
    )
    grad_fine, grad_mid, grad_coarse = call(
        feature_out_kernel,
        [(f0.shape[1:], BF), (f1.shape[1:], BF), ((n2, f2.shape[1]), BF)],
        [],
        (meta, own, received),
        True,
    )

    grad_conv, grad_cw, grad_cb, grad_bw, grad_s0, grad_s1, grad_s2 = call(
        far_out_kernel,
        [(conv.shape, F32)] + rows,
        room,
        (meta, *grads[4:], grad_conv, *half),
        True,
        in_place=(5, 12),
        aliases={5: 0},
    )
    return (
        class_out[None],
        box_out[None],
        grad_fine[None],
        grad_mid[None],
        grad_coarse.T[None],
        grad_s0,
        grad_s1,
        grad_s2,
        grad_conv,
        grad_gains.transpose(1, 0, 2),
        grad_shifts.transpose(1, 0, 2),
        grad_cw,
        grad_cb,
        grad_bw.transpose(1, 0, 2),
        grad_bb,
    )


def solution(mesh):
    placed = (
        P("dp", "chan", None),
        P("dp", "chan", None),
        P("dp", "chan", None),
        P("dp"),
        P("chan", None),
        P("chan", None),
        P("chan", None),
        P(None, None, None, "chan", None),
        P(None, None, "chan"),
        P(None, None, "chan"),
        P(None, "chan", None),
        P(None, "chan"),
        P(None, None, "chan"),
        P(),
        P("dp", "chan", None),
        P("dp", None, None),
    )
    return jax.shard_map(
        shards,
        mesh=mesh,
        in_specs=placed,
        out_specs=(
            P("dp", "chan", None),
            P("dp", None, None),
            P("dp", "chan", None),
            P("dp", "chan", None),
            P("dp", "chan", None),
            P("chan", None),
            P("chan", None),
            P("chan", None),
            P(None, None, None, "chan", None),
            P(None, None, "chan"),
            P(None, None, "chan"),
            P(None, "chan", None),
            P(None, "chan"),
            P(None, None, "chan"),
            P(),
        ),
        check_vma=False,
    )
```
